32 devices in a mesh: dp: 8 (over y, x, core), fsdp: 4 (over z).
Axes of the slice: x: 2, y: 2, z: 4, core: 2. Of those that a mesh axis runs over, the one named last changes fastest.
Arguments:
- activations: bfloat16 [16, 1152, 2048], P('dp', 'fsdp'), may hold values from -6 to 6
- cotangent: bfloat16 [16, 1152, 2048], P('dp', 'fsdp'), may hold values from -6 to 6
- continuation_lengths: int32 [16, 2], P('dp'), may hold values from 16 to 64, as said below
- query_weight: float32 [2048, 2048], P('dp', 'fsdp'), may hold values from -0.125 to 0.125
- key_weight: float32 [2048, 1024], P('dp', 'fsdp'), may hold values from -0.125 to 0.125
- value_weight: float32 [2048, 1024], P('dp', 'fsdp'), may hold values from -0.125 to 0.125
- output_weight: float32 [2048, 2048], P('dp', 'fsdp'), may hold values from -0.5 to 0.5
- gate_weight: float32 [2048, 8192], P('dp', 'fsdp'), may hold values from -0.125 to 0.125
- up_weight: float32 [2048, 8192], P('dp', 'fsdp'), may hold values from -0.125 to 0.125
- down_weight: float32 [8192, 2048], P('dp', 'fsdp'), may hold values from -0.0625 to 0.0625
- attention_gain: float32 [2048], replicated, may hold values from 0.5 to 1.5
- feedforward_gain: float32 [2048], replicated, may hold values from 0.5 to 1.5
- moment_query: float32 [2048, 2048], P('dp', 'fsdp'), may hold values from -4 to 4
- moment_key: float32 [2048, 1024], P('dp', 'fsdp'), may hold values from -4 to 4
- moment_value: float32 [2048, 1024], P('dp', 'fsdp'), may hold values from -4 to 4
- moment_output: float32 [2048, 2048], P('dp', 'fsdp'), may hold values from -4 to 4
- moment_gate: float32 [2048, 8192], P('dp', 'fsdp'), may hold values from -4 to 4
- moment_up: float32 [2048, 8192], P('dp', 'fsdp'), may hold values from -4 to 4
- moment_down: float32 [8192, 2048], P('dp', 'fsdp'), may hold values from -4 to 4
- moment_attention: float32 [2048], replicated, may hold values from -4 to 4
- moment_feedforward: float32 [2048], replicated, may hold values from -4 to 4
Outputs:
- outputs: bfloat16 [16, 1152, 2048], P('dp', 'fsdp')
- input_grad: bfloat16 [16, 1152, 2048], P('dp', 'fsdp')
- grad_norm: float32 [], replicated
- moment_query_next: float32 [2048, 2048], P('dp', 'fsdp')
- moment_key_next: float32 [2048, 1024], P('dp', 'fsdp')
- moment_value_next: float32 [2048, 1024], P('dp', 'fsdp')
- moment_output_next: float32 [2048, 2048], P('dp', 'fsdp')
- moment_gate_next: float32 [2048, 8192], P('dp', 'fsdp')
- moment_up_next: float32 [2048, 8192], P('dp', 'fsdp')
- moment_down_next: float32 [8192, 2048], P('dp', 'fsdp')
- moment_attention_next: float32 [2048], replicated
- moment_feedforward_next: float32 [2048], replicated
- query_weight_next: float32 [2048, 2048], P('dp', 'fsdp')
- key_weight_next: float32 [2048, 1024], P('dp', 'fsdp')
- value_weight_next: float32 [2048, 1024], P('dp', 'fsdp')
- output_weight_next: float32 [2048, 2048], P('dp', 'fsdp')
- gate_weight_next: float32 [2048, 8192], P('dp', 'fsdp')
- up_weight_next: float32 [2048, 8192], P('dp', 'fsdp')
- down_weight_next: float32 [8192, 2048], P('dp', 'fsdp')
- attention_gain_next: float32 [2048], replicated
- feedforward_gain_next: float32 [2048], replicated
The draws below stay inside these ranges and needn't reach their ends.
Inputs may be any that keep to these rules, and one draw needn't show every extreme that they name: `continuation_lengths`: every group has one continuation with all 64 tokens live.
All inputs are finite; a program needn't handle non-finite values.
Results may differ from the reference program's by a relative error of at most 0.024.
Values may be sent and summed in bfloat16 or wider, within the bound.
A program may use at most 512 MiB of HBM per device.

```python
import math
from functools import reduce
import jax
import jax.numpy as jnp
from jax import lax

D = 2048
HEADS = 8
KV_HEADS = 4
HEAD = 256
FF = 8192
PROMPT = 1024
CONT = 64
NCONT = 2
KV_DIM = 1024
GROUP_TOK = 1152
GROUPS = 16


def draw_continuation_lengths(key, part):
    key = jax.random.fold_in(key, 7)
    first_key, second_key = jax.random.split(key)
    lengths = jax.random.randint(first_key, (GROUPS, NCONT), CONT // 4, CONT + 1)
    longest = jax.random.randint(second_key, (GROUPS, 1), 0, NCONT)
    slots = jnp.arange(NCONT, dtype=jnp.int32)[None, :]
    return jnp.where(slots == longest, CONT, lengths).astype(jnp.int32)


def block_levels(rng, dims, shards, least, largest):
    def one(axis_at, shards_of):
        heights = jax.random.uniform(jax.random.fold_in(jax.random.fold_in(rng, 6), axis_at), (shards_of,), jnp.float32, least / len(shards), largest / len(shards))
        return jnp.repeat(jnp.exp(heights), dims[axis_at] // shards_of).reshape((-1,) + (1,) * (len(dims) - axis_at - 1))

    level = one(*shards[0])
    for cut in shards[1:]:
        level = level * one(*cut)
    return level


def noise(rng, extent, scale, most, pieces=(), held_as=jnp.bfloat16):
    array = scale * jax.random.normal(rng, extent, jnp.float32)
    if pieces:
        array = array * block_levels(rng, extent, pieces, -0.22, 0.18)
    return jnp.clip(array, -most, most).astype(held_as)


def setup_inputs(seed: int = 0) -> dict:
    seeds = jax.random.split(jax.random.key(seed), 22)
    activations = noise(seeds[0], (GROUPS, GROUP_TOK, D), 1.0, 6.0, ((0, 8), (1, 4)))
    cotangent = noise(seeds[1], (GROUPS, GROUP_TOK, D), 1.0, 6.0, ((0, 8), (1, 4)))
    continuation_lengths = draw_continuation_lengths(jax.random.fold_in(seeds[21], 71), 0)
    query_weight = noise(seeds[3], (D, D), D ** -0.5, 0.125, ((0, 8), (1, 4)), jnp.float32)
    key_weight = noise(seeds[4], (D, KV_DIM), D ** -0.5, 0.125, ((0, 8), (1, 4)), jnp.float32)
    value_weight = noise(seeds[5], (D, KV_DIM), D ** -0.5, 0.125, ((0, 8), (1, 4)), jnp.float32)
    output_weight = noise(seeds[6], (D, D), (D // 16) ** -0.5, 0.5, ((0, 8), (1, 4)), jnp.float32)
    gate_weight = noise(seeds[7], (D, FF), D ** -0.5, 0.125, ((0, 8), (1, 4)), jnp.float32)
    up_weight = noise(seeds[8], (D, FF), D ** -0.5, 0.125, ((0, 8), (1, 4)), jnp.float32)
    down_weight = noise(seeds[9], (FF, D), FF ** -0.5, 0.0625, ((0, 8), (1, 4)), jnp.float32)
    attention_gain = jnp.clip(1.0 + 0.1 * jax.random.normal(seeds[10], (D,), jnp.float32), 0.5, 1.5)
    feedforward_gain = jnp.clip(1.0 + 0.1 * jax.random.normal(seeds[11], (D,), jnp.float32), 0.5, 1.5)
    moment_query = noise(seeds[12], (D, D), 0.25, 4.0, ((0, 8), (1, 4)), jnp.float32)
    moment_key = noise(seeds[13], (D, KV_DIM), 0.25, 4.0, ((0, 8), (1, 4)), jnp.float32)
    moment_value = noise(seeds[14], (D, KV_DIM), 0.25, 4.0, ((0, 8), (1, 4)), jnp.float32)
    moment_output = noise(seeds[15], (D, D), 0.25, 4.0, ((0, 8), (1, 4)), jnp.float32)
    moment_gate = noise(seeds[16], (D, FF), 0.25, 4.0, ((0, 8), (1, 4)), jnp.float32)
    moment_up = noise(seeds[17], (D, FF), 0.25, 4.0, ((0, 8), (1, 4)), jnp.float32)
    moment_down = noise(seeds[18], (FF, D), 0.25, 4.0, ((0, 8), (1, 4)), jnp.float32)
    moment_attention = noise(seeds[19], (D,), 0.25, 4.0, (), jnp.float32)
    moment_feedforward = noise(seeds[20], (D,), 0.25, 4.0, (), jnp.float32)
    return {"activations": activations, "cotangent": cotangent, "continuation_lengths": continuation_lengths, "query_weight": query_weight, "key_weight": key_weight, "value_weight": value_weight, "output_weight": output_weight, "gate_weight": gate_weight, "up_weight": up_weight, "down_weight": down_weight, "attention_gain": attention_gain, "feedforward_gain": feedforward_gain, "moment_query": moment_query, "moment_key": moment_key, "moment_value": moment_value, "moment_output": moment_output, "moment_gate": moment_gate, "moment_up": moment_up, "moment_down": moment_down, "moment_attention": moment_attention, "moment_feedforward": moment_feedforward}


@jax.custom_vjp
def low(v):
    return lax.optimization_barrier(v.astype(jnp.bfloat16)).astype(jnp.float32)

@jax.custom_vjp
def low_back(v):
    return v

def low_keep(v):
    return (low(v), None)

def low_pass(kept, grad):
    return (grad,)

def back_keep(v):
    return (v, None)

def back_low(kept, grad):
    return (low(grad),)
low.defvjp(low_keep, low_pass)
low_back.defvjp(back_keep, back_low)
epsilon = 1e-06
rope_base = 1000042.0
step_size = 0.2
gain_step = 4.0
decay_rate = 0.1
clip_level = 0.25
floor_score = -1e+30

def product(left, right):
    return jnp.dot(left, right, precision=lax.Precision.HIGHEST, preferred_element_type=jnp.float32)

def rms_scale(values, gain):
    return values * lax.rsqrt(lax.optimization_barrier(jnp.mean(values * values, axis=-1, keepdims=True)) + epsilon) * gain

def rope_angles(places):
    halfway = HEAD // 2
    freqs = rope_base ** (-(jnp.arange(halfway).astype(jnp.float32) * 2.0 / HEAD))
    angles = places.astype(jnp.float32)[:, None] * freqs[None, :]
    return (jnp.cos(angles), jnp.sin(angles))

def token_places(index):
    inside = index - PROMPT
    return jnp.where(index < PROMPT, index, PROMPT + inside % CONT)

def segment_of(index):
    return jnp.where(index < PROMPT, -1, (index - PROMPT) // CONT)

def visible(query_index, key_index, lengths):
    key_segment = segment_of(key_index)
    key_offset = key_index - PROMPT - key_segment * CONT
    slots = jnp.arange(NCONT, dtype=jnp.int32)
    limits = lax.optimization_barrier(jnp.sum(jnp.where(key_segment[:, None] == slots[None, :], lengths[None, :], 0), axis=1))
    alive = key_offset < limits
    same = segment_of(query_index)[:, None] == key_segment[None, :]
    causal = key_index[None, :] <= query_index[:, None]
    return causal & ((key_index < PROMPT)[None, :] | same & alive[None, :])

def rotate(values, cosine, sine):
    halfway = values.shape[-1] // 2
    first, second = (values[..., :halfway], values[..., halfway:])
    cosine, sine = (cosine[:, None, :], sine[:, None, :])
    return jnp.concatenate([first * cosine - second * sine, second * cosine + first * sine], axis=-1)

def layer(weight_set, gain_set, inputs, lengths):
    query_weight, key_weight, value_weight, output_weight, gate_weight, up_weight, down_weight = weight_set
    attention_gain, feedforward_gain = gain_set
    index = jnp.arange(GROUP_TOK, dtype=jnp.int32)
    cosine, sine = rope_angles(token_places(index))
    allowed = visible(index, index, lengths)
    normed = low(rms_scale(inputs, attention_gain))
    queries = low_back(product(normed, query_weight)).reshape(GROUP_TOK, HEADS, HEAD)
    keys = low_back(product(normed, key_weight)).reshape(GROUP_TOK, KV_HEADS, HEAD)
    values = low(low_back(product(normed, value_weight))).reshape(GROUP_TOK, KV_HEADS, HEAD)
    queries = low(rotate(queries, cosine, sine)).reshape(GROUP_TOK, KV_HEADS, HEADS // KV_HEADS, HEAD)
    keys = low(rotate(keys, cosine, sine))
    scores = jnp.einsum('qgrd,kgd->grqk', queries, keys, precision=lax.Precision.HIGHEST) * (1.0 / math.sqrt(HEAD))
    scores = jnp.where(allowed[None, None], low_back(scores), floor_score)
    probs = low(jax.nn.softmax(scores, axis=-1))
    mixed = jnp.einsum('grqk,kgd->qgrd', probs, values, precision=lax.Precision.HIGHEST).reshape(GROUP_TOK, D)
    mixed = low(low_back(mixed))
    middle = inputs + low_back(product(mixed, output_weight))
    normed_two = low(rms_scale(middle, feedforward_gain))
    gate = low_back(product(normed_two, gate_weight))
    upward = low_back(product(normed_two, up_weight))
    hidden = low(jax.nn.silu(gate) * upward)
    return middle + low_back(product(hidden, down_weight))

def reference(activations, cotangent, continuation_lengths, query_weight, key_weight, value_weight, output_weight, gate_weight, up_weight, down_weight, attention_gain, feedforward_gain, moment_query, moment_key, moment_value, moment_output, moment_gate, moment_up, moment_down, moment_attention, moment_feedforward):
    weight_set = (query_weight, key_weight, value_weight, output_weight, gate_weight, up_weight, down_weight)
    gain_set = (attention_gain, feedforward_gain)

    def group_step(carry, item):
        weight_sums, gain_sums = carry
        inputs, outgrad, lengths = item

        def forward(weights_in, gains_in, values_in):
            return layer(weights_in, gains_in, values_in, lengths)
        result, pullback = jax.vjp(forward, weight_set, gain_set, inputs.astype(jnp.float32))
        weight_grads, gain_grads, input_grad = pullback(outgrad.astype(jnp.float32))
        weight_sums = jax.tree.map(jnp.add, weight_sums, weight_grads)
        gain_sums = jax.tree.map(jnp.add, gain_sums, gain_grads)
        return ((weight_sums, gain_sums), (result.astype(jnp.bfloat16), input_grad.astype(jnp.bfloat16)))
    start_carry = (jax.tree.map(jnp.zeros_like, weight_set), jax.tree.map(jnp.zeros_like, gain_set))
    (weight_sums, gain_sums), (outputs, input_grad) = lax.scan(group_step, start_carry, (activations, cotangent, continuation_lengths))
    gradients = list(weight_sums) + list(gain_sums)
    square_sum = reduce(jnp.add, [jnp.sum(gradient * gradient) for gradient in gradients])
    grad_norm = jnp.sqrt(square_sum)
    entry_count = 0
    for gradient in gradients:
        entry_count = entry_count + gradient.size
    limit = clip_level * math.sqrt(entry_count)
    factor = limit / jnp.maximum(grad_norm, limit)
    old_moments = [moment_query, moment_key, moment_value, moment_output, moment_gate, moment_up, moment_down, moment_attention, moment_feedforward]
    old_params = list(weight_set) + list(gain_set)
    new_moments = [0.5 * moment + 0.5 * factor * gradient for moment, gradient in zip(old_moments, gradients)]
    new_params = []
    for place, param in enumerate(old_params):
        if place < 7:
            new_params.append(param - step_size * (new_moments[place] + decay_rate * param))
        else:
            new_params.append(param - gain_step * new_moments[place])
    return (outputs, input_grad, grad_norm, new_moments[0], new_moments[1], new_moments[2], new_moments[3], new_moments[4], new_moments[5], new_moments[6], new_moments[7], new_moments[8], new_params[0], new_params[1], new_params[2], new_params[3], new_params[4], new_params[5], new_params[6], new_params[7], new_params[8])
```

```python
from functools import reduce
import math

import jax
import jax.numpy as jnp
from jax import lax
from jax.experimental import pallas as pl
from jax.experimental.pallas import tpu as pltpu
from jax.sharding import PartitionSpec as P

D = 2048
HEADS = 8
KV_HEADS = 4
HEAD = 256
FF = 8192
PROMPT = 1024
CONT = 64
NCONT = 2


epsilon = 1e-06
rope_base = 1000042.0
step_size = 0.2
gain_step = 4.0
decay_rate = 0.1
clip_level = 0.25
floor_score = -1e30


def rms_rows(values, gain):
    factor = lax.rsqrt(jnp.mean(values * values, axis=-1, keepdims=True) + epsilon)
    return (values * factor * gain, factor)


def rms_back(values, factor, gain, gradient):
    scaled = values * factor
    gain_grad = jnp.sum(gradient * scaled, axis=0)
    pulled = gradient * gain
    return (
        factor * (pulled - scaled * jnp.mean(pulled * scaled, axis=-1, keepdims=True)),
        gain_grad,
    )


def rope_angles(places):
    halfway = HEAD // 2
    freqs = rope_base ** (-(jnp.arange(halfway).astype(jnp.float32) * 2.0 / HEAD))
    angles = places.astype(jnp.float32)[:, None] * freqs[None, :]
    return (jnp.cos(angles), jnp.sin(angles))


def token_places(index):
    inside = index - PROMPT
    return jnp.where(index < PROMPT, index, PROMPT + inside % CONT)


def segment_of(index):
    return jnp.where(index < PROMPT, -1, (index - PROMPT) // CONT)


def visible(query_index, key_index, lengths):
    key_segment = segment_of(key_index)
    key_offset = key_index - PROMPT - key_segment * CONT
    slots = jnp.arange(NCONT, dtype=jnp.int32)
    limits = jnp.sum(jnp.where(key_segment[:, None] == slots[None, :], lengths[None, :], 0), axis=1)
    alive = key_offset < limits
    same = segment_of(query_index)[:, None] == key_segment[None, :]
    causal = key_index[None, :] <= query_index[:, None]
    return causal & ((key_index < PROMPT)[None, :] | same & alive[None, :])


def rotate(values, cosine, sine):
    halfway = values.shape[-1] // 2
    first, second = (values[..., :halfway], values[..., halfway:])
    cosine, sine = (cosine[:, None, :], sine[:, None, :])
    return jnp.concatenate(
        [first * cosine - second * sine, second * cosine + first * sine], axis=-1
    )


def rotate_back(grads, cosine, sine):
    halfway = grads.shape[-1] // 2
    first, second = (grads[..., :halfway], grads[..., halfway:])
    cosine, sine = (cosine[:, None, :], sine[:, None, :])
    return jnp.concatenate(
        [first * cosine + second * sine, second * cosine - first * sine], axis=-1
    )


def join_blocks(pieces, shard_count):
    height = pieces[0].shape[0]
    return jnp.concatenate(
        [member.reshape(height, shard_count, -1) for member in pieces], axis=2
    ).reshape(height, -1)


def split_blocks(merged, breadths, shard_count):
    height = merged.shape[0]
    blocks = merged.reshape(height, shard_count, -1)
    result = []
    offset = 0
    for breadth in breadths:
        result.append(
            blocks[:, :, offset : offset + breadth].reshape(height, shard_count * breadth)
        )
        offset = offset + breadth
    return result


def ahead(operand, shard):
    return jnp.dot(
        operand,
        lax.all_gather(shard, "fsdp", axis=1, tiled=True),
        preferred_element_type=jnp.float32,
    )


def behind(gradient, shard):
    return lax.dot_general(
        gradient,
        lax.all_gather(shard, "fsdp", axis=1, tiled=True),
        (((1,), (1,)), ((), ())),
        preferred_element_type=jnp.float32,
    )


def weight_term(gradient, operand):
    operand_all = lax.all_gather(operand, "fsdp", axis=0, tiled=True)
    owned_columns = lax.all_to_all(gradient, "fsdp", split_axis=1, concat_axis=0, tiled=True)
    return lax.dot_general(
        owned_columns, operand_all, (((0,), (0,)), ((), ())), preferred_element_type=jnp.float32
    )


def on_device(
    activations,
    cotangent,
    continuation_lengths,
    query_weight,
    key_weight,
    value_weight,
    output_weight,
    gate_weight,
    up_weight,
    down_weight,
    attention_gain,
    feedforward_gain,
    moment_query,
    moment_key,
    moment_value,
    moment_output,
    moment_gate,
    moment_up,
    moment_down,
    moment_attention,
    moment_feedforward,
):
    shard_count = lax.axis_size("fsdp")
    kv_width = KV_HEADS * HEAD
    repeat = HEADS // KV_HEADS
    scale = 1.0 / math.sqrt(HEAD)
    gathered = (
        lax.all_gather(query_weight.astype(jnp.bfloat16), "dp", axis=0, tiled=True),
        lax.all_gather(key_weight.astype(jnp.bfloat16), "dp", axis=0, tiled=True),
        lax.all_gather(value_weight.astype(jnp.bfloat16), "dp", axis=0, tiled=True),
        lax.all_gather(output_weight.astype(jnp.bfloat16), "dp", axis=0, tiled=True),
        lax.all_gather(gate_weight.astype(jnp.bfloat16), "dp", axis=0, tiled=True),
        lax.all_gather(up_weight.astype(jnp.bfloat16), "dp", axis=0, tiled=True),
        lax.all_gather(down_weight.astype(jnp.bfloat16), "dp", axis=0, tiled=True),
    )
    merged_attn = join_blocks(gathered[0:3], 1)
    merged_output = gathered[3]
    merged_ffn = join_blocks(gathered[4:6], 1)
    merged_down = gathered[6]
    query_cols = D // shard_count
    key_cols = kv_width // shard_count
    ffn_cols = FF // shard_count
    attn_breadths = (query_cols, key_cols, key_cols)
    ffn_breadths = (ffn_cols, ffn_cols)
    local_rows = activations.shape[1]
    group_rows = local_rows * shard_count
    query_index = lax.axis_index("fsdp") * local_rows + jnp.arange(local_rows, dtype=jnp.int32)
    key_index = jnp.arange(group_rows, dtype=jnp.int32)
    cosine, sine = rope_angles(token_places(query_index))
    sums = [jnp.zeros((matrix.shape[1], matrix.shape[0]), jnp.float32) for matrix in gathered]
    attention_sum = jnp.zeros((D,), jnp.float32)
    feedforward_sum = jnp.zeros((D,), jnp.float32)
    output_list = []
    input_list = []
    for micro_batch in range(activations.shape[0]):
        allowed = visible(query_index, key_index, continuation_lengths[micro_batch])
        inputs = activations[micro_batch].astype(jnp.float32)
        normed_float, factor_one = rms_rows(inputs, attention_gain)
        normed = normed_float.astype(jnp.bfloat16)
        pre_query, pre_key, pre_value = split_blocks(
            ahead(normed, merged_attn), attn_breadths, shard_count
        )
        queries = (
            rotate(pre_query.reshape(local_rows, HEADS, HEAD), cosine, sine)
            .astype(jnp.bfloat16)
            .reshape(local_rows, KV_HEADS, repeat, HEAD)
        )
        keys = rotate(pre_key.reshape(local_rows, KV_HEADS, HEAD), cosine, sine).astype(
            jnp.bfloat16
        )
        values = pre_value.astype(jnp.bfloat16).reshape(local_rows, KV_HEADS, HEAD)
        keys_all, values_all = (
            lax.all_gather(keys, "fsdp", axis=0, tiled=True),
            lax.all_gather(values, "fsdp", axis=0, tiled=True),
        )
        raw = (
            jnp.einsum("qgrd,kgd->grqk", queries, keys_all, preferred_element_type=jnp.float32)
            * scale
        )
        raw = jnp.where(allowed[None, None], raw, floor_score)
        highest = jnp.max(raw, axis=-1, keepdims=True)
        exponent = jnp.exp(raw - highest)
        denominator = jnp.sum(exponent, axis=-1, keepdims=True)
        logsum = highest + jnp.log(denominator)
        probs_low = (exponent / denominator).astype(jnp.bfloat16)
        mixed = (
            jnp.einsum("grqk,kgd->qgrd", probs_low, values_all, preferred_element_type=jnp.float32)
            .reshape(local_rows, D)
            .astype(jnp.bfloat16)
        )
        middle = inputs + ahead(mixed, merged_output)
        normed_two_float, factor_two = rms_rows(middle, feedforward_gain)
        normed_two = normed_two_float.astype(jnp.bfloat16)
        gate, upward = split_blocks(ahead(normed_two, merged_ffn), ffn_breadths, shard_count)
        sigmoid = jax.nn.sigmoid(gate)
        swish = gate * sigmoid
        hidden = (swish * upward).astype(jnp.bfloat16)
        result = middle + ahead(hidden, merged_down)
        output_list.append(result.astype(jnp.bfloat16))
        out_grad = cotangent[micro_batch]
        hidden_grad = behind(out_grad, merged_down)
        sums[6] = sums[6] + weight_term(out_grad, hidden)
        gate_grad = (hidden_grad * upward * sigmoid * (1.0 + gate * (1.0 - sigmoid))).astype(
            jnp.bfloat16
        )
        up_grad = (hidden_grad * swish).astype(jnp.bfloat16)
        ffn_grad = join_blocks((gate_grad, up_grad), shard_count)
        ffn_term = weight_term(ffn_grad, normed_two)
        sums[4] = sums[4] + ffn_term[:ffn_cols]
        sums[5] = sums[5] + ffn_term[ffn_cols:]
        normed_two_grad = behind(ffn_grad, merged_ffn)
        middle_back, feed_gain_grad = rms_back(
            middle, factor_two, feedforward_gain, normed_two_grad
        )
        middle_grad = out_grad.astype(jnp.float32) + middle_back
        branch_grad = middle_grad.astype(jnp.bfloat16)
        sums[3] = sums[3] + weight_term(branch_grad, mixed)
        mixed_grad = (
            behind(branch_grad, merged_output)
            .astype(jnp.bfloat16)
            .reshape(local_rows, KV_HEADS, repeat, HEAD)
        )
        raw_again = (
            jnp.einsum("qgrd,kgd->grqk", queries, keys_all, preferred_element_type=jnp.float32)
            * scale
        )
        raw_again = jnp.where(allowed[None, None], raw_again, floor_score)
        probs_again = jnp.exp(raw_again - logsum)
        value_part = jnp.einsum(
            "grqk,qgrd->kgd",
            probs_again.astype(jnp.bfloat16),
            mixed_grad,
            preferred_element_type=jnp.float32,
        )
        prob_grad = jnp.einsum(
            "qgrd,kgd->grqk", mixed_grad, values_all, preferred_element_type=jnp.float32
        )
        inner = jnp.sum(probs_again * prob_grad, axis=-1, keepdims=True)
        score_grad = (probs_again * (prob_grad - inner)).astype(jnp.bfloat16)
        query_grad = (
            jnp.einsum("grqk,kgd->qgrd", score_grad, keys_all, preferred_element_type=jnp.float32)
            * scale
        )
        key_part = (
            jnp.einsum("grqk,qgrd->kgd", score_grad, queries, preferred_element_type=jnp.float32)
            * scale
        )
        key_grad, value_grad = (
            lax.psum_scatter(
                key_part.astype(jnp.bfloat16), "fsdp", scatter_dimension=0, tiled=True
            ).astype(jnp.float32),
            lax.psum_scatter(
                value_part.astype(jnp.bfloat16), "fsdp", scatter_dimension=0, tiled=True
            ).astype(jnp.float32),
        )
        pre_query_grad = (
            rotate_back(query_grad.reshape(local_rows, HEADS, HEAD), cosine, sine)
            .reshape(local_rows, D)
            .astype(jnp.bfloat16)
        )
        pre_key_grad = (
            rotate_back(key_grad, cosine, sine).reshape(local_rows, kv_width).astype(jnp.bfloat16)
        )
        pre_value_grad = value_grad.reshape(local_rows, kv_width).astype(jnp.bfloat16)
        attn_grad = join_blocks((pre_query_grad, pre_key_grad, pre_value_grad), shard_count)
        attn_term = weight_term(attn_grad, normed)
        sums[0] = sums[0] + attn_term[:query_cols]
        sums[1] = sums[1] + attn_term[query_cols : query_cols + key_cols]
        sums[2] = sums[2] + attn_term[query_cols + key_cols :]
        normed_grad = behind(attn_grad, merged_attn)
        input_back, attn_gain_grad = rms_back(inputs, factor_one, attention_gain, normed_grad)
        input_list.append((middle_grad + input_back).astype(jnp.bfloat16))
        attention_sum = attention_sum + attn_gain_grad
        feedforward_sum = feedforward_sum + feed_gain_grad
    reduced = (
        lax.psum_scatter(
            sums[0].astype(jnp.bfloat16), "dp", scatter_dimension=1, tiled=True
        ).astype(jnp.float32),
        lax.psum_scatter(
            sums[1].astype(jnp.bfloat16), "dp", scatter_dimension=1, tiled=True
        ).astype(jnp.float32),
        lax.psum_scatter(
            sums[2].astype(jnp.bfloat16), "dp", scatter_dimension=1, tiled=True
        ).astype(jnp.float32),
        lax.psum_scatter(
            sums[3].astype(jnp.bfloat16), "dp", scatter_dimension=1, tiled=True
        ).astype(jnp.float32),
        lax.psum_scatter(
            sums[4].astype(jnp.bfloat16), "dp", scatter_dimension=1, tiled=True
        ).astype(jnp.float32),
        lax.psum_scatter(
            sums[5].astype(jnp.bfloat16), "dp", scatter_dimension=1, tiled=True
        ).astype(jnp.float32),
        lax.psum_scatter(
            sums[6].astype(jnp.bfloat16), "dp", scatter_dimension=1, tiled=True
        ).astype(jnp.float32),
    )
    owner_grads = [owned.T for owned in reduced]
    local_square = reduce(jnp.add, [jnp.sum(owned * owned) for owned in owner_grads])
    attention_total, feedforward_total, square_total = lax.psum(
        (attention_sum, feedforward_sum, local_square), ("dp", "fsdp")
    )
    square_sum = (
        square_total
        + jnp.sum(attention_total * attention_total)
        + jnp.sum(feedforward_total * feedforward_total)
    )
    grad_norm = jnp.sqrt(square_sum)
    entry_count = 2 * D * D + 2 * D * kv_width + 3 * D * FF + 2 * D
    limit = clip_level * math.sqrt(entry_count)
    factor = limit / jnp.maximum(grad_norm, limit)
    gradients = owner_grads + [attention_total, feedforward_total]
    old_moments = [
        moment_query,
        moment_key,
        moment_value,
        moment_output,
        moment_gate,
        moment_up,
        moment_down,
        moment_attention,
        moment_feedforward,
    ]
    old_params = [
        query_weight,
        key_weight,
        value_weight,
        output_weight,
        gate_weight,
        up_weight,
        down_weight,
        attention_gain,
        feedforward_gain,
    ]
    new_moments = [
        0.5 * moment + 0.5 * factor * gradient for moment, gradient in zip(old_moments, gradients)
    ]
    new_params = []
    for place, param in enumerate(old_params):
        if place < 7:
            new_params.append(param - step_size * (new_moments[place] + decay_rate * param))
        else:
            new_params.append(param - gain_step * new_moments[place])
    outputs = jnp.stack(output_list)
    input_grad = jnp.stack(input_list)
    return (
        outputs,
        input_grad,
        grad_norm,
        new_moments[0],
        new_moments[1],
        new_moments[2],
        new_moments[3],
        new_moments[4],
        new_moments[5],
        new_moments[6],
        new_moments[7],
        new_moments[8],
        new_params[0],
        new_params[1],
        new_params[2],
        new_params[3],
        new_params[4],
        new_params[5],
        new_params[6],
        new_params[7],
        new_params[8],
    )


CORE, SIDE_A, SIDE_B = 1, 2, 4
CHIPS = 4
CHUNKS = 4
MB = 1024 * 1024


def across(value, mask):
    count = lax.axis_size("dp")
    return lax.ppermute(value, "dp", [(place, place ^ mask) for place in range(count)])


def along(value, mask):
    count = lax.axis_size("fsdp")
    return lax.ppermute(value, "fsdp", [(place, place ^ mask) for place in range(count)])


def pick(values, index):
    return lax.dynamic_index_in_dim(values, index, 0, keepdims=False)


def to_planes(array, core, plane):
    halves = array.reshape(2, 2, array.shape[1] // 2, array.shape[2]).swapaxes(0, 1)
    keep = pick(halves, core)
    came = across(pick(halves, 1 - core), CORE)
    swap = core == 1
    parts = jnp.concatenate([jnp.where(swap, came, keep), jnp.where(swap, keep, came)])
    found = [pick(parts, plane)]
    for mask in range(1, CHUNKS):
        found.append(along(pick(parts, plane ^ mask), mask))
    stacked = jnp.stack(found)
    return [pick(stacked, chunk ^ plane) for chunk in range(CHUNKS)]


def from_planes(chunks, core, plane):
    stacked = jnp.stack(chunks)
    found = [pick(stacked, plane)]
    for mask in range(1, CHUNKS):
        found.append(along(pick(stacked, plane ^ mask), mask))
    found = jnp.stack(found)
    groups = [pick(found, label ^ plane) for label in range(CHUNKS)]
    pairs = jnp.stack([jnp.stack(groups[:2]), jnp.stack(groups[2:])])
    keep = pick(pairs, core)
    came = across(pick(pairs, 1 - core), CORE)
    swap = core == 1
    return jnp.concatenate([jnp.where(swap, came, keep), jnp.where(swap, keep, came)], axis=1)


def gather_pair(first, second):
    first_near = jnp.stack([first, across(first, SIDE_A)])
    second_near = jnp.stack([second, across(second, SIDE_B)])
    first_far = across(first_near, SIDE_B)
    second_far = across(second_near, SIDE_A)
    own = [first_near, first_far, second_near, second_far]
    return [piece for near in own for piece in (near, across(near, CORE))]


def scatter_pair(partials):
    sums = []
    for side, (own, other) in enumerate(partials):
        last, first = (SIDE_A, SIDE_B) if side == 0 else (SIDE_B, SIDE_A)
        came = across(other, CORE)
        far = (own[2:].astype(jnp.float32) + came[2:].astype(jnp.float32)).astype(jnp.bfloat16)
        came_far = across(far, first)
        near = (
            own[1].astype(jnp.float32)
            + came[1].astype(jnp.float32)
            + came_far[1].astype(jnp.float32)
        ).astype(jnp.bfloat16)
        came_near = across(near, last)
        sums.append(
            own[0].astype(jnp.float32)
            + came[0].astype(jnp.float32)
            + came_far[0].astype(jnp.float32)
            + came_near.astype(jnp.float32)
        )
    return jnp.stack(sums)


def piece_specs(rows, width):
    def first_near(chunk, chip):
        return (jnp.where(chunk == 0, jnp.minimum(chip, 1), 1), 0, 0)

    def first_far(chunk, chip):
        return (jnp.where(chunk == 0, jnp.maximum(chip - 2, 0), 1), 0, 0)

    def second(chunk, chip):
        return (jnp.where(chunk == 0, 0, chip // 2), 0, 0)

    return [
        pl.BlockSpec((1, rows, width), index_map)
        for index_map in (first_near, first_near, first_far, first_far, second, second, second, second)
    ]


def load_pieces(refs, target, chunk, chip):
    rows = target.shape[0] // 2
    choices = (
        (chunk == 0) & (chip < 2),
        (chunk == 0) & (chip >= 2),
        (chunk == 1) & (chip % 2 == 0),
        (chunk == 1) & (chip % 2 == 1),
    )
    for place, chosen in enumerate(choices):

        @pl.when(chosen)
        def _():
            target[:rows] = refs[2 * place][0]
            target[rows:] = refs[2 * place + 1][0]


def scatter_specs(rows, width):
    def first(chunk, chip):
        return (jnp.where(chunk == 0, chip, CHIPS - 1), 0, 0)

    def second(chunk, chip):
        return (jnp.where(chunk == 0, 0, (chip % 2) * 2 + chip // 2), 0, 0)

    return [pl.BlockSpec((1, rows, width), index_map) for index_map in (first, first, second, second)]


def store_partial(refs, value, chunk):
    rows = value.shape[0] // 2
    for place in range(2):

        @pl.when(chunk == place)
        def _():
            refs[2 * place][0] = value[:rows]
            refs[2 * place + 1][0] = value[rows:]


def dot(left, right):
    return jnp.dot(left, right, preferred_element_type=jnp.float32)


def dot_t(left, right):
    return lax.dot_general(
        left, right, (((1,), (1,)), ((), ())), preferred_element_type=jnp.float32
    )


def dot_tn(left, right):
    return lax.dot_general(
        left, right, (((0,), (0,)), ((), ())), preferred_element_type=jnp.float32
    )


def spin(values, cosine, sine):
    halfway = values.shape[1] // 2
    first, second = values[:, :halfway], values[:, halfway:]
    return jnp.concatenate(
        [first * cosine - second * sine, second * cosine + first * sine], axis=1
    )


def spin_back(values, cosine, sine):
    return spin(values, cosine, -sine)


def whole(shape):
    return pl.BlockSpec(shape, lambda *_: (0,) * len(shape), pipeline_mode=pl.Buffered(1))


def params(megabytes):
    return pltpu.CompilerParams(vmem_limit_bytes=megabytes * MB)


def project(pieces, weight, cosine, sine):
    rows, width = pieces[0].shape[1:]
    tokens = 2 * rows

    def kernel(*refs):
        pieces_in, (weight_ref, cosine_ref, sine_ref, out, joined, held) = refs[:8], refs[8:]
        chunk, chip = pl.program_id(0), pl.program_id(1)
        load_pieces(pieces_in, held, chunk, chip)
        values = held[...]
        joined[0, 0] = values
        product = dot(values, weight_ref[...])
        angles = (cosine_ref[0], sine_ref[0])
        query = spin(product[:, :HEAD], *angles) * (1.0 / math.sqrt(HEAD))
        key = spin(product[:, HEAD : 2 * HEAD], *angles)
        out[0, 0] = jnp.concatenate([query, key, product[:, 2 * HEAD :]], axis=1).astype(jnp.bfloat16)

    here = lambda chunk, chip: (chunk, chip, 0, 0)
    table = pl.BlockSpec((1, tokens, HEAD // 2), lambda chunk, chip: (chunk, 0, 0))
    return pl.pallas_call(
        kernel,
        grid=(2, CHIPS),
        in_specs=piece_specs(rows, width) + [whole(weight.shape), table, table],
        out_specs=[
            pl.BlockSpec((1, 1, tokens, 3 * HEAD), here),
            pl.BlockSpec((1, 1, tokens, width), here),
        ],
        out_shape=[
            jax.ShapeDtypeStruct((2, CHIPS, tokens, 3 * HEAD), jnp.bfloat16),
            jax.ShapeDtypeStruct((2, CHIPS, tokens, width), jnp.bfloat16),
        ],
        scratch_shapes=[pltpu.VMEM((tokens, width), jnp.bfloat16)],
        compiler_params=params(40),
        cost_estimate=pl.CostEstimate(
            flops=2 * 2 * CHIPS * tokens * width * 3 * HEAD,
            bytes_accessed=3 * 2 * CHIPS * tokens * width * 2,
            transcendentals=0,
        ),
    )(*pieces, weight, cosine, sine)


def seen(place_q, place_k, chunk, count, tokens, lengths_ref, chip):
    query_index = tokens * chunk + place_q
    key_index = place_k[:, :count]
    ahead_or_here = key_index <= query_index
    if tokens * (chunk + 1) <= PROMPT:
        return ahead_or_here

    def segment(index):
        found = jnp.full(index.shape, -1, jnp.int32)
        for slot in range(NCONT):
            found = jnp.where(index >= PROMPT + slot * CONT, slot, found)
        return found

    key_segment, query_segment = segment(key_index), segment(query_index)
    end = jnp.full(key_index.shape, PROMPT, jnp.int32)
    for slot in range(NCONT):
        end = jnp.where(
            key_segment == slot, PROMPT + slot * CONT + lengths_ref[chip, slot], end
        )
    alive = key_index < end
    return ahead_or_here & ((key_segment < 0) | ((key_segment == query_segment) & alive))


def attend(pair, states, lengths, place_q, place_k, output_weight):
    tokens = states[0].shape[2]
    rows = tokens // 2
    width = output_weight.shape[1]
    blocks = 2 * (pair + 1)

    def kernel(*refs):
        state_refs = refs[: pair + 1]
        lengths_ref, place_q_ref, place_k_ref, weight_ref = refs[pair + 1 : pair + 5]
        mixed_ref, outs, (keys, values) = refs[pair + 5], refs[pair + 6 : pair + 10], refs[pair + 10 :]
        chunk_at, chip = pl.program_id(1), pl.program_id(0)

        @pl.when(chunk_at == 0)
        def _():
            for block in range(blocks):
                ref = state_refs[block // 2]
                span = pl.ds(block * tokens, tokens)
                keys[span] = ref[block % 2, 0, :, HEAD : 2 * HEAD]
                values[span] = ref[block % 2, 0, :, 2 * HEAD :]

        for side in range(2):

            @pl.when(chunk_at == side)
            def _():
                chunk = 2 * pair + side
                count = tokens * (chunk + 1)
                scores = dot_t(state_refs[pair][side, 0, :, :HEAD], keys[:count])
                mask = seen(
                    place_q_ref[...], place_k_ref[...], chunk, count, tokens, lengths_ref, chip
                )
                scores = jnp.where(mask, scores, floor_score)
                highest = jnp.max(scores, axis=1, keepdims=True)
                exponent = jnp.exp(scores - highest)
                total = jnp.sum(exponent, axis=1, keepdims=True)
                probs = (exponent * (1.0 / total)).astype(jnp.bfloat16)
                mixed = dot(probs, values[:count]).astype(jnp.bfloat16)
                mixed_ref[0, 0] = mixed
                store_partial(outs, dot(mixed, weight_ref[...]).astype(jnp.bfloat16), chunk_at)

    turned = [
        pl.BlockSpec(spec.block_shape, (lambda index_map: lambda chip, chunk: index_map(chip, chunk))(index_map))
        for spec, index_map in zip(scatter_specs(rows, width), pair_maps())
    ]
    return pl.pallas_call(
        kernel,
        grid=(CHIPS, 2),
        in_specs=[
            pl.BlockSpec((2, 1, tokens, 3 * HEAD), lambda chip, chunk: (0, chip, 0, 0))
            for _ in range(pair + 1)
        ]
        + [
            pl.BlockSpec(memory_space=pltpu.SMEM),
            whole(place_q.shape),
            whole(place_k.shape),
            whole(output_weight.shape),
        ],
        out_specs=[pl.BlockSpec((1, 1, tokens, HEAD), lambda chip, chunk: (chunk, chip, 0, 0))] + turned,
        out_shape=[jax.ShapeDtypeStruct((2, CHIPS, tokens, HEAD), jnp.bfloat16)]
        + [jax.ShapeDtypeStruct((CHIPS, rows, width), jnp.bfloat16)] * 4,
        scratch_shapes=[pltpu.VMEM((blocks * tokens, HEAD), jnp.bfloat16)] * 2,
        compiler_params=params(40),
        cost_estimate=pl.CostEstimate(
            flops=2 * CHIPS * 2 * tokens * (2 * blocks * tokens * HEAD + HEAD * width),
            bytes_accessed=CHIPS * tokens * (2 * width * 2 + blocks * 3 * HEAD * 2),
            transcendentals=CHIPS * 2 * tokens * blocks * tokens,
        ),
    )(*states[: pair + 1], lengths, place_q, place_k, output_weight)


def pair_maps():
    def first(chip, chunk):
        return (chip, 0, 0)

    def second(chip, chunk):
        return ((chip % 2) * 2 + chip // 2, 0, 0)

    return (first, first, second, second)


def attend_back(pair, pieces, states, lengths, place_q, place_k, output_weight, weight, cosine, sine, carry):
    rows, width = pieces[0].shape[1:]
    tokens = 2 * rows
    blocks = 2 * (pair + 1)
    count_in = 8 + (pair + 1) + 7 + (0 if carry is None else 2)
    earlier = pair > 0

    def kernel(*refs):
        pieces_in, state_refs = refs[:8], refs[8 : 9 + pair]
        lengths_ref, place_q_ref, place_k_ref, out_weight, weight_ref, cosine_ref, sine_ref = refs[
            9 + pair : 16 + pair
        ]
        carried = refs[16 + pair : count_in]
        grads_ref, joined, *outs = refs[count_in : count_in + 6]
        handed = refs[count_in + 6 : count_in + 6 + (2 if earlier else 0)]
        held, keys, values, key_grads, value_grads, query_grads = refs[-6:]
        chip, step = pl.program_id(0), pl.program_id(1)

        def gather(side):
            near, far = (0, 2) if side == 0 else (4, 6)
            chosen = chip < 2 if side == 0 else chip % 2 == 0
            for base, when in ((near, chosen), (far, jnp.logical_not(chosen))):

                @pl.when(when)
                def _():
                    held[side, :rows] = pieces_in[base][0]
                    held[side, rows:] = pieces_in[base + 1][0]

        @pl.when(step == 0)
        def _():
            for block in range(blocks):
                ref = state_refs[block // 2]
                span = pl.ds(block * tokens, tokens)
                keys[span] = ref[block % 2, 0, :, HEAD : 2 * HEAD]
                values[span] = ref[block % 2, 0, :, 2 * HEAD :]
            if carried:
                for block in range(2):
                    span = pl.ds(block * tokens, tokens)
                    key_grads[span] = carried[0][block, 0]
                    value_grads[span] = carried[1][block, 0]
            else:
                key_grads[...] = jnp.zeros_like(key_grads)
                value_grads[...] = jnp.zeros_like(value_grads)
            for side in range(2):
                gather(side)

        for side in range(2):

            @pl.when(step == side)
            def _():
                chunk = 2 * pair + side
                count = tokens * (chunk + 1)
                branch = held[side]
                joined[0, 0] = branch
                mixed_grad = dot_t(branch, out_weight[...]).astype(jnp.bfloat16)
                query = state_refs[pair][side, 0, :, :HEAD]
                scores = dot_t(query, keys[:count])
                mask = seen(
                    place_q_ref[...], place_k_ref[...], chunk, count, tokens, lengths_ref, chip
                )
                scores = jnp.where(mask, scores, floor_score)
                highest = jnp.max(scores, axis=1, keepdims=True)
                exponent = jnp.exp(scores - highest)
                probs = exponent * (1.0 / jnp.sum(exponent, axis=1, keepdims=True))
                value_grads[:count] += dot_tn(probs.astype(jnp.bfloat16), mixed_grad)
                prob_grad = dot_t(mixed_grad, values[:count])
                inner = jnp.sum(probs * prob_grad, axis=1, keepdims=True)
                score_grad = (probs * (prob_grad - inner)).astype(jnp.bfloat16)
                key_grads[:count] += dot_tn(score_grad, query)
                query_grad = dot(score_grad, keys[:count]) * (1.0 / math.sqrt(HEAD))
                query_grads[side] = spin_back(query_grad, cosine_ref[side], sine_ref[side]).astype(
                    jnp.bfloat16
                )

        for side in range(2):

            @pl.when(step == 2 + side)
            def _():
                span = pl.ds((2 * pair + side) * tokens, tokens)
                key_grad = spin_back(key_grads[span], cosine_ref[side], sine_ref[side])
                grads = jnp.concatenate(
                    [
                        query_grads[side],
                        key_grad.astype(jnp.bfloat16),
                        value_grads[span].astype(jnp.bfloat16),
                    ],
                    axis=1,
                )
                grads_ref[0, 0] = grads
                partial = dot_t(grads, weight_ref[...]).astype(jnp.bfloat16)
                outs[2 * side][0] = partial[:rows]
                outs[2 * side + 1][0] = partial[rows:]
                if earlier:
                    span = pl.ds(side * tokens, tokens)
                    handed[0][side, 0] = key_grads[span]
                    handed[1][side, 0] = value_grads[span]

    def piece(index_map):
        return pl.BlockSpec((1, rows, width), index_map)

    first_near = piece(lambda chip, step: (jnp.minimum(chip, 1), 0, 0))
    first_far = piece(lambda chip, step: (jnp.maximum(chip - 2, 0), 0, 0))
    second = piece(lambda chip, step: (chip // 2, 0, 0))
    state = pl.BlockSpec((2, 1, tokens, 3 * HEAD), lambda chip, step: (0, chip, 0, 0))
    carry_spec = pl.BlockSpec((2, 1, tokens, HEAD), lambda chip, step: (0, chip, 0, 0))
    carry_shape = jax.ShapeDtypeStruct((2, CHIPS, tokens, HEAD), jnp.float32)
    return pl.pallas_call(
        kernel,
        grid=(CHIPS, 4),
        in_specs=[first_near, first_near, first_far, first_far, second, second, second, second]
        + [state] * (pair + 1)
        + [
            pl.BlockSpec(memory_space=pltpu.SMEM),
            whole(place_q.shape),
            whole(place_k.shape),
            whole(output_weight.shape),
            whole(weight.shape),
            whole(cosine.shape),
            whole(sine.shape),
        ]
        + ([] if carry is None else [carry_spec] * 2),
        out_specs=[
            pl.BlockSpec((1, 1, tokens, 3 * HEAD), lambda chip, step: (jnp.maximum(step - 2, 0), chip, 0, 0)),
            pl.BlockSpec((1, 1, tokens, width), lambda chip, step: (jnp.minimum(step, 1), chip, 0, 0)),
        ]
        + [pl.BlockSpec((1, rows, width), index_map) for index_map in pair_maps()]
        + ([carry_spec] * 2 if earlier else []),
        out_shape=[
            jax.ShapeDtypeStruct((2, CHIPS, tokens, 3 * HEAD), jnp.bfloat16),
            jax.ShapeDtypeStruct((2, CHIPS, tokens, width), jnp.bfloat16),
        ]
        + [jax.ShapeDtypeStruct((CHIPS, rows, width), jnp.bfloat16)] * 4
        + ([carry_shape] * 2 if earlier else []),
        scratch_shapes=[
            pltpu.VMEM((2, tokens, width), jnp.bfloat16),
            pltpu.VMEM((blocks * tokens, HEAD), jnp.bfloat16),
            pltpu.VMEM((blocks * tokens, HEAD), jnp.bfloat16),
            pltpu.VMEM((blocks * tokens, HEAD), jnp.float32),
            pltpu.VMEM((blocks * tokens, HEAD), jnp.float32),
            pltpu.VMEM((2, tokens, HEAD), jnp.bfloat16),
        ],
        compiler_params=params(56),
        cost_estimate=pl.CostEstimate(
            flops=2 * CHIPS * 2 * tokens * (5 * blocks * tokens * HEAD + 4 * HEAD * width),
            bytes_accessed=CHIPS * tokens * (6 * width * 2 + blocks * 3 * HEAD * 2),
            transcendentals=CHIPS * 2 * tokens * blocks * tokens,
        ),
    )(
        *pieces,
        *states[: pair + 1],
        lengths,
        place_q,
        place_k,
        output_weight,
        weight,
        cosine,
        sine,
        *(() if carry is None else carry),
    )


def feed_forward(pieces, out_grads, weights, units):
    rows, width = pieces[0].shape[1:]
    tokens = 2 * rows
    shards, _, columns = weights.shape
    share = columns // 2

    def kernel(*refs):
        pieces_in, grads_in, weight_ref = refs[:8], refs[8:16], refs[16]
        joined, joined_grad, hidden_ref, unit_grads, *outs = refs[17:29]
        held, held_grad = refs[29:]
        chunk, chip = pl.program_id(0), pl.program_id(1)
        load_pieces(pieces_in, held, chunk, chip)
        load_pieces(grads_in, held_grad, chunk, chip)
        joined[0, 0] = held[...]
        joined_grad[0, 0] = held_grad[...]
        hidden_grad = dot_t(held_grad[:, :columns], weight_ref[0, width:, :])
        for shard in range(1, shards):
            hidden_grad += dot_t(
                held_grad[:, shard * columns : (shard + 1) * columns], weight_ref[shard, width:, :]
            )
        for shard in range(shards):
            both = dot(held[...], weight_ref[shard, :width, :])
            gate, upward = both[:, :share], both[:, share:]
            grad = hidden_grad[:, shard * share : (shard + 1) * share]
            sigmoid = jax.nn.sigmoid(gate)
            swish = gate * sigmoid
            hidden_ref[0, 0, :, shard * share : (shard + 1) * share] = (swish * upward).astype(jnp.bfloat16)
            gate_grad = grad * upward * sigmoid * (1.0 + gate * (1.0 - sigmoid))
            unit_grads[0, 0, :, shard * columns : shard * columns + share] = gate_grad.astype(jnp.bfloat16)
            unit_grads[0, 0, :, shard * columns + share : (shard + 1) * columns] = (grad * swish).astype(
                jnp.bfloat16
            )
        back = dot_t(unit_grads[0, 0, :, :columns], weight_ref[0, :width, :])
        for shard in range(1, shards):
            back += dot_t(
                unit_grads[0, 0, :, shard * columns : (shard + 1) * columns], weight_ref[shard, :width, :]
            )
        store_partial(outs[:4], back.astype(jnp.bfloat16), chunk)
        for shard in range(shards):
            span = slice(shard * columns, (shard + 1) * columns)
            value = dot(hidden_ref[0, 0], weight_ref[shard, width:, :]).astype(jnp.bfloat16)
            for place in range(2):

                @pl.when(chunk == place)
                def _():
                    outs[4 + 2 * place][0, :, span] = value[:rows]
                    outs[5 + 2 * place][0, :, span] = value[rows:]

    here = lambda chunk, chip: (chunk, chip, 0, 0)
    return pl.pallas_call(
        kernel,
        grid=(2, CHIPS),
        in_specs=piece_specs(rows, width) * 2 + [whole(weights.shape)],
        out_specs=[
            pl.BlockSpec((1, 1, tokens, width), here),
            pl.BlockSpec((1, 1, tokens, width), here),
            pl.BlockSpec((1, 1, tokens, units), here),
            pl.BlockSpec((1, 1, tokens, 2 * units), here),
        ]
        + scatter_specs(rows, width) * 2,
        out_shape=[
            jax.ShapeDtypeStruct((2, CHIPS, tokens, width), jnp.bfloat16),
            jax.ShapeDtypeStruct((2, CHIPS, tokens, width), jnp.bfloat16),
            jax.ShapeDtypeStruct((2, CHIPS, tokens, units), jnp.bfloat16),
            jax.ShapeDtypeStruct((2, CHIPS, tokens, 2 * units), jnp.bfloat16),
        ]
        + [jax.ShapeDtypeStruct((CHIPS, rows, width), jnp.bfloat16)] * 8,
        scratch_shapes=[pltpu.VMEM((tokens, width), jnp.bfloat16)] * 2,
        compiler_params=params(60),
        cost_estimate=pl.CostEstimate(
            flops=2 * CHIPS * tokens * width * units * 2 * 6,
            bytes_accessed=2 * CHIPS * tokens * (6 * width + 3 * units) * 2 + weights.size * 2,
            transcendentals=2 * CHIPS * tokens * units,
        ),
    )(*pieces, *out_grads, weights)


def token_dot(left, right):
    return lax.dot_general(
        left.reshape(-1, left.shape[-1]),
        right.reshape(-1, right.shape[-1]),
        (((0,), (0,)), ((), ())),
        preferred_element_type=jnp.float32,
    )


def exchange(value, axis):
    return lax.all_to_all(value, axis, split_axis=0, concat_axis=0, tiled=True)


def plane_device(
    activations,
    cotangent,
    continuation_lengths,
    query_weight,
    key_weight,
    value_weight,
    output_weight,
    gate_weight,
    up_weight,
    down_weight,
    attention_gain,
    feedforward_gain,
    moment_query,
    moment_key,
    moment_value,
    moment_output,
    moment_gate,
    moment_up,
    moment_down,
    moment_attention,
    moment_feedforward,
):
    devices, planes = lax.axis_size("dp"), lax.axis_size("fsdp")
    place, plane = lax.axis_index("dp"), lax.axis_index("fsdp")
    core = place % 2
    low = jnp.bfloat16
    kv_width = KV_HEADS * HEAD
    tokens = activations.shape[1]
    half = tokens // 2

    inputs = to_planes(activations, core, plane)

    in_rows = query_weight.shape[0]
    sub_rows = in_rows // planes
    mixed_kv = jnp.stack([key_weight.astype(low), value_weight.astype(low)], axis=1)
    block = jnp.concatenate([query_weight.astype(low).reshape(in_rows, 2, HEAD), mixed_kv], axis=2)
    block = exchange(block.reshape(planes, sub_rows, 2, 2 * HEAD), "fsdp")
    block = block.transpose(0, 2, 1, 3).reshape(devices, sub_rows, 2 * HEAD)
    block = exchange(block, "dp")
    attention_block = jnp.concatenate(
        [block.reshape(devices * sub_rows, 2 * HEAD), output_weight.astype(low)], axis=0
    )
    attention_all = lax.all_gather(attention_block, "fsdp", axis=0, tiled=False)
    spread = devices * sub_rows
    packed = (
        attention_all[:, :spread]
        .reshape(planes, devices, sub_rows, 2 * HEAD)
        .transpose(1, 0, 2, 3)
        .reshape(D, 2 * HEAD)
    )
    other_half = across(packed[:, HEAD:], CORE)
    key_part = jnp.where(core == 0, packed[:, HEAD:], other_half)
    value_part = jnp.where(core == 0, other_half, packed[:, HEAD:])
    head_weight = jnp.concatenate([packed[:, :HEAD], key_part, value_part], axis=1)
    head_output = attention_all[:, spread:].transpose(1, 0, 2).reshape(HEAD, D)

    strip = 128
    runs = gate_weight.shape[1] // (devices * strip)
    units = runs * strip * planes
    gate_up = jnp.stack(
        [
            gate_weight.astype(low).reshape(in_rows, runs, devices, strip),
            up_weight.astype(low).reshape(in_rows, runs, devices, strip),
        ]
    )
    gate_up = gate_up.transpose(3, 1, 0, 2, 4).reshape(devices, in_rows, 2 * runs * strip)
    gate_up = exchange(gate_up, "dp").reshape(devices * in_rows, 2 * runs * strip)
    down_columns = down_weight.shape[1]
    down = exchange(down_weight.astype(low).reshape(devices, strip, down_columns), "dp")
    feed_block = jnp.concatenate([gate_up, down.reshape(devices * strip, down_columns)], axis=0)
    feed_weights = lax.all_gather(feed_block, "fsdp", axis=0, tiled=False)

    out_grads = to_planes(cotangent, core, plane)

    all_lengths = lax.all_gather(continuation_lengths, "dp", axis=0, tiled=True)
    first_core = place - core
    lengths = jnp.stack(
        [
            pick(all_lengths, ((first_core ^ mask) + plane // 2) * 2 + plane % 2)
            for mask in (0, SIDE_A, SIDE_B, SIDE_A + SIDE_B)
        ]
    )

    inside = jnp.concatenate(
        [core * half + jnp.arange(half), (1 - core) * half + jnp.arange(half)]
    ).astype(jnp.int32)
    order = (tokens * jnp.arange(CHUNKS, dtype=jnp.int32)[:, None] + inside[None, :]).reshape(-1)
    cosine, sine = rope_angles(token_places(order))
    cosine = cosine.reshape(2, 2, tokens, HEAD // 2)
    sine = sine.reshape(2, 2, tokens, HEAD // 2)
    place_q, place_k = inside[:, None], order[None, :]

    xs, ones, states, joins, mixes, middles, twos = [], [], [], [], [], [], []
    near_pieces, grad_pieces, grad_rows = [], [], []
    for pair in range(2):
        own = jnp.stack(inputs[2 * pair : 2 * pair + 2]).astype(jnp.float32)
        normed, factor = rms_rows(own, attention_gain)
        normed = normed.astype(low)
        xs.append(own)
        ones.append(factor)
        state, joined = project(
            gather_pair(normed[0], normed[1]), head_weight, cosine[pair], sine[pair]
        )
        states.append(state)
        joins.append(joined)
    for pair in range(2):
        grad_rows.append(out_grads[2 * pair : 2 * pair + 2])
        grad_pieces.append(gather_pair(*grad_rows[pair]))
    for pair in range(2):
        mixed, *partials = attend(pair, states, lengths, place_q, place_k, head_output)
        mixes.append(mixed)
        middle = xs[pair] + scatter_pair([partials[:2], partials[2:]])
        middles.append(middle)
        normed_two, factor_two = rms_rows(middle, feedforward_gain)
        normed_two = normed_two.astype(low)
        twos.append(factor_two)
        near_pieces.append(gather_pair(normed_two[0], normed_two[1]))

    feed_sums, out_chunks, branches = [], [], []
    middle_grads, branch_pieces = [None, None], [None, None]
    feedforward_sum = jnp.zeros((D,), jnp.float32)
    late_outputs = [None, None]
    for pair in (1, 0):
        joined_two, joined_grad, hidden, unit_grads, *partials = feed_forward(
            near_pieces[pair], grad_pieces[pair], feed_weights, units
        )
        feed_sums.append((joined_two, joined_grad, hidden, unit_grads))
        normed_grad = scatter_pair([partials[0:2], partials[2:4]])
        back, gain_grad = rms_back(
            middles[pair].reshape(-1, D), twos[pair].reshape(-1, 1), feedforward_gain, normed_grad.reshape(-1, D)
        )
        feedforward_sum = feedforward_sum + gain_grad
        middle_grads[pair] = jnp.stack(grad_rows[pair]).astype(jnp.float32) + back.reshape(2, half, D)
        branch = middle_grads[pair].astype(low)
        branch_pieces[pair] = gather_pair(branch[0], branch[1])
        late_outputs[pair] = partials[4:]
    gate_up_sum = reduce(jnp.add, [token_dot(two, grads) for two, _, _, grads in feed_sums])
    down_sum = reduce(jnp.add, [token_dot(hidden, grads) for _, grads, hidden, _ in feed_sums])
    feed_grad = jnp.concatenate([gate_up_sum.astype(low), down_sum.astype(low)], axis=0)
    feed_grad = feed_grad.reshape(-1, planes, 2 * runs * strip).transpose(1, 0, 2)
    feed_grad = lax.psum_scatter(feed_grad, "fsdp", scatter_dimension=0, tiled=False)
    gate_up_owned = exchange(feed_grad[:D].reshape(devices, in_rows, 2 * runs * strip), "dp")
    gate_up_owned = gate_up_owned.reshape(devices, in_rows, 2, runs, strip).transpose(2, 1, 3, 0, 4)
    gate_up_owned = gate_up_owned.reshape(2, in_rows, runs * devices * strip)
    down_owned = exchange(feed_grad[D:].reshape(devices, strip, down_columns), "dp")
    down_owned = down_owned.reshape(devices * strip, down_columns)

    out_chunks = [None] * CHUNKS
    for pair in range(2):
        result = middles[pair] + scatter_pair([late_outputs[pair][0:2], late_outputs[pair][2:4]])
        out_chunks[2 * pair], out_chunks[2 * pair + 1] = result[0].astype(low), result[1].astype(low)
    outputs = from_planes(out_chunks, core, plane)

    carry = None
    in_chunks = [None] * CHUNKS
    head_terms, output_terms = [], []
    attention_sum = jnp.zeros((D,), jnp.float32)
    for pair in (1, 0):
        head_grads, joined_branch, *rest = attend_back(
            pair,
            branch_pieces[pair],
            states,
            lengths,
            place_q,
            place_k,
            head_output,
            head_weight,
            cosine[pair],
            sine[pair],
            carry,
        )
        partials, carry = rest[:4], rest[4:]
        head_terms.append(token_dot(joins[pair], head_grads))
        output_terms.append(token_dot(mixes[pair], joined_branch))
        normed_grad = scatter_pair([partials[0:2], partials[2:4]])
        back, gain_grad = rms_back(
            xs[pair].reshape(-1, D), ones[pair].reshape(-1, 1), attention_gain, normed_grad.reshape(-1, D)
        )
        attention_sum = attention_sum + gain_grad
        result = (middle_grads[pair] + back.reshape(2, half, D)).astype(low)
        in_chunks[2 * pair], in_chunks[2 * pair + 1] = result[0], result[1]
    head_sum = reduce(jnp.add, head_terms).astype(low)
    output_sum = reduce(jnp.add, output_terms).astype(low)
    given = jnp.where(core == 0, head_sum[:, 2 * HEAD :], head_sum[:, HEAD : 2 * HEAD])
    kept = jnp.where(core == 0, head_sum[:, HEAD : 2 * HEAD], head_sum[:, 2 * HEAD :])
    kv_sum = (kept.astype(jnp.float32) + across(given, CORE).astype(jnp.float32)).astype(low)
    head_sum = jnp.concatenate([head_sum[:, :HEAD], kv_sum], axis=1)
    head_sum = head_sum.reshape(devices, planes, sub_rows, 2 * HEAD).transpose(1, 0, 2, 3)
    head_sum = head_sum.reshape(planes, spread, 2 * HEAD)
    output_sum = output_sum.reshape(HEAD, planes, 2 * HEAD).transpose(1, 0, 2)
    attention_grad = lax.psum_scatter(
        jnp.concatenate([head_sum, output_sum], axis=1), "fsdp", scatter_dimension=0, tiled=False
    )
    output_owned = attention_grad[spread:]
    block = exchange(attention_grad[:spread].reshape(devices, sub_rows, 2 * HEAD), "dp")
    block = block.reshape(planes, 2, sub_rows, 2 * HEAD).transpose(0, 2, 1, 3)
    block = exchange(block, "fsdp").reshape(in_rows, 2, 2 * HEAD)
    query_owned = block[:, :, :HEAD].reshape(in_rows, 2 * HEAD)
    key_owned, value_owned = block[:, 0, HEAD:], block[:, 1, HEAD:]
    input_grad = from_planes(in_chunks, core, plane)

    owner_grads = [
        owned.astype(jnp.float32)
        for owned in (
            query_owned,
            key_owned,
            value_owned,
            output_owned,
            gate_up_owned[0],
            gate_up_owned[1],
            down_owned,
        )
    ]
    local_square = reduce(jnp.add, [jnp.sum(owned * owned) for owned in owner_grads])
    attention_total, feedforward_total, square_total = lax.psum(
        (attention_sum, feedforward_sum, local_square), ("dp", "fsdp")
    )
    square_sum = (
        square_total
        + jnp.sum(attention_total * attention_total)
        + jnp.sum(feedforward_total * feedforward_total)
    )
    grad_norm = jnp.sqrt(square_sum)
    entry_count = 2 * D * D + 2 * D * kv_width + 3 * D * FF + 2 * D
    limit = clip_level * math.sqrt(entry_count)
    factor = limit / jnp.maximum(grad_norm, limit)
    gradients = owner_grads + [attention_total, feedforward_total]
    old_moments = [
        moment_query,
        moment_key,
        moment_value,
        moment_output,
        moment_gate,
        moment_up,
        moment_down,
        moment_attention,
        moment_feedforward,
    ]
    old_params = [
        query_weight,
        key_weight,
        value_weight,
        output_weight,
        gate_weight,
        up_weight,
        down_weight,
        attention_gain,
        feedforward_gain,
    ]
    new_moments = [
        0.5 * moment + 0.5 * factor * gradient for moment, gradient in zip(old_moments, gradients)
    ]
    new_params = []
    for at, param in enumerate(old_params):
        if at < 7:
            new_params.append(param - step_size * (new_moments[at] + decay_rate * param))
        else:
            new_params.append(param - gain_step * new_moments[at])
    return (outputs, input_grad, grad_norm, *new_moments, *new_params)


def solution(mesh):
    whole_groups_on_planes = mesh.shape["dp"] == HEADS and mesh.shape["fsdp"] == KV_HEADS
    body = plane_device if whole_groups_on_planes else on_device
    placed = (
        P("dp", "fsdp", None),
        P("dp", "fsdp", None),
        P("dp", None),
        P("dp", "fsdp"),
        P("dp", "fsdp"),
        P("dp", "fsdp"),
        P("dp", "fsdp"),
        P("dp", "fsdp"),
        P("dp", "fsdp"),
        P("dp", "fsdp"),
        P(),
        P(),
        P("dp", "fsdp"),
        P("dp", "fsdp"),
        P("dp", "fsdp"),
        P("dp", "fsdp"),
        P("dp", "fsdp"),
        P("dp", "fsdp"),
        P("dp", "fsdp"),
        P(),
        P(),
    )
    return jax.shard_map(
        body,
        mesh=mesh,
        in_specs=placed,
        out_specs=(
            P("dp", "fsdp", None),
            P("dp", "fsdp", None),
            P(),
            P("dp", "fsdp"),
            P("dp", "fsdp"),
            P("dp", "fsdp"),
            P("dp", "fsdp"),
            P("dp", "fsdp"),
            P("dp", "fsdp"),
            P("dp", "fsdp"),
            P(),
            P(),
            P("dp", "fsdp"),
            P("dp", "fsdp"),
            P("dp", "fsdp"),
            P("dp", "fsdp"),
            P("dp", "fsdp"),
            P("dp", "fsdp"),
            P("dp", "fsdp"),
            P(),
            P(),
        ),
        check_vma=False,
    )
```

```python
from functools import reduce
import math

import jax
import jax.numpy as jnp
from jax import lax
from jax.experimental import pallas as pl
from jax.experimental.pallas import tpu as pltpu
from jax.sharding import PartitionSpec as P

D = 2048
HEADS = 8
KV_HEADS = 4
HEAD = 256
FF = 8192
PROMPT = 1024
CONT = 64
NCONT = 2


epsilon = 1e-06
rope_base = 1000042.0
step_size = 0.2
gain_step = 4.0
decay_rate = 0.1
clip_level = 0.25
floor_score = -1e30


def rms_rows(values, gain):
    factor = lax.rsqrt(jnp.mean(values * values, axis=-1, keepdims=True) + epsilon)
    return (values * factor * gain, factor)


def rms_back(values, factor, gain, gradient):
    scaled = values * factor
    gain_grad = jnp.sum(gradient * scaled, axis=0)
    pulled = gradient * gain
    return (
        factor * (pulled - scaled * jnp.mean(pulled * scaled, axis=-1, keepdims=True)),
        gain_grad,
    )


def rope_angles(places):
    halfway = HEAD // 2
    freqs = rope_base ** (-(jnp.arange(halfway).astype(jnp.float32) * 2.0 / HEAD))
    angles = places.astype(jnp.float32)[:, None] * freqs[None, :]
    return (jnp.cos(angles), jnp.sin(angles))


def token_places(index):
    inside = index - PROMPT
    return jnp.where(index < PROMPT, index, PROMPT + inside % CONT)


def segment_of(index):
    return jnp.where(index < PROMPT, -1, (index - PROMPT) // CONT)


def visible(query_index, key_index, lengths):
    key_segment = segment_of(key_index)
    key_offset = key_index - PROMPT - key_segment * CONT
    slots = jnp.arange(NCONT, dtype=jnp.int32)
    limits = jnp.sum(jnp.where(key_segment[:, None] == slots[None, :], lengths[None, :], 0), axis=1)
    alive = key_offset < limits
    same = segment_of(query_index)[:, None] == key_segment[None, :]
    causal = key_index[None, :] <= query_index[:, None]
    return causal & ((key_index < PROMPT)[None, :] | same & alive[None, :])


def rotate(values, cosine, sine):
    halfway = values.shape[-1] // 2
    first, second = (values[..., :halfway], values[..., halfway:])
    cosine, sine = (cosine[:, None, :], sine[:, None, :])
    return jnp.concatenate(
        [first * cosine - second * sine, second * cosine + first * sine], axis=-1
    )


def rotate_back(grads, cosine, sine):
    halfway = grads.shape[-1] // 2
    first, second = (grads[..., :halfway], grads[..., halfway:])
    cosine, sine = (cosine[:, None, :], sine[:, None, :])
    return jnp.concatenate(
        [first * cosine + second * sine, second * cosine - first * sine], axis=-1
    )


def join_blocks(pieces, shard_count):
    height = pieces[0].shape[0]
    return jnp.concatenate(
        [member.reshape(height, shard_count, -1) for member in pieces], axis=2
    ).reshape(height, -1)


def split_blocks(merged, breadths, shard_count):
    height = merged.shape[0]
    blocks = merged.reshape(height, shard_count, -1)
    result = []
    offset = 0
    for breadth in breadths:
        result.append(
            blocks[:, :, offset : offset + breadth].reshape(height, shard_count * breadth)
        )
        offset = offset + breadth
    return result


def ahead(operand, shard):
    return jnp.dot(
        operand,
        lax.all_gather(shard, "fsdp", axis=1, tiled=True),
        preferred_element_type=jnp.float32,
    )


def behind(gradient, shard):
    return lax.dot_general(
        gradient,
        lax.all_gather(shard, "fsdp", axis=1, tiled=True),
        (((1,), (1,)), ((), ())),
        preferred_element_type=jnp.float32,
    )


def weight_term(gradient, operand):
    operand_all = lax.all_gather(operand, "fsdp", axis=0, tiled=True)
    owned_columns = lax.all_to_all(gradient, "fsdp", split_axis=1, concat_axis=0, tiled=True)
    return lax.dot_general(
        owned_columns, operand_all, (((0,), (0,)), ((), ())), preferred_element_type=jnp.float32
    )


def on_device(
    activations,
    cotangent,
    continuation_lengths,
    query_weight,
    key_weight,
    value_weight,
    output_weight,
    gate_weight,
    up_weight,
    down_weight,
    attention_gain,
    feedforward_gain,
    moment_query,
    moment_key,
    moment_value,
    moment_output,
    moment_gate,
    moment_up,
    moment_down,
    moment_attention,
    moment_feedforward,
):
    shard_count = lax.axis_size("fsdp")
    kv_width = KV_HEADS * HEAD
    repeat = HEADS // KV_HEADS
    scale = 1.0 / math.sqrt(HEAD)
    gathered = (
        lax.all_gather(query_weight.astype(jnp.bfloat16), "dp", axis=0, tiled=True),
        lax.all_gather(key_weight.astype(jnp.bfloat16), "dp", axis=0, tiled=True),
        lax.all_gather(value_weight.astype(jnp.bfloat16), "dp", axis=0, tiled=True),
        lax.all_gather(output_weight.astype(jnp.bfloat16), "dp", axis=0, tiled=True),
        lax.all_gather(gate_weight.astype(jnp.bfloat16), "dp", axis=0, tiled=True),
        lax.all_gather(up_weight.astype(jnp.bfloat16), "dp", axis=0, tiled=True),
        lax.all_gather(down_weight.astype(jnp.bfloat16), "dp", axis=0, tiled=True),
    )
    merged_attn = join_blocks(gathered[0:3], 1)
    merged_output = gathered[3]
    merged_ffn = join_blocks(gathered[4:6], 1)
    merged_down = gathered[6]
    query_cols = D // shard_count
    key_cols = kv_width // shard_count
    ffn_cols = FF // shard_count
    attn_breadths = (query_cols, key_cols, key_cols)
    ffn_breadths = (ffn_cols, ffn_cols)
    local_rows = activations.shape[1]
    group_rows = local_rows * shard_count
    query_index = lax.axis_index("fsdp") * local_rows + jnp.arange(local_rows, dtype=jnp.int32)
    key_index = jnp.arange(group_rows, dtype=jnp.int32)
    cosine, sine = rope_angles(token_places(query_index))
    sums = [jnp.zeros((matrix.shape[1], matrix.shape[0]), jnp.float32) for matrix in gathered]
    attention_sum = jnp.zeros((D,), jnp.float32)
    feedforward_sum = jnp.zeros((D,), jnp.float32)
    output_list = []
    input_list = []
    for micro_batch in range(activations.shape[0]):
        allowed = visible(query_index, key_index, continuation_lengths[micro_batch])
        inputs = activations[micro_batch].astype(jnp.float32)
        normed_float, factor_one = rms_rows(inputs, attention_gain)
        normed = normed_float.astype(jnp.bfloat16)
        pre_query, pre_key, pre_value = split_blocks(
            ahead(normed, merged_attn), attn_breadths, shard_count
        )
        queries = (
            rotate(pre_query.reshape(local_rows, HEADS, HEAD), cosine, sine)
            .astype(jnp.bfloat16)
            .reshape(local_rows, KV_HEADS, repeat, HEAD)
        )
        keys = rotate(pre_key.reshape(local_rows, KV_HEADS, HEAD), cosine, sine).astype(
            jnp.bfloat16
        )
        values = pre_value.astype(jnp.bfloat16).reshape(local_rows, KV_HEADS, HEAD)
        keys_all, values_all = (
            lax.all_gather(keys, "fsdp", axis=0, tiled=True),
            lax.all_gather(values, "fsdp", axis=0, tiled=True),
        )
        raw = (
            jnp.einsum("qgrd,kgd->grqk", queries, keys_all, preferred_element_type=jnp.float32)
            * scale
        )
        raw = jnp.where(allowed[None, None], raw, floor_score)
        highest = jnp.max(raw, axis=-1, keepdims=True)
        exponent = jnp.exp(raw - highest)
        denominator = jnp.sum(exponent, axis=-1, keepdims=True)
        logsum = highest + jnp.log(denominator)
        probs_low = (exponent / denominator).astype(jnp.bfloat16)
        mixed = (
            jnp.einsum("grqk,kgd->qgrd", probs_low, values_all, preferred_element_type=jnp.float32)
            .reshape(local_rows, D)
            .astype(jnp.bfloat16)
        )
        middle = inputs + ahead(mixed, merged_output)
        normed_two_float, factor_two = rms_rows(middle, feedforward_gain)
        normed_two = normed_two_float.astype(jnp.bfloat16)
        gate, upward = split_blocks(ahead(normed_two, merged_ffn), ffn_breadths, shard_count)
        sigmoid = jax.nn.sigmoid(gate)
        swish = gate * sigmoid
        hidden = (swish * upward).astype(jnp.bfloat16)
        result = middle + ahead(hidden, merged_down)
        output_list.append(result.astype(jnp.bfloat16))
        out_grad = cotangent[micro_batch]
        hidden_grad = behind(out_grad, merged_down)
        sums[6] = sums[6] + weight_term(out_grad, hidden)
        gate_grad = (hidden_grad * upward * sigmoid * (1.0 + gate * (1.0 - sigmoid))).astype(
            jnp.bfloat16
        )
        up_grad = (hidden_grad * swish).astype(jnp.bfloat16)
        ffn_grad = join_blocks((gate_grad, up_grad), shard_count)
        ffn_term = weight_term(ffn_grad, normed_two)
        sums[4] = sums[4] + ffn_term[:ffn_cols]
        sums[5] = sums[5] + ffn_term[ffn_cols:]
        normed_two_grad = behind(ffn_grad, merged_ffn)
        middle_back, feed_gain_grad = rms_back(
            middle, factor_two, feedforward_gain, normed_two_grad
        )
        middle_grad = out_grad.astype(jnp.float32) + middle_back
        branch_grad = middle_grad.astype(jnp.bfloat16)
        sums[3] = sums[3] + weight_term(branch_grad, mixed)
        mixed_grad = (
            behind(branch_grad, merged_output)
            .astype(jnp.bfloat16)
            .reshape(local_rows, KV_HEADS, repeat, HEAD)
        )
        raw_again = (
            jnp.einsum("qgrd,kgd->grqk", queries, keys_all, preferred_element_type=jnp.float32)
            * scale
        )
        raw_again = jnp.where(allowed[None, None], raw_again, floor_score)
        probs_again = jnp.exp(raw_again - logsum)
        value_part = jnp.einsum(
            "grqk,qgrd->kgd",
            probs_again.astype(jnp.bfloat16),
            mixed_grad,
            preferred_element_type=jnp.float32,
        )
        prob_grad = jnp.einsum(
            "qgrd,kgd->grqk", mixed_grad, values_all, preferred_element_type=jnp.float32
        )
        inner = jnp.sum(probs_again * prob_grad, axis=-1, keepdims=True)
        score_grad = (probs_again * (prob_grad - inner)).astype(jnp.bfloat16)
        query_grad = (
            jnp.einsum("grqk,kgd->qgrd", score_grad, keys_all, preferred_element_type=jnp.float32)
            * scale
        )
        key_part = (
            jnp.einsum("grqk,qgrd->kgd", score_grad, queries, preferred_element_type=jnp.float32)
            * scale
        )
        key_grad, value_grad = (
            lax.psum_scatter(
                key_part.astype(jnp.bfloat16), "fsdp", scatter_dimension=0, tiled=True
            ).astype(jnp.float32),
            lax.psum_scatter(
                value_part.astype(jnp.bfloat16), "fsdp", scatter_dimension=0, tiled=True
            ).astype(jnp.float32),
        )
        pre_query_grad = (
            rotate_back(query_grad.reshape(local_rows, HEADS, HEAD), cosine, sine)
            .reshape(local_rows, D)
            .astype(jnp.bfloat16)
        )
        pre_key_grad = (
            rotate_back(key_grad, cosine, sine).reshape(local_rows, kv_width).astype(jnp.bfloat16)
        )
        pre_value_grad = value_grad.reshape(local_rows, kv_width).astype(jnp.bfloat16)
        attn_grad = join_blocks((pre_query_grad, pre_key_grad, pre_value_grad), shard_count)
        attn_term = weight_term(attn_grad, normed)
        sums[0] = sums[0] + attn_term[:query_cols]
        sums[1] = sums[1] + attn_term[query_cols : query_cols + key_cols]
        sums[2] = sums[2] + attn_term[query_cols + key_cols :]
        normed_grad = behind(attn_grad, merged_attn)
        input_back, attn_gain_grad = rms_back(inputs, factor_one, attention_gain, normed_grad)
        input_list.append((middle_grad + input_back).astype(jnp.bfloat16))
        attention_sum = attention_sum + attn_gain_grad
        feedforward_sum = feedforward_sum + feed_gain_grad
    reduced = (
        lax.psum_scatter(
            sums[0].astype(jnp.bfloat16), "dp", scatter_dimension=1, tiled=True
        ).astype(jnp.float32),
        lax.psum_scatter(
            sums[1].astype(jnp.bfloat16), "dp", scatter_dimension=1, tiled=True
        ).astype(jnp.float32),
        lax.psum_scatter(
            sums[2].astype(jnp.bfloat16), "dp", scatter_dimension=1, tiled=True
        ).astype(jnp.float32),
        lax.psum_scatter(
            sums[3].astype(jnp.bfloat16), "dp", scatter_dimension=1, tiled=True
        ).astype(jnp.float32),
        lax.psum_scatter(
            sums[4].astype(jnp.bfloat16), "dp", scatter_dimension=1, tiled=True
        ).astype(jnp.float32),
        lax.psum_scatter(
            sums[5].astype(jnp.bfloat16), "dp", scatter_dimension=1, tiled=True
        ).astype(jnp.float32),
        lax.psum_scatter(
            sums[6].astype(jnp.bfloat16), "dp", scatter_dimension=1, tiled=True
        ).astype(jnp.float32),
    )
    owner_grads = [owned.T for owned in reduced]
    local_square = reduce(jnp.add, [jnp.sum(owned * owned) for owned in owner_grads])
    attention_total, feedforward_total, square_total = lax.psum(
        (attention_sum, feedforward_sum, local_square), ("dp", "fsdp")
    )
    square_sum = (
        square_total
        + jnp.sum(attention_total * attention_total)
        + jnp.sum(feedforward_total * feedforward_total)
    )
    grad_norm = jnp.sqrt(square_sum)
    entry_count = 2 * D * D + 2 * D * kv_width + 3 * D * FF + 2 * D
    limit = clip_level * math.sqrt(entry_count)
    factor = limit / jnp.maximum(grad_norm, limit)
    gradients = owner_grads + [attention_total, feedforward_total]
    old_moments = [
        moment_query,
        moment_key,
        moment_value,
        moment_output,
        moment_gate,
        moment_up,
        moment_down,
        moment_attention,
        moment_feedforward,
    ]
    old_params = [
        query_weight,
        key_weight,
        value_weight,
        output_weight,
        gate_weight,
        up_weight,
        down_weight,
        attention_gain,
        feedforward_gain,
    ]
    new_moments = [
        0.5 * moment + 0.5 * factor * gradient for moment, gradient in zip(old_moments, gradients)
    ]
    new_params = []
    for place, param in enumerate(old_params):
        if place < 7:
            new_params.append(param - step_size * (new_moments[place] + decay_rate * param))
        else:
            new_params.append(param - gain_step * new_moments[place])
    outputs = jnp.stack(output_list)
    input_grad = jnp.stack(input_list)
    return (
        outputs,
        input_grad,
        grad_norm,
        new_moments[0],
        new_moments[1],
        new_moments[2],
        new_moments[3],
        new_moments[4],
        new_moments[5],
        new_moments[6],
        new_moments[7],
        new_moments[8],
        new_params[0],
        new_params[1],
        new_params[2],
        new_params[3],
        new_params[4],
        new_params[5],
        new_params[6],
        new_params[7],
        new_params[8],
    )


CORE, SIDE_A, SIDE_B = 1, 2, 4
CHIPS = 4
CHUNKS = 4
MB = 1024 * 1024


def across(value, mask):
    count = lax.axis_size("dp")
    return lax.ppermute(value, "dp", [(place, place ^ mask) for place in range(count)])


def along(value, mask):
    count = lax.axis_size("fsdp")
    return lax.ppermute(value, "fsdp", [(place, place ^ mask) for place in range(count)])


def pick(values, index):
    return lax.dynamic_index_in_dim(values, index, 0, keepdims=False)


def after(value, *earlier):
    return lax.optimization_barrier((value, earlier))[0]


def trade_planes(parts, plane):
    found = [pick(parts, plane)]
    for mask in range(1, CHUNKS):
        found.append(along(pick(parts, plane ^ mask), mask))
    found = jnp.stack(found)
    return [pick(found, label ^ plane) for label in range(CHUNKS)]


def gather_planes(block):
    one, two = along(block, 1), along(block, 2)
    return [block, one, two, along(two, 1)]


def sum_planes(parts):
    two = (parts[2].astype(jnp.float32) + along(parts[3], 1).astype(jnp.float32)).astype(jnp.bfloat16)
    return (
        parts[0].astype(jnp.float32)
        + along(parts[1], 1).astype(jnp.float32)
        + along(two, 2).astype(jnp.float32)
    )


def sum_all(value):
    for mask in (CORE, SIDE_A, SIDE_B):
        value = value + across(value, mask)
    for mask in (1, 2):
        value = value + along(value, mask)
    return value


def to_planes(array, core, plane):
    halves = array.reshape(2, 2, array.shape[1] // 2, array.shape[2]).swapaxes(0, 1)
    keep = pick(halves, core)
    came = across(pick(halves, 1 - core), CORE)
    swap = core == 1
    parts = jnp.concatenate([jnp.where(swap, came, keep), jnp.where(swap, keep, came)])
    return trade_planes(parts, plane)


def from_planes(chunks, core, plane):
    groups = trade_planes(jnp.stack(chunks), plane)
    pairs = jnp.stack([jnp.stack(groups[:2]), jnp.stack(groups[2:])])
    keep = pick(pairs, core)
    came = across(pick(pairs, 1 - core), CORE)
    swap = core == 1
    return jnp.concatenate([jnp.where(swap, came, keep), jnp.where(swap, keep, came)], axis=1)


MESH = pl.DeviceIdType.MESH
SLOT = {0: 0, SIDE_A: 1, SIDE_B: 2}
ROUTES = ((SIDE_A, SIDE_B), (SIDE_B, SIDE_A))
STRIPE = 16


def peer(mask):
    place = lax.axis_index("dp")
    other = place + mask - 2 * mask * lax.rem(lax.div(place, mask), 2)
    return (other, lax.axis_index("fsdp"))


def meet():
    barrier = pltpu.get_barrier_semaphore()
    for mask in (CORE, SIDE_A, SIDE_B):
        pl.semaphore_signal(barrier, inc=1, device_id=peer(mask), device_id_type=MESH)
    pl.semaphore_wait(barrier, 3)


class Remote:
    def __init__(self, wires, source, target, mask):
        self.wires, self.source, self.target, self.mask = wires, source, target, mask
        self.place = wires.count
        wires.count += 1

    def make(self):
        return pltpu.make_async_remote_copy(
            src_ref=self.source,
            dst_ref=self.target,
            send_sem=self.wires.send.at[self.place],
            recv_sem=self.wires.recv.at[self.place],
            device_id=peer(self.mask),
            device_id_type=MESH,
        )

    def start(self):
        self.make().start()

    def arrived(self):
        self.make().wait_recv()

    def left(self):
        self.make().wait_send()


class Wires:
    def __init__(self, send, recv, local):
        self.send, self.recv, self.local = send, recv, local
        self.count = 0
        self.local_count = 0

    def load(self, pairs):
        copies = [
            pltpu.make_async_copy(source, target, self.local.at[place])
            for place, (source, target) in enumerate(pairs)
        ]
        for copy in copies:
            copy.start()
        for copy in copies:
            copy.wait()


class Gather:
    def __init__(self, wires, own, target):
        rows = target.shape[2] // 2
        self.wires, self.own = wires, own
        self.near, self.far, self.core_first, self.core_near, self.core_far = [], [], [], [], []
        self.home = []

        def place(chunk, slot, half):
            return target.at[chunk, slot, pl.ds(half * rows, rows)]

        for chunk, (first, second) in enumerate(ROUTES):
            near, far = SLOT[first], SLOT[second]
            self.home.append((own[chunk], place(chunk, 0, 0)))
            self.near.append(Remote(wires, own[chunk], place(chunk, near, 0), first))
            self.core_first.append(Remote(wires, own[chunk], place(chunk, 0, 1), CORE))
            self.far.append(Remote(wires, own[chunk], place(chunk, far, 0), second))
            self.far.append(Remote(wires, place(chunk, near, 0), place(chunk, 3, 0), second))
            self.core_near.append(Remote(wires, place(chunk, near, 0), place(chunk, near, 1), CORE))
            self.core_far.append(Remote(wires, place(chunk, far, 0), place(chunk, far, 1), CORE))
            self.core_far.append(Remote(wires, place(chunk, 3, 0), place(chunk, 3, 1), CORE))

    def first(self):
        for copy in self.near + self.core_first:
            copy.start()
        self.wires.load(self.home)

    def second(self):
        for chunk, copy in enumerate(self.near):
            copy.arrived()
            self.far[2 * chunk].start()
            self.far[2 * chunk + 1].start()
            self.core_near[chunk].start()

    def third(self):
        for place, copy in enumerate(self.far):
            copy.arrived()
            self.core_far[place].start()

    def last(self):
        for copy in self.core_first + self.core_near + self.core_far:
            copy.arrived()
        for copy in self.near + self.far + self.core_first + self.core_near + self.core_far:
            copy.left()

    def steps(self):
        return [self.first, self.second, self.third, self.last]


class Scatter:
    def __init__(self, wires, own, other, landing, stage, done):
        from_core, from_far, from_near = landing
        self.wires, self.own, self.landing, self.stage, self.done = wires, own, landing, stage, done
        self.core = [Remote(wires, other.at[chunk], from_core.at[chunk], CORE) for chunk in range(2)]
        self.far = [
            Remote(wires, stage[0].at[chunk], from_far.at[chunk], first)
            for chunk, (_, first) in enumerate(ROUTES)
        ]
        self.near = [
            Remote(wires, stage[2].at[chunk, 0], from_near.at[chunk], last)
            for chunk, (last, _) in enumerate(ROUTES)
        ]

    def first(self):
        for copy in self.core:
            copy.start()

    def second(self):
        left, right = self.stage[:2]
        pairs = []
        for chunk, (_, first) in enumerate(ROUTES):
            self.core[chunk].arrived()
            for place, slot in enumerate((SLOT[first], 3)):
                pairs.append((self.own.at[chunk, slot], left.at[chunk, place]))
                pairs.append((self.landing[0].at[chunk, slot], right.at[chunk, place]))
        self.wires.load(pairs)
        for chunk in range(2):

            @pl.loop(0, left.shape[2] // STRIPE)
            def _(step):
                span = pl.ds(step * STRIPE, STRIPE)
                total = left[chunk, :, span].astype(jnp.float32) + right[chunk, :, span].astype(jnp.float32)
                left[chunk, :, span] = total.astype(jnp.bfloat16)

            self.far[chunk].start()

    def third(self):
        stage = self.stage[2]
        pairs = []
        for chunk, (last, _) in enumerate(ROUTES):
            self.far[chunk].arrived()
            pairs.append((self.own.at[chunk, SLOT[last]], stage.at[chunk, 0]))
            pairs.append((self.landing[0].at[chunk, SLOT[last]], stage.at[chunk, 1]))
            pairs.append((self.landing[1].at[chunk, 1], stage.at[chunk, 2]))
        self.wires.load(pairs)
        for chunk in range(2):

            @pl.loop(0, stage.shape[2] // STRIPE)
            def _(step):
                span = pl.ds(step * STRIPE, STRIPE)
                total = stage[chunk, 0, span].astype(jnp.float32)
                for place in range(1, 3):
                    total += stage[chunk, place, span].astype(jnp.float32)
                stage[chunk, 0, span] = total.astype(jnp.bfloat16)

            self.near[chunk].start()
        for copy in self.far:
            copy.left()

    def last(self):
        stage = self.stage[3]
        for chunk in range(2):
            self.near[chunk].arrived()
            self.wires.load(
                [
                    (self.own.at[chunk, 0], stage.at[0]),
                    (self.landing[0].at[chunk, 0], stage.at[1]),
                    (self.landing[1].at[chunk, 0], stage.at[2]),
                    (self.landing[2].at[chunk], stage.at[3]),
                ]
            )

            @pl.loop(0, stage.shape[1] // STRIPE)
            def _(step):
                span = pl.ds(step * STRIPE, STRIPE)
                total = stage[0, span].astype(jnp.float32)
                for place in range(1, 4):
                    total += stage[place, span].astype(jnp.float32)
                self.done(chunk, span, total)

        for copy in self.near + self.core:
            copy.left()

    def steps(self):
        return [self.first, self.second, self.third, self.last]


def stage_shapes(rows, width):
    return [
        pltpu.VMEM((2, 2, rows, width), jnp.bfloat16),
        pltpu.VMEM((2, 2, rows, width), jnp.bfloat16),
        pltpu.VMEM((2, 3, rows, width), jnp.bfloat16),
        pltpu.VMEM((4, rows, width), jnp.bfloat16),
    ]


def landing_shapes(rows, width):
    return [
        jax.ShapeDtypeStruct((2, CHIPS, rows, width), jnp.bfloat16),
        jax.ShapeDtypeStruct((2, 2, rows, width), jnp.bfloat16),
        jax.ShapeDtypeStruct((2, rows, width), jnp.bfloat16),
    ]


def partial_shapes(rows, width):
    return [jax.ShapeDtypeStruct((2, CHIPS, rows, width), jnp.bfloat16)] * 2


def wire_shapes(count):
    return [
        pltpu.SemaphoreType.DMA((count,)),
        pltpu.SemaphoreType.DMA((count,)),
        pltpu.SemaphoreType.DMA((8,)),
    ]


def call(kernel, identity, inputs, outputs, scratch, megabytes):
    return pl.pallas_call(
        kernel,
        in_specs=[pl.BlockSpec(memory_space=place) for _, place in inputs],
        out_specs=[pl.BlockSpec(memory_space=place) for _, place in outputs],
        out_shape=[shape for shape, _ in outputs],
        scratch_shapes=scratch,
        compiler_params=pltpu.CompilerParams(
            collective_id=identity, has_side_effects=True, vmem_limit_bytes=megabytes * MB
        ),
    )(*[array for array, _ in inputs])


HBM, VMEM, SMEM = pl.ANY, pltpu.VMEM, pltpu.SMEM


def at_step(step, actions):
    for when, action in actions.items():
        pl.when(step == when)(action)


def project_phase(gathered, states, weight_ref, cosine, sine, actions):
    tokens = gathered.shape[2]

    def body(rows_ref, cosine_ref, sine_ref, out):
        at_step(pl.program_id(0) * CHIPS + pl.program_id(1), actions)
        product = dot(rows_ref[0, 0], weight_ref[...])
        angles = (cosine_ref[0], sine_ref[0])
        query = spin(product[:, :HEAD], *angles) * (1.0 / math.sqrt(HEAD))
        key = spin(product[:, HEAD : 2 * HEAD], *angles)
        out[0, 0] = jnp.concatenate([query, key, product[:, 2 * HEAD :]], axis=1).astype(jnp.bfloat16)

    here = lambda chunk, chip: (chunk, chip, 0, 0)
    table = pl.BlockSpec((1, tokens, HEAD // 2), lambda chunk, chip: (chunk, 0, 0))
    pltpu.emit_pipeline(
        body,
        grid=(2, CHIPS),
        in_specs=[pl.BlockSpec((1, 1, tokens, gathered.shape[3]), here), table, table],
        out_specs=[pl.BlockSpec((1, 1, tokens, 3 * HEAD), here)],
    )(gathered, cosine, sine, states)


def attend_phase(pair, states, mixed, own, other, lengths_ref, places, weight_ref, keys, values, actions):
    tokens, rows, width = mixed.shape[2], own.shape[2], own.shape[3]
    blocks = 2 * (pair + 1)

    def body(*refs):
        state_refs, (mixed_ref, own_ref, other_ref) = refs[: pair + 1], refs[pair + 1 :]
        chip, side_at = pl.program_id(0), pl.program_id(1)
        at_step(2 * chip + side_at, actions)

        @pl.when(side_at == 0)
        def _():
            for block in range(blocks):
                ref = state_refs[block // 2]
                keys[pl.ds(block * tokens, tokens)] = ref[block % 2, 0, :, HEAD : 2 * HEAD]
                values[pl.ds(block * tokens, tokens)] = ref[block % 2, 0, :, 2 * HEAD :]

        for side in range(2):

            @pl.when(side_at == side)
            def _():
                chunk = 2 * pair + side
                count = tokens * (chunk + 1)
                scores = dot_t(state_refs[pair][side, 0, :, :HEAD], keys[:count])
                mask = seen(places[0][...], places[1][...], chunk, count, tokens, lengths_ref, chip)
                scores = jnp.where(mask, scores, floor_score)
                highest = jnp.max(scores, axis=1, keepdims=True)
                exponent = jnp.exp(scores - highest)
                total = jnp.sum(exponent, axis=1, keepdims=True)
                probs = (exponent * (1.0 / total)).astype(jnp.bfloat16)
                mixed_ref[0, 0] = dot(probs, values[:count]).astype(jnp.bfloat16)

        partial = dot(mixed_ref[0, 0], weight_ref[...]).astype(jnp.bfloat16)
        own_ref[0, 0] = partial[:rows]
        other_ref[0, 0] = partial[rows:]

    here = lambda chip, side: (side, chip, 0, 0)
    state = pl.BlockSpec((2, 1, tokens, 3 * HEAD), lambda chip, side: (0, chip, 0, 0))
    pltpu.emit_pipeline(
        body,
        grid=(CHIPS, 2),
        in_specs=[state] * (pair + 1),
        out_specs=[pl.BlockSpec((1, 1, tokens, HEAD), here)] + [pl.BlockSpec((1, 1, rows, width), here)] * 2,
    )(*states[: pair + 1], mixed, own, other)


def attend_back_phase(
    pair, branch, states, head_grads, own, other, lengths_ref, places, out_weight, weight_ref,
    tables, keys, values, sums, late_sums, actions
):
    tokens, rows, width = branch.shape[2], own.shape[2], own.shape[3]
    blocks = 2 * (pair + 1)
    edge = 2 * tokens

    def body(*refs):
        branch_ref, state_refs = refs[0], refs[1 : pair + 2]
        cosine_ref, sine_ref, grads_ref, own_ref, other_ref = refs[pair + 2 :]
        chip, step = pl.program_id(0), pl.program_id(1)
        at_step(2 * chip + step, actions)

        @pl.when(step == 0)
        def _():
            for block in range(blocks):
                ref = state_refs[block // 2]
                keys[pl.ds(block * tokens, tokens)] = ref[block % 2, 0, :, HEAD : 2 * HEAD]
                values[pl.ds(block * tokens, tokens)] = ref[block % 2, 0, :, 2 * HEAD :]
            if pair == 1:
                for place in range(2):
                    sums[place][chip] = jnp.zeros(sums[place].shape[1:], jnp.float32)
                    late_sums[place][...] = jnp.zeros(late_sums[place].shape, jnp.float32)

        def add(place, term):
            early = min(term.shape[0], edge)
            sums[place][chip, :early] += term[:early]
            if term.shape[0] > edge:
                late_sums[place][: term.shape[0] - edge] += term[edge:]

        for side in range(2):

            @pl.when(step == 1 - side)
            def _():
                chunk = 2 * pair + side
                count = tokens * (chunk + 1)
                mixed_grad = dot_t(branch_ref[0, 0], out_weight[...]).astype(jnp.bfloat16)
                query = state_refs[pair][side, 0, :, :HEAD]
                scores = dot_t(query, keys[:count])
                mask = seen(places[0][...], places[1][...], chunk, count, tokens, lengths_ref, chip)
                scores = jnp.where(mask, scores, floor_score)
                highest = jnp.max(scores, axis=1, keepdims=True)
                exponent = jnp.exp(scores - highest)
                probs = exponent * (1.0 / jnp.sum(exponent, axis=1, keepdims=True))
                add(1, dot_tn(probs.astype(jnp.bfloat16), mixed_grad))
                prob_grad = dot_t(mixed_grad, values[:count])
                inner = jnp.sum(probs * prob_grad, axis=1, keepdims=True)
                score_grad = (probs * (prob_grad - inner)).astype(jnp.bfloat16)
                add(0, dot_tn(score_grad, query))
                query_grad = dot(score_grad, keys[:count]) * (1.0 / math.sqrt(HEAD))
                angles = (cosine_ref[0], sine_ref[0])
                span = slice(side * tokens, (side + 1) * tokens)
                if pair == 1:
                    key_grad, value_grad = late_sums[0][span], late_sums[1][span]
                else:
                    key_grad, value_grad = sums[0][chip, span], sums[1][chip, span]
                grads_ref[0, 0] = jnp.concatenate(
                    [spin_back(query_grad, *angles), spin_back(key_grad, *angles), value_grad], axis=1
                ).astype(jnp.bfloat16)

        partial = dot_t(grads_ref[0, 0], weight_ref[...]).astype(jnp.bfloat16)
        own_ref[0, 0] = partial[:rows]
        other_ref[0, 0] = partial[rows:]

    here = lambda chip, step: (1 - step, chip, 0, 0)
    state = pl.BlockSpec((2, 1, tokens, 3 * HEAD), lambda chip, step: (0, chip, 0, 0))
    table = pl.BlockSpec((1, tokens, HEAD // 2), lambda chip, step: (1 - step, 0, 0))
    pltpu.emit_pipeline(
        body,
        grid=(CHIPS, 2),
        in_specs=[pl.BlockSpec((1, 1, tokens, width), here)] + [state] * (pair + 1) + [table] * 2,
        out_specs=[pl.BlockSpec((1, 1, tokens, 3 * HEAD), here)]
        + [pl.BlockSpec((1, 1, rows, width), here)] * 2,
    )(branch, *states[: pair + 1], *tables, head_grads, own, other)


def feed_phase(rows_in, grads_in, hidden, unit_grads, back_parts, out_parts, weights, actions):
    tokens, width = rows_in.shape[2:]
    rows = tokens // 2
    shards, columns = weights.shape[0], weights.shape[2]
    share = columns // 2

    def body(rows_ref, out_grad_ref, hidden_ref, units_ref, back_own, back_other, out_own, out_other):
        at_step(pl.program_id(0) * CHIPS + pl.program_id(1), actions)
        hidden_grad = None
        for shard in range(shards):
            grad = out_grad_ref[0, 0, :, shard * columns : (shard + 1) * columns]
            term = dot_t(grad, weights[shard, width:, :])
            hidden_grad = term if hidden_grad is None else hidden_grad + term
        back = None
        for shard in range(shards):
            both = dot(rows_ref[0, 0], weights[shard, :width, :])
            gate, upward = both[:, :share], both[:, share:]
            grad = hidden_grad[:, shard * share : (shard + 1) * share]
            sigmoid = jax.nn.sigmoid(gate)
            swish = gate * sigmoid
            hidden_ref[0, 0, :, shard * share : (shard + 1) * share] = (swish * upward).astype(jnp.bfloat16)
            gate_grad = grad * upward * sigmoid * (1.0 + gate * (1.0 - sigmoid))
            units_ref[shard, 0, 0] = jnp.concatenate([gate_grad, grad * swish], axis=1).astype(jnp.bfloat16)
            term = dot_t(units_ref[shard, 0, 0], weights[shard, :width, :])
            back = term if back is None else back + term
        back = back.astype(jnp.bfloat16)
        back_own[0, 0] = back[:rows]
        back_other[0, 0] = back[rows:]
        for shard in range(shards):
            span = slice(shard * columns, (shard + 1) * columns)
            value = dot(hidden_ref[0, 0], weights[shard, width:, :]).astype(jnp.bfloat16)
            out_own[0, 0, :, span] = value[:rows]
            out_other[0, 0, :, span] = value[rows:]

    here = lambda chunk, chip: (chunk, chip, 0, 0)
    wide = pl.BlockSpec((1, 1, tokens, width), here)
    narrow = pl.BlockSpec((1, 1, rows, width), here)
    pltpu.emit_pipeline(
        body,
        grid=(2, CHIPS),
        in_specs=[wide, wide],
        out_specs=[
            pl.BlockSpec((1, 1, tokens, hidden.shape[3]), here),
            pl.BlockSpec((shards, 1, 1, tokens, columns), lambda chunk, chip: (0, chunk, chip, 0, 0)),
        ]
        + [narrow] * 4,
    )(rows_in, grads_in, hidden, unit_grads, *back_parts, *out_parts)


def bf16(*shape):
    return jax.ShapeDtypeStruct(shape, jnp.bfloat16)


def f32(*shape):
    return jax.ShapeDtypeStruct(shape, jnp.float32)


def gather_and_project(normed, out_grads, weight, cosine, sine):
    _, rows, width = normed.shape
    tokens = 2 * rows
    whole_pair = bf16(2, CHIPS, tokens, width)

    def kernel(normed_ref, grads_ref, weight_ref, cosine_ref, sine_ref, *refs):
        gathered, grads, states, wires = refs[:2], refs[2:4], refs[4:6], Wires(*refs[6:])
        meet()
        rows_moves = [
            Gather(wires, [normed_ref.at[2 * pair], normed_ref.at[2 * pair + 1]], gathered[pair])
            for pair in range(2)
        ]
        grad_moves = [
            Gather(wires, [grads_ref.at[2 * pair], grads_ref.at[2 * pair + 1]], grads[pair])
            for pair in range(2)
        ]
        rows_moves[0].first()
        rows_moves[0].second()
        rows_moves[1].first()
        rows_moves[0].third()
        rows_moves[1].second()
        grad_moves[0].first()
        rows_moves[0].last()
        project_phase(
            gathered[0], states[0], weight_ref, cosine_ref.at[0], sine_ref.at[0],
            {4: rows_moves[1].third, 6: grad_moves[0].second},
        )
        grad_moves[1].first()
        rows_moves[1].last()
        project_phase(
            gathered[1], states[1], weight_ref, cosine_ref.at[1], sine_ref.at[1],
            {4: grad_moves[0].third, 6: grad_moves[1].second},
        )
        grad_moves[0].last()
        grad_moves[1].third()
        grad_moves[1].last()

    outs = call(
        kernel,
        1,
        [(normed, HBM), (out_grads, HBM), (weight, VMEM), (cosine, HBM), (sine, HBM)],
        [(whole_pair, HBM)] * 4 + [(bf16(2, CHIPS, tokens, 3 * HEAD), HBM)] * 2,
        wire_shapes(60),
        40,
    )
    return outs[:2], outs[2:4], outs[4:6]


def attend_and_norm(states, lengths, places, out_weight, inputs, gain):
    _, rows, width = inputs.shape
    tokens = 2 * rows

    def kernel(*refs):
        states_in, (lengths_ref, place_q, place_k, weight_ref, inputs_ref, gain_ref) = refs[:2], refs[2:8]
        mixed, middle, normed, target = refs[8:10], refs[10], refs[11], refs[12]
        parts, landings = (refs[13:15], refs[15:17]), (refs[17:20], refs[20:23])
        stage, keys, values, wires = refs[23:27], refs[27], refs[28], Wires(*refs[29:])
        meet()

        def finish(pair):
            def done(chunk, span, total):
                at = 2 * pair + chunk
                total = total + inputs_ref[at, span].astype(jnp.float32)
                middle[at, span] = total
                factor = lax.rsqrt(jnp.mean(total * total, axis=1, keepdims=True) + epsilon)
                normed[at, span] = (total * factor * gain_ref[...]).astype(jnp.bfloat16)

            return done

        sums = [
            Scatter(wires, *parts[pair], landings[pair], stage, finish(pair)) for pair in range(2)
        ]
        move = Gather(wires, [normed.at[2], normed.at[3]], target)
        places_in = (place_q, place_k)
        attend_phase(
            1, states_in, mixed[1], *parts[1], lengths_ref, places_in, weight_ref, keys, values, {}
        )
        sums[1].first()
        attend_phase(
            0, states_in, mixed[0], *parts[0], lengths_ref, places_in, weight_ref, keys, values,
            {5: sums[1].second},
        )
        sums[0].first()
        sums[1].third()
        sums[0].second()
        sums[1].last()
        move.first()
        sums[0].third()
        move.second()
        sums[0].last()
        move.third()
        move.last()

    pair_parts = [(shape, HBM) for shape in partial_shapes(rows, width)]
    landing = [(shape, HBM) for shape in landing_shapes(rows, width)]
    outs = call(
        kernel,
        2,
        [(state, HBM) for state in states]
        + [(lengths, SMEM), (places[0], VMEM), (places[1], VMEM), (out_weight, VMEM)]
        + [(inputs, VMEM), (gain, VMEM)],
        [(bf16(2, CHIPS, tokens, HEAD), HBM)] * 2
        + [(f32(CHUNKS, rows, width), VMEM), (bf16(CHUNKS, rows, width), VMEM)]
        + [(bf16(2, CHIPS, tokens, width), HBM)]
        + pair_parts * 2
        + landing * 2,
        stage_shapes(rows, width)
        + [pltpu.VMEM((CHUNKS * tokens, HEAD), jnp.bfloat16)] * 2
        + wire_shapes(30),
        56,
    )
    return outs[:2], outs[2], outs[3], outs[4]


def norm_back(values, gain, gradient):
    factor = lax.rsqrt(jnp.mean(values * values, axis=1, keepdims=True) + epsilon)
    scaled = values * factor
    pulled = gradient * gain
    back = factor * (pulled - scaled * jnp.mean(pulled * scaled, axis=1, keepdims=True))
    return back, gradient * scaled


def feed_forward(normed_own, normed_late, out_grads, weights, middle, out_grad_own, gain, units):
    _, rows, width = middle.shape
    tokens = 2 * rows
    shards, columns = weights.shape[0], weights.shape[2]
    whole_pair = bf16(2, CHIPS, tokens, width)

    def kernel(*refs):
        normed_ref, normed_late_ref, *grads = refs[:4]
        weight_ref, middle_ref, own_grad, gain_ref = refs[4:8]
        normed_early, branch = refs[8:10]
        hidden, unit_grads = refs[10:12], refs[12:14]
        back_parts, out_parts = (refs[14:16], refs[16:18]), (refs[18:20], refs[20:22])
        middle_grad, gain_sum, landing = refs[22], refs[23], refs[24:27]
        stage, own_branch, wires = refs[27:31], refs[31], Wires(*refs[32:])
        meet()
        gain_sum[...] = jnp.zeros(gain_sum.shape, jnp.float32)

        def done(chunk, span, total):
            back, gain_terms = norm_back(middle_ref[2 + chunk, span], gain_ref[...], total)
            gain_sum[...] += gain_terms
            back = back + own_grad[2 + chunk, span].astype(jnp.float32)
            middle_grad[chunk, span] = back
            own_branch[chunk, span] = back.astype(jnp.bfloat16)

        move = Gather(wires, [normed_ref.at[0], normed_ref.at[1]], normed_early)
        sums = Scatter(wires, *back_parts[1], landing, stage, done)
        late_move = Gather(wires, [own_branch.at[0], own_branch.at[1]], branch)
        move.first()
        feed_phase(
            normed_late_ref, grads[1], hidden[1], unit_grads[1], back_parts[1], out_parts[1], weight_ref,
            {2: move.second, 5: move.third},
        )
        sums.first()
        move.last()
        feed_phase(
            normed_early, grads[0], hidden[0], unit_grads[0], back_parts[0], out_parts[0], weight_ref,
            {1: sums.second, 4: sums.third, 6: lambda: (sums.last(), late_move.first()) and None},
        )
        late_move.second()
        late_move.third()
        late_move.last()

    outs = call(
        kernel,
        3,
        [(normed_own, HBM), (normed_late, HBM)]
        + [(grads, HBM) for grads in out_grads]
        + [(weights, VMEM), (middle, VMEM), (out_grad_own, VMEM), (gain, VMEM)],
        [(whole_pair, HBM)] * 2
        + [(bf16(2, CHIPS, tokens, units), HBM)] * 2
        + [(bf16(shards, 2, CHIPS, tokens, columns), HBM)] * 2
        + [(shape, HBM) for shape in partial_shapes(rows, width)] * 4
        + [(f32(2, rows, width), VMEM), (f32(STRIPE, width), VMEM)]
        + [(shape, HBM) for shape in landing_shapes(rows, width)],
        stage_shapes(rows, width) + [pltpu.VMEM((2, rows, width), jnp.bfloat16)] + wire_shapes(40),
        62,
    )
    return outs[0], outs[1], outs[2:4], outs[4:6], outs[6:8], (outs[10:12], outs[12:14]), outs[14], outs[15]


def attend_back(
    states, lengths, places, out_weight, weight, cosine, sine, branch_late, back_early, out_parts,
    middle, out_grad_own, inputs, middle_grad_late, gains
):
    _, rows, width = middle.shape
    tokens = 2 * rows

    def kernel(*refs):
        states_in, (lengths_ref, place_q, place_k, out_ref, weight_ref, cosine_ref, sine_ref) = (
            refs[:2],
            refs[2:9],
        )
        late_branch, back_parts, outs_in = refs[9], refs[10:12], (refs[12:14], refs[14:16])
        middle_ref, own_grad, inputs_ref, late_grad, gain_one, gain_two = refs[16:22]
        head_grads, early_branch, outputs, input_grad = refs[22:24], refs[24], refs[25], refs[26]
        gain_sums = refs[27]
        parts = (refs[28:30], refs[30:32])
        landings = [refs[32 + 3 * place : 35 + 3 * place] for place in range(5)]
        stage, early_grad, own_branch, keys, values = refs[47:51], refs[51], refs[52], refs[53], refs[54]
        sums, late_sums, wires = refs[55:57], refs[57:59], Wires(*refs[59:])
        meet()
        gain_sums[...] = jnp.zeros(gain_sums.shape, jnp.float32)

        def middle_done(chunk, span, total):
            back, gain_terms = norm_back(
                middle_ref[chunk, span].astype(jnp.float32), gain_two[...], total
            )
            gain_sums[1] += gain_terms
            back = back + own_grad[chunk, span].astype(jnp.float32)
            early_grad[chunk, span] = back
            own_branch[chunk, span] = back.astype(jnp.bfloat16)

        def output_done(pair):
            def done(chunk, span, total):
                at = 2 * pair + chunk
                outputs[at, span] = (middle_ref[at, span] + total).astype(jnp.bfloat16)

            return done

        def input_done(pair):
            def done(chunk, span, total):
                at = 2 * pair + chunk
                back, gain_terms = norm_back(
                    inputs_ref[at, span].astype(jnp.float32), gain_one[...], total
                )
                gain_sums[0] += gain_terms
                direct = late_grad if pair == 1 else early_grad
                input_grad[at, span] = (direct[chunk, span] + back).astype(jnp.bfloat16)

            return done

        middle_sum = Scatter(wires, *back_parts, landings[0], stage, middle_done)
        move = Gather(wires, [own_branch.at[0], own_branch.at[1]], early_branch)
        output_sums = [
            Scatter(wires, *outs_in[pair], landings[1 + pair], stage, output_done(pair))
            for pair in range(2)
        ]
        input_sums = [
            Scatter(wires, *parts[pair], landings[3 + pair], stage, input_done(pair)) for pair in range(2)
        ]

        def back_through(pair, branch, actions):
            attend_back_phase(
                pair, branch, states_in, head_grads[pair], *parts[pair], lengths_ref,
                (place_q, place_k), out_ref, weight_ref, (cosine_ref.at[pair], sine_ref.at[pair]),
                keys, values, sums, late_sums, actions,
            )

        def both(*steps):
            def run():
                for step in steps:
                    step()

            return run

        middle_sum.first()
        output_sums[1].first()
        back_through(
            1,
            late_branch,
            {1: middle_sum.second, 5: middle_sum.third, 7: both(middle_sum.last, move.first)},
        )
        move.second()
        input_sums[1].first()
        output_sums[1].second()
        move.third()
        move.last()
        output_sums[0].first()
        back_through(
            0,
            early_branch,
            {
                1: both(output_sums[1].third, input_sums[1].second),
                4: both(output_sums[1].last, input_sums[1].third),
                6: both(input_sums[1].last, output_sums[0].second),
            },
        )
        input_sums[0].first()
        output_sums[0].third()
        input_sums[0].second()
        output_sums[0].last()
        input_sums[0].third()
        input_sums[0].last()

    outs = call(
        kernel,
        4,
        [(state, HBM) for state in states]
        + [(lengths, SMEM), (places[0], VMEM), (places[1], VMEM), (out_weight, VMEM), (weight, VMEM)]
        + [(cosine, HBM), (sine, HBM), (branch_late, HBM)]
        + [(part, HBM) for part in back_early]
        + [(part, HBM) for parts in out_parts for part in parts]
        + [(middle, VMEM), (out_grad_own, VMEM), (inputs, VMEM), (middle_grad_late, VMEM)]
        + [(gains[0], VMEM), (gains[1], VMEM)],
        [(bf16(2, CHIPS, tokens, 3 * HEAD), HBM)] * 2
        + [(bf16(2, CHIPS, tokens, width), HBM)]
        + [(bf16(CHUNKS, rows, width), VMEM)] * 2
        + [(f32(2, STRIPE, width), VMEM)]
        + [(shape, HBM) for shape in partial_shapes(rows, width)] * 2
        + [(shape, HBM) for shape in landing_shapes(rows, width)] * 5,
        stage_shapes(rows, width)
        + [pltpu.VMEM((2, rows, width), jnp.float32), pltpu.VMEM((2, rows, width), jnp.bfloat16)]
        + [pltpu.VMEM((CHUNKS * tokens, HEAD), jnp.bfloat16)] * 2
        + [pltpu.VMEM((CHIPS, 2 * tokens, HEAD), jnp.float32)] * 2
        + [pltpu.VMEM((2 * tokens, HEAD), jnp.float32)] * 2
        + wire_shapes(50),
        63,
    )
    return outs[:2], outs[2], outs[3], outs[4], outs[5]


def unit_weight_grads(unit_grads, rows_in):
    shards, _, _, tokens, columns = unit_grads[0].shape
    width = rows_in[0].shape[3]

    def kernel(late_units, late_rows, early_units, early_rows, out, total):
        step = pl.program_id(1)

        @pl.when(step == 0)
        def _():
            total[...] = jnp.zeros(total.shape, jnp.float32)

        for place, (units, rows_ref) in enumerate(((late_units, late_rows), (early_units, early_rows))):

            @pl.when(lax.div(step, 2) == place)
            def _():
                left = units[0, 0].reshape(CHIPS * tokens, columns)
                right = rows_ref[0].reshape(CHIPS * tokens, width)
                total[...] += dot_tn(left, right)

        @pl.when(step == 3)
        def _():
            out[0] = total[...].astype(jnp.bfloat16)

    late = lambda step: jnp.minimum(step, 1)
    early = lambda step: jnp.maximum(step - 2, 0)
    specs = []
    for at in (late, early):
        specs.append(
            pl.BlockSpec(
                (1, 1, CHIPS, tokens, columns),
                (lambda at: lambda shard, step: (shard, at(step), 0, 0, 0))(at),
            )
        )
        specs.append(
            pl.BlockSpec(
                (1, CHIPS, tokens, width), (lambda at: lambda shard, step: (at(step), 0, 0, 0))(at)
            )
        )
    return pl.pallas_call(
        kernel,
        grid=(shards, 4),
        in_specs=specs,
        out_specs=pl.BlockSpec((1, columns, width), lambda shard, step: (shard, 0, 0)),
        out_shape=bf16(shards, columns, width),
        scratch_shapes=[pltpu.VMEM((columns, width), jnp.float32)],
        compiler_params=params(60),
    )(unit_grads[1], rows_in[1], unit_grads[0], rows_in[0])


def dot(left, right):
    return jnp.dot(left, right, preferred_element_type=jnp.float32)


def dot_t(left, right):
    return lax.dot_general(
        left, right, (((1,), (1,)), ((), ())), preferred_element_type=jnp.float32
    )


def dot_tn(left, right):
    return lax.dot_general(
        left, right, (((0,), (0,)), ((), ())), preferred_element_type=jnp.float32
    )


def spin(values, cosine, sine):
    halfway = values.shape[1] // 2
    first, second = values[:, :halfway], values[:, halfway:]
    return jnp.concatenate(
        [first * cosine - second * sine, second * cosine + first * sine], axis=1
    )


def spin_back(values, cosine, sine):
    return spin(values, cosine, -sine)


def whole(shape):
    return pl.BlockSpec(shape, lambda *_: (0,) * len(shape), pipeline_mode=pl.Buffered(1))


def params(megabytes):
    return pltpu.CompilerParams(vmem_limit_bytes=megabytes * MB)


def seen(place_q, place_k, chunk, count, tokens, lengths_ref, chip):
    query_index = tokens * chunk + place_q
    key_index = place_k[:, :count]
    ahead_or_here = key_index <= query_index
    if tokens * (chunk + 1) <= PROMPT:
        return ahead_or_here

    def segment(index):
        found = jnp.full(index.shape, -1, jnp.int32)
        for slot in range(NCONT):
            found = jnp.where(index >= PROMPT + slot * CONT, slot, found)
        return found

    key_segment, query_segment = segment(key_index), segment(query_index)
    end = jnp.full(key_index.shape, PROMPT, jnp.int32)
    for slot in range(NCONT):
        end = jnp.where(
            key_segment == slot, PROMPT + slot * CONT + lengths_ref[chip, slot], end
        )
    alive = key_index < end
    return ahead_or_here & ((key_segment < 0) | ((key_segment == query_segment) & alive))


def token_dot(left, right):
    return lax.dot_general(
        left.reshape(-1, left.shape[-1]),
        right.reshape(-1, right.shape[-1]),
        (((0,), (0,)), ((), ())),
        preferred_element_type=jnp.float32,
    )


def exchange(value, axis):
    return lax.all_to_all(value, axis, split_axis=0, concat_axis=0, tiled=True)


def plane_device(
    activations,
    cotangent,
    continuation_lengths,
    query_weight,
    key_weight,
    value_weight,
    output_weight,
    gate_weight,
    up_weight,
    down_weight,
    attention_gain,
    feedforward_gain,
    moment_query,
    moment_key,
    moment_value,
    moment_output,
    moment_gate,
    moment_up,
    moment_down,
    moment_attention,
    moment_feedforward,
):
    devices, planes = lax.axis_size("dp"), lax.axis_size("fsdp")
    place, plane = lax.axis_index("dp"), lax.axis_index("fsdp")
    core = place % 2
    low = jnp.bfloat16
    kv_width = KV_HEADS * HEAD
    tokens = activations.shape[1]
    half = tokens // 2

    inputs = to_planes(activations, core, plane)

    in_rows = query_weight.shape[0]
    sub_rows = in_rows // planes
    spread = devices * sub_rows
    mixed_kv = jnp.stack([key_weight.astype(low), value_weight.astype(low)], axis=1)
    block = jnp.concatenate([query_weight.astype(low).reshape(in_rows, 2, HEAD), mixed_kv], axis=2)
    block = jnp.stack(trade_planes(block.reshape(planes, sub_rows, 2, 2 * HEAD), plane))
    block = block.transpose(0, 2, 1, 3).reshape(devices, sub_rows, 2 * HEAD)
    block = exchange(block, "dp")
    attention_block = jnp.concatenate(
        [block.reshape(spread, 2 * HEAD), output_weight.astype(low)], axis=0
    )
    found = jnp.stack(gather_planes(after(attention_block, inputs)))
    attention_all = jnp.stack([pick(found, label ^ plane) for label in range(CHUNKS)])
    packed = (
        attention_all[:, :spread]
        .reshape(planes, devices, sub_rows, 2 * HEAD)
        .transpose(1, 0, 2, 3)
        .reshape(D, 2 * HEAD)
    )
    other_half = across(packed[:, HEAD:], CORE)
    key_part = jnp.where(core == 0, packed[:, HEAD:], other_half)
    value_part = jnp.where(core == 0, other_half, packed[:, HEAD:])
    head_weight = jnp.concatenate([packed[:, :HEAD], key_part, value_part], axis=1)
    head_output = attention_all[:, spread:].transpose(1, 0, 2).reshape(HEAD, D)

    strip = 128
    runs = gate_weight.shape[1] // (devices * strip)
    units = runs * strip * planes
    gate_up = jnp.stack(
        [
            gate_weight.astype(low).reshape(in_rows, runs, devices, strip),
            up_weight.astype(low).reshape(in_rows, runs, devices, strip),
        ]
    )
    gate_up = gate_up.transpose(3, 1, 0, 2, 4).reshape(devices, in_rows, 2 * runs * strip)
    gate_up = exchange(gate_up, "dp").reshape(devices * in_rows, 2 * runs * strip)
    down_columns = down_weight.shape[1]
    down = exchange(down_weight.astype(low).reshape(devices, strip, down_columns), "dp")
    feed_block = jnp.concatenate([gate_up, down.reshape(devices * strip, down_columns)], axis=0)

    out_grads = to_planes(after(cotangent, attention_all), core, plane)
    feed_weights = lax.all_gather(after(feed_block, out_grads), "fsdp", axis=0, tiled=False)

    others = across(continuation_lengths, CORE)
    swap = core == 1
    here = jnp.concatenate(
        [
            jnp.where(swap, others, continuation_lengths),
            jnp.where(swap, continuation_lengths, others),
        ]
    )
    here = pick(here, plane)
    near = jnp.stack([here, across(here, SIDE_A)])
    lengths = jnp.concatenate([near, across(near, SIDE_B)])

    inside = jnp.concatenate(
        [core * half + jnp.arange(half), (1 - core) * half + jnp.arange(half)]
    ).astype(jnp.int32)
    order = (tokens * jnp.arange(CHUNKS, dtype=jnp.int32)[:, None] + inside[None, :]).reshape(-1)
    cosine, sine = rope_angles(token_places(order))
    cosine = cosine.reshape(2, 2, tokens, HEAD // 2)
    sine = sine.reshape(2, 2, tokens, HEAD // 2)
    place_q, place_k = inside[:, None], order[None, :]
    blocks = plane ^ jnp.arange(CHUNKS, dtype=jnp.int32)

    own_inputs, own_grads = jnp.stack(inputs), jnp.stack(out_grads)
    normed, _ = rms_rows(own_inputs.astype(jnp.float32), attention_gain)
    gain_one, gain_two = attention_gain[None, :], feedforward_gain[None, :]
    rows_all, grads_all, states = gather_and_project(
        normed.astype(low), own_grads, head_weight, cosine, sine
    )
    mixed, middle, normed_two, normed_late = attend_and_norm(
        states, lengths, (place_q, place_k), head_output, own_inputs, gain_two
    )
    normed_early, branch_late, hidden, unit_grads, back_early, out_parts, middle_grad, gain_sum = feed_forward(
        normed_two, normed_late, grads_all, feed_weights, middle, own_grads, gain_two, units
    )
    unit_sum = unit_weight_grads(unit_grads, (normed_early, normed_late))
    unit_sum = lax.psum_scatter(unit_sum, "fsdp", scatter_dimension=0, tiled=False)
    down_sum = reduce(jnp.add, [token_dot(hidden[pair], grads_all[pair]) for pair in (1, 0)]).astype(low)
    down_sum = down_sum.reshape(-1, planes, down_columns).transpose(1, 0, 2)
    down_sum = lax.psum_scatter(down_sum, "fsdp", scatter_dimension=0, tiled=False)
    head_grads, branch_early, own_outputs, own_input_grad, gain_sums = attend_back(
        states,
        lengths,
        (place_q, place_k),
        head_output,
        head_weight,
        cosine,
        sine,
        branch_late,
        back_early,
        out_parts,
        middle,
        own_grads,
        own_inputs,
        middle_grad,
        (gain_one, gain_two),
    )
    outputs = from_planes([own_outputs[chunk] for chunk in range(CHUNKS)], core, plane)
    input_grad = from_planes([own_input_grad[chunk] for chunk in range(CHUNKS)], core, plane)
    attention_sum = jnp.sum(gain_sums[0], axis=0)
    feedforward_sum = jnp.sum(gain_sums[1] + gain_sum, axis=0)

    strips = runs * strip
    unit_sum = unit_sum.reshape(2 * strips, devices, in_rows).swapaxes(0, 1)
    unit_sum = exchange(unit_sum, "dp").reshape(devices, 2, runs, strip, in_rows)
    gate_up_owned = unit_sum.transpose(1, 4, 2, 0, 3).reshape(2, in_rows, runs * devices * strip)
    down_owned = exchange(down_sum.reshape(devices, strip, down_columns), "dp")
    down_owned = down_owned.reshape(devices * strip, down_columns)
    head_sum = reduce(
        jnp.add, [token_dot(rows_all[pair], head_grads[pair]) for pair in (1, 0)]
    ).astype(low)
    branches = (branch_early, branch_late)
    output_sum = reduce(jnp.add, [token_dot(mixed[pair], branches[pair]) for pair in (1, 0)]).astype(low)
    given = jnp.where(core == 0, head_sum[:, 2 * HEAD :], head_sum[:, HEAD : 2 * HEAD])
    kept = jnp.where(core == 0, head_sum[:, HEAD : 2 * HEAD], head_sum[:, 2 * HEAD :])
    kv_sum = (kept.astype(jnp.float32) + across(given, CORE).astype(jnp.float32)).astype(low)
    head_sum = jnp.concatenate([head_sum[:, :HEAD], kv_sum], axis=1)
    head_sum = head_sum.reshape(devices, planes, sub_rows, 2 * HEAD).transpose(1, 0, 2, 3)
    head_sum = head_sum.reshape(planes, spread, 2 * HEAD)
    output_sum = output_sum.reshape(HEAD, planes, 2 * HEAD).transpose(1, 0, 2)
    attention_parts = jnp.concatenate([head_sum, output_sum], axis=1)
    attention_grad = sum_planes([pick(attention_parts, blocks[shard]) for shard in range(CHUNKS)])
    output_owned = attention_grad[spread:]
    block = exchange(attention_grad[:spread].astype(low).reshape(devices, sub_rows, 2 * HEAD), "dp")
    block = block.reshape(planes, 2, sub_rows, 2 * HEAD).transpose(0, 2, 1, 3)
    block = jnp.stack(trade_planes(block, plane)).reshape(in_rows, 2, 2 * HEAD)
    query_owned = block[:, :, :HEAD].reshape(in_rows, 2 * HEAD)
    key_owned, value_owned = block[:, 0, HEAD:], block[:, 1, HEAD:]
    owner_grads = [
        owned.astype(jnp.float32)
        for owned in (
            query_owned,
            key_owned,
            value_owned,
            output_owned,
            gate_up_owned[0],
            gate_up_owned[1],
            down_owned,
        )
    ]
    local_square = reduce(jnp.add, [jnp.sum(owned * owned) for owned in owner_grads])
    attention_total, feedforward_total = sum_all(jnp.stack([attention_sum, feedforward_sum]))
    square_total = sum_all(jnp.full((8, 128), local_square))[0, 0]
    square_sum = (
        square_total
        + jnp.sum(attention_total * attention_total)
        + jnp.sum(feedforward_total * feedforward_total)
    )
    grad_norm = jnp.sqrt(square_sum)
    entry_count = 2 * D * D + 2 * D * kv_width + 3 * D * FF + 2 * D
    limit = clip_level * math.sqrt(entry_count)
    factor = limit / jnp.maximum(grad_norm, limit)
    gradients = owner_grads + [attention_total, feedforward_total]
    old_moments = [
        moment_query,
        moment_key,
        moment_value,
        moment_output,
        moment_gate,
        moment_up,
        moment_down,
        moment_attention,
        moment_feedforward,
    ]
    old_params = [
        query_weight,
        key_weight,
        value_weight,
        output_weight,
        gate_weight,
        up_weight,
        down_weight,
        attention_gain,
        feedforward_gain,
    ]
    new_moments = [
        0.5 * moment + 0.5 * factor * gradient for moment, gradient in zip(old_moments, gradients)
    ]
    new_params = []
    for at, param in enumerate(old_params):
        if at < 7:
            new_params.append(param - step_size * (new_moments[at] + decay_rate * param))
        else:
            new_params.append(param - gain_step * new_moments[at])
    return (outputs, input_grad, grad_norm, *new_moments, *new_params)


def solution(mesh):
    whole_groups_on_planes = mesh.shape["dp"] == HEADS and mesh.shape["fsdp"] == KV_HEADS
    body = plane_device if whole_groups_on_planes else on_device
    placed = (
        P("dp", "fsdp", None),
        P("dp", "fsdp", None),
        P("dp", None),
        P("dp", "fsdp"),
        P("dp", "fsdp"),
        P("dp", "fsdp"),
        P("dp", "fsdp"),
        P("dp", "fsdp"),
        P("dp", "fsdp"),
        P("dp", "fsdp"),
        P(),
        P(),
        P("dp", "fsdp"),
        P("dp", "fsdp"),
        P("dp", "fsdp"),
        P("dp", "fsdp"),
        P("dp", "fsdp"),
        P("dp", "fsdp"),
        P("dp", "fsdp"),
        P(),
        P(),
    )
    return jax.shard_map(
        body,
        mesh=mesh,
        in_specs=placed,
        out_specs=(
            P("dp", "fsdp", None),
            P("dp", "fsdp", None),
            P(),
            P("dp", "fsdp"),
            P("dp", "fsdp"),
            P("dp", "fsdp"),
            P("dp", "fsdp"),
            P("dp", "fsdp"),
            P("dp", "fsdp"),
            P("dp", "fsdp"),
            P(),
            P(),
            P("dp", "fsdp"),
            P("dp", "fsdp"),
            P("dp", "fsdp"),
            P("dp", "fsdp"),
            P("dp", "fsdp"),
            P("dp", "fsdp"),
            P("dp", "fsdp"),
            P(),
            P(),
        ),
        check_vma=False,
    )
```

```python
from functools import reduce
import math

import jax
import jax.numpy as jnp
from jax import lax
from jax.experimental import pallas as pl
from jax.experimental.pallas import tpu as pltpu
from jax.sharding import PartitionSpec as P

D = 2048
HEADS = 8
KV_HEADS = 4
HEAD = 256
FF = 8192
PROMPT = 1024
CONT = 64
NCONT = 2


epsilon = 1e-06
rope_base = 1000042.0
step_size = 0.2
gain_step = 4.0
decay_rate = 0.1
clip_level = 0.25
floor_score = -1e30


def rms_rows(values, gain):
    factor = lax.rsqrt(jnp.mean(values * values, axis=-1, keepdims=True) + epsilon)
    return (values * factor * gain, factor)


def rms_back(values, factor, gain, gradient):
    scaled = values * factor
    gain_grad = jnp.sum(gradient * scaled, axis=0)
    pulled = gradient * gain
    return (
        factor * (pulled - scaled * jnp.mean(pulled * scaled, axis=-1, keepdims=True)),
        gain_grad,
    )


def rope_angles(places):
    halfway = HEAD // 2
    freqs = rope_base ** (-(jnp.arange(halfway).astype(jnp.float32) * 2.0 / HEAD))
    angles = places.astype(jnp.float32)[:, None] * freqs[None, :]
    return (jnp.cos(angles), jnp.sin(angles))


def token_places(index):
    inside = index - PROMPT
    return jnp.where(index < PROMPT, index, PROMPT + inside % CONT)


def segment_of(index):
    return jnp.where(index < PROMPT, -1, (index - PROMPT) // CONT)


def visible(query_index, key_index, lengths):
    key_segment = segment_of(key_index)
    key_offset = key_index - PROMPT - key_segment * CONT
    slots = jnp.arange(NCONT, dtype=jnp.int32)
    limits = jnp.sum(jnp.where(key_segment[:, None] == slots[None, :], lengths[None, :], 0), axis=1)
    alive = key_offset < limits
    same = segment_of(query_index)[:, None] == key_segment[None, :]
    causal = key_index[None, :] <= query_index[:, None]
    return causal & ((key_index < PROMPT)[None, :] | same & alive[None, :])


def rotate(values, cosine, sine):
    halfway = values.shape[-1] // 2
    first, second = (values[..., :halfway], values[..., halfway:])
    cosine, sine = (cosine[:, None, :], sine[:, None, :])
    return jnp.concatenate(
        [first * cosine - second * sine, second * cosine + first * sine], axis=-1
    )


def rotate_back(grads, cosine, sine):
    halfway = grads.shape[-1] // 2
    first, second = (grads[..., :halfway], grads[..., halfway:])
    cosine, sine = (cosine[:, None, :], sine[:, None, :])
    return jnp.concatenate(
        [first * cosine + second * sine, second * cosine - first * sine], axis=-1
    )


def join_blocks(pieces, shard_count):
    height = pieces[0].shape[0]
    return jnp.concatenate(
        [member.reshape(height, shard_count, -1) for member in pieces], axis=2
    ).reshape(height, -1)


def split_blocks(merged, breadths, shard_count):
    height = merged.shape[0]
    blocks = merged.reshape(height, shard_count, -1)
    result = []
    offset = 0
    for breadth in breadths:
        result.append(
            blocks[:, :, offset : offset + breadth].reshape(height, shard_count * breadth)
        )
        offset = offset + breadth
    return result


def ahead(operand, shard):
    return jnp.dot(
        operand,
        lax.all_gather(shard, "fsdp", axis=1, tiled=True),
        preferred_element_type=jnp.float32,
    )


def behind(gradient, shard):
    return lax.dot_general(
        gradient,
        lax.all_gather(shard, "fsdp", axis=1, tiled=True),
        (((1,), (1,)), ((), ())),
        preferred_element_type=jnp.float32,
    )


def weight_term(gradient, operand):
    operand_all = lax.all_gather(operand, "fsdp", axis=0, tiled=True)
    owned_columns = lax.all_to_all(gradient, "fsdp", split_axis=1, concat_axis=0, tiled=True)
    return lax.dot_general(
        owned_columns, operand_all, (((0,), (0,)), ((), ())), preferred_element_type=jnp.float32
    )


def on_device(
    activations,
    cotangent,
    continuation_lengths,
    query_weight,
    key_weight,
    value_weight,
    output_weight,
    gate_weight,
    up_weight,
    down_weight,
    attention_gain,
    feedforward_gain,
    moment_query,
    moment_key,
    moment_value,
    moment_output,
    moment_gate,
    moment_up,
    moment_down,
    moment_attention,
    moment_feedforward,
):
    shard_count = lax.axis_size("fsdp")
    kv_width = KV_HEADS * HEAD
    repeat = HEADS // KV_HEADS
    scale = 1.0 / math.sqrt(HEAD)
    gathered = (
        lax.all_gather(query_weight.astype(jnp.bfloat16), "dp", axis=0, tiled=True),
        lax.all_gather(key_weight.astype(jnp.bfloat16), "dp", axis=0, tiled=True),
        lax.all_gather(value_weight.astype(jnp.bfloat16), "dp", axis=0, tiled=True),
        lax.all_gather(output_weight.astype(jnp.bfloat16), "dp", axis=0, tiled=True),
        lax.all_gather(gate_weight.astype(jnp.bfloat16), "dp", axis=0, tiled=True),
        lax.all_gather(up_weight.astype(jnp.bfloat16), "dp", axis=0, tiled=True),
        lax.all_gather(down_weight.astype(jnp.bfloat16), "dp", axis=0, tiled=True),
    )
    merged_attn = join_blocks(gathered[0:3], 1)
    merged_output = gathered[3]
    merged_ffn = join_blocks(gathered[4:6], 1)
    merged_down = gathered[6]
    query_cols = D // shard_count
    key_cols = kv_width // shard_count
    ffn_cols = FF // shard_count
    attn_breadths = (query_cols, key_cols, key_cols)
    ffn_breadths = (ffn_cols, ffn_cols)
    local_rows = activations.shape[1]
    group_rows = local_rows * shard_count
    query_index = lax.axis_index("fsdp") * local_rows + jnp.arange(local_rows, dtype=jnp.int32)
    key_index = jnp.arange(group_rows, dtype=jnp.int32)
    cosine, sine = rope_angles(token_places(query_index))
    sums = [jnp.zeros((matrix.shape[1], matrix.shape[0]), jnp.float32) for matrix in gathered]
    attention_sum = jnp.zeros((D,), jnp.float32)
    feedforward_sum = jnp.zeros((D,), jnp.float32)
    output_list = []
    input_list = []
    for micro_batch in range(activations.shape[0]):
        allowed = visible(query_index, key_index, continuation_lengths[micro_batch])
        inputs = activations[micro_batch].astype(jnp.float32)
        normed_float, factor_one = rms_rows(inputs, attention_gain)
        normed = normed_float.astype(jnp.bfloat16)
        pre_query, pre_key, pre_value = split_blocks(
            ahead(normed, merged_attn), attn_breadths, shard_count
        )
        queries = (
            rotate(pre_query.reshape(local_rows, HEADS, HEAD), cosine, sine)
            .astype(jnp.bfloat16)
            .reshape(local_rows, KV_HEADS, repeat, HEAD)
        )
        keys = rotate(pre_key.reshape(local_rows, KV_HEADS, HEAD), cosine, sine).astype(
            jnp.bfloat16
        )
        values = pre_value.astype(jnp.bfloat16).reshape(local_rows, KV_HEADS, HEAD)
        keys_all, values_all = (
            lax.all_gather(keys, "fsdp", axis=0, tiled=True),
            lax.all_gather(values, "fsdp", axis=0, tiled=True),
        )
        raw = (
            jnp.einsum("qgrd,kgd->grqk", queries, keys_all, preferred_element_type=jnp.float32)
            * scale
        )
        raw = jnp.where(allowed[None, None], raw, floor_score)
        highest = jnp.max(raw, axis=-1, keepdims=True)
        exponent = jnp.exp(raw - highest)
        denominator = jnp.sum(exponent, axis=-1, keepdims=True)
        logsum = highest + jnp.log(denominator)
        probs_low = (exponent / denominator).astype(jnp.bfloat16)
        mixed = (
            jnp.einsum("grqk,kgd->qgrd", probs_low, values_all, preferred_element_type=jnp.float32)
            .reshape(local_rows, D)
            .astype(jnp.bfloat16)
        )
        middle = inputs + ahead(mixed, merged_output)
        normed_two_float, factor_two = rms_rows(middle, feedforward_gain)
        normed_two = normed_two_float.astype(jnp.bfloat16)
        gate, upward = split_blocks(ahead(normed_two, merged_ffn), ffn_breadths, shard_count)
        sigmoid = jax.nn.sigmoid(gate)
        swish = gate * sigmoid
        hidden = (swish * upward).astype(jnp.bfloat16)
        result = middle + ahead(hidden, merged_down)
        output_list.append(result.astype(jnp.bfloat16))
        out_grad = cotangent[micro_batch]
        hidden_grad = behind(out_grad, merged_down)
        sums[6] = sums[6] + weight_term(out_grad, hidden)
        gate_grad = (hidden_grad * upward * sigmoid * (1.0 + gate * (1.0 - sigmoid))).astype(
            jnp.bfloat16
        )
        up_grad = (hidden_grad * swish).astype(jnp.bfloat16)
        ffn_grad = join_blocks((gate_grad, up_grad), shard_count)
        ffn_term = weight_term(ffn_grad, normed_two)
        sums[4] = sums[4] + ffn_term[:ffn_cols]
        sums[5] = sums[5] + ffn_term[ffn_cols:]
        normed_two_grad = behind(ffn_grad, merged_ffn)
        middle_back, feed_gain_grad = rms_back(
            middle, factor_two, feedforward_gain, normed_two_grad
        )
        middle_grad = out_grad.astype(jnp.float32) + middle_back
        branch_grad = middle_grad.astype(jnp.bfloat16)
        sums[3] = sums[3] + weight_term(branch_grad, mixed)
        mixed_grad = (
            behind(branch_grad, merged_output)
            .astype(jnp.bfloat16)
            .reshape(local_rows, KV_HEADS, repeat, HEAD)
        )
        raw_again = (
            jnp.einsum("qgrd,kgd->grqk", queries, keys_all, preferred_element_type=jnp.float32)
            * scale
        )
        raw_again = jnp.where(allowed[None, None], raw_again, floor_score)
        probs_again = jnp.exp(raw_again - logsum)
        value_part = jnp.einsum(
            "grqk,qgrd->kgd",
            probs_again.astype(jnp.bfloat16),
            mixed_grad,
            preferred_element_type=jnp.float32,
        )
        prob_grad = jnp.einsum(
            "qgrd,kgd->grqk", mixed_grad, values_all, preferred_element_type=jnp.float32
        )
        inner = jnp.sum(probs_again * prob_grad, axis=-1, keepdims=True)
        score_grad = (probs_again * (prob_grad - inner)).astype(jnp.bfloat16)
        query_grad = (
            jnp.einsum("grqk,kgd->qgrd", score_grad, keys_all, preferred_element_type=jnp.float32)
            * scale
        )
        key_part = (
            jnp.einsum("grqk,qgrd->kgd", score_grad, queries, preferred_element_type=jnp.float32)
            * scale
        )
        key_grad, value_grad = (
            lax.psum_scatter(
                key_part.astype(jnp.bfloat16), "fsdp", scatter_dimension=0, tiled=True
            ).astype(jnp.float32),
            lax.psum_scatter(
                value_part.astype(jnp.bfloat16), "fsdp", scatter_dimension=0, tiled=True
            ).astype(jnp.float32),
        )
        pre_query_grad = (
            rotate_back(query_grad.reshape(local_rows, HEADS, HEAD), cosine, sine)
            .reshape(local_rows, D)
            .astype(jnp.bfloat16)
        )
        pre_key_grad = (
            rotate_back(key_grad, cosine, sine).reshape(local_rows, kv_width).astype(jnp.bfloat16)
        )
        pre_value_grad = value_grad.reshape(local_rows, kv_width).astype(jnp.bfloat16)
        attn_grad = join_blocks((pre_query_grad, pre_key_grad, pre_value_grad), shard_count)
        attn_term = weight_term(attn_grad, normed)
        sums[0] = sums[0] + attn_term[:query_cols]
        sums[1] = sums[1] + attn_term[query_cols : query_cols + key_cols]
        sums[2] = sums[2] + attn_term[query_cols + key_cols :]
        normed_grad = behind(attn_grad, merged_attn)
        input_back, attn_gain_grad = rms_back(inputs, factor_one, attention_gain, normed_grad)
        input_list.append((middle_grad + input_back).astype(jnp.bfloat16))
        attention_sum = attention_sum + attn_gain_grad
        feedforward_sum = feedforward_sum + feed_gain_grad
    reduced = (
        lax.psum_scatter(
            sums[0].astype(jnp.bfloat16), "dp", scatter_dimension=1, tiled=True
        ).astype(jnp.float32),
        lax.psum_scatter(
            sums[1].astype(jnp.bfloat16), "dp", scatter_dimension=1, tiled=True
        ).astype(jnp.float32),
        lax.psum_scatter(
            sums[2].astype(jnp.bfloat16), "dp", scatter_dimension=1, tiled=True
        ).astype(jnp.float32),
        lax.psum_scatter(
            sums[3].astype(jnp.bfloat16), "dp", scatter_dimension=1, tiled=True
        ).astype(jnp.float32),
        lax.psum_scatter(
            sums[4].astype(jnp.bfloat16), "dp", scatter_dimension=1, tiled=True
        ).astype(jnp.float32),
        lax.psum_scatter(
            sums[5].astype(jnp.bfloat16), "dp", scatter_dimension=1, tiled=True
        ).astype(jnp.float32),
        lax.psum_scatter(
            sums[6].astype(jnp.bfloat16), "dp", scatter_dimension=1, tiled=True
        ).astype(jnp.float32),
    )
    owner_grads = [owned.T for owned in reduced]
    local_square = reduce(jnp.add, [jnp.sum(owned * owned) for owned in owner_grads])
    attention_total, feedforward_total, square_total = lax.psum(
        (attention_sum, feedforward_sum, local_square), ("dp", "fsdp")
    )
    square_sum = (
        square_total
        + jnp.sum(attention_total * attention_total)
        + jnp.sum(feedforward_total * feedforward_total)
    )
    grad_norm = jnp.sqrt(square_sum)
    entry_count = 2 * D * D + 2 * D * kv_width + 3 * D * FF + 2 * D
    limit = clip_level * math.sqrt(entry_count)
    factor = limit / jnp.maximum(grad_norm, limit)
    gradients = owner_grads + [attention_total, feedforward_total]
    old_moments = [
        moment_query,
        moment_key,
        moment_value,
        moment_output,
        moment_gate,
        moment_up,
        moment_down,
        moment_attention,
        moment_feedforward,
    ]
    old_params = [
        query_weight,
        key_weight,
        value_weight,
        output_weight,
        gate_weight,
        up_weight,
        down_weight,
        attention_gain,
        feedforward_gain,
    ]
    new_moments = [
        0.5 * moment + 0.5 * factor * gradient for moment, gradient in zip(old_moments, gradients)
    ]
    new_params = []
    for place, param in enumerate(old_params):
        if place < 7:
            new_params.append(param - step_size * (new_moments[place] + decay_rate * param))
        else:
            new_params.append(param - gain_step * new_moments[place])
    outputs = jnp.stack(output_list)
    input_grad = jnp.stack(input_list)
    return (
        outputs,
        input_grad,
        grad_norm,
        new_moments[0],
        new_moments[1],
        new_moments[2],
        new_moments[3],
        new_moments[4],
        new_moments[5],
        new_moments[6],
        new_moments[7],
        new_moments[8],
        new_params[0],
        new_params[1],
        new_params[2],
        new_params[3],
        new_params[4],
        new_params[5],
        new_params[6],
        new_params[7],
        new_params[8],
    )


CORE, SIDE_A, SIDE_B = 1, 2, 4
CHIPS = 4
CHUNKS = 4
MB = 1024 * 1024


def across(value, mask):
    count = lax.axis_size("dp")
    return lax.ppermute(value, "dp", [(place, place ^ mask) for place in range(count)])


def along(value, mask):
    count = lax.axis_size("fsdp")
    return lax.ppermute(value, "fsdp", [(place, place ^ mask) for place in range(count)])


def pick(values, index):
    return lax.dynamic_index_in_dim(values, index, 0, keepdims=False)


def after(value, *earlier):
    return lax.optimization_barrier((value, earlier))[0]


def trade_planes(parts, plane):
    found = [pick(parts, plane)]
    for mask in range(1, CHUNKS):
        found.append(along(pick(parts, plane ^ mask), mask))
    found = jnp.stack(found)
    return [pick(found, label ^ plane) for label in range(CHUNKS)]


def gather_planes(block):
    one, two = along(block, 1), along(block, 2)
    return [block, one, two, along(two, 1)]


def sum_planes(parts):
    two = (parts[2].astype(jnp.float32) + along(parts[3], 1).astype(jnp.float32)).astype(jnp.bfloat16)
    return (
        parts[0].astype(jnp.float32)
        + along(parts[1], 1).astype(jnp.float32)
        + along(two, 2).astype(jnp.float32)
    )


def sum_all(value):
    for mask in (CORE, SIDE_A, SIDE_B):
        value = value + across(value, mask)
    for mask in (1, 2):
        value = value + along(value, mask)
    return value


def to_planes(array, core, plane):
    halves = array.reshape(2, 2, array.shape[1] // 2, array.shape[2]).swapaxes(0, 1)
    keep = pick(halves, core)
    came = across(pick(halves, 1 - core), CORE)
    swap = core == 1
    parts = jnp.concatenate([jnp.where(swap, came, keep), jnp.where(swap, keep, came)])
    return trade_planes(parts, plane)


def from_planes(chunks, core, plane):
    groups = trade_planes(jnp.stack(chunks), plane)
    pairs = jnp.stack([jnp.stack(groups[:2]), jnp.stack(groups[2:])])
    keep = pick(pairs, core)
    came = across(pick(pairs, 1 - core), CORE)
    swap = core == 1
    return jnp.concatenate([jnp.where(swap, came, keep), jnp.where(swap, keep, came)], axis=1)


MESH = pl.DeviceIdType.MESH
SLOT = {0: 0, SIDE_A: 1, SIDE_B: 2}
ROUTES = ((SIDE_A, SIDE_B), (SIDE_B, SIDE_A))
STRIPE = 16


def flip(place, mask):
    for bit in (1, 2, 4):
        if mask & bit:
            place = place + bit - 2 * bit * lax.rem(lax.div(place, bit), 2)
    return place


def peer(mask, planes=0):
    return (flip(lax.axis_index("dp"), mask), flip(lax.axis_index("fsdp"), planes))


SIDES = ((CORE, 0), (SIDE_A, 0), (SIDE_B, 0))
PLANE = tuple((mask, 0) for mask in range(1, 8))
PLANES = tuple((0, mask) for mask in range(1, CHUNKS))


def meet(others):
    barrier = pltpu.get_barrier_semaphore()
    for mask, planes in others:
        pl.semaphore_signal(barrier, inc=1, device_id=peer(mask, planes), device_id_type=MESH)
    pl.semaphore_wait(barrier, len(others))


class Remote:
    def __init__(self, wires, source, target, mask, planes=0):
        self.wires, self.source, self.target, self.mask = wires, source, target, (mask, planes)
        self.place = wires.count
        wires.count += 1

    def make(self):
        return pltpu.make_async_remote_copy(
            src_ref=self.source,
            dst_ref=self.target,
            send_sem=self.wires.send.at[self.place],
            recv_sem=self.wires.recv.at[self.place],
            device_id=peer(*self.mask),
            device_id_type=MESH,
        )

    def start(self):
        self.make().start()

    def arrived(self):
        self.make().wait_recv()

    def left(self):
        self.make().wait_send()


class Wires:
    def __init__(self, send, recv, local):
        self.send, self.recv, self.local = send, recv, local
        self.count = 0
        self.local_count = 0

    def load(self, pairs):
        copies = [
            pltpu.make_async_copy(source, target, self.local.at[place])
            for place, (source, target) in enumerate(pairs)
        ]
        for copy in copies:
            copy.start()
        for copy in copies:
            copy.wait()


class Gather:
    def __init__(self, wires, own, target):
        rows = target.shape[2] // 2
        self.wires, self.own = wires, own
        self.near, self.far, self.core_first, self.core_near, self.core_far = [], [], [], [], []
        self.home = []

        def place(chunk, slot, half):
            return target.at[chunk, slot, pl.ds(half * rows, rows)]

        for chunk, (first, second) in enumerate(ROUTES):
            near, far = SLOT[first], SLOT[second]
            self.home.append((own[chunk], place(chunk, 0, 0)))
            self.near.append(Remote(wires, own[chunk], place(chunk, near, 0), first))
            self.core_first.append(Remote(wires, own[chunk], place(chunk, 0, 1), CORE))
            self.far.append(Remote(wires, own[chunk], place(chunk, far, 0), second))
            self.far.append(Remote(wires, place(chunk, near, 0), place(chunk, 3, 0), second))
            self.core_near.append(Remote(wires, place(chunk, near, 0), place(chunk, near, 1), CORE))
            self.core_far.append(Remote(wires, place(chunk, far, 0), place(chunk, far, 1), CORE))
            self.core_far.append(Remote(wires, place(chunk, 3, 0), place(chunk, 3, 1), CORE))

    def first(self):
        for copy in self.near + self.core_first:
            copy.start()
        self.wires.load(self.home)

    def second(self):
        for chunk, copy in enumerate(self.near):
            copy.arrived()
            self.far[2 * chunk].start()
            self.far[2 * chunk + 1].start()
            self.core_near[chunk].start()

    def third(self):
        for place, copy in enumerate(self.far):
            copy.arrived()
            self.core_far[place].start()

    def last(self):
        for copy in self.core_first + self.core_near + self.core_far:
            copy.arrived()
        for copy in self.near + self.far + self.core_first + self.core_near + self.core_far:
            copy.left()

    def steps(self):
        return [self.first, self.second, self.third, self.last]


class Scatter:
    def __init__(self, wires, own, other, landing, stage, done):
        from_core, from_far, from_near = landing
        self.wires, self.own, self.landing, self.stage, self.done = wires, own, landing, stage, done
        self.core = [Remote(wires, other.at[chunk], from_core.at[chunk], CORE) for chunk in range(2)]
        self.far = [
            Remote(wires, stage[0].at[chunk], from_far.at[chunk], first)
            for chunk, (_, first) in enumerate(ROUTES)
        ]
        self.near = [
            Remote(wires, stage[2].at[chunk, 0], from_near.at[chunk], last)
            for chunk, (last, _) in enumerate(ROUTES)
        ]

    def first(self):
        for copy in self.core:
            copy.start()

    def second(self):
        left, right = self.stage[:2]
        pairs = []
        for chunk, (_, first) in enumerate(ROUTES):
            self.core[chunk].arrived()
            for place, slot in enumerate((SLOT[first], 3)):
                pairs.append((self.own.at[chunk, slot], left.at[chunk, place]))
                pairs.append((self.landing[0].at[chunk, slot], right.at[chunk, place]))
        self.wires.load(pairs)
        for chunk in range(2):

            @pl.loop(0, left.shape[2] // STRIPE)
            def _(step):
                span = pl.ds(step * STRIPE, STRIPE)
                total = left[chunk, :, span].astype(jnp.float32) + right[chunk, :, span].astype(jnp.float32)
                left[chunk, :, span] = total.astype(jnp.bfloat16)

            self.far[chunk].start()

    def third(self):
        stage = self.stage[2]
        pairs = []
        for chunk, (last, _) in enumerate(ROUTES):
            self.far[chunk].arrived()
            pairs.append((self.own.at[chunk, SLOT[last]], stage.at[chunk, 0]))
            pairs.append((self.landing[0].at[chunk, SLOT[last]], stage.at[chunk, 1]))
            pairs.append((self.landing[1].at[chunk, 1], stage.at[chunk, 2]))
        self.wires.load(pairs)
        for chunk in range(2):

            @pl.loop(0, stage.shape[2] // STRIPE)
            def _(step):
                span = pl.ds(step * STRIPE, STRIPE)
                total = stage[chunk, 0, span].astype(jnp.float32)
                for place in range(1, 3):
                    total += stage[chunk, place, span].astype(jnp.float32)
                stage[chunk, 0, span] = total.astype(jnp.bfloat16)

            self.near[chunk].start()
        for copy in self.far:
            copy.left()

    def last(self):
        stage = self.stage[3]
        for chunk in range(2):
            self.near[chunk].arrived()
            self.wires.load(
                [
                    (self.own.at[chunk, 0], stage.at[0]),
                    (self.landing[0].at[chunk, 0], stage.at[1]),
                    (self.landing[1].at[chunk, 0], stage.at[2]),
                    (self.landing[2].at[chunk], stage.at[3]),
                ]
            )

            @pl.loop(0, stage.shape[1] // STRIPE)
            def _(step):
                span = pl.ds(step * STRIPE, STRIPE)
                total = stage[0, span].astype(jnp.float32)
                for place in range(1, 4):
                    total += stage[place, span].astype(jnp.float32)
                self.done(chunk, span, total)

        for copy in self.near + self.core:
            copy.left()

    def steps(self):
        return [self.first, self.second, self.third, self.last]


def stage_shapes(rows, width):
    return [
        pltpu.VMEM((2, 2, rows, width), jnp.bfloat16),
        pltpu.VMEM((2, 2, rows, width), jnp.bfloat16),
        pltpu.VMEM((2, 3, rows, width), jnp.bfloat16),
        pltpu.VMEM((4, rows, width), jnp.bfloat16),
    ]


def landing_shapes(rows, width):
    return [
        jax.ShapeDtypeStruct((2, CHIPS, rows, width), jnp.bfloat16),
        jax.ShapeDtypeStruct((2, 2, rows, width), jnp.bfloat16),
        jax.ShapeDtypeStruct((2, rows, width), jnp.bfloat16),
    ]


def partial_shapes(rows, width):
    return [jax.ShapeDtypeStruct((2, CHIPS, rows, width), jnp.bfloat16)] * 2


def wire_shapes(count):
    return [
        pltpu.SemaphoreType.DMA((count,)),
        pltpu.SemaphoreType.DMA((count,)),
        pltpu.SemaphoreType.DMA((8,)),
    ]


def call(kernel, identity, inputs, outputs, scratch, megabytes):
    return pl.pallas_call(
        kernel,
        in_specs=[pl.BlockSpec(memory_space=place) for _, place in inputs],
        out_specs=[pl.BlockSpec(memory_space=place) for _, place in outputs],
        out_shape=[shape for shape, _ in outputs],
        scratch_shapes=scratch,
        compiler_params=pltpu.CompilerParams(
            collective_id=identity, has_side_effects=True, vmem_limit_bytes=megabytes * MB
        ),
    )(*[array for array, _ in inputs])


HBM, VMEM, SMEM = pl.ANY, pltpu.VMEM, pltpu.SMEM


def at_step(step, actions):
    for when, action in actions.items():
        pl.when(step == when)(action)


def project_phase(gathered, states, weight_ref, cosine, sine, actions):
    tokens = gathered.shape[2]

    def body(rows_ref, cosine_ref, sine_ref, out):
        at_step(pl.program_id(0) * CHIPS + pl.program_id(1), actions)
        product = dot(rows_ref[0, 0], weight_ref[...].reshape(D, 3 * HEAD))
        angles = (cosine_ref[0], sine_ref[0])
        query = spin(product[:, :HEAD], *angles) * (1.0 / math.sqrt(HEAD))
        key = spin(product[:, HEAD : 2 * HEAD], *angles)
        out[0, 0] = jnp.concatenate([query, key, product[:, 2 * HEAD :]], axis=1).astype(jnp.bfloat16)

    here = lambda chunk, chip: (chunk, chip, 0, 0)
    table = pl.BlockSpec((1, tokens, HEAD // 2), lambda chunk, chip: (chunk, 0, 0))
    pltpu.emit_pipeline(
        body,
        grid=(2, CHIPS),
        in_specs=[pl.BlockSpec((1, 1, tokens, gathered.shape[3]), here), table, table],
        out_specs=[pl.BlockSpec((1, 1, tokens, 3 * HEAD), here)],
    )(gathered, cosine, sine, states)


def attend_phase(pair, states, mixed, own, other, lengths_ref, places, weight_ref, keys, values, actions):
    tokens, rows, width = mixed.shape[2], own.shape[2], own.shape[3]
    blocks = 2 * (pair + 1)

    def body(*refs):
        state_refs, (mixed_ref, own_ref, other_ref) = refs[: pair + 1], refs[pair + 1 :]
        chip, side_at = pl.program_id(0), pl.program_id(1)
        at_step(2 * chip + side_at, actions)

        @pl.when(side_at == 0)
        def _():
            for block in range(blocks):
                ref = state_refs[block // 2]
                keys[pl.ds(block * tokens, tokens)] = ref[block % 2, 0, :, HEAD : 2 * HEAD]
                values[pl.ds(block * tokens, tokens)] = ref[block % 2, 0, :, 2 * HEAD :]

        for side in range(2):

            @pl.when(side_at == side)
            def _():
                chunk = 2 * pair + side
                count = tokens * (chunk + 1)
                scores = dot_t(state_refs[pair][side, 0, :, :HEAD], keys[:count])
                mask = seen(places[0][...], places[1][...], chunk, count, tokens, lengths_ref, chip)
                scores = jnp.where(mask, scores, floor_score)
                highest = jnp.max(scores, axis=1, keepdims=True)
                exponent = jnp.exp(scores - highest)
                total = jnp.sum(exponent, axis=1, keepdims=True)
                probs = (exponent * (1.0 / total)).astype(jnp.bfloat16)
                mixed_ref[0, 0] = dot(probs, values[:count]).astype(jnp.bfloat16)

        partial = dot(mixed_ref[0, 0], weight_ref[...]).astype(jnp.bfloat16)
        own_ref[0, 0] = partial[:rows]
        other_ref[0, 0] = partial[rows:]

    here = lambda chip, side: (side, chip, 0, 0)
    state = pl.BlockSpec((2, 1, tokens, 3 * HEAD), lambda chip, side: (0, chip, 0, 0))
    pltpu.emit_pipeline(
        body,
        grid=(CHIPS, 2),
        in_specs=[state] * (pair + 1),
        out_specs=[pl.BlockSpec((1, 1, tokens, HEAD), here)] + [pl.BlockSpec((1, 1, rows, width), here)] * 2,
    )(*states[: pair + 1], mixed, own, other)


def attend_back_phase(
    pair, branch, states, head_grads, own, other, lengths_ref, places, out_weight, weight_ref,
    tables, keys, values, sums, late_sums, actions
):
    tokens, rows, width = branch.shape[2], own.shape[2], own.shape[3]
    blocks = 2 * (pair + 1)
    edge = 2 * tokens

    def body(*refs):
        branch_ref, state_refs = refs[0], refs[1 : pair + 2]
        cosine_ref, sine_ref, grads_ref, own_ref, other_ref = refs[pair + 2 :]
        chip, step = pl.program_id(0), pl.program_id(1)
        at_step(2 * chip + step, actions)

        @pl.when(step == 0)
        def _():
            for block in range(blocks):
                ref = state_refs[block // 2]
                keys[pl.ds(block * tokens, tokens)] = ref[block % 2, 0, :, HEAD : 2 * HEAD]
                values[pl.ds(block * tokens, tokens)] = ref[block % 2, 0, :, 2 * HEAD :]
            if pair == 1:
                for place in range(2):
                    sums[place][chip] = jnp.zeros(sums[place].shape[1:], jnp.float32)
                    late_sums[place][...] = jnp.zeros(late_sums[place].shape, jnp.float32)

        def add(place, term):
            early = min(term.shape[0], edge)
            sums[place][chip, :early] += term[:early]
            if term.shape[0] > edge:
                late_sums[place][: term.shape[0] - edge] += term[edge:]

        for side in range(2):

            @pl.when(step == 1 - side)
            def _():
                chunk = 2 * pair + side
                count = tokens * (chunk + 1)
                mixed_grad = dot_t(branch_ref[0, 0], out_weight[...]).astype(jnp.bfloat16)
                query = state_refs[pair][side, 0, :, :HEAD]
                scores = dot_t(query, keys[:count])
                mask = seen(places[0][...], places[1][...], chunk, count, tokens, lengths_ref, chip)
                scores = jnp.where(mask, scores, floor_score)
                highest = jnp.max(scores, axis=1, keepdims=True)
                exponent = jnp.exp(scores - highest)
                probs = exponent * (1.0 / jnp.sum(exponent, axis=1, keepdims=True))
                add(1, dot_tn(probs.astype(jnp.bfloat16), mixed_grad))
                prob_grad = dot_t(mixed_grad, values[:count])
                inner = jnp.sum(probs * prob_grad, axis=1, keepdims=True)
                score_grad = (probs * (prob_grad - inner)).astype(jnp.bfloat16)
                add(0, dot_tn(score_grad, query))
                query_grad = dot(score_grad, keys[:count]) * (1.0 / math.sqrt(HEAD))
                angles = (cosine_ref[0], sine_ref[0])
                span = slice(side * tokens, (side + 1) * tokens)
                if pair == 1:
                    key_grad, value_grad = late_sums[0][span], late_sums[1][span]
                else:
                    key_grad, value_grad = sums[0][chip, span], sums[1][chip, span]
                grads_ref[0, 0] = jnp.concatenate(
                    [spin_back(query_grad, *angles), spin_back(key_grad, *angles), value_grad], axis=1
                ).astype(jnp.bfloat16)

        partial = dot_t(grads_ref[0, 0], weight_ref[...].reshape(D, 3 * HEAD)).astype(jnp.bfloat16)
        own_ref[0, 0] = partial[:rows]
        other_ref[0, 0] = partial[rows:]

    here = lambda chip, step: (1 - step, chip, 0, 0)
    state = pl.BlockSpec((2, 1, tokens, 3 * HEAD), lambda chip, step: (0, chip, 0, 0))
    table = pl.BlockSpec((1, tokens, HEAD // 2), lambda chip, step: (1 - step, 0, 0))
    pltpu.emit_pipeline(
        body,
        grid=(CHIPS, 2),
        in_specs=[pl.BlockSpec((1, 1, tokens, width), here)] + [state] * (pair + 1) + [table] * 2,
        out_specs=[pl.BlockSpec((1, 1, tokens, 3 * HEAD), here)]
        + [pl.BlockSpec((1, 1, rows, width), here)] * 2,
    )(branch, *states[: pair + 1], *tables, head_grads, own, other)


def feed_phase(rows_in, grads_in, hidden, unit_grads, back_parts, out_parts, weights, actions):
    tokens, width = rows_in.shape[2:]
    rows = tokens // 2
    shards, columns = weights.shape[0], weights.shape[2]
    share = columns // 2

    def body(rows_ref, out_grad_ref, hidden_ref, units_ref, back_own, back_other, out_own, out_other):
        at_step(pl.program_id(0) * CHIPS + pl.program_id(1), actions)
        hidden_grad = None
        for shard in range(shards):
            grad = out_grad_ref[0, 0, :, shard * columns : (shard + 1) * columns]
            term = dot_t(grad, weights[shard, width:, :])
            hidden_grad = term if hidden_grad is None else hidden_grad + term
        back = None
        for shard in range(shards):
            both = dot(rows_ref[0, 0], weights[shard, :width, :])
            gate, upward = both[:, :share], both[:, share:]
            grad = hidden_grad[:, shard * share : (shard + 1) * share]
            sigmoid = jax.nn.sigmoid(gate)
            swish = gate * sigmoid
            hidden_ref[0, 0, :, shard * share : (shard + 1) * share] = (swish * upward).astype(jnp.bfloat16)
            gate_grad = grad * upward * sigmoid * (1.0 + gate * (1.0 - sigmoid))
            units_ref[shard, 0, 0] = jnp.concatenate([gate_grad, grad * swish], axis=1).astype(jnp.bfloat16)
            term = dot_t(units_ref[shard, 0, 0], weights[shard, :width, :])
            back = term if back is None else back + term
        back = back.astype(jnp.bfloat16)
        back_own[0, 0] = back[:rows]
        back_other[0, 0] = back[rows:]
        for shard in range(shards):
            span = slice(shard * columns, (shard + 1) * columns)
            value = dot(hidden_ref[0, 0], weights[shard, width:, :]).astype(jnp.bfloat16)
            out_own[0, 0, :, span] = value[:rows]
            out_other[0, 0, :, span] = value[rows:]

    here = lambda chunk, chip: (chunk, chip, 0, 0)
    wide = pl.BlockSpec((1, 1, tokens, width), here)
    narrow = pl.BlockSpec((1, 1, rows, width), here)
    pltpu.emit_pipeline(
        body,
        grid=(2, CHIPS),
        in_specs=[wide, wide],
        out_specs=[
            pl.BlockSpec((1, 1, tokens, hidden.shape[3]), here),
            pl.BlockSpec((shards, 1, 1, tokens, columns), lambda chunk, chip: (0, chunk, chip, 0, 0)),
        ]
        + [narrow] * 4,
    )(rows_in, grads_in, hidden, unit_grads, *back_parts, *out_parts)


def bf16(*shape):
    return jax.ShapeDtypeStruct(shape, jnp.bfloat16)


def f32(*shape):
    return jax.ShapeDtypeStruct(shape, jnp.float32)


def start_up(
    activations, cotangent, head_block, out_block, unit_block, down_block, lengths_block, gain
):
    _, tokens, width = activations.shape
    rows = tokens // 2
    devices, unit_rows, columns = unit_block.shape
    down_rows = down_block.shape[1]
    planes, _, sub_rows, _ = head_block.shape
    edge = devices * unit_rows

    def kernel(*refs):
        act, cot, head_in, out_in, unit_in, down_in, length_in, gain_ref = refs[:8]
        own_rows, own_grads, gathered = refs[8], refs[9], refs[10:12]
        head_weight, head_output, feed_own, lengths_all = refs[12:16]
        act_groups, cot_groups, traded, spread, other_half, normed = refs[16:22]
        wires = Wires(*refs[22:])
        place, plane = lax.axis_index("dp"), lax.axis_index("fsdp")
        core = lax.rem(place, 2)

        def half(index):
            return pl.ds(pl.multiple_of(index * rows, STRIPE), rows)

        def move(source, target):
            @pl.loop(0, rows // STRIPE)
            def _(step):
                span = pl.ds(step * STRIPE, STRIPE)
                target[span] = source[span]

        def trade(array, groups, own):
            label = [2 * core + group for group in range(2)]
            inside = [
                Remote(wires, array.at[group, half(1 - core)], groups.at[label[group]], CORE)
                for group in range(2)
            ]
            outside = [
                Remote(wires, groups.at[flip(plane, mask)], own.at[plane], 0, mask)
                for mask in range(1, CHUNKS)
            ]

            def keep():
                for group in range(2):
                    move(array.at[group, half(core)], groups.at[label[group]])

            return inside, keep, outside, lambda: move(groups.at[plane], own.at[plane])

        act_inside, act_keep, act_outside, act_own = trade(act, act_groups, own_rows)
        cot_inside, cot_keep, cot_outside, cot_own = trade(cot, cot_groups, own_grads)
        head_trade = [
            Remote(wires, head_in.at[flip(plane, mask)], traded.at[plane], 0, mask)
            for mask in range(1, CHUNKS)
        ]
        head_spread, feed_spread = [], []
        for mask in range(1, devices):
            other = flip(place, mask)
            head_spread.append(
                Remote(
                    wires,
                    traded.at[lax.div(other, 2), lax.rem(other, 2)],
                    spread.at[place, plane],
                    mask,
                )
            )
            feed_spread.append(
                Remote(
                    wires,
                    unit_in.at[other],
                    feed_own.at[pl.ds(pl.multiple_of(place * unit_rows, unit_rows), unit_rows)],
                    mask,
                )
            )
            feed_spread.append(
                Remote(
                    wires,
                    down_in.at[other],
                    feed_own.at[pl.ds(pl.multiple_of(edge + place * down_rows, down_rows), down_rows)],
                    mask,
                )
            )
            feed_spread.append(Remote(wires, length_in, lengths_all.at[place], mask))

        def over_planes(block):
            mine, theirs = block(plane), block(flip(plane, 2))
            return (
                [Remote(wires, mine, mine, 0, 1), Remote(wires, mine, mine, 0, 2)],
                Remote(wires, theirs, theirs, 0, 1),
            )

        head_near, head_relay = over_planes(lambda index: spread.at[:, index])
        out_near, out_relay = over_planes(
            lambda index: head_output.at[:, pl.ds(pl.multiple_of(index * columns, columns), columns)]
        )
        core_half = Remote(wires, spread.at[:, :, :, pl.ds(HEAD, HEAD)], other_half, CORE)
        moves = [
            Gather(wires, [normed.at[2 * pair], normed.at[2 * pair + 1]], gathered[pair])
            for pair in range(2)
        ]

        meet(PLANE + PLANES)
        for copy in act_inside + cot_inside + head_trade + feed_spread:
            copy.start()
        act_keep()
        for copy in act_inside:
            copy.arrived()
        for copy in act_outside:
            copy.start()
        cot_keep()
        act_own()
        traded[plane] = head_in[plane]
        columns_at = pl.ds(pl.multiple_of(plane * columns, columns), columns)
        head_output[:, columns_at] = out_in[...]
        feed_own[pl.ds(pl.multiple_of(place * unit_rows, unit_rows), unit_rows)] = unit_in[place]
        feed_own[pl.ds(pl.multiple_of(edge + place * down_rows, down_rows), down_rows)] = down_in[place]
        lengths_all[place] = length_in[...]
        for copy in head_trade:
            copy.arrived()
        for copy in head_spread:
            copy.start()
        spread[place, plane] = traded[lax.div(place, 2), core]
        for copy in head_spread + cot_inside:
            copy.arrived()
        cot_own()
        for copy in act_outside:
            copy.arrived()
        for copy in head_near + out_near:
            copy.start()

        for chunk in range(CHUNKS):

            @pl.loop(0, rows // STRIPE)
            def _(step):
                span = pl.ds(step * STRIPE, STRIPE)
                values = own_rows[chunk, span].astype(jnp.float32)
                factor = lax.rsqrt(jnp.mean(values * values, axis=1, keepdims=True) + epsilon)
                normed[chunk, span] = (values * factor * gain_ref[...]).astype(jnp.bfloat16)

        moves[0].first()
        moves[0].second()
        moves[1].first()
        moves[0].third()
        moves[1].second()
        for copy in head_near + out_near:
            copy.arrived()
        head_relay.start()
        out_relay.start()
        for copy in cot_outside:
            copy.start()
        moves[0].last()
        moves[1].third()
        head_relay.arrived()
        core_half.start()
        moves[1].last()
        out_relay.arrived()
        core_half.arrived()
        head_weight[:, :, :, :HEAD] = spread[:, :, :, :HEAD]
        for index in range(2):

            @pl.when(core == index)
            def _():
                mine, theirs = (1 + index) * HEAD, (2 - index) * HEAD
                head_weight[:, :, :, mine : mine + HEAD] = spread[:, :, :, HEAD:]
                head_weight[:, :, :, theirs : theirs + HEAD] = other_half[...]

        for copy in feed_spread + cot_outside:
            copy.arrived()
        for copy in (
            act_inside + cot_inside + head_trade + feed_spread + act_outside + head_spread
            + head_near + out_near + [head_relay, out_relay, core_half] + cot_outside
        ):
            copy.left()

    own = bf16(CHUNKS, rows, width)
    outs = call(
        kernel,
        1,
        [(activations, VMEM), (cotangent, VMEM), (head_block, VMEM), (out_block, VMEM)]
        + [(unit_block, VMEM), (down_block, VMEM), (lengths_block, VMEM), (gain, VMEM)],
        [(own, VMEM), (own, VMEM)]
        + [(bf16(2, CHIPS, tokens, width), HBM)] * 2
        + [(bf16(devices, planes, sub_rows, 3 * HEAD), VMEM), (bf16(HEAD, width), VMEM)]
        + [(bf16(devices * (unit_rows + down_rows), columns), VMEM)]
        + [(jax.ShapeDtypeStruct((devices,) + lengths_block.shape, jnp.int32), VMEM)],
        [
            pltpu.VMEM((CHUNKS, rows, width), jnp.bfloat16),
            pltpu.VMEM((CHUNKS, rows, width), jnp.bfloat16),
            pltpu.VMEM((planes, 2, sub_rows, columns), jnp.bfloat16),
            pltpu.VMEM((devices, planes, sub_rows, columns), jnp.bfloat16),
            pltpu.VMEM((devices, planes, sub_rows, HEAD), jnp.bfloat16),
            pltpu.VMEM((CHUNKS, rows, width), jnp.bfloat16),
        ]
        + wire_shapes(90),
        56,
    )
    return outs[0], outs[1], outs[2:4], outs[4], outs[5], outs[6], outs[7]


def attend_and_norm(
    rows_all, out_grads, feed_own, weight, cosine, sine, lengths, places, out_weight, inputs, gain
):
    _, rows, width = inputs.shape
    tokens = 2 * rows
    planes = CHUNKS
    whole_pair = bf16(2, CHIPS, tokens, width)

    def kernel(*refs):
        gathered, grads_ref, feed_ref, head_ref, cosine_ref, sine_ref = refs[:2], *refs[2:7]
        lengths_ref, place_q, place_k, weight_ref, inputs_ref, gain_ref = refs[7:13]
        refs = refs[13:]
        states, mixed, middle, normed, target, grads_all, feed_all = refs[:2], refs[2:4], *refs[4:9]
        parts, landings = (refs[9:11], refs[11:13]), (refs[13:16], refs[16:19])
        stage, keys, values, normed_late = refs[19:23], refs[23], refs[24], refs[25]
        wires = Wires(*refs[26:])
        plane = lax.axis_index("fsdp")

        def finish(pair):
            def done(chunk, span, total):
                at = 2 * pair + chunk
                total = total + inputs_ref[at, span].astype(jnp.float32)
                middle[at, span] = total
                factor = lax.rsqrt(jnp.mean(total * total, axis=1, keepdims=True) + epsilon)
                kept = normed if pair == 0 else normed_late
                kept[chunk, span] = (total * factor * gain_ref[...]).astype(jnp.bfloat16)

            return done

        sums = [
            Scatter(wires, *parts[pair], landings[pair], stage, finish(pair)) for pair in range(2)
        ]
        move = Gather(wires, [normed_late.at[0], normed_late.at[1]], target)
        grad_move = Gather(wires, [grads_ref.at[2], grads_ref.at[3]], grads_all)
        near = Remote(wires, feed_ref, feed_all.at[plane], 0, 1)
        across_middle = Remote(wires, feed_ref, feed_all.at[plane], 0, 2)
        relay = Remote(
            wires, feed_all.at[flip(plane, 2)], feed_all.at[flip(plane, 2)], 0, 1
        )
        places_in = (place_q, place_k)

        meet(SIDES + PLANES[:2])
        near.start()
        across_middle.start()
        grad_move.first()
        wires.load([(feed_ref, feed_all.at[plane])])
        project_phase(
            gathered[0], states[0], head_ref, cosine_ref.at[0], sine_ref.at[0], {7: grad_move.second}
        )
        project_phase(gathered[1], states[1], head_ref, cosine_ref.at[1], sine_ref.at[1], {})
        attend_phase(
            1, states, mixed[1], *parts[1], lengths_ref, places_in, weight_ref, keys, values,
            {3: grad_move.third},
        )
        sums[1].first()
        attend_phase(
            0, states, mixed[0], *parts[0], lengths_ref, places_in, weight_ref, keys, values,
            {5: sums[1].second},
        )
        sums[0].first()
        grad_move.last()
        sums[1].third()
        sums[0].second()
        sums[1].last()
        move.first()
        sums[0].third()
        across_middle.arrived()
        relay.start()
        move.second()
        sums[0].last()
        move.third()
        move.last()
        near.arrived()
        relay.arrived()
        for copy in (near, across_middle, relay):
            copy.left()

    pair_parts = [(shape, HBM) for shape in partial_shapes(rows, width)]
    landing = [(shape, HBM) for shape in landing_shapes(rows, width)]
    outs = call(
        kernel,
        2,
        [(rows_all[0], HBM), (rows_all[1], HBM), (out_grads, VMEM), (feed_own, VMEM)]
        + [(weight, VMEM), (cosine, HBM), (sine, HBM)]
        + [(lengths, SMEM), (places[0], VMEM), (places[1], VMEM), (out_weight, VMEM)]
        + [(inputs, VMEM), (gain, VMEM)],
        [(bf16(2, CHIPS, tokens, 3 * HEAD), HBM)] * 2
        + [(bf16(2, CHIPS, tokens, HEAD), HBM)] * 2
        + [(f32(CHUNKS, rows, width), VMEM), (bf16(2, rows, width), VMEM)]
        + [(whole_pair, HBM)] * 2
        + [(bf16(planes, *feed_own.shape), HBM)]
        + pair_parts * 2
        + landing * 2,
        stage_shapes(rows, width)
        + [pltpu.VMEM((CHUNKS * tokens, HEAD), jnp.bfloat16)] * 2
        + [pltpu.VMEM((2, rows, width), jnp.bfloat16)]
        + wire_shapes(50),
        60,
    )
    return outs[:2], outs[2:4], outs[4], outs[5], outs[6], outs[7], outs[8]


def norm_back(values, gain, gradient):
    factor = lax.rsqrt(jnp.mean(values * values, axis=1, keepdims=True) + epsilon)
    scaled = values * factor
    pulled = gradient * gain
    back = factor * (pulled - scaled * jnp.mean(pulled * scaled, axis=1, keepdims=True))
    return back, gradient * scaled


def feed_forward(normed_own, normed_late, grads_late, weights, middle, out_grad_own, gain, units):
    _, rows, width = middle.shape
    tokens = 2 * rows
    shards, columns = weights.shape[0], weights.shape[2]
    whole_pair = bf16(2, CHIPS, tokens, width)

    def kernel(*refs):
        normed_ref, normed_late_ref, grads_late_ref = refs[:3]
        weight_ref, middle_ref, own_grad, gain_ref = refs[3:7]
        refs = (None, *refs)
        normed_early, branch, grads_early = refs[8], refs[9], refs[27]
        hidden, unit_grads = refs[10:12], refs[12:14]
        back_parts, out_parts = (refs[14:16], refs[16:18]), (refs[18:20], refs[20:22])
        middle_grad, gain_sum, landing = refs[22], refs[23], refs[24:27]
        stage, own_branch, wires = refs[28:32], refs[32], Wires(*refs[33:])
        meet(SIDES)
        gain_sum[...] = jnp.zeros(gain_sum.shape, jnp.float32)

        def done(chunk, span, total):
            back, gain_terms = norm_back(middle_ref[2 + chunk, span], gain_ref[...], total)
            gain_sum[...] += gain_terms
            back = back + own_grad[2 + chunk, span].astype(jnp.float32)
            middle_grad[chunk, span] = back
            own_branch[chunk, span] = back.astype(jnp.bfloat16)

        move = Gather(wires, [normed_ref.at[0], normed_ref.at[1]], normed_early)
        sums = Scatter(wires, *back_parts[1], landing, stage, done)
        late_move = Gather(wires, [own_branch.at[0], own_branch.at[1]], branch)
        grad_move = Gather(wires, [own_grad.at[0], own_grad.at[1]], grads_early)
        move.first()
        grad_move.first()
        feed_phase(
            normed_late_ref, grads_late_ref, hidden[1], unit_grads[1], back_parts[1], out_parts[1],
            weight_ref,
            {2: move.second, 3: grad_move.second, 5: move.third, 7: grad_move.third},
        )
        sums.first()
        move.last()
        grad_move.last()
        feed_phase(
            normed_early, grads_early, hidden[0], unit_grads[0], back_parts[0], out_parts[0], weight_ref,
            {1: sums.second, 4: sums.third, 6: lambda: (sums.last(), late_move.first()) and None},
        )
        late_move.second()
        late_move.third()
        late_move.last()

    outs = call(
        kernel,
        3,
        [(normed_own, VMEM), (normed_late, HBM), (grads_late, HBM)]
        + [(weights, VMEM), (middle, VMEM), (out_grad_own, VMEM), (gain, VMEM)],
        [(whole_pair, HBM)] * 2
        + [(bf16(2, CHIPS, tokens, units), HBM)] * 2
        + [(bf16(shards, 2, CHIPS, tokens, columns), HBM)] * 2
        + [(shape, HBM) for shape in partial_shapes(rows, width)] * 4
        + [(f32(2, rows, width), VMEM), (f32(STRIPE, width), VMEM)]
        + [(shape, HBM) for shape in landing_shapes(rows, width)]
        + [(whole_pair, HBM)],
        stage_shapes(rows, width) + [pltpu.VMEM((2, rows, width), jnp.bfloat16)] + wire_shapes(50),
        62,
    )
    return outs[19], outs[0], outs[1], outs[2:4], outs[4:6], outs[6:8], (outs[10:12], outs[12:14]), outs[14], outs[15]


def attend_back(
    states, lengths, places, out_weight, weight, cosine, sine, branch_late, back_early, out_parts,
    middle, out_grad_own, inputs, middle_grad_late, gains
):
    _, rows, width = middle.shape
    tokens = 2 * rows

    def kernel(*refs):
        states_in, (lengths_ref, place_q, place_k, out_ref, weight_ref, cosine_ref, sine_ref) = (
            refs[:2],
            refs[2:9],
        )
        late_branch, back_parts, outs_in = refs[9], refs[10:12], (refs[12:14], refs[14:16])
        middle_ref, own_grad, inputs_ref, late_grad, gain_one, gain_two = refs[16:22]
        head_grads, early_branch, outputs, input_grad = refs[22:24], refs[24], refs[25], refs[26]
        gain_sums = refs[27]
        parts = (refs[28:30], refs[30:32])
        landings = [refs[32 + 3 * place : 35 + 3 * place] for place in range(5)]
        stage, early_grad, own_branch, keys, values = refs[47:51], refs[51], refs[52], refs[53], refs[54]
        sums, late_sums, wires = refs[55:57], refs[57:59], Wires(*refs[59:])
        meet(SIDES)
        gain_sums[...] = jnp.zeros(gain_sums.shape, jnp.float32)

        def middle_done(chunk, span, total):
            back, gain_terms = norm_back(
                middle_ref[chunk, span].astype(jnp.float32), gain_two[...], total
            )
            gain_sums[1] += gain_terms
            back = back + own_grad[chunk, span].astype(jnp.float32)
            early_grad[chunk, span] = back
            own_branch[chunk, span] = back.astype(jnp.bfloat16)

        def output_done(pair):
            def done(chunk, span, total):
                at = 2 * pair + chunk
                outputs[at, span] = (middle_ref[at, span] + total).astype(jnp.bfloat16)

            return done

        def input_done(pair):
            def done(chunk, span, total):
                at = 2 * pair + chunk
                back, gain_terms = norm_back(
                    inputs_ref[at, span].astype(jnp.float32), gain_one[...], total
                )
                gain_sums[0] += gain_terms
                direct = late_grad if pair == 1 else early_grad
                input_grad[at, span] = (direct[chunk, span] + back).astype(jnp.bfloat16)

            return done

        middle_sum = Scatter(wires, *back_parts, landings[0], stage, middle_done)
        move = Gather(wires, [own_branch.at[0], own_branch.at[1]], early_branch)
        output_sums = [
            Scatter(wires, *outs_in[pair], landings[1 + pair], stage, output_done(pair))
            for pair in range(2)
        ]
        input_sums = [
            Scatter(wires, *parts[pair], landings[3 + pair], stage, input_done(pair)) for pair in range(2)
        ]

        def back_through(pair, branch, actions):
            attend_back_phase(
                pair, branch, states_in, head_grads[pair], *parts[pair], lengths_ref,
                (place_q, place_k), out_ref, weight_ref, (cosine_ref.at[pair], sine_ref.at[pair]),
                keys, values, sums, late_sums, actions,
            )

        def both(*steps):
            def run():
                for step in steps:
                    step()

            return run

        middle_sum.first()
        output_sums[1].first()
        back_through(
            1,
            late_branch,
            {1: middle_sum.second, 5: middle_sum.third, 7: both(middle_sum.last, move.first)},
        )
        move.second()
        input_sums[1].first()
        output_sums[1].second()
        move.third()
        move.last()
        output_sums[0].first()
        back_through(
            0,
            early_branch,
            {
                1: both(output_sums[1].third, input_sums[1].second),
                4: both(output_sums[1].last, input_sums[1].third),
                6: both(input_sums[1].last, output_sums[0].second),
            },
        )
        input_sums[0].first()
        output_sums[0].third()
        input_sums[0].second()
        output_sums[0].last()
        input_sums[0].third()
        input_sums[0].last()

    outs = call(
        kernel,
        4,
        [(state, HBM) for state in states]
        + [(lengths, SMEM), (places[0], VMEM), (places[1], VMEM), (out_weight, VMEM), (weight, VMEM)]
        + [(cosine, HBM), (sine, HBM), (branch_late, HBM)]
        + [(part, HBM) for part in back_early]
        + [(part, HBM) for parts in out_parts for part in parts]
        + [(middle, VMEM), (out_grad_own, VMEM), (inputs, VMEM), (middle_grad_late, VMEM)]
        + [(gains[0], VMEM), (gains[1], VMEM)],
        [(bf16(2, CHIPS, tokens, 3 * HEAD), HBM)] * 2
        + [(bf16(2, CHIPS, tokens, width), HBM)]
        + [(bf16(CHUNKS, rows, width), VMEM)] * 2
        + [(f32(2, STRIPE, width), VMEM)]
        + [(shape, HBM) for shape in partial_shapes(rows, width)] * 2
        + [(shape, HBM) for shape in landing_shapes(rows, width)] * 5,
        stage_shapes(rows, width)
        + [pltpu.VMEM((2, rows, width), jnp.float32), pltpu.VMEM((2, rows, width), jnp.bfloat16)]
        + [pltpu.VMEM((CHUNKS * tokens, HEAD), jnp.bfloat16)] * 2
        + [pltpu.VMEM((CHIPS, 2 * tokens, HEAD), jnp.float32)] * 2
        + [pltpu.VMEM((2 * tokens, HEAD), jnp.float32)] * 2
        + wire_shapes(50),
        63,
    )
    return outs[:2], outs[2], outs[3], outs[4], outs[5]


def unit_weight_grads(unit_grads, rows_in):
    shards, _, _, tokens, columns = unit_grads[0].shape
    width = rows_in[0].shape[3]

    def kernel(late_units, late_rows, early_units, early_rows, out, total):
        step = pl.program_id(1)

        @pl.when(step == 0)
        def _():
            total[...] = jnp.zeros(total.shape, jnp.float32)

        for place, (units, rows_ref) in enumerate(((late_units, late_rows), (early_units, early_rows))):

            @pl.when(lax.div(step, 2) == place)
            def _():
                left = units[0, 0].reshape(CHIPS * tokens, columns)
                right = rows_ref[0].reshape(CHIPS * tokens, width)
                total[...] += dot_tn(left, right)

        @pl.when(step == 3)
        def _():
            out[0] = total[...].astype(jnp.bfloat16)

    late = lambda step: jnp.minimum(step, 1)
    early = lambda step: jnp.maximum(step - 2, 0)
    specs = []
    for at in (late, early):
        specs.append(
            pl.BlockSpec(
                (1, 1, CHIPS, tokens, columns),
                (lambda at: lambda shard, step: (shard, at(step), 0, 0, 0))(at),
            )
        )
        specs.append(
            pl.BlockSpec(
                (1, CHIPS, tokens, width), (lambda at: lambda shard, step: (at(step), 0, 0, 0))(at)
            )
        )
    return pl.pallas_call(
        kernel,
        grid=(shards, 4),
        in_specs=specs,
        out_specs=pl.BlockSpec((1, columns, width), lambda shard, step: (shard, 0, 0)),
        out_shape=bf16(shards, columns, width),
        scratch_shapes=[pltpu.VMEM((columns, width), jnp.float32)],
        compiler_params=params(60),
    )(unit_grads[1], rows_in[1], unit_grads[0], rows_in[0])


def dot(left, right):
    return jnp.dot(left, right, preferred_element_type=jnp.float32)


def dot_t(left, right):
    return lax.dot_general(
        left, right, (((1,), (1,)), ((), ())), preferred_element_type=jnp.float32
    )


def dot_tn(left, right):
    return lax.dot_general(
        left, right, (((0,), (0,)), ((), ())), preferred_element_type=jnp.float32
    )


def spin(values, cosine, sine):
    halfway = values.shape[1] // 2
    first, second = values[:, :halfway], values[:, halfway:]
    return jnp.concatenate(
        [first * cosine - second * sine, second * cosine + first * sine], axis=1
    )


def spin_back(values, cosine, sine):
    return spin(values, cosine, -sine)


def whole(shape):
    return pl.BlockSpec(shape, lambda *_: (0,) * len(shape), pipeline_mode=pl.Buffered(1))


def params(megabytes):
    return pltpu.CompilerParams(vmem_limit_bytes=megabytes * MB)


def seen(place_q, place_k, chunk, count, tokens, lengths_ref, chip):
    query_index = tokens * chunk + place_q
    key_index = place_k[:, :count]
    ahead_or_here = key_index <= query_index
    if tokens * (chunk + 1) <= PROMPT:
        return ahead_or_here

    def segment(index):
        found = jnp.full(index.shape, -1, jnp.int32)
        for slot in range(NCONT):
            found = jnp.where(index >= PROMPT + slot * CONT, slot, found)
        return found

    key_segment, query_segment = segment(key_index), segment(query_index)
    end = jnp.full(key_index.shape, PROMPT, jnp.int32)
    for slot in range(NCONT):
        end = jnp.where(
            key_segment == slot, PROMPT + slot * CONT + lengths_ref[chip, slot], end
        )
    alive = key_index < end
    return ahead_or_here & ((key_segment < 0) | ((key_segment == query_segment) & alive))


def token_dot(left, right):
    return lax.dot_general(
        left.reshape(-1, left.shape[-1]),
        right.reshape(-1, right.shape[-1]),
        (((0,), (0,)), ((), ())),
        preferred_element_type=jnp.float32,
    )


def exchange(value, axis):
    return lax.all_to_all(value, axis, split_axis=0, concat_axis=0, tiled=True)


def plane_device(
    activations,
    cotangent,
    continuation_lengths,
    query_weight,
    key_weight,
    value_weight,
    output_weight,
    gate_weight,
    up_weight,
    down_weight,
    attention_gain,
    feedforward_gain,
    moment_query,
    moment_key,
    moment_value,
    moment_output,
    moment_gate,
    moment_up,
    moment_down,
    moment_attention,
    moment_feedforward,
):
    devices, planes = lax.axis_size("dp"), lax.axis_size("fsdp")
    place, plane = lax.axis_index("dp"), lax.axis_index("fsdp")
    core = place % 2
    low = jnp.bfloat16
    kv_width = KV_HEADS * HEAD
    tokens = activations.shape[1]
    half = tokens // 2

    in_rows = query_weight.shape[0]
    sub_rows = in_rows // planes
    spread = devices * sub_rows

    mixed_kv = jnp.stack([key_weight.astype(low), value_weight.astype(low)], axis=1)
    block = jnp.concatenate([query_weight.astype(low).reshape(in_rows, 2, HEAD), mixed_kv], axis=2)
    head_block = block.reshape(planes, sub_rows, 2, 2 * HEAD).swapaxes(1, 2)

    strip = 128
    runs = gate_weight.shape[1] // (devices * strip)
    units = runs * strip * planes
    gate_up = jnp.stack(
        [
            gate_weight.astype(low).reshape(in_rows, runs, devices, strip),
            up_weight.astype(low).reshape(in_rows, runs, devices, strip),
        ]
    )
    gate_up = gate_up.transpose(3, 1, 0, 2, 4).reshape(devices, in_rows, 2 * runs * strip)
    down_columns = down_weight.shape[1]
    down = down_weight.astype(low).reshape(devices, strip, down_columns)

    gain_one, gain_two = attention_gain[None, :], feedforward_gain[None, :]
    length_block = jnp.zeros((8, 128), jnp.int32).at[:2, :NCONT].set(continuation_lengths)
    own_inputs, own_grads, rows_all, head_weight, head_output, feed_own, all_lengths = start_up(
        activations,
        cotangent,
        head_block,
        output_weight.astype(low),
        gate_up,
        down,
        length_block,
        gain_one,
    )

    first_core = place - core
    lengths = jnp.stack(
        [
            pick(pick(all_lengths, (first_core ^ mask) + plane // 2), plane % 2)[:NCONT]
            for mask in (0, SIDE_A, SIDE_B, SIDE_A + SIDE_B)
        ]
    )

    inside = jnp.concatenate(
        [core * half + jnp.arange(half), (1 - core) * half + jnp.arange(half)]
    ).astype(jnp.int32)
    order = (tokens * jnp.arange(CHUNKS, dtype=jnp.int32)[:, None] + inside[None, :]).reshape(-1)
    cosine, sine = rope_angles(token_places(order))
    cosine = cosine.reshape(2, 2, tokens, HEAD // 2)
    sine = sine.reshape(2, 2, tokens, HEAD // 2)
    place_q, place_k = inside[:, None], order[None, :]
    blocks = plane ^ jnp.arange(CHUNKS, dtype=jnp.int32)

    states, mixed, middle, normed_two, normed_late, grads_late, feed_weights = attend_and_norm(
        rows_all,
        own_grads,
        feed_own,
        head_weight,
        cosine,
        sine,
        lengths,
        (place_q, place_k),
        head_output,
        own_inputs,
        gain_two,
    )
    (
        grads_early,
        normed_early,
        branch_late,
        hidden,
        unit_grads,
        back_early,
        out_parts,
        middle_grad,
        gain_sum,
    ) = feed_forward(normed_two, normed_late, grads_late, feed_weights, middle, own_grads, gain_two, units)
    grads_all = (grads_early, grads_late)
    unit_sum = unit_weight_grads(unit_grads, (normed_early, normed_late))
    unit_sum = lax.psum_scatter(unit_sum, "fsdp", scatter_dimension=0, tiled=False)
    down_sum = reduce(jnp.add, [token_dot(hidden[pair], grads_all[pair]) for pair in (1, 0)]).astype(low)
    down_sum = down_sum.reshape(-1, planes, down_columns).transpose(1, 0, 2)
    down_sum = lax.psum_scatter(down_sum, "fsdp", scatter_dimension=0, tiled=False)
    head_grads, branch_early, own_outputs, own_input_grad, gain_sums = attend_back(
        states,
        lengths,
        (place_q, place_k),
        head_output,
        head_weight,
        cosine,
        sine,
        branch_late,
        back_early,
        out_parts,
        middle,
        own_grads,
        own_inputs,
        middle_grad,
        (gain_one, gain_two),
    )
    outputs = from_planes([own_outputs[chunk] for chunk in range(CHUNKS)], core, plane)
    input_grad = from_planes([own_input_grad[chunk] for chunk in range(CHUNKS)], core, plane)
    attention_sum = jnp.sum(gain_sums[0], axis=0)
    feedforward_sum = jnp.sum(gain_sums[1] + gain_sum, axis=0)

    strips = runs * strip
    unit_sum = unit_sum.reshape(2 * strips, devices, in_rows).swapaxes(0, 1)
    unit_sum = exchange(unit_sum, "dp").reshape(devices, 2, runs, strip, in_rows)
    gate_up_owned = unit_sum.transpose(1, 4, 2, 0, 3).reshape(2, in_rows, runs * devices * strip)
    down_owned = exchange(down_sum.reshape(devices, strip, down_columns), "dp")
    down_owned = down_owned.reshape(devices * strip, down_columns)
    head_sum = reduce(
        jnp.add, [token_dot(rows_all[pair], head_grads[pair]) for pair in (1, 0)]
    ).astype(low)
    branches = (branch_early, branch_late)
    output_sum = reduce(jnp.add, [token_dot(mixed[pair], branches[pair]) for pair in (1, 0)]).astype(low)
    given = jnp.where(core == 0, head_sum[:, 2 * HEAD :], head_sum[:, HEAD : 2 * HEAD])
    kept = jnp.where(core == 0, head_sum[:, HEAD : 2 * HEAD], head_sum[:, 2 * HEAD :])
    kv_sum = (kept.astype(jnp.float32) + across(given, CORE).astype(jnp.float32)).astype(low)
    head_sum = jnp.concatenate([head_sum[:, :HEAD], kv_sum], axis=1)
    head_sum = head_sum.reshape(devices, planes, sub_rows, 2 * HEAD).transpose(1, 0, 2, 3)
    head_sum = head_sum.reshape(planes, spread, 2 * HEAD)
    output_sum = output_sum.reshape(HEAD, planes, 2 * HEAD).transpose(1, 0, 2)
    attention_parts = jnp.concatenate([head_sum, output_sum], axis=1)
    attention_grad = sum_planes([pick(attention_parts, blocks[shard]) for shard in range(CHUNKS)])
    output_owned = attention_grad[spread:]
    block = exchange(attention_grad[:spread].astype(low).reshape(devices, sub_rows, 2 * HEAD), "dp")
    block = block.reshape(planes, 2, sub_rows, 2 * HEAD).transpose(0, 2, 1, 3)
    block = jnp.stack(trade_planes(block, plane)).reshape(in_rows, 2, 2 * HEAD)
    query_owned = block[:, :, :HEAD].reshape(in_rows, 2 * HEAD)
    key_owned, value_owned = block[:, 0, HEAD:], block[:, 1, HEAD:]
    owner_grads = [
        owned.astype(jnp.float32)
        for owned in (
            query_owned,
            key_owned,
            value_owned,
            output_owned,
            gate_up_owned[0],
            gate_up_owned[1],
            down_owned,
        )
    ]
    local_square = reduce(jnp.add, [jnp.sum(owned * owned) for owned in owner_grads])
    attention_total, feedforward_total = sum_all(jnp.stack([attention_sum, feedforward_sum]))
    square_total = sum_all(jnp.full((8, 128), local_square))[0, 0]
    square_sum = (
        square_total
        + jnp.sum(attention_total * attention_total)
        + jnp.sum(feedforward_total * feedforward_total)
    )
    grad_norm = jnp.sqrt(square_sum)
    entry_count = 2 * D * D + 2 * D * kv_width + 3 * D * FF + 2 * D
    limit = clip_level * math.sqrt(entry_count)
    factor = limit / jnp.maximum(grad_norm, limit)
    gradients = owner_grads + [attention_total, feedforward_total]
    old_moments = [
        moment_query,
        moment_key,
        moment_value,
        moment_output,
        moment_gate,
        moment_up,
        moment_down,
        moment_attention,
        moment_feedforward,
    ]
    old_params = [
        query_weight,
        key_weight,
        value_weight,
        output_weight,
        gate_weight,
        up_weight,
        down_weight,
        attention_gain,
        feedforward_gain,
    ]
    new_moments = [
        0.5 * moment + 0.5 * factor * gradient for moment, gradient in zip(old_moments, gradients)
    ]
    new_params = []
    for at, param in enumerate(old_params):
        if at < 7:
            new_params.append(param - step_size * (new_moments[at] + decay_rate * param))
        else:
            new_params.append(param - gain_step * new_moments[at])
    return (outputs, input_grad, grad_norm, *new_moments, *new_params)


def solution(mesh):
    whole_groups_on_planes = mesh.shape["dp"] == HEADS and mesh.shape["fsdp"] == KV_HEADS
    body = plane_device if whole_groups_on_planes else on_device
    placed = (
        P("dp", "fsdp", None),
        P("dp", "fsdp", None),
        P("dp", None),
        P("dp", "fsdp"),
        P("dp", "fsdp"),
        P("dp", "fsdp"),
        P("dp", "fsdp"),
        P("dp", "fsdp"),
        P("dp", "fsdp"),
        P("dp", "fsdp"),
        P(),
        P(),
        P("dp", "fsdp"),
        P("dp", "fsdp"),
        P("dp", "fsdp"),
        P("dp", "fsdp"),
        P("dp", "fsdp"),
        P("dp", "fsdp"),
        P("dp", "fsdp"),
        P(),
        P(),
    )
    return jax.shard_map(
        body,
        mesh=mesh,
        in_specs=placed,
        out_specs=(
            P("dp", "fsdp", None),
            P("dp", "fsdp", None),
            P(),
            P("dp", "fsdp"),
            P("dp", "fsdp"),
            P("dp", "fsdp"),
            P("dp", "fsdp"),
            P("dp", "fsdp"),
            P("dp", "fsdp"),
            P("dp", "fsdp"),
            P(),
            P(),
            P("dp", "fsdp"),
            P("dp", "fsdp"),
            P("dp", "fsdp"),
            P("dp", "fsdp"),
            P("dp", "fsdp"),
            P("dp", "fsdp"),
            P("dp", "fsdp"),
            P(),
            P(),
        ),
        check_vma=False,
    )
```

```python
from functools import reduce
import math

import jax
import jax.numpy as jnp
from jax import lax
from jax.experimental import pallas as pl
from jax.experimental.pallas import tpu as pltpu
from jax.sharding import PartitionSpec as P

D = 2048
HEADS = 8
KV_HEADS = 4
HEAD = 256
FF = 8192
PROMPT = 1024
CONT = 64
NCONT = 2


epsilon = 1e-06
rope_base = 1000042.0
step_size = 0.2
gain_step = 4.0
decay_rate = 0.1
clip_level = 0.25
floor_score = -1e30


def rms_rows(values, gain):
    factor = lax.rsqrt(jnp.mean(values * values, axis=-1, keepdims=True) + epsilon)
    return (values * factor * gain, factor)


def rms_back(values, factor, gain, gradient):
    scaled = values * factor
    gain_grad = jnp.sum(gradient * scaled, axis=0)
    pulled = gradient * gain
    return (
        factor * (pulled - scaled * jnp.mean(pulled * scaled, axis=-1, keepdims=True)),
        gain_grad,
    )


def rope_angles(places):
    halfway = HEAD // 2
    freqs = rope_base ** (-(jnp.arange(halfway).astype(jnp.float32) * 2.0 / HEAD))
    angles = places.astype(jnp.float32)[:, None] * freqs[None, :]
    return (jnp.cos(angles), jnp.sin(angles))


def token_places(index):
    inside = index - PROMPT
    return jnp.where(index < PROMPT, index, PROMPT + inside % CONT)


def segment_of(index):
    return jnp.where(index < PROMPT, -1, (index - PROMPT) // CONT)


def visible(query_index, key_index, lengths):
    key_segment = segment_of(key_index)
    key_offset = key_index - PROMPT - key_segment * CONT
    slots = jnp.arange(NCONT, dtype=jnp.int32)
    limits = jnp.sum(jnp.where(key_segment[:, None] == slots[None, :], lengths[None, :], 0), axis=1)
    alive = key_offset < limits
    same = segment_of(query_index)[:, None] == key_segment[None, :]
    causal = key_index[None, :] <= query_index[:, None]
    return causal & ((key_index < PROMPT)[None, :] | same & alive[None, :])


def rotate(values, cosine, sine):
    halfway = values.shape[-1] // 2
    first, second = (values[..., :halfway], values[..., halfway:])
    cosine, sine = (cosine[:, None, :], sine[:, None, :])
    return jnp.concatenate(
        [first * cosine - second * sine, second * cosine + first * sine], axis=-1
    )


def rotate_back(grads, cosine, sine):
    halfway = grads.shape[-1] // 2
    first, second = (grads[..., :halfway], grads[..., halfway:])
    cosine, sine = (cosine[:, None, :], sine[:, None, :])
    return jnp.concatenate(
        [first * cosine + second * sine, second * cosine - first * sine], axis=-1
    )


def join_blocks(pieces, shard_count):
    height = pieces[0].shape[0]
    return jnp.concatenate(
        [member.reshape(height, shard_count, -1) for member in pieces], axis=2
    ).reshape(height, -1)


def split_blocks(merged, breadths, shard_count):
    height = merged.shape[0]
    blocks = merged.reshape(height, shard_count, -1)
    result = []
    offset = 0
    for breadth in breadths:
        result.append(
            blocks[:, :, offset : offset + breadth].reshape(height, shard_count * breadth)
        )
        offset = offset + breadth
    return result


def ahead(operand, shard):
    return jnp.dot(
        operand,
        lax.all_gather(shard, "fsdp", axis=1, tiled=True),
        preferred_element_type=jnp.float32,
    )


def behind(gradient, shard):
    return lax.dot_general(
        gradient,
        lax.all_gather(shard, "fsdp", axis=1, tiled=True),
        (((1,), (1,)), ((), ())),
        preferred_element_type=jnp.float32,
    )


def weight_term(gradient, operand):
    operand_all = lax.all_gather(operand, "fsdp", axis=0, tiled=True)
    owned_columns = lax.all_to_all(gradient, "fsdp", split_axis=1, concat_axis=0, tiled=True)
    return lax.dot_general(
        owned_columns, operand_all, (((0,), (0,)), ((), ())), preferred_element_type=jnp.float32
    )


def on_device(
    activations,
    cotangent,
    continuation_lengths,
    query_weight,
    key_weight,
    value_weight,
    output_weight,
    gate_weight,
    up_weight,
    down_weight,
    attention_gain,
    feedforward_gain,
    moment_query,
    moment_key,
    moment_value,
    moment_output,
    moment_gate,
    moment_up,
    moment_down,
    moment_attention,
    moment_feedforward,
):
    shard_count = lax.axis_size("fsdp")
    kv_width = KV_HEADS * HEAD
    repeat = HEADS // KV_HEADS
    scale = 1.0 / math.sqrt(HEAD)
    gathered = (
        lax.all_gather(query_weight.astype(jnp.bfloat16), "dp", axis=0, tiled=True),
        lax.all_gather(key_weight.astype(jnp.bfloat16), "dp", axis=0, tiled=True),
        lax.all_gather(value_weight.astype(jnp.bfloat16), "dp", axis=0, tiled=True),
        lax.all_gather(output_weight.astype(jnp.bfloat16), "dp", axis=0, tiled=True),
        lax.all_gather(gate_weight.astype(jnp.bfloat16), "dp", axis=0, tiled=True),
        lax.all_gather(up_weight.astype(jnp.bfloat16), "dp", axis=0, tiled=True),
        lax.all_gather(down_weight.astype(jnp.bfloat16), "dp", axis=0, tiled=True),
    )
    merged_attn = join_blocks(gathered[0:3], 1)
    merged_output = gathered[3]
    merged_ffn = join_blocks(gathered[4:6], 1)
    merged_down = gathered[6]
    query_cols = D // shard_count
    key_cols = kv_width // shard_count
    ffn_cols = FF // shard_count
    attn_breadths = (query_cols, key_cols, key_cols)
    ffn_breadths = (ffn_cols, ffn_cols)
    local_rows = activations.shape[1]
    group_rows = local_rows * shard_count
    query_index = lax.axis_index("fsdp") * local_rows + jnp.arange(local_rows, dtype=jnp.int32)
    key_index = jnp.arange(group_rows, dtype=jnp.int32)
    cosine, sine = rope_angles(token_places(query_index))
    sums = [jnp.zeros((matrix.shape[1], matrix.shape[0]), jnp.float32) for matrix in gathered]
    attention_sum = jnp.zeros((D,), jnp.float32)
    feedforward_sum = jnp.zeros((D,), jnp.float32)
    output_list = []
    input_list = []
    for micro_batch in range(activations.shape[0]):
        allowed = visible(query_index, key_index, continuation_lengths[micro_batch])
        inputs = activations[micro_batch].astype(jnp.float32)
        normed_float, factor_one = rms_rows(inputs, attention_gain)
        normed = normed_float.astype(jnp.bfloat16)
        pre_query, pre_key, pre_value = split_blocks(
            ahead(normed, merged_attn), attn_breadths, shard_count
        )
        queries = (
            rotate(pre_query.reshape(local_rows, HEADS, HEAD), cosine, sine)
            .astype(jnp.bfloat16)
            .reshape(local_rows, KV_HEADS, repeat, HEAD)
        )
        keys = rotate(pre_key.reshape(local_rows, KV_HEADS, HEAD), cosine, sine).astype(
            jnp.bfloat16
        )
        values = pre_value.astype(jnp.bfloat16).reshape(local_rows, KV_HEADS, HEAD)
        keys_all, values_all = (
            lax.all_gather(keys, "fsdp", axis=0, tiled=True),
            lax.all_gather(values, "fsdp", axis=0, tiled=True),
        )
        raw = (
            jnp.einsum("qgrd,kgd->grqk", queries, keys_all, preferred_element_type=jnp.float32)
            * scale
        )
        raw = jnp.where(allowed[None, None], raw, floor_score)
        highest = jnp.max(raw, axis=-1, keepdims=True)
        exponent = jnp.exp(raw - highest)
        denominator = jnp.sum(exponent, axis=-1, keepdims=True)
        logsum = highest + jnp.log(denominator)
        probs_low = (exponent / denominator).astype(jnp.bfloat16)
        mixed = (
            jnp.einsum("grqk,kgd->qgrd", probs_low, values_all, preferred_element_type=jnp.float32)
            .reshape(local_rows, D)
            .astype(jnp.bfloat16)
        )
        middle = inputs + ahead(mixed, merged_output)
        normed_two_float, factor_two = rms_rows(middle, feedforward_gain)
        normed_two = normed_two_float.astype(jnp.bfloat16)
        gate, upward = split_blocks(ahead(normed_two, merged_ffn), ffn_breadths, shard_count)
        sigmoid = jax.nn.sigmoid(gate)
        swish = gate * sigmoid
        hidden = (swish * upward).astype(jnp.bfloat16)
        result = middle + ahead(hidden, merged_down)
        output_list.append(result.astype(jnp.bfloat16))
        out_grad = cotangent[micro_batch]
        hidden_grad = behind(out_grad, merged_down)
        sums[6] = sums[6] + weight_term(out_grad, hidden)
        gate_grad = (hidden_grad * upward * sigmoid * (1.0 + gate * (1.0 - sigmoid))).astype(
            jnp.bfloat16
        )
        up_grad = (hidden_grad * swish).astype(jnp.bfloat16)
        ffn_grad = join_blocks((gate_grad, up_grad), shard_count)
        ffn_term = weight_term(ffn_grad, normed_two)
        sums[4] = sums[4] + ffn_term[:ffn_cols]
        sums[5] = sums[5] + ffn_term[ffn_cols:]
        normed_two_grad = behind(ffn_grad, merged_ffn)
        middle_back, feed_gain_grad = rms_back(
            middle, factor_two, feedforward_gain, normed_two_grad
        )
        middle_grad = out_grad.astype(jnp.float32) + middle_back
        branch_grad = middle_grad.astype(jnp.bfloat16)
        sums[3] = sums[3] + weight_term(branch_grad, mixed)
        mixed_grad = (
            behind(branch_grad, merged_output)
            .astype(jnp.bfloat16)
            .reshape(local_rows, KV_HEADS, repeat, HEAD)
        )
        raw_again = (
            jnp.einsum("qgrd,kgd->grqk", queries, keys_all, preferred_element_type=jnp.float32)
            * scale
        )
        raw_again = jnp.where(allowed[None, None], raw_again, floor_score)
        probs_again = jnp.exp(raw_again - logsum)
        value_part = jnp.einsum(
            "grqk,qgrd->kgd",
            probs_again.astype(jnp.bfloat16),
            mixed_grad,
            preferred_element_type=jnp.float32,
        )
        prob_grad = jnp.einsum(
            "qgrd,kgd->grqk", mixed_grad, values_all, preferred_element_type=jnp.float32
        )
        inner = jnp.sum(probs_again * prob_grad, axis=-1, keepdims=True)
        score_grad = (probs_again * (prob_grad - inner)).astype(jnp.bfloat16)
        query_grad = (
            jnp.einsum("grqk,kgd->qgrd", score_grad, keys_all, preferred_element_type=jnp.float32)
            * scale
        )
        key_part = (
            jnp.einsum("grqk,qgrd->kgd", score_grad, queries, preferred_element_type=jnp.float32)
            * scale
        )
        key_grad, value_grad = (
            lax.psum_scatter(
                key_part.astype(jnp.bfloat16), "fsdp", scatter_dimension=0, tiled=True
            ).astype(jnp.float32),
            lax.psum_scatter(
                value_part.astype(jnp.bfloat16), "fsdp", scatter_dimension=0, tiled=True
            ).astype(jnp.float32),
        )
        pre_query_grad = (
            rotate_back(query_grad.reshape(local_rows, HEADS, HEAD), cosine, sine)
            .reshape(local_rows, D)
            .astype(jnp.bfloat16)
        )
        pre_key_grad = (
            rotate_back(key_grad, cosine, sine).reshape(local_rows, kv_width).astype(jnp.bfloat16)
        )
        pre_value_grad = value_grad.reshape(local_rows, kv_width).astype(jnp.bfloat16)
        attn_grad = join_blocks((pre_query_grad, pre_key_grad, pre_value_grad), shard_count)
        attn_term = weight_term(attn_grad, normed)
        sums[0] = sums[0] + attn_term[:query_cols]
        sums[1] = sums[1] + attn_term[query_cols : query_cols + key_cols]
        sums[2] = sums[2] + attn_term[query_cols + key_cols :]
        normed_grad = behind(attn_grad, merged_attn)
        input_back, attn_gain_grad = rms_back(inputs, factor_one, attention_gain, normed_grad)
        input_list.append((middle_grad + input_back).astype(jnp.bfloat16))
        attention_sum = attention_sum + attn_gain_grad
        feedforward_sum = feedforward_sum + feed_gain_grad
    reduced = (
        lax.psum_scatter(
            sums[0].astype(jnp.bfloat16), "dp", scatter_dimension=1, tiled=True
        ).astype(jnp.float32),
        lax.psum_scatter(
            sums[1].astype(jnp.bfloat16), "dp", scatter_dimension=1, tiled=True
        ).astype(jnp.float32),
        lax.psum_scatter(
            sums[2].astype(jnp.bfloat16), "dp", scatter_dimension=1, tiled=True
        ).astype(jnp.float32),
        lax.psum_scatter(
            sums[3].astype(jnp.bfloat16), "dp", scatter_dimension=1, tiled=True
        ).astype(jnp.float32),
        lax.psum_scatter(
            sums[4].astype(jnp.bfloat16), "dp", scatter_dimension=1, tiled=True
        ).astype(jnp.float32),
        lax.psum_scatter(
            sums[5].astype(jnp.bfloat16), "dp", scatter_dimension=1, tiled=True
        ).astype(jnp.float32),
        lax.psum_scatter(
            sums[6].astype(jnp.bfloat16), "dp", scatter_dimension=1, tiled=True
        ).astype(jnp.float32),
    )
    owner_grads = [owned.T for owned in reduced]
    local_square = reduce(jnp.add, [jnp.sum(owned * owned) for owned in owner_grads])
    attention_total, feedforward_total, square_total = lax.psum(
        (attention_sum, feedforward_sum, local_square), ("dp", "fsdp")
    )
    square_sum = (
        square_total
        + jnp.sum(attention_total * attention_total)
        + jnp.sum(feedforward_total * feedforward_total)
    )
    grad_norm = jnp.sqrt(square_sum)
    entry_count = 2 * D * D + 2 * D * kv_width + 3 * D * FF + 2 * D
    limit = clip_level * math.sqrt(entry_count)
    factor = limit / jnp.maximum(grad_norm, limit)
    gradients = owner_grads + [attention_total, feedforward_total]
    old_moments = [
        moment_query,
        moment_key,
        moment_value,
        moment_output,
        moment_gate,
        moment_up,
        moment_down,
        moment_attention,
        moment_feedforward,
    ]
    old_params = [
        query_weight,
        key_weight,
        value_weight,
        output_weight,
        gate_weight,
        up_weight,
        down_weight,
        attention_gain,
        feedforward_gain,
    ]
    new_moments = [
        0.5 * moment + 0.5 * factor * gradient for moment, gradient in zip(old_moments, gradients)
    ]
    new_params = []
    for place, param in enumerate(old_params):
        if place < 7:
            new_params.append(param - step_size * (new_moments[place] + decay_rate * param))
        else:
            new_params.append(param - gain_step * new_moments[place])
    outputs = jnp.stack(output_list)
    input_grad = jnp.stack(input_list)
    return (
        outputs,
        input_grad,
        grad_norm,
        new_moments[0],
        new_moments[1],
        new_moments[2],
        new_moments[3],
        new_moments[4],
        new_moments[5],
        new_moments[6],
        new_moments[7],
        new_moments[8],
        new_params[0],
        new_params[1],
        new_params[2],
        new_params[3],
        new_params[4],
        new_params[5],
        new_params[6],
        new_params[7],
        new_params[8],
    )


CORE, SIDE_A, SIDE_B = 1, 2, 4
CHIPS = 4
CHUNKS = 4
MB = 1024 * 1024


def across(value, mask):
    count = lax.axis_size("dp")
    return lax.ppermute(value, "dp", [(place, place ^ mask) for place in range(count)])


def along(value, mask):
    count = lax.axis_size("fsdp")
    return lax.ppermute(value, "fsdp", [(place, place ^ mask) for place in range(count)])


def pick(values, index):
    return lax.dynamic_index_in_dim(values, index, 0, keepdims=False)


def after(value, *earlier):
    return lax.optimization_barrier((value, earlier))[0]


def trade_planes(parts, plane):
    found = [pick(parts, plane)]
    for mask in range(1, CHUNKS):
        found.append(along(pick(parts, plane ^ mask), mask))
    found = jnp.stack(found)
    return [pick(found, label ^ plane) for label in range(CHUNKS)]


def gather_planes(block):
    one, two = along(block, 1), along(block, 2)
    return [block, one, two, along(two, 1)]


def sum_planes(parts):
    two = (parts[2].astype(jnp.float32) + along(parts[3], 1).astype(jnp.float32)).astype(jnp.bfloat16)
    return (
        parts[0].astype(jnp.float32)
        + along(parts[1], 1).astype(jnp.float32)
        + along(two, 2).astype(jnp.float32)
    )


def sum_all(value):
    for mask in (CORE, SIDE_A, SIDE_B):
        value = value + across(value, mask)
    for mask in (1, 2):
        value = value + along(value, mask)
    return value


def to_planes(array, core, plane):
    halves = array.reshape(2, 2, array.shape[1] // 2, array.shape[2]).swapaxes(0, 1)
    keep = pick(halves, core)
    came = across(pick(halves, 1 - core), CORE)
    swap = core == 1
    parts = jnp.concatenate([jnp.where(swap, came, keep), jnp.where(swap, keep, came)])
    return trade_planes(parts, plane)


def from_planes(chunks, core, plane):
    groups = trade_planes(jnp.stack(chunks), plane)
    pairs = jnp.stack([jnp.stack(groups[:2]), jnp.stack(groups[2:])])
    keep = pick(pairs, core)
    came = across(pick(pairs, 1 - core), CORE)
    swap = core == 1
    return jnp.concatenate([jnp.where(swap, came, keep), jnp.where(swap, keep, came)], axis=1)


MESH = pl.DeviceIdType.MESH
SLOT = {0: 0, SIDE_A: 1, SIDE_B: 2}
ROUTES = ((SIDE_A, SIDE_B), (SIDE_B, SIDE_A))
STRIPE = 16


def flip(place, mask):
    for bit in (1, 2, 4):
        if mask & bit:
            place = place + bit - 2 * bit * lax.rem(lax.div(place, bit), 2)
    return place


def peer(mask, planes=0):
    return (flip(lax.axis_index("dp"), mask), flip(lax.axis_index("fsdp"), planes))


SIDES = ((CORE, 0), (SIDE_A, 0), (SIDE_B, 0))
PLANE = tuple((mask, 0) for mask in range(1, 8))
PLANES = tuple((0, mask) for mask in range(1, CHUNKS))


def meet(others):
    barrier = pltpu.get_barrier_semaphore()
    for mask, planes in others:
        pl.semaphore_signal(barrier, inc=1, device_id=peer(mask, planes), device_id_type=MESH)
    pl.semaphore_wait(barrier, len(others))


class Remote:
    def __init__(self, wires, source, target, mask, planes=0):
        self.wires, self.source, self.target, self.mask = wires, source, target, (mask, planes)
        self.place = wires.count
        wires.count += 1

    def make(self):
        return pltpu.make_async_remote_copy(
            src_ref=self.source,
            dst_ref=self.target,
            send_sem=self.wires.send.at[self.place],
            recv_sem=self.wires.recv.at[self.place],
            device_id=peer(*self.mask),
            device_id_type=MESH,
        )

    def start(self):
        self.make().start()

    def arrived(self):
        self.make().wait_recv()

    def left(self):
        self.make().wait_send()


class Wires:
    def __init__(self, send, recv, local):
        self.send, self.recv, self.local = send, recv, local
        self.count = 0
        self.local_count = 0

    def load(self, pairs):
        copies = [
            pltpu.make_async_copy(source, target, self.local.at[place])
            for place, (source, target) in enumerate(pairs)
        ]
        for copy in copies:
            copy.start()
        for copy in copies:
            copy.wait()


class Gather:
    def __init__(self, wires, own, target):
        rows = target.shape[2] // 2
        self.wires, self.own = wires, own
        self.near, self.far, self.core_first, self.core_near, self.core_far = [], [], [], [], []
        self.home = []

        def place(chunk, slot, half):
            return target.at[chunk, slot, pl.ds(half * rows, rows)]

        for chunk, (first, second) in enumerate(ROUTES):
            near, far = SLOT[first], SLOT[second]
            self.home.append((own[chunk], place(chunk, 0, 0)))
            self.near.append(Remote(wires, own[chunk], place(chunk, near, 0), first))
            self.core_first.append(Remote(wires, own[chunk], place(chunk, 0, 1), CORE))
            self.far.append(Remote(wires, own[chunk], place(chunk, far, 0), second))
            self.far.append(Remote(wires, place(chunk, near, 0), place(chunk, 3, 0), second))
            self.core_near.append(Remote(wires, place(chunk, near, 0), place(chunk, near, 1), CORE))
            self.core_far.append(Remote(wires, place(chunk, far, 0), place(chunk, far, 1), CORE))
            self.core_far.append(Remote(wires, place(chunk, 3, 0), place(chunk, 3, 1), CORE))

    def first(self):
        for copy in self.near + self.core_first:
            copy.start()
        self.wires.load(self.home)

    def second(self):
        for chunk, copy in enumerate(self.near):
            copy.arrived()
            self.far[2 * chunk].start()
            self.far[2 * chunk + 1].start()
            self.core_near[chunk].start()

    def third(self):
        for place, copy in enumerate(self.far):
            copy.arrived()
            self.core_far[place].start()

    def last(self):
        for copy in self.core_first + self.core_near + self.core_far:
            copy.arrived()
        for copy in self.near + self.far + self.core_first + self.core_near + self.core_far:
            copy.left()

    def steps(self):
        return [self.first, self.second, self.third, self.last]


class Scatter:
    def __init__(self, wires, own, other, landing, stage, done):
        from_core, from_far, from_near = landing
        self.wires, self.own, self.landing, self.stage, self.done = wires, own, landing, stage, done
        self.core = [Remote(wires, other.at[chunk], from_core.at[chunk], CORE) for chunk in range(2)]
        self.far = [
            Remote(wires, stage[0].at[chunk], from_far.at[chunk], first)
            for chunk, (_, first) in enumerate(ROUTES)
        ]
        self.near = [
            Remote(wires, stage[2].at[chunk, 0], from_near.at[chunk], last)
            for chunk, (last, _) in enumerate(ROUTES)
        ]

    def first(self):
        for copy in self.core:
            copy.start()

    def second(self):
        left, right = self.stage[:2]
        pairs = []
        for chunk, (_, first) in enumerate(ROUTES):
            self.core[chunk].arrived()
            for place, slot in enumerate((SLOT[first], 3)):
                pairs.append((self.own.at[chunk, slot], left.at[chunk, place]))
                pairs.append((self.landing[0].at[chunk, slot], right.at[chunk, place]))
        self.wires.load(pairs)
        for chunk in range(2):

            @pl.loop(0, left.shape[2] // STRIPE)
            def _(step):
                span = pl.ds(step * STRIPE, STRIPE)
                total = left[chunk, :, span].astype(jnp.float32) + right[chunk, :, span].astype(jnp.float32)
                left[chunk, :, span] = total.astype(jnp.bfloat16)

            self.far[chunk].start()

    def third(self):
        stage = self.stage[2]
        pairs = []
        for chunk, (last, _) in enumerate(ROUTES):
            self.far[chunk].arrived()
            pairs.append((self.own.at[chunk, SLOT[last]], stage.at[chunk, 0]))
            pairs.append((self.landing[0].at[chunk, SLOT[last]], stage.at[chunk, 1]))
            pairs.append((self.landing[1].at[chunk, 1], stage.at[chunk, 2]))
        self.wires.load(pairs)
        for chunk in range(2):

            @pl.loop(0, stage.shape[2] // STRIPE)
            def _(step):
                span = pl.ds(step * STRIPE, STRIPE)
                total = stage[chunk, 0, span].astype(jnp.float32)
                for place in range(1, 3):
                    total += stage[chunk, place, span].astype(jnp.float32)
                stage[chunk, 0, span] = total.astype(jnp.bfloat16)

            self.near[chunk].start()
        for copy in self.far:
            copy.left()

    def last(self):
        stage = self.stage[3]
        for chunk in range(2):
            self.near[chunk].arrived()
            self.wires.load(
                [
                    (self.own.at[chunk, 0], stage.at[0]),
                    (self.landing[0].at[chunk, 0], stage.at[1]),
                    (self.landing[1].at[chunk, 0], stage.at[2]),
                    (self.landing[2].at[chunk], stage.at[3]),
                ]
            )

            @pl.loop(0, stage.shape[1] // STRIPE)
            def _(step):
                span = pl.ds(step * STRIPE, STRIPE)
                total = stage[0, span].astype(jnp.float32)
                for place in range(1, 4):
                    total += stage[place, span].astype(jnp.float32)
                self.done(chunk, span, total)

        for copy in self.near + self.core:
            copy.left()

    def steps(self):
        return [self.first, self.second, self.third, self.last]


def stage_shapes(rows, width):
    return [
        pltpu.VMEM((2, 2, rows, width), jnp.bfloat16),
        pltpu.VMEM((2, 2, rows, width), jnp.bfloat16),
        pltpu.VMEM((2, 3, rows, width), jnp.bfloat16),
        pltpu.VMEM((4, rows, width), jnp.bfloat16),
    ]


def landing_shapes(rows, width):
    return [
        jax.ShapeDtypeStruct((2, CHIPS, rows, width), jnp.bfloat16),
        jax.ShapeDtypeStruct((2, 2, rows, width), jnp.bfloat16),
        jax.ShapeDtypeStruct((2, rows, width), jnp.bfloat16),
    ]


def partial_shapes(rows, width):
    return [jax.ShapeDtypeStruct((2, CHIPS, rows, width), jnp.bfloat16)] * 2


def wire_shapes(count):
    return [
        pltpu.SemaphoreType.DMA((count,)),
        pltpu.SemaphoreType.DMA((count,)),
        pltpu.SemaphoreType.DMA((8,)),
    ]


def call(kernel, identity, inputs, outputs, scratch, megabytes):
    return pl.pallas_call(
        kernel,
        in_specs=[pl.BlockSpec(memory_space=place) for _, place in inputs],
        out_specs=[pl.BlockSpec(memory_space=place) for _, place in outputs],
        out_shape=[shape for shape, _ in outputs],
        scratch_shapes=scratch,
        compiler_params=pltpu.CompilerParams(
            collective_id=identity, has_side_effects=True, vmem_limit_bytes=megabytes * MB
        ),
    )(*[array for array, _ in inputs])


HBM, VMEM, SMEM = pl.ANY, pltpu.VMEM, pltpu.SMEM


def move_rows(source, target):
    @pl.loop(0, source.shape[0] // STRIPE)
    def _(step):
        span = pl.ds(step * STRIPE, STRIPE)
        target[span] = source[span]


def half_rows(index, rows):
    return pl.ds(pl.multiple_of(index * rows, STRIPE), rows)


def columns_of(index, columns):
    return pl.ds(pl.multiple_of(index * columns, columns), columns)


def at_step(step, actions):
    for when, action in actions.items():
        pl.when(step == when)(action)


def project_phase(gathered, states, weight_ref, cosine, sine, actions):
    tokens = gathered.shape[2]

    def body(rows_ref, cosine_ref, sine_ref, out):
        at_step(pl.program_id(0) * CHIPS + pl.program_id(1), actions)
        product = dot(rows_ref[0, 0], weight_ref[...].reshape(D, 3 * HEAD))
        angles = (cosine_ref[0], sine_ref[0])
        query = spin(product[:, :HEAD], *angles) * (1.0 / math.sqrt(HEAD))
        key = spin(product[:, HEAD : 2 * HEAD], *angles)
        out[0, 0] = jnp.concatenate([query, key, product[:, 2 * HEAD :]], axis=1).astype(jnp.bfloat16)

    here = lambda chunk, chip: (chunk, chip, 0, 0)
    table = pl.BlockSpec((1, tokens, HEAD // 2), lambda chunk, chip: (chunk, 0, 0))
    pltpu.emit_pipeline(
        body,
        grid=(2, CHIPS),
        in_specs=[pl.BlockSpec((1, 1, tokens, gathered.shape[3]), here), table, table],
        out_specs=[pl.BlockSpec((1, 1, tokens, 3 * HEAD), here)],
    )(gathered, cosine, sine, states)


def attend_phase(pair, states, mixed, own, other, lengths_ref, places, weight_ref, keys, values, actions):
    tokens, rows, width = mixed.shape[2], own.shape[2], own.shape[3]
    blocks = 2 * (pair + 1)

    def body(*refs):
        state_refs, (mixed_ref, own_ref, other_ref) = refs[: pair + 1], refs[pair + 1 :]
        chip, side_at = pl.program_id(0), pl.program_id(1)
        at_step(2 * chip + side_at, actions)

        @pl.when(side_at == 0)
        def _():
            for block in range(blocks):
                ref = state_refs[block // 2]
                keys[pl.ds(block * tokens, tokens)] = ref[block % 2, 0, :, HEAD : 2 * HEAD]
                values[pl.ds(block * tokens, tokens)] = ref[block % 2, 0, :, 2 * HEAD :]

        for side in range(2):

            @pl.when(side_at == side)
            def _():
                chunk = 2 * pair + side
                count = tokens * (chunk + 1)
                scores = dot_t(state_refs[pair][side, 0, :, :HEAD], keys[:count])
                mask = seen(places[0][...], places[1][...], chunk, count, tokens, lengths_ref, chip)
                scores = jnp.where(mask, scores, floor_score)
                highest = jnp.max(scores, axis=1, keepdims=True)
                exponent = jnp.exp(scores - highest)
                total = jnp.sum(exponent, axis=1, keepdims=True)
                probs = (exponent * (1.0 / total)).astype(jnp.bfloat16)
                mixed_ref[0, 0] = dot(probs, values[:count]).astype(jnp.bfloat16)

        partial = dot(mixed_ref[0, 0], weight_ref[...]).astype(jnp.bfloat16)
        own_ref[0, 0] = partial[:rows]
        other_ref[0, 0] = partial[rows:]

    here = lambda chip, side: (side, chip, 0, 0)
    state = pl.BlockSpec((2, 1, tokens, 3 * HEAD), lambda chip, side: (0, chip, 0, 0))
    pltpu.emit_pipeline(
        body,
        grid=(CHIPS, 2),
        in_specs=[state] * (pair + 1),
        out_specs=[pl.BlockSpec((1, 1, tokens, HEAD), here)] + [pl.BlockSpec((1, 1, rows, width), here)] * 2,
    )(*states[: pair + 1], mixed, own, other)


def attend_back_phase(
    pair, branch, states, head_grads, own, other, lengths_ref, places, out_weight, weight_ref,
    tables, keys, values, sums, late_sums, actions
):
    tokens, rows, width = branch.shape[2], own.shape[2], own.shape[3]
    blocks = 2 * (pair + 1)
    edge = 2 * tokens

    def body(*refs):
        branch_ref, state_refs = refs[0], refs[1 : pair + 2]
        cosine_ref, sine_ref, grads_ref, own_ref, other_ref = refs[pair + 2 :]
        chip, step = pl.program_id(0), pl.program_id(1)
        at_step(2 * chip + step, actions)

        @pl.when(step == 0)
        def _():
            for block in range(blocks):
                ref = state_refs[block // 2]
                keys[pl.ds(block * tokens, tokens)] = ref[block % 2, 0, :, HEAD : 2 * HEAD]
                values[pl.ds(block * tokens, tokens)] = ref[block % 2, 0, :, 2 * HEAD :]
            if pair == 1:
                for place in range(2):
                    sums[place][chip] = jnp.zeros(sums[place].shape[1:], jnp.float32)
                    late_sums[place][...] = jnp.zeros(late_sums[place].shape, jnp.float32)

        def add(place, term):
            early = min(term.shape[0], edge)
            sums[place][chip, :early] += term[:early]
            if term.shape[0] > edge:
                late_sums[place][: term.shape[0] - edge] += term[edge:]

        for side in range(2):

            @pl.when(step == 1 - side)
            def _():
                chunk = 2 * pair + side
                count = tokens * (chunk + 1)
                mixed_grad = dot_t(branch_ref[0, 0], out_weight[...]).astype(jnp.bfloat16)
                query = state_refs[pair][side, 0, :, :HEAD]
                scores = dot_t(query, keys[:count])
                mask = seen(places[0][...], places[1][...], chunk, count, tokens, lengths_ref, chip)
                scores = jnp.where(mask, scores, floor_score)
                highest = jnp.max(scores, axis=1, keepdims=True)
                exponent = jnp.exp(scores - highest)
                probs = exponent * (1.0 / jnp.sum(exponent, axis=1, keepdims=True))
                add(1, dot_tn(probs.astype(jnp.bfloat16), mixed_grad))
                prob_grad = dot_t(mixed_grad, values[:count])
                inner = jnp.sum(probs * prob_grad, axis=1, keepdims=True)
                score_grad = (probs * (prob_grad - inner)).astype(jnp.bfloat16)
                add(0, dot_tn(score_grad, query))
                query_grad = dot(score_grad, keys[:count]) * (1.0 / math.sqrt(HEAD))
                angles = (cosine_ref[0], sine_ref[0])
                span = slice(side * tokens, (side + 1) * tokens)
                if pair == 1:
                    key_grad, value_grad = late_sums[0][span], late_sums[1][span]
                else:
                    key_grad, value_grad = sums[0][chip, span], sums[1][chip, span]
                grads_ref[0, 0] = jnp.concatenate(
                    [spin_back(query_grad, *angles), spin_back(key_grad, *angles), value_grad], axis=1
                ).astype(jnp.bfloat16)

        partial = dot_t(grads_ref[0, 0], weight_ref[...].reshape(D, 3 * HEAD)).astype(jnp.bfloat16)
        own_ref[0, 0] = partial[:rows]
        other_ref[0, 0] = partial[rows:]

    here = lambda chip, step: (1 - step, chip, 0, 0)
    state = pl.BlockSpec((2, 1, tokens, 3 * HEAD), lambda chip, step: (0, chip, 0, 0))
    table = pl.BlockSpec((1, tokens, HEAD // 2), lambda chip, step: (1 - step, 0, 0))
    pltpu.emit_pipeline(
        body,
        grid=(CHIPS, 2),
        in_specs=[pl.BlockSpec((1, 1, tokens, width), here)] + [state] * (pair + 1) + [table] * 2,
        out_specs=[pl.BlockSpec((1, 1, tokens, 3 * HEAD), here)]
        + [pl.BlockSpec((1, 1, rows, width), here)] * 2,
    )(branch, *states[: pair + 1], *tables, head_grads, own, other)


def feed_phase(rows_in, grads_in, hidden, unit_grads, back_parts, out_parts, weights, actions):
    tokens, width = rows_in.shape[2:]
    rows = tokens // 2
    shards, columns = weights.shape[0], weights.shape[2]
    share = columns // 2

    def body(rows_ref, out_grad_ref, hidden_ref, units_ref, back_own, back_other, out_own, out_other):
        at_step(pl.program_id(0) * CHIPS + pl.program_id(1), actions)
        hidden_grad = None
        for shard in range(shards):
            grad = out_grad_ref[0, 0, :, shard * columns : (shard + 1) * columns]
            term = dot_t(grad, weights[shard, width:, :])
            hidden_grad = term if hidden_grad is None else hidden_grad + term
        back = None
        for shard in range(shards):
            both = dot(rows_ref[0, 0], weights[shard, :width, :])
            gate, upward = both[:, :share], both[:, share:]
            grad = hidden_grad[:, shard * share : (shard + 1) * share]
            sigmoid = jax.nn.sigmoid(gate)
            swish = gate * sigmoid
            hidden_ref[0, 0, :, shard * share : (shard + 1) * share] = (swish * upward).astype(jnp.bfloat16)
            gate_grad = grad * upward * sigmoid * (1.0 + gate * (1.0 - sigmoid))
            units_ref[shard, 0, 0] = jnp.concatenate([gate_grad, grad * swish], axis=1).astype(jnp.bfloat16)
            term = dot_t(units_ref[shard, 0, 0], weights[shard, :width, :])
            back = term if back is None else back + term
        back = back.astype(jnp.bfloat16)
        back_own[0, 0] = back[:rows]
        back_other[0, 0] = back[rows:]
        for shard in range(shards):
            span = slice(shard * columns, (shard + 1) * columns)
            value = dot(hidden_ref[0, 0], weights[shard, width:, :]).astype(jnp.bfloat16)
            out_own[0, 0, :, span] = value[:rows]
            out_other[0, 0, :, span] = value[rows:]

    here = lambda chunk, chip: (chunk, chip, 0, 0)
    wide = pl.BlockSpec((1, 1, tokens, width), here)
    narrow = pl.BlockSpec((1, 1, rows, width), here)
    pltpu.emit_pipeline(
        body,
        grid=(2, CHIPS),
        in_specs=[wide, wide],
        out_specs=[
            pl.BlockSpec((1, 1, tokens, hidden.shape[3]), here),
            pl.BlockSpec((shards, 1, 1, tokens, columns), lambda chunk, chip: (0, chunk, chip, 0, 0)),
        ]
        + [narrow] * 4,
    )(rows_in, grads_in, hidden, unit_grads, *back_parts, *out_parts)


def bf16(*shape):
    return jax.ShapeDtypeStruct(shape, jnp.bfloat16)


def f32(*shape):
    return jax.ShapeDtypeStruct(shape, jnp.float32)


def start_up(
    activations, cotangent, head_block, out_block, unit_block, down_block, lengths_block, gain
):
    _, tokens, width = activations.shape
    rows = tokens // 2
    devices, unit_rows, columns = unit_block.shape
    down_rows = down_block.shape[1]
    planes, _, sub_rows, _ = head_block.shape
    edge = devices * unit_rows

    def kernel(*refs):
        act, cot, head_in, out_in, unit_in, down_in, length_in, gain_ref = refs[:8]
        own_rows, own_grads, gathered = refs[8], refs[9], refs[10:12]
        head_weight, head_output, feed_own, lengths_all = refs[12:16]
        act_groups, cot_groups, traded, spread, other_half, normed = refs[16:22]
        wires = Wires(*refs[22:])
        place, plane = lax.axis_index("dp"), lax.axis_index("fsdp")
        core = lax.rem(place, 2)

        def half(index):
            return pl.ds(pl.multiple_of(index * rows, STRIPE), rows)

        def move(source, target):
            @pl.loop(0, rows // STRIPE)
            def _(step):
                span = pl.ds(step * STRIPE, STRIPE)
                target[span] = source[span]

        def trade(array, groups, own):
            label = [2 * core + group for group in range(2)]
            inside = [
                Remote(wires, array.at[group, half(1 - core)], groups.at[label[group]], CORE)
                for group in range(2)
            ]
            outside = [
                Remote(wires, groups.at[flip(plane, mask)], own.at[plane], 0, mask)
                for mask in range(1, CHUNKS)
            ]

            def keep():
                for group in range(2):
                    move(array.at[group, half(core)], groups.at[label[group]])

            return inside, keep, outside, lambda: move(groups.at[plane], own.at[plane])

        act_inside, act_keep, act_outside, act_own = trade(act, act_groups, own_rows)
        cot_inside, cot_keep, cot_outside, cot_own = trade(cot, cot_groups, own_grads)
        head_trade = [
            Remote(wires, head_in.at[flip(plane, mask)], traded.at[plane], 0, mask)
            for mask in range(1, CHUNKS)
        ]
        head_spread, feed_spread = [], []
        for mask in range(1, devices):
            other = flip(place, mask)
            head_spread.append(
                Remote(
                    wires,
                    traded.at[lax.div(other, 2), lax.rem(other, 2)],
                    spread.at[place, plane],
                    mask,
                )
            )
            feed_spread.append(
                Remote(
                    wires,
                    unit_in.at[other],
                    feed_own.at[pl.ds(pl.multiple_of(place * unit_rows, unit_rows), unit_rows)],
                    mask,
                )
            )
            feed_spread.append(
                Remote(
                    wires,
                    down_in.at[other],
                    feed_own.at[pl.ds(pl.multiple_of(edge + place * down_rows, down_rows), down_rows)],
                    mask,
                )
            )
            feed_spread.append(Remote(wires, length_in, lengths_all.at[place], mask))

        def over_planes(block):
            mine, theirs = block(plane), block(flip(plane, 2))
            return (
                [Remote(wires, mine, mine, 0, 1), Remote(wires, mine, mine, 0, 2)],
                Remote(wires, theirs, theirs, 0, 1),
            )

        head_near, head_relay = over_planes(lambda index: spread.at[:, index])
        out_near, out_relay = over_planes(
            lambda index: head_output.at[:, pl.ds(pl.multiple_of(index * columns, columns), columns)]
        )
        core_half = Remote(wires, spread.at[:, :, :, pl.ds(HEAD, HEAD)], other_half, CORE)
        moves = [
            Gather(wires, [normed.at[2 * pair], normed.at[2 * pair + 1]], gathered[pair])
            for pair in range(2)
        ]

        meet(PLANE + PLANES)
        for copy in act_inside + cot_inside + head_trade + feed_spread:
            copy.start()
        act_keep()
        for copy in act_inside:
            copy.arrived()
        for copy in act_outside:
            copy.start()
        cot_keep()
        act_own()
        traded[plane] = head_in[plane]
        columns_at = pl.ds(pl.multiple_of(plane * columns, columns), columns)
        head_output[:, columns_at] = out_in[...]
        feed_own[pl.ds(pl.multiple_of(place * unit_rows, unit_rows), unit_rows)] = unit_in[place]
        feed_own[pl.ds(pl.multiple_of(edge + place * down_rows, down_rows), down_rows)] = down_in[place]
        lengths_all[place] = length_in[...]
        for copy in head_trade:
            copy.arrived()
        for copy in head_spread:
            copy.start()
        spread[place, plane] = traded[lax.div(place, 2), core]
        for copy in head_spread + cot_inside:
            copy.arrived()
        cot_own()
        for copy in act_outside:
            copy.arrived()
        for copy in head_near + out_near:
            copy.start()

        for chunk in range(CHUNKS):

            @pl.loop(0, rows // STRIPE)
            def _(step):
                span = pl.ds(step * STRIPE, STRIPE)
                values = own_rows[chunk, span].astype(jnp.float32)
                factor = lax.rsqrt(jnp.mean(values * values, axis=1, keepdims=True) + epsilon)
                normed[chunk, span] = (values * factor * gain_ref[...]).astype(jnp.bfloat16)

        moves[0].first()
        moves[0].second()
        moves[1].first()
        moves[0].third()
        moves[1].second()
        for copy in head_near + out_near:
            copy.arrived()
        head_relay.start()
        out_relay.start()
        for copy in cot_outside:
            copy.start()
        moves[0].last()
        moves[1].third()
        head_relay.arrived()
        core_half.start()
        moves[1].last()
        out_relay.arrived()
        core_half.arrived()
        head_weight[:, :, :, :HEAD] = spread[:, :, :, :HEAD]
        for index in range(2):

            @pl.when(core == index)
            def _():
                mine, theirs = (1 + index) * HEAD, (2 - index) * HEAD
                head_weight[:, :, :, mine : mine + HEAD] = spread[:, :, :, HEAD:]
                head_weight[:, :, :, theirs : theirs + HEAD] = other_half[...]

        for copy in feed_spread + cot_outside:
            copy.arrived()
        for copy in (
            act_inside + cot_inside + head_trade + feed_spread + act_outside + head_spread
            + head_near + out_near + [head_relay, out_relay, core_half] + cot_outside
        ):
            copy.left()

    own = bf16(CHUNKS, rows, width)
    outs = call(
        kernel,
        1,
        [(activations, VMEM), (cotangent, VMEM), (head_block, VMEM), (out_block, VMEM)]
        + [(unit_block, VMEM), (down_block, VMEM), (lengths_block, VMEM), (gain, VMEM)],
        [(own, VMEM), (own, VMEM)]
        + [(bf16(2, CHIPS, tokens, width), HBM)] * 2
        + [(bf16(devices, planes, sub_rows, 3 * HEAD), VMEM), (bf16(HEAD, width), VMEM)]
        + [(bf16(devices * (unit_rows + down_rows), columns), VMEM)]
        + [(jax.ShapeDtypeStruct((devices,) + lengths_block.shape, jnp.int32), VMEM)],
        [
            pltpu.VMEM((CHUNKS, rows, width), jnp.bfloat16),
            pltpu.VMEM((CHUNKS, rows, width), jnp.bfloat16),
            pltpu.VMEM((planes, 2, sub_rows, columns), jnp.bfloat16),
            pltpu.VMEM((devices, planes, sub_rows, columns), jnp.bfloat16),
            pltpu.VMEM((devices, planes, sub_rows, HEAD), jnp.bfloat16),
            pltpu.VMEM((CHUNKS, rows, width), jnp.bfloat16),
        ]
        + wire_shapes(90),
        56,
    )
    return outs[0], outs[1], outs[2:4], outs[4], outs[5], outs[6], outs[7]


def attend_and_norm(
    rows_all, out_grads, feed_own, weight, cosine, sine, lengths, places, out_weight, inputs, gain
):
    _, rows, width = inputs.shape
    tokens = 2 * rows
    planes = CHUNKS
    whole_pair = bf16(2, CHIPS, tokens, width)

    def kernel(*refs):
        gathered, grads_ref, feed_ref, head_ref, cosine_ref, sine_ref = refs[:2], *refs[2:7]
        lengths_ref, place_q, place_k, weight_ref, inputs_ref, gain_ref = refs[7:13]
        refs = refs[13:]
        states, mixed, middle, normed, target, grads_all, feed_all = refs[:2], refs[2:4], *refs[4:9]
        parts, landings = (refs[9:11], refs[11:13]), (refs[13:16], refs[16:19])
        stage, keys, values, normed_late = refs[19:23], refs[23], refs[24], refs[25]
        wires = Wires(*refs[26:])
        plane = lax.axis_index("fsdp")

        def finish(pair):
            def done(chunk, span, total):
                at = 2 * pair + chunk
                total = total + inputs_ref[at, span].astype(jnp.float32)
                middle[at, span] = total
                factor = lax.rsqrt(jnp.mean(total * total, axis=1, keepdims=True) + epsilon)
                kept = normed if pair == 0 else normed_late
                kept[chunk, span] = (total * factor * gain_ref[...]).astype(jnp.bfloat16)

            return done

        sums = [
            Scatter(wires, *parts[pair], landings[pair], stage, finish(pair)) for pair in range(2)
        ]
        move = Gather(wires, [normed_late.at[0], normed_late.at[1]], target)
        grad_move = Gather(wires, [grads_ref.at[2], grads_ref.at[3]], grads_all)
        near = Remote(wires, feed_ref, feed_all.at[plane], 0, 1)
        across_middle = Remote(wires, feed_ref, feed_all.at[plane], 0, 2)
        relay = Remote(
            wires, feed_all.at[flip(plane, 2)], feed_all.at[flip(plane, 2)], 0, 1
        )
        places_in = (place_q, place_k)

        meet(SIDES + PLANES[:2])
        near.start()
        across_middle.start()
        grad_move.first()
        wires.load([(feed_ref, feed_all.at[plane])])
        project_phase(
            gathered[0], states[0], head_ref, cosine_ref.at[0], sine_ref.at[0], {7: grad_move.second}
        )
        project_phase(gathered[1], states[1], head_ref, cosine_ref.at[1], sine_ref.at[1], {})
        attend_phase(
            1, states, mixed[1], *parts[1], lengths_ref, places_in, weight_ref, keys, values,
            {3: grad_move.third},
        )
        sums[1].first()
        attend_phase(
            0, states, mixed[0], *parts[0], lengths_ref, places_in, weight_ref, keys, values,
            {5: sums[1].second},
        )
        sums[0].first()
        grad_move.last()
        sums[1].third()
        sums[0].second()
        sums[1].last()
        move.first()
        sums[0].third()
        across_middle.arrived()
        relay.start()
        move.second()
        sums[0].last()
        move.third()
        move.last()
        near.arrived()
        relay.arrived()
        for copy in (near, across_middle, relay):
            copy.left()

    pair_parts = [(shape, HBM) for shape in partial_shapes(rows, width)]
    landing = [(shape, HBM) for shape in landing_shapes(rows, width)]
    outs = call(
        kernel,
        2,
        [(rows_all[0], HBM), (rows_all[1], HBM), (out_grads, VMEM), (feed_own, VMEM)]
        + [(weight, VMEM), (cosine, HBM), (sine, HBM)]
        + [(lengths, SMEM), (places[0], VMEM), (places[1], VMEM), (out_weight, VMEM)]
        + [(inputs, VMEM), (gain, VMEM)],
        [(bf16(2, CHIPS, tokens, 3 * HEAD), HBM)] * 2
        + [(bf16(2, CHIPS, tokens, HEAD), HBM)] * 2
        + [(f32(CHUNKS, rows, width), VMEM), (bf16(2, rows, width), VMEM)]
        + [(whole_pair, HBM)] * 2
        + [(bf16(planes, *feed_own.shape), HBM)]
        + pair_parts * 2
        + landing * 2,
        stage_shapes(rows, width)
        + [pltpu.VMEM((CHUNKS * tokens, HEAD), jnp.bfloat16)] * 2
        + [pltpu.VMEM((2, rows, width), jnp.bfloat16)]
        + wire_shapes(50),
        60,
    )
    return outs[:2], outs[2:4], outs[4], outs[5], outs[6], outs[7], outs[8]


def norm_back(values, gain, gradient):
    factor = lax.rsqrt(jnp.mean(values * values, axis=1, keepdims=True) + epsilon)
    scaled = values * factor
    pulled = gradient * gain
    back = factor * (pulled - scaled * jnp.mean(pulled * scaled, axis=1, keepdims=True))
    return back, gradient * scaled


def feed_forward(normed_own, normed_late, grads_late, weights, middle, out_grad_own, gain, units):
    _, rows, width = middle.shape
    tokens = 2 * rows
    shards, columns = weights.shape[0], weights.shape[2]
    whole_pair = bf16(2, CHIPS, tokens, width)

    def kernel(*refs):
        normed_ref, normed_late_ref, grads_late_ref = refs[:3]
        weight_ref, middle_ref, own_grad, gain_ref = refs[3:7]
        refs = (None, *refs)
        normed_early, branch, grads_early = refs[8], refs[9], refs[27]
        hidden, unit_grads = refs[10:12], refs[12:14]
        back_parts, out_parts = (refs[14:16], refs[16:18]), (refs[18:20], refs[20:22])
        middle_grad, gain_sum, landing = refs[22], refs[23], refs[24:27]
        stage, own_branch, wires = refs[28:32], refs[32], Wires(*refs[33:])
        meet(SIDES)
        gain_sum[...] = jnp.zeros(gain_sum.shape, jnp.float32)

        def done(chunk, span, total):
            back, gain_terms = norm_back(middle_ref[2 + chunk, span], gain_ref[...], total)
            gain_sum[...] += gain_terms
            back = back + own_grad[2 + chunk, span].astype(jnp.float32)
            middle_grad[chunk, span] = back
            own_branch[chunk, span] = back.astype(jnp.bfloat16)

        move = Gather(wires, [normed_ref.at[0], normed_ref.at[1]], normed_early)
        sums = Scatter(wires, *back_parts[1], landing, stage, done)
        late_move = Gather(wires, [own_branch.at[0], own_branch.at[1]], branch)
        grad_move = Gather(wires, [own_grad.at[0], own_grad.at[1]], grads_early)
        move.first()
        grad_move.first()
        feed_phase(
            normed_late_ref, grads_late_ref, hidden[1], unit_grads[1], back_parts[1], out_parts[1],
            weight_ref,
            {2: move.second, 3: grad_move.second, 5: move.third, 7: grad_move.third},
        )
        sums.first()
        move.last()
        grad_move.last()
        feed_phase(
            normed_early, grads_early, hidden[0], unit_grads[0], back_parts[0], out_parts[0], weight_ref,
            {1: sums.second, 4: sums.third, 6: lambda: (sums.last(), late_move.first()) and None},
        )
        late_move.second()
        late_move.third()
        late_move.last()

    outs = call(
        kernel,
        3,
        [(normed_own, VMEM), (normed_late, HBM), (grads_late, HBM)]
        + [(weights, VMEM), (middle, VMEM), (out_grad_own, VMEM), (gain, VMEM)],
        [(whole_pair, HBM)] * 2
        + [(bf16(2, CHIPS, tokens, units), HBM)] * 2
        + [(bf16(shards, 2, CHIPS, tokens, columns), HBM)] * 2
        + [(shape, HBM) for shape in partial_shapes(rows, width)] * 4
        + [(f32(2, rows, width), VMEM), (f32(STRIPE, width), VMEM)]
        + [(shape, HBM) for shape in landing_shapes(rows, width)]
        + [(whole_pair, HBM)],
        stage_shapes(rows, width) + [pltpu.VMEM((2, rows, width), jnp.bfloat16)] + wire_shapes(50),
        62,
    )
    return outs[19], outs[0], outs[1], outs[2:4], outs[4:6], outs[6:8], (outs[10:12], outs[12:14]), outs[14], outs[15]


def attend_back(
    states, lengths, places, out_weight, weight, cosine, sine, branch_late, back_early, out_parts,
    middle, out_grad_own, inputs, middle_grad_late, gains
):
    _, rows, width = middle.shape
    tokens = 2 * rows

    def kernel(*refs):
        states_in, (lengths_ref, place_q, place_k, out_ref, weight_ref, cosine_ref, sine_ref) = (
            refs[:2],
            refs[2:9],
        )
        late_branch, back_parts, outs_in = refs[9], refs[10:12], (refs[12:14], refs[14:16])
        middle_ref, own_grad, inputs_ref, late_grad, gain_one, gain_two = refs[16:22]
        head_grads, early_branch, output_groups, input_grad = refs[22:24], refs[24], refs[25], refs[26]
        gain_sums = refs[27]
        parts = (refs[28:30], refs[30:32])
        landings = [refs[32 + 3 * place : 35 + 3 * place] for place in range(5)]
        stage, early_grad, own_branch, keys, values = refs[47:51], refs[51], refs[52], refs[53], refs[54]
        sums, late_sums, outputs, wires = refs[55:57], refs[57:59], refs[59], Wires(*refs[60:])
        plane = lax.axis_index("fsdp")
        meet(SIDES + PLANES)
        gain_sums[...] = jnp.zeros(gain_sums.shape, jnp.float32)

        def middle_done(chunk, span, total):
            back, gain_terms = norm_back(
                middle_ref[chunk, span].astype(jnp.float32), gain_two[...], total
            )
            gain_sums[1] += gain_terms
            back = back + own_grad[chunk, span].astype(jnp.float32)
            early_grad[chunk, span] = back
            own_branch[chunk, span] = back.astype(jnp.bfloat16)

        def output_done(pair):
            def done(chunk, span, total):
                at = 2 * pair + chunk
                outputs[at, span] = (middle_ref[at, span] + total).astype(jnp.bfloat16)

            return done

        def input_done(pair):
            def done(chunk, span, total):
                at = 2 * pair + chunk
                back, gain_terms = norm_back(
                    inputs_ref[at, span].astype(jnp.float32), gain_one[...], total
                )
                gain_sums[0] += gain_terms
                direct = late_grad if pair == 1 else early_grad
                input_grad[at, span] = (direct[chunk, span] + back).astype(jnp.bfloat16)

            return done

        middle_sum = Scatter(wires, *back_parts, landings[0], stage, middle_done)
        move = Gather(wires, [own_branch.at[0], own_branch.at[1]], early_branch)
        output_sums = [
            Scatter(wires, *outs_in[pair], landings[1 + pair], stage, output_done(pair))
            for pair in range(2)
        ]
        input_sums = [
            Scatter(wires, *parts[pair], landings[3 + pair], stage, input_done(pair)) for pair in range(2)
        ]

        def back_through(pair, branch, actions):
            attend_back_phase(
                pair, branch, states_in, head_grads[pair], *parts[pair], lengths_ref,
                (place_q, place_k), out_ref, weight_ref, (cosine_ref.at[pair], sine_ref.at[pair]),
                keys, values, sums, late_sums, actions,
            )

        def both(*steps):
            def run():
                for step in steps:
                    step()

            return run

        back_to_planes = [
            Remote(wires, outputs.at[flip(plane, mask)], output_groups.at[plane], 0, mask)
            for mask in range(1, CHUNKS)
        ]

        def send_back():
            for copy in back_to_planes:
                copy.start()
            wires.load([(outputs.at[plane], output_groups.at[plane])])

        middle_sum.first()
        output_sums[1].first()
        output_sums[0].first()
        back_through(
            1,
            late_branch,
            {
                1: middle_sum.second,
                4: middle_sum.third,
                6: both(middle_sum.last, move.first),
                7: move.second,
            },
        )
        input_sums[1].first()
        output_sums[1].second()
        move.third()
        move.last()
        back_through(
            0,
            early_branch,
            {
                0: output_sums[1].third,
                2: both(output_sums[1].last, output_sums[0].second),
                4: output_sums[0].third,
                6: both(output_sums[0].last, send_back),
                7: input_sums[1].second,
            },
        )
        input_sums[0].first()
        input_sums[1].third()
        input_sums[0].second()
        input_sums[1].last()
        input_sums[0].third()
        input_sums[0].last()
        for copy in back_to_planes:
            copy.arrived()
        for copy in back_to_planes:
            copy.left()

    outs = call(
        kernel,
        4,
        [(state, HBM) for state in states]
        + [(lengths, SMEM), (places[0], VMEM), (places[1], VMEM), (out_weight, VMEM), (weight, VMEM)]
        + [(cosine, HBM), (sine, HBM), (branch_late, HBM)]
        + [(part, HBM) for part in back_early]
        + [(part, HBM) for parts in out_parts for part in parts]
        + [(middle, VMEM), (out_grad_own, VMEM), (inputs, VMEM), (middle_grad_late, VMEM)]
        + [(gains[0], VMEM), (gains[1], VMEM)],
        [(bf16(2, CHIPS, tokens, 3 * HEAD), HBM)] * 2
        + [(bf16(2, CHIPS, tokens, width), HBM)]
        + [(bf16(CHUNKS, rows, width), HBM), (bf16(CHUNKS, rows, width), VMEM)]
        + [(f32(2, STRIPE, width), VMEM)]
        + [(shape, HBM) for shape in partial_shapes(rows, width)] * 2
        + [(shape, HBM) for shape in landing_shapes(rows, width)] * 5,
        stage_shapes(rows, width)
        + [pltpu.VMEM((2, rows, width), jnp.float32), pltpu.VMEM((2, rows, width), jnp.bfloat16)]
        + [pltpu.VMEM((CHUNKS * tokens, HEAD), jnp.bfloat16)] * 2
        + [pltpu.VMEM((CHIPS, 2 * tokens, HEAD), jnp.float32)] * 2
        + [pltpu.VMEM((2 * tokens, HEAD), jnp.float32)] * 2
        + [pltpu.VMEM((CHUNKS, rows, width), jnp.bfloat16)]
        + wire_shapes(60),
        63,
    )
    return outs[:2], outs[2], outs[3], outs[4], outs[5]


def finish(head_sum, output_sum, unit_sum, down_sum, output_groups, input_grad, gain_sums):
    devices, planes, sub_rows, _ = head_sum.shape
    strips = unit_sum.shape[0]
    _, down_rows, columns = down_sum.shape
    _, rows, width = input_grad.shape
    in_rows = width // devices

    def kernel(*refs):
        heads, outs_in, units_in, downs_in, output_groups_ref, grads_ref, gains = refs[:7]
        outputs, input_out, head_out, output_out, units, downs, gain_out, square_out = refs[7:15]
        grad_groups, combined, other_half, mine, gathered = refs[15:20]
        head_landing, output_landing, head_two, output_two = refs[20:24]
        gain_parts, square_parts, wires = refs[24], refs[25], Wires(*refs[26:])
        place, plane = lax.axis_index("dp"), lax.axis_index("fsdp")
        core = lax.rem(place, 2)

        def part(mask):
            return combined.at[:, flip(plane, mask)], outs_in.at[:, columns_of(flip(plane, mask), columns)]

        def both(sources, targets, mask):
            return [Remote(wires, source, target, 0, mask) for source, target in zip(sources, targets)]

        landing = [(head_landing.at[index], output_landing.at[index]) for index in range(3)]
        third = both(part(3), landing[0], 1)
        first = both(part(1), landing[1], 1)
        second = both((head_two, output_two), landing[2], 2)
        core_half = Remote(wires, heads.at[:, :, :, columns_of(2 - core, HEAD)], other_half, CORE)
        rows_back = [
            Remote(wires, grads_ref.at[flip(plane, mask)], grad_groups.at[plane], 0, mask)
            for mask in range(1, CHUNKS)
        ]
        spread, heads_back = [], []
        for mask in range(1, devices):
            other = flip(place, mask)
            spread.append(Remote(wires, units_in.at[:, columns_of(other, in_rows)], units.at[place], mask))
            spread.append(Remote(wires, downs_in.at[other], downs.at[place], mask))
            heads_back.append(Remote(wires, mine.at[other], gathered.at[place], mask))
        heads_over = [
            Remote(wires, gathered.at[pl.ds(2 * flip(plane, mask), 2)], head_out.at[plane], 0, mask)
            for mask in range(1, CHUNKS)
        ]

        def to_owners(groups, target):
            copies = []
            for group in range(2):
                copies.append(
                    Remote(
                        wires,
                        groups.at[2 * (1 - core) + group],
                        target.at[group, half_rows(core, rows)],
                        CORE,
                    )
                )
            return copies

        outputs_in = to_owners(output_groups_ref, outputs)
        grads_in = to_owners(grad_groups, input_out)

        def sum_over(parts_ref):
            steps = [(mask, 0) for mask in (CORE, SIDE_A, SIDE_B)] + [(0, 1), (0, 2)]
            copies = [
                Remote(wires, parts_ref.at[2 * index], parts_ref.at[2 * index + 1], mask, over)
                for index, (mask, over) in enumerate(steps)
            ]

            def step(index):
                copies[index].arrived()
                copies[index].left()
                parts_ref[2 * index + 2] = parts_ref[2 * index] + parts_ref[2 * index + 1]
                if index + 1 < len(copies):
                    copies[index + 1].start()

            return copies[0].start, step, len(steps)

        gains_start, gains_step, count = sum_over(gain_parts)
        squares_start, squares_step, _ = sum_over(square_parts)

        gain_parts[0] = jnp.concatenate(
            [jnp.sum(gains[index], axis=0, keepdims=True) for index in range(2)]
            + [jnp.zeros((6, width), jnp.float32)]
        )
        meet(PLANE + PLANES)
        core_half.start()
        for copy in spread + outputs_in:
            copy.start()
        gains_start()
        for index in range(planes):
            combined[:, index, :, :HEAD] = heads[:, index, :, :HEAD]
        core_half.arrived()
        for index in range(2):

            @pl.when(core == index)
            def _():
                kept = (1 + index) * HEAD
                for block in range(planes):
                    total = heads[:, block, :, kept : kept + HEAD].astype(jnp.float32) + other_half[
                        :, block
                    ].astype(jnp.float32)
                    combined[:, block, :, HEAD:] = total.astype(jnp.bfloat16)

        for copy in third + first:
            copy.start()
        units[place] = units_in[:, columns_of(place, in_rows)]
        downs[place] = downs_in[place]
        for group in range(2):
            move_rows(
                output_groups_ref.at[2 * core + group], outputs.at[group, half_rows(core, rows)]
            )
        move_rows(grads_ref.at[plane], grad_groups.at[plane])
        for copy in third:
            copy.arrived()
        head_two[...] = (
            combined[:, flip(plane, 2)].astype(jnp.float32) + head_landing[0].astype(jnp.float32)
        ).astype(jnp.bfloat16)
        output_two[...] = (
            outs_in[:, columns_of(flip(plane, 2), columns)].astype(jnp.float32)
            + output_landing[0].astype(jnp.float32)
        ).astype(jnp.bfloat16)
        for copy in second:
            copy.start()
        gains_step(0)
        for copy in rows_back:
            copy.start()
        for index in range(1, count):
            gains_step(index)
        for copy in first + second:
            copy.arrived()
        total = combined[:, plane].astype(jnp.float32)
        for index in (1, 2):
            total += head_landing[index].astype(jnp.float32)
        mine[...] = total.astype(jnp.bfloat16)
        for copy in heads_back:
            copy.start()
        gathered[place] = mine[place]
        total = outs_in[:, columns_of(plane, columns)].astype(jnp.float32)
        for index in (1, 2):
            total += output_landing[index].astype(jnp.float32)
        output_out[...] = total
        square = jnp.sum(total * total)
        for copy in heads_back:
            copy.arrived()
        for copy in heads_over:
            copy.start()
        head_out[plane] = gathered[pl.ds(2 * plane, 2)]
        for copy in spread:
            copy.arrived()
        for index in range(devices):
            for ref in (units, downs):
                values = ref[index].astype(jnp.float32)
                square += jnp.sum(values * values)
        for copy in heads_over:
            copy.arrived()
        for index in range(planes):
            values = head_out[index].astype(jnp.float32)
            square += jnp.sum(values * values)
        square_parts[0] = jnp.full(square_parts.shape[1:], square, jnp.float32)
        squares_start()
        for index in range(count):
            squares_step(index)
        gain_out[...] = gain_parts[2 * count]
        square_out[...] = square_parts[2 * count]
        for copy in rows_back:
            copy.arrived()
        for copy in grads_in:
            copy.start()
        for group in range(2):
            move_rows(grad_groups.at[2 * core + group], input_out.at[group, half_rows(core, rows)])
        for copy in outputs_in + grads_in:
            copy.arrived()
        for copy in (
            third + first + second + [core_half] + rows_back + spread + heads_back + heads_over
            + outputs_in + grads_in
        ):
            copy.left()

    own = bf16(2, 2 * rows, width)
    return call(
        kernel,
        5,
        [
            (array, VMEM)
            for array in (
                head_sum, output_sum, unit_sum, down_sum, output_groups, input_grad, gain_sums
            )
        ],
        [(own, VMEM)] * 2
        + [(bf16(planes, 2, sub_rows, columns), VMEM), (f32(HEAD, columns), VMEM)]
        + [(bf16(devices, strips, in_rows), VMEM), (bf16(devices, down_rows, columns), VMEM)]
        + [(f32(8, width), VMEM), (f32(8, 128), VMEM)],
        [
            pltpu.VMEM((CHUNKS, rows, width), jnp.bfloat16),
            pltpu.VMEM((devices, planes, sub_rows, columns), jnp.bfloat16),
            pltpu.VMEM((devices, planes, sub_rows, HEAD), jnp.bfloat16),
            pltpu.VMEM((devices, sub_rows, columns), jnp.bfloat16),
            pltpu.VMEM((devices, sub_rows, columns), jnp.bfloat16),
            pltpu.VMEM((3, devices, sub_rows, columns), jnp.bfloat16),
            pltpu.VMEM((3, HEAD, columns), jnp.bfloat16),
            pltpu.VMEM((devices, sub_rows, columns), jnp.bfloat16),
            pltpu.VMEM((HEAD, columns), jnp.bfloat16),
            pltpu.VMEM((11, 8, width), jnp.float32),
            pltpu.VMEM((11, 8, 128), jnp.float32),
        ]
        + wire_shapes(70),
        62,
    )


def unit_weight_grads(unit_grads, rows_in):
    shards, _, _, tokens, columns = unit_grads[0].shape
    width = rows_in[0].shape[3]

    def kernel(late_units, late_rows, early_units, early_rows, out, total):
        step = pl.program_id(1)

        @pl.when(step == 0)
        def _():
            total[...] = jnp.zeros(total.shape, jnp.float32)

        for place, (units, rows_ref) in enumerate(((late_units, late_rows), (early_units, early_rows))):

            @pl.when(lax.div(step, 2) == place)
            def _():
                left = units[0, 0].reshape(CHIPS * tokens, columns)
                right = rows_ref[0].reshape(CHIPS * tokens, width)
                total[...] += dot_tn(left, right)

        @pl.when(step == 3)
        def _():
            out[0] = total[...].astype(jnp.bfloat16)

    late = lambda step: jnp.minimum(step, 1)
    early = lambda step: jnp.maximum(step - 2, 0)
    specs = []
    for at in (late, early):
        specs.append(
            pl.BlockSpec(
                (1, 1, CHIPS, tokens, columns),
                (lambda at: lambda shard, step: (shard, at(step), 0, 0, 0))(at),
            )
        )
        specs.append(
            pl.BlockSpec(
                (1, CHIPS, tokens, width), (lambda at: lambda shard, step: (at(step), 0, 0, 0))(at)
            )
        )
    return pl.pallas_call(
        kernel,
        grid=(shards, 4),
        in_specs=specs,
        out_specs=pl.BlockSpec((1, columns, width), lambda shard, step: (shard, 0, 0)),
        out_shape=bf16(shards, columns, width),
        scratch_shapes=[pltpu.VMEM((columns, width), jnp.float32)],
        compiler_params=params(60),
    )(unit_grads[1], rows_in[1], unit_grads[0], rows_in[0])


def dot(left, right):
    return jnp.dot(left, right, preferred_element_type=jnp.float32)


def dot_t(left, right):
    return lax.dot_general(
        left, right, (((1,), (1,)), ((), ())), preferred_element_type=jnp.float32
    )


def dot_tn(left, right):
    return lax.dot_general(
        left, right, (((0,), (0,)), ((), ())), preferred_element_type=jnp.float32
    )


def spin(values, cosine, sine):
    halfway = values.shape[1] // 2
    first, second = values[:, :halfway], values[:, halfway:]
    return jnp.concatenate(
        [first * cosine - second * sine, second * cosine + first * sine], axis=1
    )


def spin_back(values, cosine, sine):
    return spin(values, cosine, -sine)


def whole(shape):
    return pl.BlockSpec(shape, lambda *_: (0,) * len(shape), pipeline_mode=pl.Buffered(1))


def params(megabytes):
    return pltpu.CompilerParams(vmem_limit_bytes=megabytes * MB)


def seen(place_q, place_k, chunk, count, tokens, lengths_ref, chip):
    query_index = tokens * chunk + place_q
    key_index = place_k[:, :count]
    ahead_or_here = key_index <= query_index
    if tokens * (chunk + 1) <= PROMPT:
        return ahead_or_here

    def segment(index):
        found = jnp.full(index.shape, -1, jnp.int32)
        for slot in range(NCONT):
            found = jnp.where(index >= PROMPT + slot * CONT, slot, found)
        return found

    key_segment, query_segment = segment(key_index), segment(query_index)
    end = jnp.full(key_index.shape, PROMPT, jnp.int32)
    for slot in range(NCONT):
        end = jnp.where(
            key_segment == slot, PROMPT + slot * CONT + lengths_ref[chip, slot], end
        )
    alive = key_index < end
    return ahead_or_here & ((key_segment < 0) | ((key_segment == query_segment) & alive))


def token_dot(left, right):
    return lax.dot_general(
        left.reshape(-1, left.shape[-1]),
        right.reshape(-1, right.shape[-1]),
        (((0,), (0,)), ((), ())),
        preferred_element_type=jnp.float32,
    )


def exchange(value, axis):
    return lax.all_to_all(value, axis, split_axis=0, concat_axis=0, tiled=True)


def plane_device(
    activations,
    cotangent,
    continuation_lengths,
    query_weight,
    key_weight,
    value_weight,
    output_weight,
    gate_weight,
    up_weight,
    down_weight,
    attention_gain,
    feedforward_gain,
    moment_query,
    moment_key,
    moment_value,
    moment_output,
    moment_gate,
    moment_up,
    moment_down,
    moment_attention,
    moment_feedforward,
):
    devices, planes = lax.axis_size("dp"), lax.axis_size("fsdp")
    place, plane = lax.axis_index("dp"), lax.axis_index("fsdp")
    core = place % 2
    low = jnp.bfloat16
    kv_width = KV_HEADS * HEAD
    tokens = activations.shape[1]
    half = tokens // 2

    in_rows = query_weight.shape[0]
    sub_rows = in_rows // planes
    spread = devices * sub_rows

    mixed_kv = jnp.stack([key_weight.astype(low), value_weight.astype(low)], axis=1)
    block = jnp.concatenate([query_weight.astype(low).reshape(in_rows, 2, HEAD), mixed_kv], axis=2)
    head_block = block.reshape(planes, sub_rows, 2, 2 * HEAD).swapaxes(1, 2)

    strip = 128
    runs = gate_weight.shape[1] // (devices * strip)
    units = runs * strip * planes
    gate_up = jnp.stack(
        [
            gate_weight.astype(low).reshape(in_rows, runs, devices, strip),
            up_weight.astype(low).reshape(in_rows, runs, devices, strip),
        ]
    )
    gate_up = gate_up.transpose(3, 1, 0, 2, 4).reshape(devices, in_rows, 2 * runs * strip)
    down_columns = down_weight.shape[1]
    down = down_weight.astype(low).reshape(devices, strip, down_columns)

    gain_one, gain_two = attention_gain[None, :], feedforward_gain[None, :]
    length_block = jnp.zeros((8, 128), jnp.int32).at[:2, :NCONT].set(continuation_lengths)
    own_inputs, own_grads, rows_all, head_weight, head_output, feed_own, all_lengths = start_up(
        activations,
        cotangent,
        head_block,
        output_weight.astype(low),
        gate_up,
        down,
        length_block,
        gain_one,
    )

    first_core = place - core
    lengths = jnp.stack(
        [
            pick(pick(all_lengths, (first_core ^ mask) + plane // 2), plane % 2)[:NCONT]
            for mask in (0, SIDE_A, SIDE_B, SIDE_A + SIDE_B)
        ]
    )

    inside = jnp.concatenate(
        [core * half + jnp.arange(half), (1 - core) * half + jnp.arange(half)]
    ).astype(jnp.int32)
    order = (tokens * jnp.arange(CHUNKS, dtype=jnp.int32)[:, None] + inside[None, :]).reshape(-1)
    cosine, sine = rope_angles(token_places(order))
    cosine = cosine.reshape(2, 2, tokens, HEAD // 2)
    sine = sine.reshape(2, 2, tokens, HEAD // 2)
    place_q, place_k = inside[:, None], order[None, :]
    blocks = plane ^ jnp.arange(CHUNKS, dtype=jnp.int32)

    states, mixed, middle, normed_two, normed_late, grads_late, feed_weights = attend_and_norm(
        rows_all,
        own_grads,
        feed_own,
        head_weight,
        cosine,
        sine,
        lengths,
        (place_q, place_k),
        head_output,
        own_inputs,
        gain_two,
    )
    (
        grads_early,
        normed_early,
        branch_late,
        hidden,
        unit_grads,
        back_early,
        out_parts,
        middle_grad,
        gain_sum,
    ) = feed_forward(normed_two, normed_late, grads_late, feed_weights, middle, own_grads, gain_two, units)
    grads_all = (grads_early, grads_late)
    unit_sum = unit_weight_grads(unit_grads, (normed_early, normed_late))
    unit_sum = lax.psum_scatter(unit_sum, "fsdp", scatter_dimension=0, tiled=False)
    down_sum = reduce(jnp.add, [token_dot(hidden[pair], grads_all[pair]) for pair in (1, 0)]).astype(low)
    down_sum = down_sum.reshape(-1, planes, down_columns).transpose(1, 0, 2)
    down_sum = lax.psum_scatter(down_sum, "fsdp", scatter_dimension=0, tiled=False)
    head_grads, branch_early, output_groups, own_input_grad, gain_sums = attend_back(
        states,
        lengths,
        (place_q, place_k),
        head_output,
        head_weight,
        cosine,
        sine,
        branch_late,
        back_early,
        out_parts,
        middle,
        own_grads,
        own_inputs,
        middle_grad,
        (gain_one, gain_two),
    )

    head_sum = reduce(
        jnp.add, [token_dot(rows_all[pair], head_grads[pair]) for pair in (1, 0)]
    ).astype(low)
    branches = (branch_early, branch_late)
    output_sum = reduce(jnp.add, [token_dot(mixed[pair], branches[pair]) for pair in (1, 0)]).astype(low)
    outputs, input_grad, block, output_owned, units_owned, downs_owned, gain_totals, squares = finish(
        head_sum.reshape(devices, planes, sub_rows, 3 * HEAD),
        output_sum,
        unit_sum,
        down_sum.reshape(devices, strip, down_columns),
        output_groups,
        own_input_grad,
        jnp.stack([gain_sums[0], gain_sums[1] + gain_sum]),
    )
    block = block.swapaxes(1, 2).reshape(in_rows, 2, 2 * HEAD)
    query_owned = block[:, :, :HEAD].reshape(in_rows, 2 * HEAD)
    key_owned, value_owned = block[:, 0, HEAD:], block[:, 1, HEAD:]
    gate_up_owned = units_owned.reshape(devices, 2, runs, strip, in_rows).transpose(1, 4, 2, 0, 3)
    gate_up_owned = gate_up_owned.reshape(2, in_rows, runs * devices * strip)
    down_owned = downs_owned.reshape(devices * strip, down_columns)

    owner_grads = [
        owned.astype(jnp.float32)
        for owned in (
            query_owned,
            key_owned,
            value_owned,
            output_owned,
            gate_up_owned[0],
            gate_up_owned[1],
            down_owned,
        )
    ]
    attention_total, feedforward_total = gain_totals[0], gain_totals[1]
    square_total = squares[0, 0]
    square_sum = (
        square_total
        + jnp.sum(attention_total * attention_total)
        + jnp.sum(feedforward_total * feedforward_total)
    )
    grad_norm = jnp.sqrt(square_sum)
    entry_count = 2 * D * D + 2 * D * kv_width + 3 * D * FF + 2 * D
    limit = clip_level * math.sqrt(entry_count)
    factor = limit / jnp.maximum(grad_norm, limit)
    gradients = owner_grads + [attention_total, feedforward_total]
    old_moments = [
        moment_query,
        moment_key,
        moment_value,
        moment_output,
        moment_gate,
        moment_up,
        moment_down,
        moment_attention,
        moment_feedforward,
    ]
    old_params = [
        query_weight,
        key_weight,
        value_weight,
        output_weight,
        gate_weight,
        up_weight,
        down_weight,
        attention_gain,
        feedforward_gain,
    ]
    new_moments = [
        0.5 * moment + 0.5 * factor * gradient for moment, gradient in zip(old_moments, gradients)
    ]
    new_params = []
    for at, param in enumerate(old_params):
        if at < 7:
            new_params.append(param - step_size * (new_moments[at] + decay_rate * param))
        else:
            new_params.append(param - gain_step * new_moments[at])
    return (outputs, input_grad, grad_norm, *new_moments, *new_params)


def solution(mesh):
    whole_groups_on_planes = mesh.shape["dp"] == HEADS and mesh.shape["fsdp"] == KV_HEADS
    body = plane_device if whole_groups_on_planes else on_device
    placed = (
        P("dp", "fsdp", None),
        P("dp", "fsdp", None),
        P("dp", None),
        P("dp", "fsdp"),
        P("dp", "fsdp"),
        P("dp", "fsdp"),
        P("dp", "fsdp"),
        P("dp", "fsdp"),
        P("dp", "fsdp"),
        P("dp", "fsdp"),
        P(),
        P(),
        P("dp", "fsdp"),
        P("dp", "fsdp"),
        P("dp", "fsdp"),
        P("dp", "fsdp"),
        P("dp", "fsdp"),
        P("dp", "fsdp"),
        P("dp", "fsdp"),
        P(),
        P(),
    )
    return jax.shard_map(
        body,
        mesh=mesh,
        in_specs=placed,
        out_specs=(
            P("dp", "fsdp", None),
            P("dp", "fsdp", None),
            P(),
            P("dp", "fsdp"),
            P("dp", "fsdp"),
            P("dp", "fsdp"),
            P("dp", "fsdp"),
            P("dp", "fsdp"),
            P("dp", "fsdp"),
            P("dp", "fsdp"),
            P(),
            P(),
            P("dp", "fsdp"),
            P("dp", "fsdp"),
            P("dp", "fsdp"),
            P("dp", "fsdp"),
            P("dp", "fsdp"),
            P("dp", "fsdp"),
            P("dp", "fsdp"),
            P(),
            P(),
        ),
        check_vma=False,
    )
```

```python
import functools
from functools import reduce
import math

import jax
import jax.numpy as jnp
from jax import lax
from jax.experimental import pallas as pl
from jax.experimental.pallas import tpu as pltpu
from jax.sharding import PartitionSpec as P

D = 2048
HEADS = 8
KV_HEADS = 4
HEAD = 256
FF = 8192
PROMPT = 1024
CONT = 64
NCONT = 2


epsilon = 1e-06
rope_base = 1000042.0
step_size = 0.2
gain_step = 4.0
decay_rate = 0.1
clip_level = 0.25
floor_score = -1e30


def rms_rows(values, gain):
    factor = lax.rsqrt(jnp.mean(values * values, axis=-1, keepdims=True) + epsilon)
    return (values * factor * gain, factor)


def rms_back(values, factor, gain, gradient):
    scaled = values * factor
    gain_grad = jnp.sum(gradient * scaled, axis=0)
    pulled = gradient * gain
    return (
        factor * (pulled - scaled * jnp.mean(pulled * scaled, axis=-1, keepdims=True)),
        gain_grad,
    )


def rope_angles(places):
    halfway = HEAD // 2
    freqs = rope_base ** (-(jnp.arange(halfway).astype(jnp.float32) * 2.0 / HEAD))
    angles = places.astype(jnp.float32)[:, None] * freqs[None, :]
    return (jnp.cos(angles), jnp.sin(angles))


def token_places(index):
    inside = index - PROMPT
    return jnp.where(index < PROMPT, index, PROMPT + inside % CONT)


def segment_of(index):
    return jnp.where(index < PROMPT, -1, (index - PROMPT) // CONT)


def visible(query_index, key_index, lengths):
    key_segment = segment_of(key_index)
    key_offset = key_index - PROMPT - key_segment * CONT
    slots = jnp.arange(NCONT, dtype=jnp.int32)
    limits = jnp.sum(jnp.where(key_segment[:, None] == slots[None, :], lengths[None, :], 0), axis=1)
    alive = key_offset < limits
    same = segment_of(query_index)[:, None] == key_segment[None, :]
    causal = key_index[None, :] <= query_index[:, None]
    return causal & ((key_index < PROMPT)[None, :] | same & alive[None, :])


def rotate(values, cosine, sine):
    halfway = values.shape[-1] // 2
    first, second = (values[..., :halfway], values[..., halfway:])
    cosine, sine = (cosine[:, None, :], sine[:, None, :])
    return jnp.concatenate(
        [first * cosine - second * sine, second * cosine + first * sine], axis=-1
    )


def rotate_back(grads, cosine, sine):
    halfway = grads.shape[-1] // 2
    first, second = (grads[..., :halfway], grads[..., halfway:])
    cosine, sine = (cosine[:, None, :], sine[:, None, :])
    return jnp.concatenate(
        [first * cosine + second * sine, second * cosine - first * sine], axis=-1
    )


def join_blocks(pieces, shard_count):
    height = pieces[0].shape[0]
    return jnp.concatenate(
        [member.reshape(height, shard_count, -1) for member in pieces], axis=2
    ).reshape(height, -1)


def split_blocks(merged, breadths, shard_count):
    height = merged.shape[0]
    blocks = merged.reshape(height, shard_count, -1)
    result = []
    offset = 0
    for breadth in breadths:
        result.append(
            blocks[:, :, offset : offset + breadth].reshape(height, shard_count * breadth)
        )
        offset = offset + breadth
    return result


def ahead(operand, shard):
    return jnp.dot(
        operand,
        lax.all_gather(shard, "fsdp", axis=1, tiled=True),
        preferred_element_type=jnp.float32,
    )


def behind(gradient, shard):
    return lax.dot_general(
        gradient,
        lax.all_gather(shard, "fsdp", axis=1, tiled=True),
        (((1,), (1,)), ((), ())),
        preferred_element_type=jnp.float32,
    )


def weight_term(gradient, operand):
    operand_all = lax.all_gather(operand, "fsdp", axis=0, tiled=True)
    owned_columns = lax.all_to_all(gradient, "fsdp", split_axis=1, concat_axis=0, tiled=True)
    return lax.dot_general(
        owned_columns, operand_all, (((0,), (0,)), ((), ())), preferred_element_type=jnp.float32
    )


def on_device(
    activations,
    cotangent,
    continuation_lengths,
    query_weight,
    key_weight,
    value_weight,
    output_weight,
    gate_weight,
    up_weight,
    down_weight,
    attention_gain,
    feedforward_gain,
    moment_query,
    moment_key,
    moment_value,
    moment_output,
    moment_gate,
    moment_up,
    moment_down,
    moment_attention,
    moment_feedforward,
):
    shard_count = lax.axis_size("fsdp")
    kv_width = KV_HEADS * HEAD
    repeat = HEADS // KV_HEADS
    scale = 1.0 / math.sqrt(HEAD)
    gathered = (
        lax.all_gather(query_weight.astype(jnp.bfloat16), "dp", axis=0, tiled=True),
        lax.all_gather(key_weight.astype(jnp.bfloat16), "dp", axis=0, tiled=True),
        lax.all_gather(value_weight.astype(jnp.bfloat16), "dp", axis=0, tiled=True),
        lax.all_gather(output_weight.astype(jnp.bfloat16), "dp", axis=0, tiled=True),
        lax.all_gather(gate_weight.astype(jnp.bfloat16), "dp", axis=0, tiled=True),
        lax.all_gather(up_weight.astype(jnp.bfloat16), "dp", axis=0, tiled=True),
        lax.all_gather(down_weight.astype(jnp.bfloat16), "dp", axis=0, tiled=True),
    )
    merged_attn = join_blocks(gathered[0:3], 1)
    merged_output = gathered[3]
    merged_ffn = join_blocks(gathered[4:6], 1)
    merged_down = gathered[6]
    query_cols = D // shard_count
    key_cols = kv_width // shard_count
    ffn_cols = FF // shard_count
    attn_breadths = (query_cols, key_cols, key_cols)
    ffn_breadths = (ffn_cols, ffn_cols)
    local_rows = activations.shape[1]
    group_rows = local_rows * shard_count
    query_index = lax.axis_index("fsdp") * local_rows + jnp.arange(local_rows, dtype=jnp.int32)
    key_index = jnp.arange(group_rows, dtype=jnp.int32)
    cosine, sine = rope_angles(token_places(query_index))
    sums = [jnp.zeros((matrix.shape[1], matrix.shape[0]), jnp.float32) for matrix in gathered]
    attention_sum = jnp.zeros((D,), jnp.float32)
    feedforward_sum = jnp.zeros((D,), jnp.float32)
    output_list = []
    input_list = []
    for micro_batch in range(activations.shape[0]):
        allowed = visible(query_index, key_index, continuation_lengths[micro_batch])
        inputs = activations[micro_batch].astype(jnp.float32)
        normed_float, factor_one = rms_rows(inputs, attention_gain)
        normed = normed_float.astype(jnp.bfloat16)
        pre_query, pre_key, pre_value = split_blocks(
            ahead(normed, merged_attn), attn_breadths, shard_count
        )
        queries = (
            rotate(pre_query.reshape(local_rows, HEADS, HEAD), cosine, sine)
            .astype(jnp.bfloat16)
            .reshape(local_rows, KV_HEADS, repeat, HEAD)
        )
        keys = rotate(pre_key.reshape(local_rows, KV_HEADS, HEAD), cosine, sine).astype(
            jnp.bfloat16
        )
        values = pre_value.astype(jnp.bfloat16).reshape(local_rows, KV_HEADS, HEAD)
        keys_all, values_all = (
            lax.all_gather(keys, "fsdp", axis=0, tiled=True),
            lax.all_gather(values, "fsdp", axis=0, tiled=True),
        )
        raw = (
            jnp.einsum("qgrd,kgd->grqk", queries, keys_all, preferred_element_type=jnp.float32)
            * scale
        )
        raw = jnp.where(allowed[None, None], raw, floor_score)
        highest = jnp.max(raw, axis=-1, keepdims=True)
        exponent = jnp.exp(raw - highest)
        denominator = jnp.sum(exponent, axis=-1, keepdims=True)
        logsum = highest + jnp.log(denominator)
        probs_low = (exponent / denominator).astype(jnp.bfloat16)
        mixed = (
            jnp.einsum("grqk,kgd->qgrd", probs_low, values_all, preferred_element_type=jnp.float32)
            .reshape(local_rows, D)
            .astype(jnp.bfloat16)
        )
        middle = inputs + ahead(mixed, merged_output)
        normed_two_float, factor_two = rms_rows(middle, feedforward_gain)
        normed_two = normed_two_float.astype(jnp.bfloat16)
        gate, upward = split_blocks(ahead(normed_two, merged_ffn), ffn_breadths, shard_count)
        sigmoid = jax.nn.sigmoid(gate)
        swish = gate * sigmoid
        hidden = (swish * upward).astype(jnp.bfloat16)
        result = middle + ahead(hidden, merged_down)
        output_list.append(result.astype(jnp.bfloat16))
        out_grad = cotangent[micro_batch]
        hidden_grad = behind(out_grad, merged_down)
        sums[6] = sums[6] + weight_term(out_grad, hidden)
        gate_grad = (hidden_grad * upward * sigmoid * (1.0 + gate * (1.0 - sigmoid))).astype(
            jnp.bfloat16
        )
        up_grad = (hidden_grad * swish).astype(jnp.bfloat16)
        ffn_grad = join_blocks((gate_grad, up_grad), shard_count)
        ffn_term = weight_term(ffn_grad, normed_two)
        sums[4] = sums[4] + ffn_term[:ffn_cols]
        sums[5] = sums[5] + ffn_term[ffn_cols:]
        normed_two_grad = behind(ffn_grad, merged_ffn)
        middle_back, feed_gain_grad = rms_back(
            middle, factor_two, feedforward_gain, normed_two_grad
        )
        middle_grad = out_grad.astype(jnp.float32) + middle_back
        branch_grad = middle_grad.astype(jnp.bfloat16)
        sums[3] = sums[3] + weight_term(branch_grad, mixed)
        mixed_grad = (
            behind(branch_grad, merged_output)
            .astype(jnp.bfloat16)
            .reshape(local_rows, KV_HEADS, repeat, HEAD)
        )
        raw_again = (
            jnp.einsum("qgrd,kgd->grqk", queries, keys_all, preferred_element_type=jnp.float32)
            * scale
        )
        raw_again = jnp.where(allowed[None, None], raw_again, floor_score)
        probs_again = jnp.exp(raw_again - logsum)
        value_part = jnp.einsum(
            "grqk,qgrd->kgd",
            probs_again.astype(jnp.bfloat16),
            mixed_grad,
            preferred_element_type=jnp.float32,
        )
        prob_grad = jnp.einsum(
            "qgrd,kgd->grqk", mixed_grad, values_all, preferred_element_type=jnp.float32
        )
        inner = jnp.sum(probs_again * prob_grad, axis=-1, keepdims=True)
        score_grad = (probs_again * (prob_grad - inner)).astype(jnp.bfloat16)
        query_grad = (
            jnp.einsum("grqk,kgd->qgrd", score_grad, keys_all, preferred_element_type=jnp.float32)
            * scale
        )
        key_part = (
            jnp.einsum("grqk,qgrd->kgd", score_grad, queries, preferred_element_type=jnp.float32)
            * scale
        )
        key_grad, value_grad = (
            lax.psum_scatter(
                key_part.astype(jnp.bfloat16), "fsdp", scatter_dimension=0, tiled=True
            ).astype(jnp.float32),
            lax.psum_scatter(
                value_part.astype(jnp.bfloat16), "fsdp", scatter_dimension=0, tiled=True
            ).astype(jnp.float32),
        )
        pre_query_grad = (
            rotate_back(query_grad.reshape(local_rows, HEADS, HEAD), cosine, sine)
            .reshape(local_rows, D)
            .astype(jnp.bfloat16)
        )
        pre_key_grad = (
            rotate_back(key_grad, cosine, sine).reshape(local_rows, kv_width).astype(jnp.bfloat16)
        )
        pre_value_grad = value_grad.reshape(local_rows, kv_width).astype(jnp.bfloat16)
        attn_grad = join_blocks((pre_query_grad, pre_key_grad, pre_value_grad), shard_count)
        attn_term = weight_term(attn_grad, normed)
        sums[0] = sums[0] + attn_term[:query_cols]
        sums[1] = sums[1] + attn_term[query_cols : query_cols + key_cols]
        sums[2] = sums[2] + attn_term[query_cols + key_cols :]
        normed_grad = behind(attn_grad, merged_attn)
        input_back, attn_gain_grad = rms_back(inputs, factor_one, attention_gain, normed_grad)
        input_list.append((middle_grad + input_back).astype(jnp.bfloat16))
        attention_sum = attention_sum + attn_gain_grad
        feedforward_sum = feedforward_sum + feed_gain_grad
    reduced = (
        lax.psum_scatter(
            sums[0].astype(jnp.bfloat16), "dp", scatter_dimension=1, tiled=True
        ).astype(jnp.float32),
        lax.psum_scatter(
            sums[1].astype(jnp.bfloat16), "dp", scatter_dimension=1, tiled=True
        ).astype(jnp.float32),
        lax.psum_scatter(
            sums[2].astype(jnp.bfloat16), "dp", scatter_dimension=1, tiled=True
        ).astype(jnp.float32),
        lax.psum_scatter(
            sums[3].astype(jnp.bfloat16), "dp", scatter_dimension=1, tiled=True
        ).astype(jnp.float32),
        lax.psum_scatter(
            sums[4].astype(jnp.bfloat16), "dp", scatter_dimension=1, tiled=True
        ).astype(jnp.float32),
        lax.psum_scatter(
            sums[5].astype(jnp.bfloat16), "dp", scatter_dimension=1, tiled=True
        ).astype(jnp.float32),
        lax.psum_scatter(
            sums[6].astype(jnp.bfloat16), "dp", scatter_dimension=1, tiled=True
        ).astype(jnp.float32),
    )
    owner_grads = [owned.T for owned in reduced]
    local_square = reduce(jnp.add, [jnp.sum(owned * owned) for owned in owner_grads])
    attention_total, feedforward_total, square_total = lax.psum(
        (attention_sum, feedforward_sum, local_square), ("dp", "fsdp")
    )
    square_sum = (
        square_total
        + jnp.sum(attention_total * attention_total)
        + jnp.sum(feedforward_total * feedforward_total)
    )
    grad_norm = jnp.sqrt(square_sum)
    entry_count = 2 * D * D + 2 * D * kv_width + 3 * D * FF + 2 * D
    limit = clip_level * math.sqrt(entry_count)
    factor = limit / jnp.maximum(grad_norm, limit)
    gradients = owner_grads + [attention_total, feedforward_total]
    old_moments = [
        moment_query,
        moment_key,
        moment_value,
        moment_output,
        moment_gate,
        moment_up,
        moment_down,
        moment_attention,
        moment_feedforward,
    ]
    old_params = [
        query_weight,
        key_weight,
        value_weight,
        output_weight,
        gate_weight,
        up_weight,
        down_weight,
        attention_gain,
        feedforward_gain,
    ]
    new_moments = [
        0.5 * moment + 0.5 * factor * gradient for moment, gradient in zip(old_moments, gradients)
    ]
    new_params = []
    for place, param in enumerate(old_params):
        if place < 7:
            new_params.append(param - step_size * (new_moments[place] + decay_rate * param))
        else:
            new_params.append(param - gain_step * new_moments[place])
    outputs = jnp.stack(output_list)
    input_grad = jnp.stack(input_list)
    return (
        outputs,
        input_grad,
        grad_norm,
        new_moments[0],
        new_moments[1],
        new_moments[2],
        new_moments[3],
        new_moments[4],
        new_moments[5],
        new_moments[6],
        new_moments[7],
        new_moments[8],
        new_params[0],
        new_params[1],
        new_params[2],
        new_params[3],
        new_params[4],
        new_params[5],
        new_params[6],
        new_params[7],
        new_params[8],
    )


CORE, SIDE_A, SIDE_B = 1, 2, 4
CHIPS = 4
CHUNKS = 4
MB = 1024 * 1024


def across(value, mask):
    count = lax.axis_size("dp")
    return lax.ppermute(value, "dp", [(place, place ^ mask) for place in range(count)])


def along(value, mask):
    count = lax.axis_size("fsdp")
    return lax.ppermute(value, "fsdp", [(place, place ^ mask) for place in range(count)])


def pick(values, index):
    return lax.dynamic_index_in_dim(values, index, 0, keepdims=False)


def after(value, *earlier):
    return lax.optimization_barrier((value, earlier))[0]


def trade_planes(parts, plane):
    found = [pick(parts, plane)]
    for mask in range(1, CHUNKS):
        found.append(along(pick(parts, plane ^ mask), mask))
    found = jnp.stack(found)
    return [pick(found, label ^ plane) for label in range(CHUNKS)]


def gather_planes(block):
    one, two = along(block, 1), along(block, 2)
    return [block, one, two, along(two, 1)]


def sum_planes(parts):
    two = (parts[2].astype(jnp.float32) + along(parts[3], 1).astype(jnp.float32)).astype(jnp.bfloat16)
    return (
        parts[0].astype(jnp.float32)
        + along(parts[1], 1).astype(jnp.float32)
        + along(two, 2).astype(jnp.float32)
    )


def sum_all(value):
    for mask in (CORE, SIDE_A, SIDE_B):
        value = value + across(value, mask)
    for mask in (1, 2):
        value = value + along(value, mask)
    return value


def to_planes(array, core, plane):
    halves = array.reshape(2, 2, array.shape[1] // 2, array.shape[2]).swapaxes(0, 1)
    keep = pick(halves, core)
    came = across(pick(halves, 1 - core), CORE)
    swap = core == 1
    parts = jnp.concatenate([jnp.where(swap, came, keep), jnp.where(swap, keep, came)])
    return trade_planes(parts, plane)


def from_planes(chunks, core, plane):
    groups = trade_planes(jnp.stack(chunks), plane)
    pairs = jnp.stack([jnp.stack(groups[:2]), jnp.stack(groups[2:])])
    keep = pick(pairs, core)
    came = across(pick(pairs, 1 - core), CORE)
    swap = core == 1
    return jnp.concatenate([jnp.where(swap, came, keep), jnp.where(swap, keep, came)], axis=1)


MESH = pl.DeviceIdType.MESH
SLOT = {0: 0, SIDE_A: 1, SIDE_B: 2}
ROUTES = ((SIDE_A, SIDE_B), (SIDE_B, SIDE_A))
STRIPE = 16


def flip(place, mask):
    for bit in (1, 2, 4):
        if mask & bit:
            place = place + bit - 2 * bit * lax.rem(lax.div(place, bit), 2)
    return place


def peer(mask, planes=0):
    return (flip(lax.axis_index("dp"), mask), flip(lax.axis_index("fsdp"), planes))


SIDES = ((CORE, 0), (SIDE_A, 0), (SIDE_B, 0))
PLANE = tuple((mask, 0) for mask in range(1, 8))
PLANES = tuple((0, mask) for mask in range(1, CHUNKS))


def meet(others):
    barrier = pltpu.get_barrier_semaphore()
    for mask, planes in others:
        pl.semaphore_signal(barrier, inc=1, device_id=peer(mask, planes), device_id_type=MESH)
    pl.semaphore_wait(barrier, len(others))


class Remote:
    def __init__(self, wires, source, target, mask, planes=0):
        self.wires, self.source, self.target, self.mask = wires, source, target, (mask, planes)
        self.place = wires.count
        wires.count += 1

    def make(self):
        return pltpu.make_async_remote_copy(
            src_ref=self.source,
            dst_ref=self.target,
            send_sem=self.wires.send.at[self.place],
            recv_sem=self.wires.recv.at[self.place],
            device_id=peer(*self.mask),
            device_id_type=MESH,
        )

    def start(self):
        self.make().start()

    def arrived(self):
        self.make().wait_recv()

    def left(self):
        self.make().wait_send()


class Wires:
    def __init__(self, send, recv, local):
        self.send, self.recv, self.local = send, recv, local
        self.count = 0
        self.local_count = 0

    def load(self, pairs):
        copies = [
            pltpu.make_async_copy(source, target, self.local.at[place])
            for place, (source, target) in enumerate(pairs)
        ]
        for copy in copies:
            copy.start()
        for copy in copies:
            copy.wait()


class Gather:
    def __init__(self, wires, own, target):
        rows = target.shape[2] // 2
        self.wires, self.own = wires, own
        self.near, self.far, self.core_first, self.core_near, self.core_far = [], [], [], [], []
        self.home = []

        def place(chunk, slot, half):
            return target.at[chunk, slot, pl.ds(half * rows, rows)]

        for chunk, (first, second) in enumerate(ROUTES):
            near, far = SLOT[first], SLOT[second]
            self.home.append((own[chunk], place(chunk, 0, 0)))
            self.near.append(Remote(wires, own[chunk], place(chunk, near, 0), first))
            self.core_first.append(Remote(wires, own[chunk], place(chunk, 0, 1), CORE))
            self.far.append(Remote(wires, own[chunk], place(chunk, far, 0), second))
            self.far.append(Remote(wires, place(chunk, near, 0), place(chunk, 3, 0), second))
            self.core_near.append(Remote(wires, place(chunk, near, 0), place(chunk, near, 1), CORE))
            self.core_far.append(Remote(wires, place(chunk, far, 0), place(chunk, far, 1), CORE))
            self.core_far.append(Remote(wires, place(chunk, 3, 0), place(chunk, 3, 1), CORE))

    def first(self):
        for copy in self.near + self.core_first:
            copy.start()
        self.wires.load(self.home)

    def second(self):
        for chunk, copy in enumerate(self.near):
            copy.arrived()
            self.far[2 * chunk].start()
            self.far[2 * chunk + 1].start()
            self.core_near[chunk].start()

    def third(self):
        for place, copy in enumerate(self.far):
            copy.arrived()
            self.core_far[place].start()

    def last(self):
        for copy in self.core_first + self.core_near + self.core_far:
            copy.arrived()
        for copy in self.near + self.far + self.core_first + self.core_near + self.core_far:
            copy.left()

    def steps(self):
        return [self.first, self.second, self.third, self.last]


class Scatter:
    def __init__(self, wires, own, other, landing, stage, done):
        from_core, from_far, from_near = landing
        self.wires, self.own, self.landing, self.stage, self.done = wires, own, landing, stage, done
        self.core = [Remote(wires, other.at[chunk], from_core.at[chunk], CORE) for chunk in range(2)]
        self.far = [
            Remote(wires, stage[0].at[chunk], from_far.at[chunk], first)
            for chunk, (_, first) in enumerate(ROUTES)
        ]
        self.near = [
            Remote(wires, stage[2].at[chunk, 0], from_near.at[chunk], last)
            for chunk, (last, _) in enumerate(ROUTES)
        ]

    def first(self):
        for copy in self.core:
            copy.start()

    def second(self):
        left, right = self.stage[:2]
        pairs = []
        for chunk, (_, first) in enumerate(ROUTES):
            self.core[chunk].arrived()
            for place, slot in enumerate((SLOT[first], 3)):
                pairs.append((self.own.at[chunk, slot], left.at[chunk, place]))
                pairs.append((self.landing[0].at[chunk, slot], right.at[chunk, place]))
        self.wires.load(pairs)
        for chunk in range(2):

            @pl.loop(0, left.shape[2] // STRIPE)
            def _(step):
                span = pl.ds(step * STRIPE, STRIPE)
                total = left[chunk, :, span].astype(jnp.float32) + right[chunk, :, span].astype(jnp.float32)
                left[chunk, :, span] = total.astype(jnp.bfloat16)

            self.far[chunk].start()

    def third(self):
        stage = self.stage[2]
        pairs = []
        for chunk, (last, _) in enumerate(ROUTES):
            self.far[chunk].arrived()
            pairs.append((self.own.at[chunk, SLOT[last]], stage.at[chunk, 0]))
            pairs.append((self.landing[0].at[chunk, SLOT[last]], stage.at[chunk, 1]))
            pairs.append((self.landing[1].at[chunk, 1], stage.at[chunk, 2]))
        self.wires.load(pairs)
        for chunk in range(2):

            @pl.loop(0, stage.shape[2] // STRIPE)
            def _(step):
                span = pl.ds(step * STRIPE, STRIPE)
                total = stage[chunk, 0, span].astype(jnp.float32)
                for place in range(1, 3):
                    total += stage[chunk, place, span].astype(jnp.float32)
                stage[chunk, 0, span] = total.astype(jnp.bfloat16)

            self.near[chunk].start()
        for copy in self.far:
            copy.left()

    def last(self):
        stage = self.stage[3]
        for chunk in range(2):
            self.near[chunk].arrived()
            self.wires.load(
                [
                    (self.own.at[chunk, 0], stage.at[0]),
                    (self.landing[0].at[chunk, 0], stage.at[1]),
                    (self.landing[1].at[chunk, 0], stage.at[2]),
                    (self.landing[2].at[chunk], stage.at[3]),
                ]
            )

            @pl.loop(0, stage.shape[1] // STRIPE)
            def _(step):
                span = pl.ds(step * STRIPE, STRIPE)
                total = stage[0, span].astype(jnp.float32)
                for place in range(1, 4):
                    total += stage[place, span].astype(jnp.float32)
                self.done(chunk, span, total)

        for copy in self.near + self.core:
            copy.left()

    def steps(self):
        return [self.first, self.second, self.third, self.last]


def stage_shapes(rows, width):
    return [
        pltpu.VMEM((2, 2, rows, width), jnp.bfloat16),
        pltpu.VMEM((2, 2, rows, width), jnp.bfloat16),
        pltpu.VMEM((2, 3, rows, width), jnp.bfloat16),
        pltpu.VMEM((4, rows, width), jnp.bfloat16),
    ]


def landing_shapes(rows, width):
    return [
        jax.ShapeDtypeStruct((2, CHIPS, rows, width), jnp.bfloat16),
        jax.ShapeDtypeStruct((2, 2, rows, width), jnp.bfloat16),
        jax.ShapeDtypeStruct((2, rows, width), jnp.bfloat16),
    ]


def partial_shapes(rows, width):
    return [jax.ShapeDtypeStruct((2, CHIPS, rows, width), jnp.bfloat16)] * 2


def wire_shapes(count):
    return [
        pltpu.SemaphoreType.DMA((count,)),
        pltpu.SemaphoreType.DMA((count,)),
        pltpu.SemaphoreType.DMA((8,)),
    ]


def call(kernel, identity, inputs, outputs, scratch, megabytes):
    return pl.pallas_call(
        kernel,
        in_specs=[pl.BlockSpec(memory_space=place) for _, place in inputs],
        out_specs=[pl.BlockSpec(memory_space=place) for _, place in outputs],
        out_shape=[shape for shape, _ in outputs],
        scratch_shapes=scratch,
        compiler_params=pltpu.CompilerParams(
            collective_id=identity, has_side_effects=True, vmem_limit_bytes=megabytes * MB
        ),
    )(*[array for array, _ in inputs])


HBM, VMEM, SMEM = pl.ANY, pltpu.VMEM, pltpu.SMEM


def move_rows(source, target):
    @pl.loop(0, source.shape[0] // STRIPE)
    def _(step):
        span = pl.ds(step * STRIPE, STRIPE)
        target[span] = source[span]


def half_rows(index, rows):
    return pl.ds(pl.multiple_of(index * rows, STRIPE), rows)


def columns_of(index, columns):
    return pl.ds(pl.multiple_of(index * columns, columns), columns)


def at_step(step, actions):
    for when, action in actions.items():
        pl.when(step == when)(action)


def project_phase(gathered, states, weight_ref, cosine, sine, actions):
    tokens = gathered.shape[2]

    def body(rows_ref, cosine_ref, sine_ref, out):
        at_step(pl.program_id(0) * CHIPS + pl.program_id(1), actions)
        product = dot(rows_ref[0, 0], weight_ref[...].reshape(D, 3 * HEAD))
        angles = (cosine_ref[0], sine_ref[0])
        query = spin(product[:, :HEAD], *angles) * (1.0 / math.sqrt(HEAD))
        key = spin(product[:, HEAD : 2 * HEAD], *angles)
        out[0, 0] = jnp.concatenate([query, key, product[:, 2 * HEAD :]], axis=1).astype(jnp.bfloat16)

    here = lambda chunk, chip: (chunk, chip, 0, 0)
    table = pl.BlockSpec((1, tokens, HEAD // 2), lambda chunk, chip: (chunk, 0, 0))
    pltpu.emit_pipeline(
        body,
        grid=(2, CHIPS),
        in_specs=[pl.BlockSpec((1, 1, tokens, gathered.shape[3]), here), table, table],
        out_specs=[pl.BlockSpec((1, 1, tokens, 3 * HEAD), here)],
    )(gathered, cosine, sine, states)


def attend_phase(pair, states, mixed, own, other, lengths_ref, places, weight_ref, keys, values, actions):
    tokens, rows, width = mixed.shape[2], own.shape[2], own.shape[3]
    blocks = 2 * (pair + 1)

    def body(*refs):
        state_refs, (mixed_ref, own_ref, other_ref) = refs[: pair + 1], refs[pair + 1 :]
        chip, side_at = pl.program_id(0), pl.program_id(1)
        at_step(2 * chip + side_at, actions)

        @pl.when(side_at == 0)
        def _():
            for block in range(blocks):
                ref = state_refs[block // 2]
                keys[pl.ds(block * tokens, tokens)] = ref[block % 2, 0, :, HEAD : 2 * HEAD]
                values[pl.ds(block * tokens, tokens)] = ref[block % 2, 0, :, 2 * HEAD :]

        for side in range(2):

            @pl.when(side_at == side)
            def _():
                chunk = 2 * pair + side
                count = tokens * (chunk + 1)
                scores = dot_t(state_refs[pair][side, 0, :, :HEAD], keys[:count])
                mask = seen(places[0][...], places[1][...], chunk, count, tokens, lengths_ref, chip)
                scores = jnp.where(mask, scores, floor_score)
                highest = jnp.max(scores, axis=1, keepdims=True)
                exponent = jnp.exp(scores - highest)
                total = jnp.sum(exponent, axis=1, keepdims=True)
                probs = (exponent * (1.0 / total)).astype(jnp.bfloat16)
                mixed_ref[0, 0] = dot(probs, values[:count]).astype(jnp.bfloat16)

        partial = dot(mixed_ref[0, 0], weight_ref[...]).astype(jnp.bfloat16)
        own_ref[0, 0] = partial[:rows]
        other_ref[0, 0] = partial[rows:]

    here = lambda chip, side: (side, chip, 0, 0)
    state = pl.BlockSpec((2, 1, tokens, 3 * HEAD), lambda chip, side: (0, chip, 0, 0))
    pltpu.emit_pipeline(
        body,
        grid=(CHIPS, 2),
        in_specs=[state] * (pair + 1),
        out_specs=[pl.BlockSpec((1, 1, tokens, HEAD), here)] + [pl.BlockSpec((1, 1, rows, width), here)] * 2,
    )(*states[: pair + 1], mixed, own, other)


def attend_back_phase(
    pair, branch, states, head_grads, own, other, lengths_ref, places, out_weight, weight_ref,
    tables, keys, values, sums, late_sums, actions
):
    tokens, rows, width = branch.shape[2], own.shape[2], own.shape[3]
    blocks = 2 * (pair + 1)
    edge = 2 * tokens

    def body(*refs):
        branch_ref, state_refs = refs[0], refs[1 : pair + 2]
        cosine_ref, sine_ref, grads_ref, own_ref, other_ref = refs[pair + 2 :]
        chip, step = pl.program_id(0), pl.program_id(1)
        at_step(2 * chip + step, actions)

        @pl.when(step == 0)
        def _():
            for block in range(blocks):
                ref = state_refs[block // 2]
                keys[pl.ds(block * tokens, tokens)] = ref[block % 2, 0, :, HEAD : 2 * HEAD]
                values[pl.ds(block * tokens, tokens)] = ref[block % 2, 0, :, 2 * HEAD :]
            if pair == 1:
                for place in range(2):
                    sums[place][chip] = jnp.zeros(sums[place].shape[1:], jnp.float32)
                    late_sums[place][...] = jnp.zeros(late_sums[place].shape, jnp.float32)

        def add(place, term):
            early = min(term.shape[0], edge)
            sums[place][chip, :early] += term[:early]
            if term.shape[0] > edge:
                late_sums[place][: term.shape[0] - edge] += term[edge:]

        for side in range(2):

            @pl.when(step == 1 - side)
            def _():
                chunk = 2 * pair + side
                count = tokens * (chunk + 1)
                mixed_grad = dot_t(branch_ref[0, 0], out_weight[...]).astype(jnp.bfloat16)
                query = state_refs[pair][side, 0, :, :HEAD]
                scores = dot_t(query, keys[:count])
                mask = seen(places[0][...], places[1][...], chunk, count, tokens, lengths_ref, chip)
                scores = jnp.where(mask, scores, floor_score)
                highest = jnp.max(scores, axis=1, keepdims=True)
                exponent = jnp.exp(scores - highest)
                probs = exponent * (1.0 / jnp.sum(exponent, axis=1, keepdims=True))
                add(1, dot_tn(probs.astype(jnp.bfloat16), mixed_grad))
                prob_grad = dot_t(mixed_grad, values[:count])
                inner = jnp.sum(probs * prob_grad, axis=1, keepdims=True)
                score_grad = (probs * (prob_grad - inner)).astype(jnp.bfloat16)
                add(0, dot_tn(score_grad, query))
                query_grad = dot(score_grad, keys[:count]) * (1.0 / math.sqrt(HEAD))
                angles = (cosine_ref[0], sine_ref[0])
                span = slice(side * tokens, (side + 1) * tokens)
                if pair == 1:
                    key_grad, value_grad = late_sums[0][span], late_sums[1][span]
                else:
                    key_grad, value_grad = sums[0][chip, span], sums[1][chip, span]
                grads_ref[0, 0] = jnp.concatenate(
                    [spin_back(query_grad, *angles), spin_back(key_grad, *angles), value_grad], axis=1
                ).astype(jnp.bfloat16)

        partial = dot_t(grads_ref[0, 0], weight_ref[...].reshape(D, 3 * HEAD)).astype(jnp.bfloat16)
        own_ref[0, 0] = partial[:rows]
        other_ref[0, 0] = partial[rows:]

    here = lambda chip, step: (1 - step, chip, 0, 0)
    state = pl.BlockSpec((2, 1, tokens, 3 * HEAD), lambda chip, step: (0, chip, 0, 0))
    table = pl.BlockSpec((1, tokens, HEAD // 2), lambda chip, step: (1 - step, 0, 0))
    pltpu.emit_pipeline(
        body,
        grid=(CHIPS, 2),
        in_specs=[pl.BlockSpec((1, 1, tokens, width), here)] + [state] * (pair + 1) + [table] * 2,
        out_specs=[pl.BlockSpec((1, 1, tokens, 3 * HEAD), here)]
        + [pl.BlockSpec((1, 1, rows, width), here)] * 2,
    )(branch, *states[: pair + 1], *tables, head_grads, own, other)


def feed_phase(rows_in, grads_in, hidden, unit_grads, back_parts, out_parts, weights, actions):
    tokens, width = rows_in.shape[2:]
    rows = tokens // 2
    shards, columns = weights.shape[0], weights.shape[2]
    share = columns // 2

    def body(rows_ref, out_grad_ref, hidden_ref, units_ref, back_own, back_other, out_own, out_other):
        at_step(pl.program_id(0) * CHIPS + pl.program_id(1), actions)
        hidden_grad = None
        for shard in range(shards):
            grad = out_grad_ref[0, 0, :, shard * columns : (shard + 1) * columns]
            term = dot_t(grad, weights[shard, width:, :])
            hidden_grad = term if hidden_grad is None else hidden_grad + term
        back = None
        for shard in range(shards):
            both = dot(rows_ref[0, 0], weights[shard, :width, :])
            gate, upward = both[:, :share], both[:, share:]
            grad = hidden_grad[:, shard * share : (shard + 1) * share]
            sigmoid = jax.nn.sigmoid(gate)
            swish = gate * sigmoid
            hidden_ref[0, 0, :, shard * share : (shard + 1) * share] = (swish * upward).astype(jnp.bfloat16)
            gate_grad = grad * upward * sigmoid * (1.0 + gate * (1.0 - sigmoid))
            units_ref[shard, 0, 0] = jnp.concatenate([gate_grad, grad * swish], axis=1).astype(jnp.bfloat16)
            term = dot_t(units_ref[shard, 0, 0], weights[shard, :width, :])
            back = term if back is None else back + term
        back = back.astype(jnp.bfloat16)
        back_own[0, 0] = back[:rows]
        back_other[0, 0] = back[rows:]
        for shard in range(shards):
            span = slice(shard * columns, (shard + 1) * columns)
            value = dot(hidden_ref[0, 0], weights[shard, width:, :]).astype(jnp.bfloat16)
            out_own[0, 0, :, span] = value[:rows]
            out_other[0, 0, :, span] = value[rows:]

    here = lambda chunk, chip: (chunk, chip, 0, 0)
    wide = pl.BlockSpec((1, 1, tokens, width), here)
    narrow = pl.BlockSpec((1, 1, rows, width), here)
    pltpu.emit_pipeline(
        body,
        grid=(2, CHIPS),
        in_specs=[wide, wide],
        out_specs=[
            pl.BlockSpec((1, 1, tokens, hidden.shape[3]), here),
            pl.BlockSpec((shards, 1, 1, tokens, columns), lambda chunk, chip: (0, chunk, chip, 0, 0)),
        ]
        + [narrow] * 4,
    )(rows_in, grads_in, hidden, unit_grads, *back_parts, *out_parts)


def bf16(*shape):
    return jax.ShapeDtypeStruct(shape, jnp.bfloat16)


def f32(*shape):
    return jax.ShapeDtypeStruct(shape, jnp.float32)


def start_up(
    activations, cotangent, head_block, out_block, unit_block, down_block, lengths_block, gain
):
    _, tokens, width = activations.shape
    rows = tokens // 2
    devices, unit_rows, columns = unit_block.shape
    down_rows = down_block.shape[1]
    planes, _, sub_rows, _ = head_block.shape
    edge = devices * unit_rows

    def kernel(*refs):
        act, cot, head_in, out_in, unit_in, down_in, length_in, gain_ref = refs[:8]
        own_rows, own_grads, gathered = refs[8], refs[9], refs[10:12]
        head_weight, head_output, feed_own, lengths_all = refs[12:16]
        act_groups, cot_groups, traded, spread, other_half, normed = refs[16:22]
        wires = Wires(*refs[22:])
        place, plane = lax.axis_index("dp"), lax.axis_index("fsdp")
        core = lax.rem(place, 2)

        def half(index):
            return pl.ds(pl.multiple_of(index * rows, STRIPE), rows)

        def move(source, target):
            @pl.loop(0, rows // STRIPE)
            def _(step):
                span = pl.ds(step * STRIPE, STRIPE)
                target[span] = source[span]

        def trade(array, groups, own):
            label = [2 * core + group for group in range(2)]
            inside = [
                Remote(wires, array.at[group, half(1 - core)], groups.at[label[group]], CORE)
                for group in range(2)
            ]
            outside = [
                Remote(wires, groups.at[flip(plane, mask)], own.at[plane], 0, mask)
                for mask in range(1, CHUNKS)
            ]

            def keep():
                for group in range(2):
                    move(array.at[group, half(core)], groups.at[label[group]])

            return inside, keep, outside, lambda: move(groups.at[plane], own.at[plane])

        act_inside, act_keep, act_outside, act_own = trade(act, act_groups, own_rows)
        cot_inside, cot_keep, cot_outside, cot_own = trade(cot, cot_groups, own_grads)
        head_trade = [
            Remote(wires, head_in.at[flip(plane, mask)], traded.at[plane], 0, mask)
            for mask in range(1, CHUNKS)
        ]
        head_spread, feed_spread = [], []
        for mask in range(1, devices):
            other = flip(place, mask)
            head_spread.append(
                Remote(
                    wires,
                    traded.at[lax.div(other, 2), lax.rem(other, 2)],
                    spread.at[place, plane],
                    mask,
                )
            )
            feed_spread.append(
                Remote(
                    wires,
                    unit_in.at[other],
                    feed_own.at[pl.ds(pl.multiple_of(place * unit_rows, unit_rows), unit_rows)],
                    mask,
                )
            )
            feed_spread.append(
                Remote(
                    wires,
                    down_in.at[other],
                    feed_own.at[pl.ds(pl.multiple_of(edge + place * down_rows, down_rows), down_rows)],
                    mask,
                )
            )
            feed_spread.append(Remote(wires, length_in, lengths_all.at[place], mask))

        def over_planes(block):
            mine, theirs = block(plane), block(flip(plane, 2))
            return (
                [Remote(wires, mine, mine, 0, 1), Remote(wires, mine, mine, 0, 2)],
                Remote(wires, theirs, theirs, 0, 1),
            )

        head_near, head_relay = over_planes(lambda index: spread.at[:, index])
        out_near, out_relay = over_planes(
            lambda index: head_output.at[:, pl.ds(pl.multiple_of(index * columns, columns), columns)]
        )
        core_half = Remote(wires, spread.at[:, :, :, pl.ds(HEAD, HEAD)], other_half, CORE)
        moves = [
            Gather(wires, [normed.at[2 * pair], normed.at[2 * pair + 1]], gathered[pair])
            for pair in range(2)
        ]

        meet(PLANE + PLANES)
        for copy in act_inside + cot_inside + head_trade + feed_spread:
            copy.start()
        act_keep()
        for copy in act_inside:
            copy.arrived()
        for copy in act_outside:
            copy.start()
        cot_keep()
        act_own()
        traded[plane] = head_in[plane]
        columns_at = pl.ds(pl.multiple_of(plane * columns, columns), columns)
        head_output[:, columns_at] = out_in[...]
        feed_own[pl.ds(pl.multiple_of(place * unit_rows, unit_rows), unit_rows)] = unit_in[place]
        feed_own[pl.ds(pl.multiple_of(edge + place * down_rows, down_rows), down_rows)] = down_in[place]
        lengths_all[place] = length_in[...]
        for copy in head_trade:
            copy.arrived()
        for copy in head_spread:
            copy.start()
        spread[place, plane] = traded[lax.div(place, 2), core]
        for copy in head_spread + cot_inside:
            copy.arrived()
        cot_own()
        for copy in act_outside:
            copy.arrived()
        for copy in head_near + out_near:
            copy.start()

        for chunk in range(CHUNKS):

            @pl.loop(0, rows // STRIPE)
            def _(step):
                span = pl.ds(step * STRIPE, STRIPE)
                values = own_rows[chunk, span].astype(jnp.float32)
                factor = lax.rsqrt(jnp.mean(values * values, axis=1, keepdims=True) + epsilon)
                normed[chunk, span] = (values * factor * gain_ref[...]).astype(jnp.bfloat16)

        moves[0].first()
        moves[0].second()
        moves[1].first()
        moves[0].third()
        moves[1].second()
        for copy in head_near + out_near:
            copy.arrived()
        head_relay.start()
        out_relay.start()
        for copy in cot_outside:
            copy.start()
        moves[0].last()
        moves[1].third()
        head_relay.arrived()
        core_half.start()
        moves[1].last()
        out_relay.arrived()
        core_half.arrived()
        head_weight[:, :, :, :HEAD] = spread[:, :, :, :HEAD]
        for index in range(2):

            @pl.when(core == index)
            def _():
                mine, theirs = (1 + index) * HEAD, (2 - index) * HEAD
                head_weight[:, :, :, mine : mine + HEAD] = spread[:, :, :, HEAD:]
                head_weight[:, :, :, theirs : theirs + HEAD] = other_half[...]

        for copy in feed_spread + cot_outside:
            copy.arrived()
        for copy in (
            act_inside + cot_inside + head_trade + feed_spread + act_outside + head_spread
            + head_near + out_near + [head_relay, out_relay, core_half] + cot_outside
        ):
            copy.left()

    own = bf16(CHUNKS, rows, width)
    outs = call(
        kernel,
        1,
        [(activations, VMEM), (cotangent, VMEM), (head_block, VMEM), (out_block, VMEM)]
        + [(unit_block, VMEM), (down_block, VMEM), (lengths_block, VMEM), (gain, VMEM)],
        [(own, VMEM), (own, VMEM)]
        + [(bf16(2, CHIPS, tokens, width), HBM)] * 2
        + [(bf16(devices, planes, sub_rows, 3 * HEAD), VMEM), (bf16(HEAD, width), VMEM)]
        + [(bf16(devices * (unit_rows + down_rows), columns), VMEM)]
        + [(jax.ShapeDtypeStruct((devices,) + lengths_block.shape, jnp.int32), VMEM)],
        [
            pltpu.VMEM((CHUNKS, rows, width), jnp.bfloat16),
            pltpu.VMEM((CHUNKS, rows, width), jnp.bfloat16),
            pltpu.VMEM((planes, 2, sub_rows, columns), jnp.bfloat16),
            pltpu.VMEM((devices, planes, sub_rows, columns), jnp.bfloat16),
            pltpu.VMEM((devices, planes, sub_rows, HEAD), jnp.bfloat16),
            pltpu.VMEM((CHUNKS, rows, width), jnp.bfloat16),
        ]
        + wire_shapes(90),
        56,
    )
    return outs[0], outs[1], outs[2:4], outs[4], outs[5], outs[6], outs[7]


def attend_and_norm(
    rows_all, out_grads, feed_own, weight, cosine, sine, lengths, places, out_weight, inputs, gain
):
    _, rows, width = inputs.shape
    tokens = 2 * rows
    planes = CHUNKS
    whole_pair = bf16(2, CHIPS, tokens, width)

    def kernel(*refs):
        gathered, grads_ref, feed_ref, head_ref, cosine_ref, sine_ref = refs[:2], *refs[2:7]
        lengths_ref, place_q, place_k, weight_ref, inputs_ref, gain_ref = refs[7:13]
        refs = refs[13:]
        states, mixed, middle, normed, target, grads_all, feed_all = refs[:2], refs[2:4], *refs[4:9]
        parts, landings = (refs[9:11], refs[11:13]), (refs[13:16], refs[16:19])
        stage, keys, values, normed_late = refs[19:23], refs[23], refs[24], refs[25]
        wires = Wires(*refs[26:])
        plane = lax.axis_index("fsdp")

        def finish(pair):
            def done(chunk, span, total):
                at = 2 * pair + chunk
                total = total + inputs_ref[at, span].astype(jnp.float32)
                middle[at, span] = total
                factor = lax.rsqrt(jnp.mean(total * total, axis=1, keepdims=True) + epsilon)
                kept = normed if pair == 0 else normed_late
                kept[chunk, span] = (total * factor * gain_ref[...]).astype(jnp.bfloat16)

            return done

        sums = [
            Scatter(wires, *parts[pair], landings[pair], stage, finish(pair)) for pair in range(2)
        ]
        move = Gather(wires, [normed_late.at[0], normed_late.at[1]], target)
        grad_move = Gather(wires, [grads_ref.at[2], grads_ref.at[3]], grads_all)
        near = Remote(wires, feed_ref, feed_all.at[plane], 0, 1)
        across_middle = Remote(wires, feed_ref, feed_all.at[plane], 0, 2)
        relay = Remote(
            wires, feed_all.at[flip(plane, 2)], feed_all.at[flip(plane, 2)], 0, 1
        )
        places_in = (place_q, place_k)

        meet(SIDES + PLANES[:2])
        near.start()
        across_middle.start()
        grad_move.first()
        wires.load([(feed_ref, feed_all.at[plane])])
        project_phase(
            gathered[0], states[0], head_ref, cosine_ref.at[0], sine_ref.at[0], {7: grad_move.second}
        )
        project_phase(gathered[1], states[1], head_ref, cosine_ref.at[1], sine_ref.at[1], {})
        attend_phase(
            1, states, mixed[1], *parts[1], lengths_ref, places_in, weight_ref, keys, values,
            {3: grad_move.third},
        )
        sums[1].first()
        attend_phase(
            0, states, mixed[0], *parts[0], lengths_ref, places_in, weight_ref, keys, values,
            {5: sums[1].second},
        )
        sums[0].first()
        grad_move.last()
        sums[1].third()
        sums[0].second()
        sums[1].last()
        move.first()
        sums[0].third()
        across_middle.arrived()
        relay.start()
        move.second()
        sums[0].last()
        move.third()
        move.last()
        near.arrived()
        relay.arrived()
        for copy in (near, across_middle, relay):
            copy.left()

    pair_parts = [(shape, HBM) for shape in partial_shapes(rows, width)]
    landing = [(shape, HBM) for shape in landing_shapes(rows, width)]
    outs = call(
        kernel,
        2,
        [(rows_all[0], HBM), (rows_all[1], HBM), (out_grads, VMEM), (feed_own, VMEM)]
        + [(weight, VMEM), (cosine, HBM), (sine, HBM)]
        + [(lengths, SMEM), (places[0], VMEM), (places[1], VMEM), (out_weight, VMEM)]
        + [(inputs, VMEM), (gain, VMEM)],
        [(bf16(2, CHIPS, tokens, 3 * HEAD), HBM)] * 2
        + [(bf16(2, CHIPS, tokens, HEAD), HBM)] * 2
        + [(f32(CHUNKS, rows, width), VMEM), (bf16(2, rows, width), VMEM)]
        + [(whole_pair, HBM)] * 2
        + [(bf16(planes, *feed_own.shape), HBM)]
        + pair_parts * 2
        + landing * 2,
        stage_shapes(rows, width)
        + [pltpu.VMEM((CHUNKS * tokens, HEAD), jnp.bfloat16)] * 2
        + [pltpu.VMEM((2, rows, width), jnp.bfloat16)]
        + wire_shapes(50),
        60,
    )
    return outs[:2], outs[2:4], outs[4], outs[5], outs[6], outs[7], outs[8]


def norm_back(values, gain, gradient):
    factor = lax.rsqrt(jnp.mean(values * values, axis=1, keepdims=True) + epsilon)
    scaled = values * factor
    pulled = gradient * gain
    back = factor * (pulled - scaled * jnp.mean(pulled * scaled, axis=1, keepdims=True))
    return back, gradient * scaled


def feed_forward(normed_own, normed_late, grads_late, weights, middle, out_grad_own, gain, units):
    _, rows, width = middle.shape
    tokens = 2 * rows
    shards, columns = weights.shape[0], weights.shape[2]
    whole_pair = bf16(2, CHIPS, tokens, width)

    def kernel(*refs):
        normed_ref, normed_late_ref, grads_late_ref = refs[:3]
        weight_ref, middle_ref, own_grad, gain_ref = refs[3:7]
        refs = (None, *refs)
        normed_early, branch, grads_early = refs[8], refs[9], refs[27]
        hidden, unit_grads = refs[10:12], refs[12:14]
        back_parts, out_parts = (refs[14:16], refs[16:18]), (refs[18:20], refs[20:22])
        middle_grad, gain_sum, landing = refs[22], refs[23], refs[24:27]
        stage, own_branch, wires = refs[28:32], refs[32], Wires(*refs[33:])
        meet(SIDES)
        gain_sum[...] = jnp.zeros(gain_sum.shape, jnp.float32)

        def done(chunk, span, total):
            back, gain_terms = norm_back(middle_ref[2 + chunk, span], gain_ref[...], total)
            gain_sum[...] += gain_terms
            back = back + own_grad[2 + chunk, span].astype(jnp.float32)
            middle_grad[chunk, span] = back
            own_branch[chunk, span] = back.astype(jnp.bfloat16)

        move = Gather(wires, [normed_ref.at[0], normed_ref.at[1]], normed_early)
        sums = Scatter(wires, *back_parts[1], landing, stage, done)
        late_move = Gather(wires, [own_branch.at[0], own_branch.at[1]], branch)
        grad_move = Gather(wires, [own_grad.at[0], own_grad.at[1]], grads_early)
        move.first()
        grad_move.first()
        feed_phase(
            normed_late_ref, grads_late_ref, hidden[1], unit_grads[1], back_parts[1], out_parts[1],
            weight_ref,
            {2: move.second, 3: grad_move.second, 5: move.third, 7: grad_move.third},
        )
        sums.first()
        move.last()
        grad_move.last()
        feed_phase(
            normed_early, grads_early, hidden[0], unit_grads[0], back_parts[0], out_parts[0], weight_ref,
            {1: sums.second, 4: sums.third, 6: lambda: (sums.last(), late_move.first()) and None},
        )
        late_move.second()
        late_move.third()
        late_move.last()

    outs = call(
        kernel,
        3,
        [(normed_own, VMEM), (normed_late, HBM), (grads_late, HBM)]
        + [(weights, VMEM), (middle, VMEM), (out_grad_own, VMEM), (gain, VMEM)],
        [(whole_pair, HBM)] * 2
        + [(bf16(2, CHIPS, tokens, units), HBM)] * 2
        + [(bf16(shards, 2, CHIPS, tokens, columns), HBM)] * 2
        + [(shape, HBM) for shape in partial_shapes(rows, width)] * 4
        + [(f32(2, rows, width), VMEM), (f32(STRIPE, width), VMEM)]
        + [(shape, HBM) for shape in landing_shapes(rows, width)]
        + [(whole_pair, HBM)],
        stage_shapes(rows, width) + [pltpu.VMEM((2, rows, width), jnp.bfloat16)] + wire_shapes(50),
        62,
    )
    return outs[19], outs[0], outs[1], outs[2:4], outs[4:6], outs[6:8], (outs[10:12], outs[12:14]), outs[14], outs[15]


def attend_back(
    states, lengths, places, out_weight, weight, cosine, sine, branch_late, back_early, out_parts,
    middle, out_grad_own, inputs, middle_grad_late, gains
):
    _, rows, width = middle.shape
    tokens = 2 * rows

    def kernel(*refs):
        states_in, (lengths_ref, place_q, place_k, out_ref, weight_ref, cosine_ref, sine_ref) = (
            refs[:2],
            refs[2:9],
        )
        late_branch, back_parts, outs_in = refs[9], refs[10:12], (refs[12:14], refs[14:16])
        middle_ref, own_grad, inputs_ref, late_grad, gain_one, gain_two = refs[16:22]
        head_grads, early_branch, output_groups, input_grad = refs[22:24], refs[24], refs[25], refs[26]
        gain_sums = refs[27]
        parts = (refs[28:30], refs[30:32])
        landings = [refs[32 + 3 * place : 35 + 3 * place] for place in range(5)]
        stage, early_grad, own_branch, keys, values = refs[47:51], refs[51], refs[52], refs[53], refs[54]
        sums, late_sums, outputs, wires = refs[55:57], refs[57:59], refs[59], Wires(*refs[60:])
        plane = lax.axis_index("fsdp")
        meet(SIDES + PLANES)
        gain_sums[...] = jnp.zeros(gain_sums.shape, jnp.float32)

        def middle_done(chunk, span, total):
            back, gain_terms = norm_back(
                middle_ref[chunk, span].astype(jnp.float32), gain_two[...], total
            )
            gain_sums[1] += gain_terms
            back = back + own_grad[chunk, span].astype(jnp.float32)
            early_grad[chunk, span] = back
            own_branch[chunk, span] = back.astype(jnp.bfloat16)

        def output_done(pair):
            def done(chunk, span, total):
                at = 2 * pair + chunk
                outputs[at, span] = (middle_ref[at, span] + total).astype(jnp.bfloat16)

            return done

        def input_done(pair):
            def done(chunk, span, total):
                at = 2 * pair + chunk
                back, gain_terms = norm_back(
                    inputs_ref[at, span].astype(jnp.float32), gain_one[...], total
                )
                gain_sums[0] += gain_terms
                direct = late_grad if pair == 1 else early_grad
                input_grad[at, span] = (direct[chunk, span] + back).astype(jnp.bfloat16)

            return done

        middle_sum = Scatter(wires, *back_parts, landings[0], stage, middle_done)
        move = Gather(wires, [own_branch.at[0], own_branch.at[1]], early_branch)
        output_sums = [
            Scatter(wires, *outs_in[pair], landings[1 + pair], stage, output_done(pair))
            for pair in range(2)
        ]
        input_sums = [
            Scatter(wires, *parts[pair], landings[3 + pair], stage, input_done(pair)) for pair in range(2)
        ]

        def back_through(pair, branch, actions):
            attend_back_phase(
                pair, branch, states_in, head_grads[pair], *parts[pair], lengths_ref,
                (place_q, place_k), out_ref, weight_ref, (cosine_ref.at[pair], sine_ref.at[pair]),
                keys, values, sums, late_sums, actions,
            )

        def both(*steps):
            def run():
                for step in steps:
                    step()

            return run

        back_to_planes = [
            Remote(wires, outputs.at[flip(plane, mask)], output_groups.at[plane], 0, mask)
            for mask in range(1, CHUNKS)
        ]

        def send_back():
            for copy in back_to_planes:
                copy.start()
            wires.load([(outputs.at[plane], output_groups.at[plane])])

        middle_sum.first()
        output_sums[1].first()
        output_sums[0].first()
        back_through(
            1,
            late_branch,
            {
                1: middle_sum.second,
                4: middle_sum.third,
                6: both(middle_sum.last, move.first),
                7: move.second,
            },
        )
        input_sums[1].first()
        output_sums[1].second()
        move.third()
        move.last()
        back_through(
            0,
            early_branch,
            {
                0: output_sums[1].third,
                2: both(output_sums[1].last, output_sums[0].second),
                4: output_sums[0].third,
                6: both(output_sums[0].last, send_back),
                7: input_sums[1].second,
            },
        )
        input_sums[0].first()
        input_sums[1].third()
        input_sums[0].second()
        input_sums[1].last()
        input_sums[0].third()
        input_sums[0].last()
        for copy in back_to_planes:
            copy.arrived()
        for copy in back_to_planes:
            copy.left()

    outs = call(
        kernel,
        4,
        [(state, HBM) for state in states]
        + [(lengths, SMEM), (places[0], VMEM), (places[1], VMEM), (out_weight, VMEM), (weight, VMEM)]
        + [(cosine, HBM), (sine, HBM), (branch_late, HBM)]
        + [(part, HBM) for part in back_early]
        + [(part, HBM) for parts in out_parts for part in parts]
        + [(middle, VMEM), (out_grad_own, VMEM), (inputs, VMEM), (middle_grad_late, VMEM)]
        + [(gains[0], VMEM), (gains[1], VMEM)],
        [(bf16(2, CHIPS, tokens, 3 * HEAD), HBM)] * 2
        + [(bf16(2, CHIPS, tokens, width), HBM)]
        + [(bf16(CHUNKS, rows, width), HBM), (bf16(CHUNKS, rows, width), VMEM)]
        + [(f32(2, STRIPE, width), VMEM)]
        + [(shape, HBM) for shape in partial_shapes(rows, width)] * 2
        + [(shape, HBM) for shape in landing_shapes(rows, width)] * 5,
        stage_shapes(rows, width)
        + [pltpu.VMEM((2, rows, width), jnp.float32), pltpu.VMEM((2, rows, width), jnp.bfloat16)]
        + [pltpu.VMEM((CHUNKS * tokens, HEAD), jnp.bfloat16)] * 2
        + [pltpu.VMEM((CHIPS, 2 * tokens, HEAD), jnp.float32)] * 2
        + [pltpu.VMEM((2 * tokens, HEAD), jnp.float32)] * 2
        + [pltpu.VMEM((CHUNKS, rows, width), jnp.bfloat16)]
        + wire_shapes(60),
        63,
    )
    return outs[:2], outs[2], outs[3], outs[4], outs[5]


def weight_grad_phase(rows_in, grads, total, fresh, actions):
    _, chips, tokens, width = rows_in.shape
    columns = grads.shape[3]

    def body(rows_ref, grads_ref):
        chunk, step = pl.program_id(0), pl.program_id(1)
        at_step(2 * chunk + step, actions)
        term = dot_tn(rows_ref[0].reshape(2 * tokens, width), grads_ref[0].reshape(2 * tokens, columns))
        if fresh:

            @pl.when(chunk + step == 0)
            def _():
                total[...] = jnp.zeros(total.shape, jnp.float32)

        total[...] += term

    here = lambda chunk, step: (chunk, step, 0, 0)
    pltpu.emit_pipeline(
        body,
        grid=(2, chips // 2),
        in_specs=[
            pl.BlockSpec((1, 2, tokens, width), here),
            pl.BlockSpec((1, 2, tokens, columns), here),
        ],
    )(rows_in, grads)


def finish(head_terms, output_terms, unit_sum, down_sum, output_groups, input_grad, gain_sums):
    devices, planes = lax.axis_size("dp"), lax.axis_size("fsdp")
    strips = unit_sum.shape[0]
    _, down_rows, columns = down_sum.shape
    _, rows, width = input_grad.shape
    in_rows = width // devices
    sub_rows = in_rows // planes

    def kernel(*refs):
        head_refs, output_refs, refs = refs[:4], refs[4:8], refs[8:]
        units_in, downs_in, output_groups_ref, grads_ref, gains = refs[:5]
        outputs, input_out, head_out, output_out, gate_up, downs, gain_out, square_out = refs[5:13]
        grad_groups, combined, other_half, mine, gathered = refs[13:18]
        head_landing, output_landing, head_two, output_two = refs[18:22]
        gain_parts, square_parts, units = refs[22:25]
        head_total, output_total, given, outs_in, wires = *refs[25:29], Wires(*refs[29:])
        place, plane = lax.axis_index("dp"), lax.axis_index("fsdp")
        core = lax.rem(place, 2)

        def part(mask):
            return combined.at[:, flip(plane, mask)], outs_in.at[:, columns_of(flip(plane, mask), columns)]

        def both(sources, targets, mask):
            return [Remote(wires, source, target, 0, mask) for source, target in zip(sources, targets)]

        landing = [(head_landing.at[index], output_landing.at[index]) for index in range(3)]
        third = both(part(3), landing[0], 1)
        first = both(part(1), landing[1], 1)
        second = both((head_two, output_two), landing[2], 2)
        core_half = Remote(wires, given, other_half, CORE)
        rows_back = [
            Remote(wires, grads_ref.at[flip(plane, mask)], grad_groups.at[plane], 0, mask)
            for mask in range(1, CHUNKS)
        ]
        spread, heads_back = [], []
        for mask in range(1, devices):
            other = flip(place, mask)
            spread.append(Remote(wires, units_in.at[:, columns_of(other, in_rows)], units.at[place], mask))
            spread.append(Remote(wires, downs_in.at[other], downs.at[place], mask))
            heads_back.append(Remote(wires, mine.at[other], gathered.at[place], mask))
        heads_over = [
            Remote(wires, gathered.at[pl.ds(2 * flip(plane, mask), 2)], head_out.at[plane], 0, mask)
            for mask in range(1, CHUNKS)
        ]

        def to_owners(groups, target):
            copies = []
            for group in range(2):
                copies.append(
                    Remote(
                        wires,
                        groups.at[2 * (1 - core) + group],
                        target.at[group, half_rows(core, rows)],
                        CORE,
                    )
                )
            return copies

        outputs_in = to_owners(output_groups_ref, outputs)
        grads_in = to_owners(grad_groups, input_out)

        def sum_over(parts_ref):
            steps = [(mask, 0) for mask in (CORE, SIDE_A, SIDE_B)] + [(0, 1), (0, 2)]
            copies = [
                Remote(wires, parts_ref.at[2 * index], parts_ref.at[2 * index + 1], mask, over)
                for index, (mask, over) in enumerate(steps)
            ]

            def step(index):
                copies[index].arrived()
                copies[index].left()
                parts_ref[2 * index + 2] = parts_ref[2 * index] + parts_ref[2 * index + 1]
                if index + 1 < len(copies):
                    copies[index + 1].start()

            return copies[0].start, step, len(steps)

        gains_start, gains_step, count = sum_over(gain_parts)
        squares_start, squares_step, _ = sum_over(square_parts)

        gain_parts[0] = jnp.concatenate(
            [jnp.sum(gains[index], axis=0, keepdims=True) for index in range(2)]
            + [jnp.zeros((6, width), jnp.float32)]
        )
        meet(PLANE + PLANES)
        for copy in rows_back + spread + outputs_in:
            copy.start()
        gains_start()
        units[place] = units_in[:, columns_of(place, in_rows)]
        downs[place] = downs_in[place]
        for group in range(2):
            move_rows(
                output_groups_ref.at[2 * core + group], outputs.at[group, half_rows(core, rows)]
            )
        move_rows(grads_ref.at[plane], grad_groups.at[plane])
        weight_grad_phase(head_refs[0], head_refs[1], head_total, True, {3: lambda: gains_step(0)})
        weight_grad_phase(
            head_refs[2], head_refs[3], head_total, False, {1: lambda: gains_step(1), 3: lambda: gains_step(2)}
        )

        def split(index):
            kept, sent = (1 + index) * HEAD, (2 - index) * HEAD

            @pl.loop(0, devices)
            def _(block):
                span = pl.ds(pl.multiple_of(block * in_rows, in_rows), in_rows)
                shape = (planes, sub_rows, HEAD)
                given[block] = head_total[span, sent : sent + HEAD].astype(jnp.bfloat16).reshape(shape)
                combined[block, :, :, :HEAD] = head_total[span, :HEAD].astype(jnp.bfloat16).reshape(shape)

        for index in range(2):
            pl.when(core == index)(functools.partial(split, index))
        core_half.start()
        weight_grad_phase(output_refs[0], output_refs[1], output_total, True, {})
        core_half.arrived()

        def join(index):
            kept = (1 + index) * HEAD

            @pl.loop(0, devices)
            def _(block):
                span = pl.ds(pl.multiple_of(block * in_rows, in_rows), in_rows)
                total = head_total[span, kept : kept + HEAD].reshape(planes, sub_rows, HEAD)
                total = total + other_half[block].astype(jnp.float32)
                combined[block, :, :, HEAD:] = total.astype(jnp.bfloat16)

        for index in range(2):
            pl.when(core == index)(functools.partial(join, index))
        third[0].start()
        weight_grad_phase(output_refs[2], output_refs[3], output_total, False, {})
        outs_in[...] = output_total[...].astype(jnp.bfloat16)
        third[1].start()
        third[0].arrived()
        head_two[...] = (
            combined[:, flip(plane, 2)].astype(jnp.float32) + head_landing[0].astype(jnp.float32)
        ).astype(jnp.bfloat16)
        second[0].start()
        third[1].arrived()
        output_two[...] = (
            outs_in[:, columns_of(flip(plane, 2), columns)].astype(jnp.float32)
            + output_landing[0].astype(jnp.float32)
        ).astype(jnp.bfloat16)
        second[1].start()
        for copy in first:
            copy.start()
        for index in range(3, count):
            gains_step(index)
        for copy in rows_back:
            copy.arrived()
        for copy in grads_in:
            copy.start()
        for group in range(2):
            move_rows(grad_groups.at[2 * core + group], input_out.at[group, half_rows(core, rows)])
        for copy in spread:
            copy.arrived()
        square = jnp.zeros((), jnp.float32)
        for index in range(devices):
            values = downs[index].astype(jnp.float32)
            square += jnp.sum(values * values)
            for block in range(strips // down_rows):
                values = units[index, block * down_rows : (block + 1) * down_rows].astype(jnp.float32)
                square += jnp.sum(values * values)
                matrix, run = block // 2, block % 2
                at = (run * devices + index) * down_rows
                gate_up[matrix, :, at : at + down_rows] = values.T.astype(jnp.bfloat16)
        for copy in first + second:
            copy.arrived()
        total = combined[:, plane].astype(jnp.float32)
        for index in (1, 2):
            total += head_landing[index].astype(jnp.float32)
        mine[...] = total.astype(jnp.bfloat16)
        for copy in heads_back:
            copy.start()
        gathered[place] = mine[place]
        total = outs_in[:, columns_of(plane, columns)].astype(jnp.float32)
        for index in (1, 2):
            total += output_landing[index].astype(jnp.float32)
        output_out[...] = total
        square += jnp.sum(total * total)
        for copy in heads_back:
            copy.arrived()
        for copy in heads_over:
            copy.start()
        head_out[plane] = gathered[pl.ds(2 * plane, 2)]
        for copy in heads_over:
            copy.arrived()
        for index in range(planes):
            values = head_out[index].astype(jnp.float32)
            square += jnp.sum(values * values)
        square_parts[0] = jnp.full(square_parts.shape[1:], square, jnp.float32)
        squares_start()
        for index in range(count):
            squares_step(index)
        gain_out[...] = gain_parts[2 * count]
        square_out[...] = square_parts[2 * count]
        for copy in outputs_in + grads_in:
            copy.arrived()
        for copy in (
            third + first + second + [core_half] + rows_back + spread + heads_back + heads_over
            + outputs_in + grads_in
        ):
            copy.left()

    own = bf16(2, 2 * rows, width)
    return call(
        kernel,
        5,
        [(array, HBM) for array in head_terms + output_terms]
        + [(array, VMEM) for array in (unit_sum, down_sum, output_groups, input_grad, gain_sums)],
        [(own, VMEM)] * 2
        + [(bf16(planes, 2, sub_rows, columns), VMEM), (f32(HEAD, columns), VMEM)]
        + [(bf16(2, in_rows, devices * strips // 2), VMEM), (bf16(devices, down_rows, columns), VMEM)]
        + [(f32(8, width), VMEM), (f32(8, 128), VMEM)],
        [
            pltpu.VMEM((CHUNKS, rows, width), jnp.bfloat16),
            pltpu.VMEM((devices, planes, sub_rows, columns), jnp.bfloat16),
            pltpu.VMEM((devices, planes, sub_rows, HEAD), jnp.bfloat16),
            pltpu.VMEM((devices, sub_rows, columns), jnp.bfloat16),
            pltpu.VMEM((devices, sub_rows, columns), jnp.bfloat16),
            pltpu.VMEM((3, devices, sub_rows, columns), jnp.bfloat16),
            pltpu.VMEM((3, HEAD, columns), jnp.bfloat16),
            pltpu.VMEM((devices, sub_rows, columns), jnp.bfloat16),
            pltpu.VMEM((HEAD, columns), jnp.bfloat16),
            pltpu.VMEM((11, 8, width), jnp.float32),
            pltpu.VMEM((11, 8, 128), jnp.float32),
            pltpu.VMEM((devices, strips, in_rows), jnp.bfloat16),
            pltpu.VMEM((width, 3 * HEAD), jnp.float32),
            pltpu.VMEM((HEAD, width), jnp.float32),
            pltpu.VMEM((devices, planes, sub_rows, HEAD), jnp.bfloat16),
            pltpu.VMEM((HEAD, width), jnp.bfloat16),
        ]
        + wire_shapes(70),
        62,
    )


def unit_weight_grads(unit_grads, rows_in):
    shards, _, _, tokens, columns = unit_grads[0].shape
    width = rows_in[0].shape[3]

    def kernel(late_units, late_rows, early_units, early_rows, out, total):
        step = pl.program_id(1)

        @pl.when(step == 0)
        def _():
            total[...] = jnp.zeros(total.shape, jnp.float32)

        for place, (units, rows_ref) in enumerate(((late_units, late_rows), (early_units, early_rows))):

            @pl.when(lax.div(step, 2) == place)
            def _():
                left = units[0, 0].reshape(CHIPS * tokens, columns)
                right = rows_ref[0].reshape(CHIPS * tokens, width)
                total[...] += dot_tn(left, right)

        @pl.when(step == 3)
        def _():
            out[0] = total[...].astype(jnp.bfloat16)

    late = lambda step: jnp.minimum(step, 1)
    early = lambda step: jnp.maximum(step - 2, 0)
    specs = []
    for at in (late, early):
        specs.append(
            pl.BlockSpec(
                (1, 1, CHIPS, tokens, columns),
                (lambda at: lambda shard, step: (shard, at(step), 0, 0, 0))(at),
            )
        )
        specs.append(
            pl.BlockSpec(
                (1, CHIPS, tokens, width), (lambda at: lambda shard, step: (at(step), 0, 0, 0))(at)
            )
        )
    return pl.pallas_call(
        kernel,
        grid=(shards, 4),
        in_specs=specs,
        out_specs=pl.BlockSpec((1, columns, width), lambda shard, step: (shard, 0, 0)),
        out_shape=bf16(shards, columns, width),
        scratch_shapes=[pltpu.VMEM((columns, width), jnp.float32)],
        compiler_params=params(60),
    )(unit_grads[1], rows_in[1], unit_grads[0], rows_in[0])


def dot(left, right):
    return jnp.dot(left, right, preferred_element_type=jnp.float32)


def dot_t(left, right):
    return lax.dot_general(
        left, right, (((1,), (1,)), ((), ())), preferred_element_type=jnp.float32
    )


def dot_tn(left, right):
    return lax.dot_general(
        left, right, (((0,), (0,)), ((), ())), preferred_element_type=jnp.float32
    )


def spin(values, cosine, sine):
    halfway = values.shape[1] // 2
    first, second = values[:, :halfway], values[:, halfway:]
    return jnp.concatenate(
        [first * cosine - second * sine, second * cosine + first * sine], axis=1
    )


def spin_back(values, cosine, sine):
    return spin(values, cosine, -sine)


def whole(shape):
    return pl.BlockSpec(shape, lambda *_: (0,) * len(shape), pipeline_mode=pl.Buffered(1))


def params(megabytes):
    return pltpu.CompilerParams(vmem_limit_bytes=megabytes * MB)


def seen(place_q, place_k, chunk, count, tokens, lengths_ref, chip):
    query_index = tokens * chunk + place_q
    key_index = place_k[:, :count]
    ahead_or_here = key_index <= query_index
    if tokens * (chunk + 1) <= PROMPT:
        return ahead_or_here

    def segment(index):
        found = jnp.full(index.shape, -1, jnp.int32)
        for slot in range(NCONT):
            found = jnp.where(index >= PROMPT + slot * CONT, slot, found)
        return found

    key_segment, query_segment = segment(key_index), segment(query_index)
    end = jnp.full(key_index.shape, PROMPT, jnp.int32)
    for slot in range(NCONT):
        end = jnp.where(
            key_segment == slot, PROMPT + slot * CONT + lengths_ref[chip, slot], end
        )
    alive = key_index < end
    return ahead_or_here & ((key_segment < 0) | ((key_segment == query_segment) & alive))


def token_dot(left, right):
    return lax.dot_general(
        left.reshape(-1, left.shape[-1]),
        right.reshape(-1, right.shape[-1]),
        (((0,), (0,)), ((), ())),
        preferred_element_type=jnp.float32,
    )


def exchange(value, axis):
    return lax.all_to_all(value, axis, split_axis=0, concat_axis=0, tiled=True)


def plane_device(
    activations,
    cotangent,
    continuation_lengths,
    query_weight,
    key_weight,
    value_weight,
    output_weight,
    gate_weight,
    up_weight,
    down_weight,
    attention_gain,
    feedforward_gain,
    moment_query,
    moment_key,
    moment_value,
    moment_output,
    moment_gate,
    moment_up,
    moment_down,
    moment_attention,
    moment_feedforward,
):
    devices, planes = lax.axis_size("dp"), lax.axis_size("fsdp")
    place, plane = lax.axis_index("dp"), lax.axis_index("fsdp")
    core = place % 2
    low = jnp.bfloat16
    kv_width = KV_HEADS * HEAD
    tokens = activations.shape[1]
    half = tokens // 2

    in_rows = query_weight.shape[0]
    sub_rows = in_rows // planes
    spread = devices * sub_rows

    mixed_kv = jnp.stack([key_weight.astype(low), value_weight.astype(low)], axis=1)
    block = jnp.concatenate([query_weight.astype(low).reshape(in_rows, 2, HEAD), mixed_kv], axis=2)
    head_block = block.reshape(planes, sub_rows, 2, 2 * HEAD).swapaxes(1, 2)

    strip = 128
    runs = gate_weight.shape[1] // (devices * strip)
    units = runs * strip * planes
    gate_up = jnp.stack(
        [
            gate_weight.astype(low).reshape(in_rows, runs, devices, strip),
            up_weight.astype(low).reshape(in_rows, runs, devices, strip),
        ]
    )
    gate_up = gate_up.transpose(3, 1, 0, 2, 4).reshape(devices, in_rows, 2 * runs * strip)
    down_columns = down_weight.shape[1]
    down = down_weight.astype(low).reshape(devices, strip, down_columns)

    gain_one, gain_two = attention_gain[None, :], feedforward_gain[None, :]
    length_block = jnp.zeros((8, 128), jnp.int32).at[:2, :NCONT].set(continuation_lengths)
    own_inputs, own_grads, rows_all, head_weight, head_output, feed_own, all_lengths = start_up(
        activations,
        cotangent,
        head_block,
        output_weight.astype(low),
        gate_up,
        down,
        length_block,
        gain_one,
    )

    first_core = place - core
    lengths = jnp.stack(
        [
            pick(pick(all_lengths, (first_core ^ mask) + plane // 2), plane % 2)[:NCONT]
            for mask in (0, SIDE_A, SIDE_B, SIDE_A + SIDE_B)
        ]
    )

    inside = jnp.concatenate(
        [core * half + jnp.arange(half), (1 - core) * half + jnp.arange(half)]
    ).astype(jnp.int32)
    order = (tokens * jnp.arange(CHUNKS, dtype=jnp.int32)[:, None] + inside[None, :]).reshape(-1)
    cosine, sine = rope_angles(token_places(order))
    cosine = cosine.reshape(2, 2, tokens, HEAD // 2)
    sine = sine.reshape(2, 2, tokens, HEAD // 2)
    place_q, place_k = inside[:, None], order[None, :]
    blocks = plane ^ jnp.arange(CHUNKS, dtype=jnp.int32)

    states, mixed, middle, normed_two, normed_late, grads_late, feed_weights = attend_and_norm(
        rows_all,
        own_grads,
        feed_own,
        head_weight,
        cosine,
        sine,
        lengths,
        (place_q, place_k),
        head_output,
        own_inputs,
        gain_two,
    )
    (
        grads_early,
        normed_early,
        branch_late,
        hidden,
        unit_grads,
        back_early,
        out_parts,
        middle_grad,
        gain_sum,
    ) = feed_forward(normed_two, normed_late, grads_late, feed_weights, middle, own_grads, gain_two, units)
    grads_all = (grads_early, grads_late)
    unit_sum = unit_weight_grads(unit_grads, (normed_early, normed_late))
    unit_sum = lax.psum_scatter(unit_sum, "fsdp", scatter_dimension=0, tiled=False)
    down_sum = reduce(jnp.add, [token_dot(hidden[pair], grads_all[pair]) for pair in (1, 0)]).astype(low)
    down_sum = down_sum.reshape(-1, planes, down_columns).transpose(1, 0, 2)
    down_sum = lax.psum_scatter(down_sum, "fsdp", scatter_dimension=0, tiled=False)
    head_grads, branch_early, output_groups, own_input_grad, gain_sums = attend_back(
        states,
        lengths,
        (place_q, place_k),
        head_output,
        head_weight,
        cosine,
        sine,
        branch_late,
        back_early,
        out_parts,
        middle,
        own_grads,
        own_inputs,
        middle_grad,
        (gain_one, gain_two),
    )

    outputs, input_grad, block, output_owned, gate_up_owned, downs_owned, gain_totals, squares = finish(
        [rows_all[1], head_grads[1], rows_all[0], head_grads[0]],
        [mixed[1], branch_late, mixed[0], branch_early],
        unit_sum,
        down_sum.reshape(devices, strip, down_columns),
        output_groups,
        own_input_grad,
        jnp.stack([gain_sums[0], gain_sums[1] + gain_sum]),
    )
    block = block.swapaxes(1, 2).reshape(in_rows, 2, 2 * HEAD)
    query_owned = block[:, :, :HEAD].reshape(in_rows, 2 * HEAD)
    key_owned, value_owned = block[:, 0, HEAD:], block[:, 1, HEAD:]
    down_owned = downs_owned.reshape(devices * strip, down_columns)

    owner_grads = [
        owned.astype(jnp.float32)
        for owned in (
            query_owned,
            key_owned,
            value_owned,
            output_owned,
            gate_up_owned[0],
            gate_up_owned[1],
            down_owned,
        )
    ]
    attention_total, feedforward_total = gain_totals[0], gain_totals[1]
    square_total = squares[0, 0]
    square_sum = (
        square_total
        + jnp.sum(attention_total * attention_total)
        + jnp.sum(feedforward_total * feedforward_total)
    )
    grad_norm = jnp.sqrt(square_sum)
    entry_count = 2 * D * D + 2 * D * kv_width + 3 * D * FF + 2 * D
    limit = clip_level * math.sqrt(entry_count)
    factor = limit / jnp.maximum(grad_norm, limit)
    gradients = owner_grads + [attention_total, feedforward_total]
    old_moments = [
        moment_query,
        moment_key,
        moment_value,
        moment_output,
        moment_gate,
        moment_up,
        moment_down,
        moment_attention,
        moment_feedforward,
    ]
    old_params = [
        query_weight,
        key_weight,
        value_weight,
        output_weight,
        gate_weight,
        up_weight,
        down_weight,
        attention_gain,
        feedforward_gain,
    ]
    new_moments = [
        0.5 * moment + 0.5 * factor * gradient for moment, gradient in zip(old_moments, gradients)
    ]
    new_params = []
    for at, param in enumerate(old_params):
        if at < 7:
            new_params.append(param - step_size * (new_moments[at] + decay_rate * param))
        else:
            new_params.append(param - gain_step * new_moments[at])
    return (outputs, input_grad, grad_norm, *new_moments, *new_params)


def solution(mesh):
    whole_groups_on_planes = mesh.shape["dp"] == HEADS and mesh.shape["fsdp"] == KV_HEADS
    body = plane_device if whole_groups_on_planes else on_device
    placed = (
        P("dp", "fsdp", None),
        P("dp", "fsdp", None),
        P("dp", None),
        P("dp", "fsdp"),
        P("dp", "fsdp"),
        P("dp", "fsdp"),
        P("dp", "fsdp"),
        P("dp", "fsdp"),
        P("dp", "fsdp"),
        P("dp", "fsdp"),
        P(),
        P(),
        P("dp", "fsdp"),
        P("dp", "fsdp"),
        P("dp", "fsdp"),
        P("dp", "fsdp"),
        P("dp", "fsdp"),
        P("dp", "fsdp"),
        P("dp", "fsdp"),
        P(),
        P(),
    )
    return jax.shard_map(
        body,
        mesh=mesh,
        in_specs=placed,
        out_specs=(
            P("dp", "fsdp", None),
            P("dp", "fsdp", None),
            P(),
            P("dp", "fsdp"),
            P("dp", "fsdp"),
            P("dp", "fsdp"),
            P("dp", "fsdp"),
            P("dp", "fsdp"),
            P("dp", "fsdp"),
            P("dp", "fsdp"),
            P(),
            P(),
            P("dp", "fsdp"),
            P("dp", "fsdp"),
            P("dp", "fsdp"),
            P("dp", "fsdp"),
            P("dp", "fsdp"),
            P("dp", "fsdp"),
            P("dp", "fsdp"),
            P(),
            P(),
        ),
        check_vma=False,
    )
```

```python
import functools
from functools import reduce
import math

import jax
import jax.numpy as jnp
from jax import lax
from jax.experimental import pallas as pl
from jax.experimental.pallas import tpu as pltpu
from jax.sharding import PartitionSpec as P

D = 2048
HEADS = 8
KV_HEADS = 4
HEAD = 256
FF = 8192
PROMPT = 1024
CONT = 64
NCONT = 2


epsilon = 1e-06
rope_base = 1000042.0
step_size = 0.2
gain_step = 4.0
decay_rate = 0.1
clip_level = 0.25
floor_score = -1e30


def rms_rows(values, gain):
    factor = lax.rsqrt(jnp.mean(values * values, axis=-1, keepdims=True) + epsilon)
    return (values * factor * gain, factor)


def rms_back(values, factor, gain, gradient):
    scaled = values * factor
    gain_grad = jnp.sum(gradient * scaled, axis=0)
    pulled = gradient * gain
    return (
        factor * (pulled - scaled * jnp.mean(pulled * scaled, axis=-1, keepdims=True)),
        gain_grad,
    )


def rope_angles(places):
    halfway = HEAD // 2
    freqs = rope_base ** (-(jnp.arange(halfway).astype(jnp.float32) * 2.0 / HEAD))
    angles = places.astype(jnp.float32)[:, None] * freqs[None, :]
    return (jnp.cos(angles), jnp.sin(angles))


def token_places(index):
    inside = index - PROMPT
    return jnp.where(index < PROMPT, index, PROMPT + inside % CONT)


def segment_of(index):
    return jnp.where(index < PROMPT, -1, (index - PROMPT) // CONT)


def visible(query_index, key_index, lengths):
    key_segment = segment_of(key_index)
    key_offset = key_index - PROMPT - key_segment * CONT
    slots = jnp.arange(NCONT, dtype=jnp.int32)
    limits = jnp.sum(jnp.where(key_segment[:, None] == slots[None, :], lengths[None, :], 0), axis=1)
    alive = key_offset < limits
    same = segment_of(query_index)[:, None] == key_segment[None, :]
    causal = key_index[None, :] <= query_index[:, None]
    return causal & ((key_index < PROMPT)[None, :] | same & alive[None, :])


def rotate(values, cosine, sine):
    halfway = values.shape[-1] // 2
    first, second = (values[..., :halfway], values[..., halfway:])
    cosine, sine = (cosine[:, None, :], sine[:, None, :])
    return jnp.concatenate(
        [first * cosine - second * sine, second * cosine + first * sine], axis=-1
    )


def rotate_back(grads, cosine, sine):
    halfway = grads.shape[-1] // 2
    first, second = (grads[..., :halfway], grads[..., halfway:])
    cosine, sine = (cosine[:, None, :], sine[:, None, :])
    return jnp.concatenate(
        [first * cosine + second * sine, second * cosine - first * sine], axis=-1
    )


def join_blocks(pieces, shard_count):
    height = pieces[0].shape[0]
    return jnp.concatenate(
        [member.reshape(height, shard_count, -1) for member in pieces], axis=2
    ).reshape(height, -1)


def split_blocks(merged, breadths, shard_count):
    height = merged.shape[0]
    blocks = merged.reshape(height, shard_count, -1)
    result = []
    offset = 0
    for breadth in breadths:
        result.append(
            blocks[:, :, offset : offset + breadth].reshape(height, shard_count * breadth)
        )
        offset = offset + breadth
    return result


def ahead(operand, shard):
    return jnp.dot(
        operand,
        lax.all_gather(shard, "fsdp", axis=1, tiled=True),
        preferred_element_type=jnp.float32,
    )


def behind(gradient, shard):
    return lax.dot_general(
        gradient,
        lax.all_gather(shard, "fsdp", axis=1, tiled=True),
        (((1,), (1,)), ((), ())),
        preferred_element_type=jnp.float32,
    )


def weight_term(gradient, operand):
    operand_all = lax.all_gather(operand, "fsdp", axis=0, tiled=True)
    owned_columns = lax.all_to_all(gradient, "fsdp", split_axis=1, concat_axis=0, tiled=True)
    return lax.dot_general(
        owned_columns, operand_all, (((0,), (0,)), ((), ())), preferred_element_type=jnp.float32
    )


def on_device(
    activations,
    cotangent,
    continuation_lengths,
    query_weight,
    key_weight,
    value_weight,
    output_weight,
    gate_weight,
    up_weight,
    down_weight,
    attention_gain,
    feedforward_gain,
    moment_query,
    moment_key,
    moment_value,
    moment_output,
    moment_gate,
    moment_up,
    moment_down,
    moment_attention,
    moment_feedforward,
):
    shard_count = lax.axis_size("fsdp")
    kv_width = KV_HEADS * HEAD
    repeat = HEADS // KV_HEADS
    scale = 1.0 / math.sqrt(HEAD)
    gathered = (
        lax.all_gather(query_weight.astype(jnp.bfloat16), "dp", axis=0, tiled=True),
        lax.all_gather(key_weight.astype(jnp.bfloat16), "dp", axis=0, tiled=True),
        lax.all_gather(value_weight.astype(jnp.bfloat16), "dp", axis=0, tiled=True),
        lax.all_gather(output_weight.astype(jnp.bfloat16), "dp", axis=0, tiled=True),
        lax.all_gather(gate_weight.astype(jnp.bfloat16), "dp", axis=0, tiled=True),
        lax.all_gather(up_weight.astype(jnp.bfloat16), "dp", axis=0, tiled=True),
        lax.all_gather(down_weight.astype(jnp.bfloat16), "dp", axis=0, tiled=True),
    )
    merged_attn = join_blocks(gathered[0:3], 1)
    merged_output = gathered[3]
    merged_ffn = join_blocks(gathered[4:6], 1)
    merged_down = gathered[6]
    query_cols = D // shard_count
    key_cols = kv_width // shard_count
    ffn_cols = FF // shard_count
    attn_breadths = (query_cols, key_cols, key_cols)
    ffn_breadths = (ffn_cols, ffn_cols)
    local_rows = activations.shape[1]
    group_rows = local_rows * shard_count
    query_index = lax.axis_index("fsdp") * local_rows + jnp.arange(local_rows, dtype=jnp.int32)
    key_index = jnp.arange(group_rows, dtype=jnp.int32)
    cosine, sine = rope_angles(token_places(query_index))
    sums = [jnp.zeros((matrix.shape[1], matrix.shape[0]), jnp.float32) for matrix in gathered]
    attention_sum = jnp.zeros((D,), jnp.float32)
    feedforward_sum = jnp.zeros((D,), jnp.float32)
    output_list = []
    input_list = []
    for micro_batch in range(activations.shape[0]):
        allowed = visible(query_index, key_index, continuation_lengths[micro_batch])
        inputs = activations[micro_batch].astype(jnp.float32)
        normed_float, factor_one = rms_rows(inputs, attention_gain)
        normed = normed_float.astype(jnp.bfloat16)
        pre_query, pre_key, pre_value = split_blocks(
            ahead(normed, merged_attn), attn_breadths, shard_count
        )
        queries = (
            rotate(pre_query.reshape(local_rows, HEADS, HEAD), cosine, sine)
            .astype(jnp.bfloat16)
            .reshape(local_rows, KV_HEADS, repeat, HEAD)
        )
        keys = rotate(pre_key.reshape(local_rows, KV_HEADS, HEAD), cosine, sine).astype(
            jnp.bfloat16
        )
        values = pre_value.astype(jnp.bfloat16).reshape(local_rows, KV_HEADS, HEAD)
        keys_all, values_all = (
            lax.all_gather(keys, "fsdp", axis=0, tiled=True),
            lax.all_gather(values, "fsdp", axis=0, tiled=True),
        )
        raw = (
            jnp.einsum("qgrd,kgd->grqk", queries, keys_all, preferred_element_type=jnp.float32)
            * scale
        )
        raw = jnp.where(allowed[None, None], raw, floor_score)
        highest = jnp.max(raw, axis=-1, keepdims=True)
        exponent = jnp.exp(raw - highest)
        denominator = jnp.sum(exponent, axis=-1, keepdims=True)
        logsum = highest + jnp.log(denominator)
        probs_low = (exponent / denominator).astype(jnp.bfloat16)
        mixed = (
            jnp.einsum("grqk,kgd->qgrd", probs_low, values_all, preferred_element_type=jnp.float32)
            .reshape(local_rows, D)
            .astype(jnp.bfloat16)
        )
        middle = inputs + ahead(mixed, merged_output)
        normed_two_float, factor_two = rms_rows(middle, feedforward_gain)
        normed_two = normed_two_float.astype(jnp.bfloat16)
        gate, upward = split_blocks(ahead(normed_two, merged_ffn), ffn_breadths, shard_count)
        sigmoid = jax.nn.sigmoid(gate)
        swish = gate * sigmoid
        hidden = (swish * upward).astype(jnp.bfloat16)
        result = middle + ahead(hidden, merged_down)
        output_list.append(result.astype(jnp.bfloat16))
        out_grad = cotangent[micro_batch]
        hidden_grad = behind(out_grad, merged_down)
        sums[6] = sums[6] + weight_term(out_grad, hidden)
        gate_grad = (hidden_grad * upward * sigmoid * (1.0 + gate * (1.0 - sigmoid))).astype(
            jnp.bfloat16
        )
        up_grad = (hidden_grad * swish).astype(jnp.bfloat16)
        ffn_grad = join_blocks((gate_grad, up_grad), shard_count)
        ffn_term = weight_term(ffn_grad, normed_two)
        sums[4] = sums[4] + ffn_term[:ffn_cols]
        sums[5] = sums[5] + ffn_term[ffn_cols:]
        normed_two_grad = behind(ffn_grad, merged_ffn)
        middle_back, feed_gain_grad = rms_back(
            middle, factor_two, feedforward_gain, normed_two_grad
        )
        middle_grad = out_grad.astype(jnp.float32) + middle_back
        branch_grad = middle_grad.astype(jnp.bfloat16)
        sums[3] = sums[3] + weight_term(branch_grad, mixed)
        mixed_grad = (
            behind(branch_grad, merged_output)
            .astype(jnp.bfloat16)
            .reshape(local_rows, KV_HEADS, repeat, HEAD)
        )
        raw_again = (
            jnp.einsum("qgrd,kgd->grqk", queries, keys_all, preferred_element_type=jnp.float32)
            * scale
        )
        raw_again = jnp.where(allowed[None, None], raw_again, floor_score)
        probs_again = jnp.exp(raw_again - logsum)
        value_part = jnp.einsum(
            "grqk,qgrd->kgd",
            probs_again.astype(jnp.bfloat16),
            mixed_grad,
            preferred_element_type=jnp.float32,
        )
        prob_grad = jnp.einsum(
            "qgrd,kgd->grqk", mixed_grad, values_all, preferred_element_type=jnp.float32
        )
        inner = jnp.sum(probs_again * prob_grad, axis=-1, keepdims=True)
        score_grad = (probs_again * (prob_grad - inner)).astype(jnp.bfloat16)
        query_grad = (
            jnp.einsum("grqk,kgd->qgrd", score_grad, keys_all, preferred_element_type=jnp.float32)
            * scale
        )
        key_part = (
            jnp.einsum("grqk,qgrd->kgd", score_grad, queries, preferred_element_type=jnp.float32)
            * scale
        )
        key_grad, value_grad = (
            lax.psum_scatter(
                key_part.astype(jnp.bfloat16), "fsdp", scatter_dimension=0, tiled=True
            ).astype(jnp.float32),
            lax.psum_scatter(
                value_part.astype(jnp.bfloat16), "fsdp", scatter_dimension=0, tiled=True
            ).astype(jnp.float32),
        )
        pre_query_grad = (
            rotate_back(query_grad.reshape(local_rows, HEADS, HEAD), cosine, sine)
            .reshape(local_rows, D)
            .astype(jnp.bfloat16)
        )
        pre_key_grad = (
            rotate_back(key_grad, cosine, sine).reshape(local_rows, kv_width).astype(jnp.bfloat16)
        )
        pre_value_grad = value_grad.reshape(local_rows, kv_width).astype(jnp.bfloat16)
        attn_grad = join_blocks((pre_query_grad, pre_key_grad, pre_value_grad), shard_count)
        attn_term = weight_term(attn_grad, normed)
        sums[0] = sums[0] + attn_term[:query_cols]
        sums[1] = sums[1] + attn_term[query_cols : query_cols + key_cols]
        sums[2] = sums[2] + attn_term[query_cols + key_cols :]
        normed_grad = behind(attn_grad, merged_attn)
        input_back, attn_gain_grad = rms_back(inputs, factor_one, attention_gain, normed_grad)
        input_list.append((middle_grad + input_back).astype(jnp.bfloat16))
        attention_sum = attention_sum + attn_gain_grad
        feedforward_sum = feedforward_sum + feed_gain_grad
    reduced = (
        lax.psum_scatter(
            sums[0].astype(jnp.bfloat16), "dp", scatter_dimension=1, tiled=True
        ).astype(jnp.float32),
        lax.psum_scatter(
            sums[1].astype(jnp.bfloat16), "dp", scatter_dimension=1, tiled=True
        ).astype(jnp.float32),
        lax.psum_scatter(
            sums[2].astype(jnp.bfloat16), "dp", scatter_dimension=1, tiled=True
        ).astype(jnp.float32),
        lax.psum_scatter(
            sums[3].astype(jnp.bfloat16), "dp", scatter_dimension=1, tiled=True
        ).astype(jnp.float32),
        lax.psum_scatter(
            sums[4].astype(jnp.bfloat16), "dp", scatter_dimension=1, tiled=True
        ).astype(jnp.float32),
        lax.psum_scatter(
            sums[5].astype(jnp.bfloat16), "dp", scatter_dimension=1, tiled=True
        ).astype(jnp.float32),
        lax.psum_scatter(
            sums[6].astype(jnp.bfloat16), "dp", scatter_dimension=1, tiled=True
        ).astype(jnp.float32),
    )
    owner_grads = [owned.T for owned in reduced]
    local_square = reduce(jnp.add, [jnp.sum(owned * owned) for owned in owner_grads])
    attention_total, feedforward_total, square_total = lax.psum(
        (attention_sum, feedforward_sum, local_square), ("dp", "fsdp")
    )
    square_sum = (
        square_total
        + jnp.sum(attention_total * attention_total)
        + jnp.sum(feedforward_total * feedforward_total)
    )
    grad_norm = jnp.sqrt(square_sum)
    entry_count = 2 * D * D + 2 * D * kv_width + 3 * D * FF + 2 * D
    limit = clip_level * math.sqrt(entry_count)
    factor = limit / jnp.maximum(grad_norm, limit)
    gradients = owner_grads + [attention_total, feedforward_total]
    old_moments = [
        moment_query,
        moment_key,
        moment_value,
        moment_output,
        moment_gate,
        moment_up,
        moment_down,
        moment_attention,
        moment_feedforward,
    ]
    old_params = [
        query_weight,
        key_weight,
        value_weight,
        output_weight,
        gate_weight,
        up_weight,
        down_weight,
        attention_gain,
        feedforward_gain,
    ]
    new_moments = [
        0.5 * moment + 0.5 * factor * gradient for moment, gradient in zip(old_moments, gradients)
    ]
    new_params = []
    for place, param in enumerate(old_params):
        if place < 7:
            new_params.append(param - step_size * (new_moments[place] + decay_rate * param))
        else:
            new_params.append(param - gain_step * new_moments[place])
    outputs = jnp.stack(output_list)
    input_grad = jnp.stack(input_list)
    return (
        outputs,
        input_grad,
        grad_norm,
        new_moments[0],
        new_moments[1],
        new_moments[2],
        new_moments[3],
        new_moments[4],
        new_moments[5],
        new_moments[6],
        new_moments[7],
        new_moments[8],
        new_params[0],
        new_params[1],
        new_params[2],
        new_params[3],
        new_params[4],
        new_params[5],
        new_params[6],
        new_params[7],
        new_params[8],
    )


CORE, SIDE_A, SIDE_B = 1, 2, 4
CHIPS = 4
CHUNKS = 4
MB = 1024 * 1024


def across(value, mask):
    count = lax.axis_size("dp")
    return lax.ppermute(value, "dp", [(place, place ^ mask) for place in range(count)])


def along(value, mask):
    count = lax.axis_size("fsdp")
    return lax.ppermute(value, "fsdp", [(place, place ^ mask) for place in range(count)])


def pick(values, index):
    return lax.dynamic_index_in_dim(values, index, 0, keepdims=False)


def after(value, *earlier):
    return lax.optimization_barrier((value, earlier))[0]


def trade_planes(parts, plane):
    found = [pick(parts, plane)]
    for mask in range(1, CHUNKS):
        found.append(along(pick(parts, plane ^ mask), mask))
    found = jnp.stack(found)
    return [pick(found, label ^ plane) for label in range(CHUNKS)]


def gather_planes(block):
    one, two = along(block, 1), along(block, 2)
    return [block, one, two, along(two, 1)]


def sum_planes(parts):
    two = (parts[2].astype(jnp.float32) + along(parts[3], 1).astype(jnp.float32)).astype(jnp.bfloat16)
    return (
        parts[0].astype(jnp.float32)
        + along(parts[1], 1).astype(jnp.float32)
        + along(two, 2).astype(jnp.float32)
    )


def sum_all(value):
    for mask in (CORE, SIDE_A, SIDE_B):
        value = value + across(value, mask)
    for mask in (1, 2):
        value = value + along(value, mask)
    return value


def to_planes(array, core, plane):
    halves = array.reshape(2, 2, array.shape[1] // 2, array.shape[2]).swapaxes(0, 1)
    keep = pick(halves, core)
    came = across(pick(halves, 1 - core), CORE)
    swap = core == 1
    parts = jnp.concatenate([jnp.where(swap, came, keep), jnp.where(swap, keep, came)])
    return trade_planes(parts, plane)


def from_planes(chunks, core, plane):
    groups = trade_planes(jnp.stack(chunks), plane)
    pairs = jnp.stack([jnp.stack(groups[:2]), jnp.stack(groups[2:])])
    keep = pick(pairs, core)
    came = across(pick(pairs, 1 - core), CORE)
    swap = core == 1
    return jnp.concatenate([jnp.where(swap, came, keep), jnp.where(swap, keep, came)], axis=1)


MESH = pl.DeviceIdType.MESH
SLOT = {0: 0, SIDE_A: 1, SIDE_B: 2}
ROUTES = ((SIDE_A, SIDE_B), (SIDE_B, SIDE_A))
STRIPE = 16


def flip(place, mask):
    for bit in (1, 2, 4):
        if mask & bit:
            place = place + bit - 2 * bit * lax.rem(lax.div(place, bit), 2)
    return place


def peer(mask, planes=0):
    return (flip(lax.axis_index("dp"), mask), flip(lax.axis_index("fsdp"), planes))


SIDES = ((CORE, 0), (SIDE_A, 0), (SIDE_B, 0))
PLANE = tuple((mask, 0) for mask in range(1, 8))
PLANES = tuple((0, mask) for mask in range(1, CHUNKS))


def meet(others):
    barrier = pltpu.get_barrier_semaphore()
    for mask, planes in others:
        pl.semaphore_signal(barrier, inc=1, device_id=peer(mask, planes), device_id_type=MESH)
    pl.semaphore_wait(barrier, len(others))


class Remote:
    def __init__(self, wires, source, target, mask, planes=0):
        self.wires, self.source, self.target, self.mask = wires, source, target, (mask, planes)
        self.place = wires.count
        wires.count += 1

    def make(self):
        return pltpu.make_async_remote_copy(
            src_ref=self.source,
            dst_ref=self.target,
            send_sem=self.wires.send.at[self.place],
            recv_sem=self.wires.recv.at[self.place],
            device_id=peer(*self.mask),
            device_id_type=MESH,
        )

    def start(self):
        self.make().start()

    def arrived(self):
        self.make().wait_recv()

    def left(self):
        self.make().wait_send()


class Wires:
    def __init__(self, send, recv, local):
        self.send, self.recv, self.local = send, recv, local
        self.count = 0
        self.local_count = 0

    def load(self, pairs):
        copies = [
            pltpu.make_async_copy(source, target, self.local.at[place])
            for place, (source, target) in enumerate(pairs)
        ]
        for copy in copies:
            copy.start()
        for copy in copies:
            copy.wait()


class Gather:
    def __init__(self, wires, own, target):
        rows = target.shape[2] // 2
        self.wires, self.own = wires, own
        self.near, self.far, self.core_first, self.core_near, self.core_far = [], [], [], [], []
        self.home = []

        def place(chunk, slot, half):
            return target.at[chunk, slot, pl.ds(half * rows, rows)]

        for chunk, (first, second) in enumerate(ROUTES):
            near, far = SLOT[first], SLOT[second]
            self.home.append((own[chunk], place(chunk, 0, 0)))
            self.near.append(Remote(wires, own[chunk], place(chunk, near, 0), first))
            self.core_first.append(Remote(wires, own[chunk], place(chunk, 0, 1), CORE))
            self.far.append(Remote(wires, own[chunk], place(chunk, far, 0), second))
            self.far.append(Remote(wires, place(chunk, near, 0), place(chunk, 3, 0), second))
            self.core_near.append(Remote(wires, place(chunk, near, 0), place(chunk, near, 1), CORE))
            self.core_far.append(Remote(wires, place(chunk, far, 0), place(chunk, far, 1), CORE))
            self.core_far.append(Remote(wires, place(chunk, 3, 0), place(chunk, 3, 1), CORE))

    def first(self):
        for copy in self.near + self.core_first:
            copy.start()
        self.wires.load(self.home)

    def second(self):
        for chunk, copy in enumerate(self.near):
            copy.arrived()
            self.far[2 * chunk].start()
            self.far[2 * chunk + 1].start()
            self.core_near[chunk].start()

    def third(self):
        for place, copy in enumerate(self.far):
            copy.arrived()
            self.core_far[place].start()

    def last(self):
        for copy in self.core_first + self.core_near + self.core_far:
            copy.arrived()
        for copy in self.near + self.far + self.core_first + self.core_near + self.core_far:
            copy.left()

    def steps(self):
        return [self.first, self.second, self.third, self.last]


class Scatter:
    def __init__(self, wires, own, other, landing, stage, done):
        from_core, from_far, from_near = landing
        self.wires, self.own, self.landing, self.stage, self.done = wires, own, landing, stage, done
        self.core = [Remote(wires, other.at[chunk], from_core.at[chunk], CORE) for chunk in range(2)]
        self.far = [
            Remote(wires, stage[0].at[chunk], from_far.at[chunk], first)
            for chunk, (_, first) in enumerate(ROUTES)
        ]
        self.near = [
            Remote(wires, stage[2].at[chunk, 0], from_near.at[chunk], last)
            for chunk, (last, _) in enumerate(ROUTES)
        ]

    def first(self):
        for copy in self.core:
            copy.start()

    def second(self):
        left, right = self.stage[:2]
        pairs = []
        for chunk, (_, first) in enumerate(ROUTES):
            self.core[chunk].arrived()
            for place, slot in enumerate((SLOT[first], 3)):
                pairs.append((self.own.at[chunk, slot], left.at[chunk, place]))
                pairs.append((self.landing[0].at[chunk, slot], right.at[chunk, place]))
        self.wires.load(pairs)
        for chunk in range(2):

            @pl.loop(0, left.shape[2] // STRIPE)
            def _(step):
                span = pl.ds(step * STRIPE, STRIPE)
                total = left[chunk, :, span].astype(jnp.float32) + right[chunk, :, span].astype(jnp.float32)
                left[chunk, :, span] = total.astype(jnp.bfloat16)

            self.far[chunk].start()

    def third(self):
        stage = self.stage[2]
        pairs = []
        for chunk, (last, _) in enumerate(ROUTES):
            self.far[chunk].arrived()
            pairs.append((self.own.at[chunk, SLOT[last]], stage.at[chunk, 0]))
            pairs.append((self.landing[0].at[chunk, SLOT[last]], stage.at[chunk, 1]))
            pairs.append((self.landing[1].at[chunk, 1], stage.at[chunk, 2]))
        self.wires.load(pairs)
        for chunk in range(2):

            @pl.loop(0, stage.shape[2] // STRIPE)
            def _(step):
                span = pl.ds(step * STRIPE, STRIPE)
                total = stage[chunk, 0, span].astype(jnp.float32)
                for place in range(1, 3):
                    total += stage[chunk, place, span].astype(jnp.float32)
                stage[chunk, 0, span] = total.astype(jnp.bfloat16)

            self.near[chunk].start()
        for copy in self.far:
            copy.left()

    def last(self):
        stage = self.stage[3]
        for chunk in range(2):
            self.near[chunk].arrived()
            self.wires.load(
                [
                    (self.own.at[chunk, 0], stage.at[0]),
                    (self.landing[0].at[chunk, 0], stage.at[1]),
                    (self.landing[1].at[chunk, 0], stage.at[2]),
                    (self.landing[2].at[chunk], stage.at[3]),
                ]
            )

            @pl.loop(0, stage.shape[1] // STRIPE)
            def _(step):
                span = pl.ds(step * STRIPE, STRIPE)
                total = stage[0, span].astype(jnp.float32)
                for place in range(1, 4):
                    total += stage[place, span].astype(jnp.float32)
                self.done(chunk, span, total)

        for copy in self.near + self.core:
            copy.left()

    def steps(self):
        return [self.first, self.second, self.third, self.last]


def stage_shapes(rows, width):
    return [
        pltpu.VMEM((2, 2, rows, width), jnp.bfloat16),
        pltpu.VMEM((2, 2, rows, width), jnp.bfloat16),
        pltpu.VMEM((2, 3, rows, width), jnp.bfloat16),
        pltpu.VMEM((4, rows, width), jnp.bfloat16),
    ]


def landing_shapes(rows, width):
    return [
        jax.ShapeDtypeStruct((2, CHIPS, rows, width), jnp.bfloat16),
        jax.ShapeDtypeStruct((2, 2, rows, width), jnp.bfloat16),
        jax.ShapeDtypeStruct((2, rows, width), jnp.bfloat16),
    ]


def partial_shapes(rows, width):
    return [jax.ShapeDtypeStruct((2, CHIPS, rows, width), jnp.bfloat16)] * 2


def wire_shapes(count):
    return [
        pltpu.SemaphoreType.DMA((count,)),
        pltpu.SemaphoreType.DMA((count,)),
        pltpu.SemaphoreType.DMA((8,)),
    ]


def call(kernel, identity, inputs, outputs, scratch, megabytes):
    return pl.pallas_call(
        kernel,
        in_specs=[pl.BlockSpec(memory_space=place) for _, place in inputs],
        out_specs=[pl.BlockSpec(memory_space=place) for _, place in outputs],
        out_shape=[shape for shape, _ in outputs],
        scratch_shapes=scratch,
        compiler_params=pltpu.CompilerParams(
            collective_id=identity, has_side_effects=True, vmem_limit_bytes=megabytes * MB
        ),
    )(*[array for array, _ in inputs])


HBM, VMEM, SMEM = pl.ANY, pltpu.VMEM, pltpu.SMEM


def move_rows(source, target):
    @pl.loop(0, source.shape[0] // STRIPE)
    def _(step):
        span = pl.ds(step * STRIPE, STRIPE)
        target[span] = source[span]


def half_rows(index, rows):
    return pl.ds(pl.multiple_of(index * rows, STRIPE), rows)


def columns_of(index, columns):
    return pl.ds(pl.multiple_of(index * columns, columns), columns)


def at_step(step, actions):
    for when, action in actions.items():
        pl.when(step == when)(action)


def project_phase(gathered, states, weight_ref, cosine, sine, actions):
    tokens = gathered.shape[2]

    def body(rows_ref, cosine_ref, sine_ref, out):
        at_step(pl.program_id(0) * CHIPS + pl.program_id(1), actions)
        product = dot(rows_ref[0, 0], weight_ref[...].reshape(D, 3 * HEAD))
        angles = (cosine_ref[0], sine_ref[0])
        query = spin(product[:, :HEAD], *angles) * (1.0 / math.sqrt(HEAD))
        key = spin(product[:, HEAD : 2 * HEAD], *angles)
        out[0, 0] = jnp.concatenate([query, key, product[:, 2 * HEAD :]], axis=1).astype(jnp.bfloat16)

    here = lambda chunk, chip: (chunk, chip, 0, 0)
    table = pl.BlockSpec((1, tokens, HEAD // 2), lambda chunk, chip: (chunk, 0, 0))
    pltpu.emit_pipeline(
        body,
        grid=(2, CHIPS),
        in_specs=[pl.BlockSpec((1, 1, tokens, gathered.shape[3]), here), table, table],
        out_specs=[pl.BlockSpec((1, 1, tokens, 3 * HEAD), here)],
    )(gathered, cosine, sine, states)


def attend_phase(pair, states, mixed, own, other, lengths_ref, places, weight_ref, keys, values, actions):
    tokens, rows, width = mixed.shape[2], own.shape[2], own.shape[3]
    blocks = 2 * (pair + 1)

    def body(*refs):
        state_refs, (mixed_ref, own_ref, other_ref) = refs[: pair + 1], refs[pair + 1 :]
        chip, side_at = pl.program_id(0), pl.program_id(1)
        at_step(2 * chip + side_at, actions)

        @pl.when(side_at == 0)
        def _():
            for block in range(blocks):
                ref = state_refs[block // 2]
                keys[pl.ds(block * tokens, tokens)] = ref[block % 2, 0, :, HEAD : 2 * HEAD]
                values[pl.ds(block * tokens, tokens)] = ref[block % 2, 0, :, 2 * HEAD :]

        for side in range(2):

            @pl.when(side_at == side)
            def _():
                chunk = 2 * pair + side
                count = tokens * (chunk + 1)
                scores = dot_t(state_refs[pair][side, 0, :, :HEAD], keys[:count])
                mask = seen(places[0][...], places[1][...], chunk, count, tokens, lengths_ref, chip)
                scores = jnp.where(mask, scores, floor_score)
                highest = jnp.max(scores, axis=1, keepdims=True)
                exponent = jnp.exp(scores - highest)
                total = jnp.sum(exponent, axis=1, keepdims=True)
                probs = (exponent * (1.0 / total)).astype(jnp.bfloat16)
                mixed_ref[0, 0] = dot(probs, values[:count]).astype(jnp.bfloat16)

        partial = dot(mixed_ref[0, 0], weight_ref[...]).astype(jnp.bfloat16)
        own_ref[0, 0] = partial[:rows]
        other_ref[0, 0] = partial[rows:]

    here = lambda chip, side: (side, chip, 0, 0)
    state = pl.BlockSpec((2, 1, tokens, 3 * HEAD), lambda chip, side: (0, chip, 0, 0))
    pltpu.emit_pipeline(
        body,
        grid=(CHIPS, 2),
        in_specs=[state] * (pair + 1),
        out_specs=[pl.BlockSpec((1, 1, tokens, HEAD), here)] + [pl.BlockSpec((1, 1, rows, width), here)] * 2,
    )(*states[: pair + 1], mixed, own, other)


def attend_back_phase(
    pair, branch, states, head_grads, own, other, lengths_ref, places, out_weight, weight_ref,
    tables, keys, values, sums, late_sums, actions
):
    tokens, rows, width = branch.shape[2], own.shape[2], own.shape[3]
    blocks = 2 * (pair + 1)
    edge = 2 * tokens

    def body(*refs):
        branch_ref, state_refs = refs[0], refs[1 : pair + 2]
        cosine_ref, sine_ref, grads_ref, own_ref, other_ref = refs[pair + 2 :]
        chip, step = pl.program_id(0), pl.program_id(1)
        at_step(2 * chip + step, actions)

        @pl.when(step == 0)
        def _():
            for block in range(blocks):
                ref = state_refs[block // 2]
                keys[pl.ds(block * tokens, tokens)] = ref[block % 2, 0, :, HEAD : 2 * HEAD]
                values[pl.ds(block * tokens, tokens)] = ref[block % 2, 0, :, 2 * HEAD :]
            if pair == 1:
                for place in range(2):
                    sums[place][chip] = jnp.zeros(sums[place].shape[1:], jnp.float32)
                    late_sums[place][...] = jnp.zeros(late_sums[place].shape, jnp.float32)

        def add(place, term):
            early = min(term.shape[0], edge)
            sums[place][chip, :early] += term[:early]
            if term.shape[0] > edge:
                late_sums[place][: term.shape[0] - edge] += term[edge:]

        for side in range(2):

            @pl.when(step == 1 - side)
            def _():
                chunk = 2 * pair + side
                count = tokens * (chunk + 1)
                mixed_grad = dot_t(branch_ref[0, 0], out_weight[...]).astype(jnp.bfloat16)
                query = state_refs[pair][side, 0, :, :HEAD]
                scores = dot_t(query, keys[:count])
                mask = seen(places[0][...], places[1][...], chunk, count, tokens, lengths_ref, chip)
                scores = jnp.where(mask, scores, floor_score)
                highest = jnp.max(scores, axis=1, keepdims=True)
                exponent = jnp.exp(scores - highest)
                probs = exponent * (1.0 / jnp.sum(exponent, axis=1, keepdims=True))
                add(1, dot_tn(probs.astype(jnp.bfloat16), mixed_grad))
                prob_grad = dot_t(mixed_grad, values[:count])
                inner = jnp.sum(probs * prob_grad, axis=1, keepdims=True)
                score_grad = (probs * (prob_grad - inner)).astype(jnp.bfloat16)
                add(0, dot_tn(score_grad, query))
                query_grad = dot(score_grad, keys[:count]) * (1.0 / math.sqrt(HEAD))
                angles = (cosine_ref[0], sine_ref[0])
                span = slice(side * tokens, (side + 1) * tokens)
                if pair == 1:
                    key_grad, value_grad = late_sums[0][span], late_sums[1][span]
                else:
                    key_grad, value_grad = sums[0][chip, span], sums[1][chip, span]
                grads_ref[0, 0] = jnp.concatenate(
                    [spin_back(query_grad, *angles), spin_back(key_grad, *angles), value_grad], axis=1
                ).astype(jnp.bfloat16)

        partial = dot_t(grads_ref[0, 0], weight_ref[...].reshape(D, 3 * HEAD)).astype(jnp.bfloat16)
        own_ref[0, 0] = partial[:rows]
        other_ref[0, 0] = partial[rows:]

    here = lambda chip, step: (1 - step, chip, 0, 0)
    state = pl.BlockSpec((2, 1, tokens, 3 * HEAD), lambda chip, step: (0, chip, 0, 0))
    table = pl.BlockSpec((1, tokens, HEAD // 2), lambda chip, step: (1 - step, 0, 0))
    pltpu.emit_pipeline(
        body,
        grid=(CHIPS, 2),
        in_specs=[pl.BlockSpec((1, 1, tokens, width), here)] + [state] * (pair + 1) + [table] * 2,
        out_specs=[pl.BlockSpec((1, 1, tokens, 3 * HEAD), here)]
        + [pl.BlockSpec((1, 1, rows, width), here)] * 2,
    )(branch, *states[: pair + 1], *tables, head_grads, own, other)


def feed_phase(rows_in, grads_in, hidden, unit_grads, back_parts, out_parts, weights, actions):
    tokens, width = rows_in.shape[2:]
    rows = tokens // 2
    shards, columns = weights.shape[0], weights.shape[2]
    share = columns // 2

    def body(rows_ref, out_grad_ref, hidden_ref, units_ref, back_own, back_other, out_own, out_other):
        at_step(pl.program_id(0) * CHIPS + pl.program_id(1), actions)
        hidden_grad = None
        for shard in range(shards):
            grad = out_grad_ref[0, 0, :, shard * columns : (shard + 1) * columns]
            term = dot_t(grad, weights[shard, width:, :])
            hidden_grad = term if hidden_grad is None else hidden_grad + term
        back = None
        for shard in range(shards):
            both = dot(rows_ref[0, 0], weights[shard, :width, :])
            gate, upward = both[:, :share], both[:, share:]
            grad = hidden_grad[:, shard * share : (shard + 1) * share]
            sigmoid = jax.nn.sigmoid(gate)
            swish = gate * sigmoid
            hidden_ref[0, 0, :, shard * share : (shard + 1) * share] = (swish * upward).astype(jnp.bfloat16)
            gate_grad = grad * upward * sigmoid * (1.0 + gate * (1.0 - sigmoid))
            units_ref[shard, 0, 0] = jnp.concatenate([gate_grad, grad * swish], axis=1).astype(jnp.bfloat16)
            term = dot_t(units_ref[shard, 0, 0], weights[shard, :width, :])
            back = term if back is None else back + term
        back = back.astype(jnp.bfloat16)
        back_own[0, 0] = back[:rows]
        back_other[0, 0] = back[rows:]
        for shard in range(shards):
            span = slice(shard * columns, (shard + 1) * columns)
            value = dot(hidden_ref[0, 0], weights[shard, width:, :]).astype(jnp.bfloat16)
            out_own[0, 0, :, span] = value[:rows]
            out_other[0, 0, :, span] = value[rows:]

    here = lambda chunk, chip: (chunk, chip, 0, 0)
    wide = pl.BlockSpec((1, 1, tokens, width), here)
    narrow = pl.BlockSpec((1, 1, rows, width), here)
    pltpu.emit_pipeline(
        body,
        grid=(2, CHIPS),
        in_specs=[wide, wide],
        out_specs=[
            pl.BlockSpec((1, 1, tokens, hidden.shape[3]), here),
            pl.BlockSpec((shards, 1, 1, tokens, columns), lambda chunk, chip: (0, chunk, chip, 0, 0)),
        ]
        + [narrow] * 4,
    )(rows_in, grads_in, hidden, unit_grads, *back_parts, *out_parts)


def down_grad_phase(hidden, grads, out, total, actions):
    _, chips, tokens, units = hidden[0].shape
    planes, _, columns = out.shape

    def body(*refs):
        out_ref = refs[4]
        block, step = pl.program_id(0), pl.program_id(1)
        at_step(8 * block + step, actions)

        @pl.when(step == 0)
        def _():
            total[...] = jnp.zeros(total.shape, jnp.float32)

        for place in range(2):

            @pl.when(lax.div(step, 4) == place)
            def _():
                left, right = refs[2 * place], refs[2 * place + 1]
                total[...] += dot_tn(
                    left[0].reshape(2 * tokens, units), right[0].reshape(2 * tokens, columns)
                )

        @pl.when(step == 7)
        def _():
            out_ref[0] = total[...].astype(jnp.bfloat16)

    specs, operands = [], []
    for pair in (1, 0):
        first = 0 if pair == 1 else 4

        def at(step, first=first):
            return jnp.clip(step - first, 0, 3)

        specs.append(
            pl.BlockSpec(
                (1, 2, tokens, units),
                lambda block, step, at=at: (lax.div(at(step), 2), lax.rem(at(step), 2), 0, 0),
            )
        )
        specs.append(
            pl.BlockSpec(
                (1, 2, tokens, columns),
                lambda block, step, at=at: (lax.div(at(step), 2), lax.rem(at(step), 2), 0, block),
            )
        )
        operands += [hidden[pair], grads[pair]]
    pltpu.emit_pipeline(
        body,
        grid=(planes, 8),
        in_specs=specs,
        out_specs=[pl.BlockSpec((1, units, columns), lambda block, step: (block, 0, 0))],
    )(*operands, out)


def bf16(*shape):
    return jax.ShapeDtypeStruct(shape, jnp.bfloat16)


def f32(*shape):
    return jax.ShapeDtypeStruct(shape, jnp.float32)


def start_up(
    activations, cotangent, head_block, out_block, unit_block, down_block, lengths_block, gain
):
    _, tokens, width = activations.shape
    rows = tokens // 2
    devices, unit_rows, columns = unit_block.shape
    down_rows = down_block.shape[1]
    planes, _, sub_rows, _ = head_block.shape
    edge = devices * unit_rows

    def kernel(*refs):
        act, cot, head_in, out_in, unit_in, down_in, length_in, gain_ref = refs[:8]
        own_rows, own_grads, gathered = refs[8], refs[9], refs[10:12]
        head_weight, head_output, feed_own, lengths_all = refs[12:16]
        act_groups, cot_groups, traded, spread, other_half, normed = refs[16:22]
        wires = Wires(*refs[22:])
        place, plane = lax.axis_index("dp"), lax.axis_index("fsdp")
        core = lax.rem(place, 2)

        def half(index):
            return pl.ds(pl.multiple_of(index * rows, STRIPE), rows)

        def move(source, target):
            @pl.loop(0, rows // STRIPE)
            def _(step):
                span = pl.ds(step * STRIPE, STRIPE)
                target[span] = source[span]

        def trade(array, groups, own):
            label = [2 * core + group for group in range(2)]
            inside = [
                Remote(wires, array.at[group, half(1 - core)], groups.at[label[group]], CORE)
                for group in range(2)
            ]
            outside = [
                Remote(wires, groups.at[flip(plane, mask)], own.at[plane], 0, mask)
                for mask in range(1, CHUNKS)
            ]

            def keep():
                for group in range(2):
                    move(array.at[group, half(core)], groups.at[label[group]])

            return inside, keep, outside, lambda: move(groups.at[plane], own.at[plane])

        act_inside, act_keep, act_outside, act_own = trade(act, act_groups, own_rows)
        cot_inside, cot_keep, cot_outside, cot_own = trade(cot, cot_groups, own_grads)
        head_trade = [
            Remote(wires, head_in.at[flip(plane, mask)], traded.at[plane], 0, mask)
            for mask in range(1, CHUNKS)
        ]
        head_spread, feed_spread = [], []
        for mask in range(1, devices):
            other = flip(place, mask)
            head_spread.append(
                Remote(
                    wires,
                    traded.at[lax.div(other, 2), lax.rem(other, 2)],
                    spread.at[place, plane],
                    mask,
                )
            )
            feed_spread.append(
                Remote(
                    wires,
                    unit_in.at[other],
                    feed_own.at[pl.ds(pl.multiple_of(place * unit_rows, unit_rows), unit_rows)],
                    mask,
                )
            )
            feed_spread.append(
                Remote(
                    wires,
                    down_in.at[other],
                    feed_own.at[pl.ds(pl.multiple_of(edge + place * down_rows, down_rows), down_rows)],
                    mask,
                )
            )
            feed_spread.append(Remote(wires, length_in, lengths_all.at[place], mask))

        def over_planes(block):
            mine, theirs = block(plane), block(flip(plane, 2))
            return (
                [Remote(wires, mine, mine, 0, 1), Remote(wires, mine, mine, 0, 2)],
                Remote(wires, theirs, theirs, 0, 1),
            )

        head_near, head_relay = over_planes(lambda index: spread.at[:, index])
        out_near, out_relay = over_planes(
            lambda index: head_output.at[:, pl.ds(pl.multiple_of(index * columns, columns), columns)]
        )
        core_half = Remote(wires, spread.at[:, :, :, pl.ds(HEAD, HEAD)], other_half, CORE)
        moves = [
            Gather(wires, [normed.at[2 * pair], normed.at[2 * pair + 1]], gathered[pair])
            for pair in range(2)
        ]

        meet(PLANE + PLANES)
        for copy in act_inside + cot_inside + head_trade + feed_spread:
            copy.start()
        act_keep()
        for copy in act_inside:
            copy.arrived()
        for copy in act_outside:
            copy.start()
        cot_keep()
        act_own()
        traded[plane] = head_in[plane]
        columns_at = pl.ds(pl.multiple_of(plane * columns, columns), columns)
        head_output[:, columns_at] = out_in[...]
        feed_own[pl.ds(pl.multiple_of(place * unit_rows, unit_rows), unit_rows)] = unit_in[place]
        feed_own[pl.ds(pl.multiple_of(edge + place * down_rows, down_rows), down_rows)] = down_in[place]
        lengths_all[place] = length_in[...]
        for copy in head_trade:
            copy.arrived()
        for copy in head_spread:
            copy.start()
        spread[place, plane] = traded[lax.div(place, 2), core]
        for copy in head_spread + cot_inside:
            copy.arrived()
        cot_own()
        for copy in act_outside:
            copy.arrived()
        for copy in head_near + out_near + cot_outside:
            copy.start()

        for chunk in range(CHUNKS):

            @pl.loop(0, rows // STRIPE)
            def _(step):
                span = pl.ds(step * STRIPE, STRIPE)
                values = own_rows[chunk, span].astype(jnp.float32)
                factor = lax.rsqrt(jnp.mean(values * values, axis=1, keepdims=True) + epsilon)
                normed[chunk, span] = (values * factor * gain_ref[...]).astype(jnp.bfloat16)

        moves[0].first()
        moves[0].second()
        moves[1].first()
        moves[0].third()
        moves[1].second()
        for copy in head_near + out_near:
            copy.arrived()
        head_relay.start()
        out_relay.start()
        moves[0].last()
        moves[1].third()
        head_relay.arrived()
        core_half.start()
        moves[1].last()
        out_relay.arrived()
        core_half.arrived()
        head_weight[:, :, :, :HEAD] = spread[:, :, :, :HEAD]
        for index in range(2):

            @pl.when(core == index)
            def _():
                mine, theirs = (1 + index) * HEAD, (2 - index) * HEAD
                head_weight[:, :, :, mine : mine + HEAD] = spread[:, :, :, HEAD:]
                head_weight[:, :, :, theirs : theirs + HEAD] = other_half[...]

        for copy in feed_spread + cot_outside:
            copy.arrived()
        for copy in (
            act_inside + cot_inside + head_trade + feed_spread + act_outside + head_spread
            + head_near + out_near + [head_relay, out_relay, core_half] + cot_outside
        ):
            copy.left()

    own = bf16(CHUNKS, rows, width)
    outs = call(
        kernel,
        1,
        [(activations, VMEM), (cotangent, VMEM), (head_block, VMEM), (out_block, VMEM)]
        + [(unit_block, VMEM), (down_block, VMEM), (lengths_block, VMEM), (gain, VMEM)],
        [(own, VMEM), (own, VMEM)]
        + [(bf16(2, CHIPS, tokens, width), HBM)] * 2
        + [(bf16(devices, planes, sub_rows, 3 * HEAD), VMEM), (bf16(HEAD, width), VMEM)]
        + [(bf16(devices * (unit_rows + down_rows), columns), VMEM)]
        + [(jax.ShapeDtypeStruct((devices,) + lengths_block.shape, jnp.int32), VMEM)],
        [
            pltpu.VMEM((CHUNKS, rows, width), jnp.bfloat16),
            pltpu.VMEM((CHUNKS, rows, width), jnp.bfloat16),
            pltpu.VMEM((planes, 2, sub_rows, columns), jnp.bfloat16),
            pltpu.VMEM((devices, planes, sub_rows, columns), jnp.bfloat16),
            pltpu.VMEM((devices, planes, sub_rows, HEAD), jnp.bfloat16),
            pltpu.VMEM((CHUNKS, rows, width), jnp.bfloat16),
        ]
        + wire_shapes(90),
        56,
    )
    return outs[0], outs[1], outs[2:4], outs[4], outs[5], outs[6], outs[7]


def attend_and_norm(
    rows_all, out_grads, feed_own, weight, cosine, sine, lengths, places, out_weight, inputs, gain
):
    _, rows, width = inputs.shape
    tokens = 2 * rows
    planes = CHUNKS
    whole_pair = bf16(2, CHIPS, tokens, width)

    def kernel(*refs):
        gathered, grads_ref, feed_ref, head_ref, cosine_ref, sine_ref = refs[:2], *refs[2:7]
        lengths_ref, place_q, place_k, weight_ref, inputs_ref, gain_ref = refs[7:13]
        refs = refs[13:]
        states, mixed, middle, normed, target, grads_all, feed_all = refs[:2], refs[2:4], *refs[4:9]
        parts, landings = (refs[9:11], refs[11:13]), (refs[13:16], refs[16:19])
        stage, keys, values, normed_late = refs[19:23], refs[23], refs[24], refs[25]
        wires = Wires(*refs[26:])
        plane = lax.axis_index("fsdp")

        def finish(pair):
            def done(chunk, span, total):
                at = 2 * pair + chunk
                total = total + inputs_ref[at, span].astype(jnp.float32)
                middle[at, span] = total
                factor = lax.rsqrt(jnp.mean(total * total, axis=1, keepdims=True) + epsilon)
                kept = normed if pair == 0 else normed_late
                kept[chunk, span] = (total * factor * gain_ref[...]).astype(jnp.bfloat16)

            return done

        sums = [
            Scatter(wires, *parts[pair], landings[pair], stage, finish(pair)) for pair in range(2)
        ]
        move = Gather(wires, [normed_late.at[0], normed_late.at[1]], target)
        grad_move = Gather(wires, [grads_ref.at[2], grads_ref.at[3]], grads_all)
        near = Remote(wires, feed_ref, feed_all.at[plane], 0, 1)
        across_middle = Remote(wires, feed_ref, feed_all.at[plane], 0, 2)
        relay = Remote(
            wires, feed_all.at[flip(plane, 2)], feed_all.at[flip(plane, 2)], 0, 1
        )
        places_in = (place_q, place_k)

        meet(SIDES + PLANES[:2])
        near.start()
        across_middle.start()
        grad_move.first()
        wires.load([(feed_ref, feed_all.at[plane])])
        project_phase(
            gathered[0], states[0], head_ref, cosine_ref.at[0], sine_ref.at[0], {7: grad_move.second}
        )
        project_phase(gathered[1], states[1], head_ref, cosine_ref.at[1], sine_ref.at[1], {})
        attend_phase(
            1, states, mixed[1], *parts[1], lengths_ref, places_in, weight_ref, keys, values,
            {3: grad_move.third},
        )
        sums[1].first()
        attend_phase(
            0, states, mixed[0], *parts[0], lengths_ref, places_in, weight_ref, keys, values,
            {5: sums[1].second},
        )
        sums[0].first()
        grad_move.last()
        sums[1].third()
        sums[0].second()
        sums[1].last()
        move.first()
        sums[0].third()
        across_middle.arrived()
        relay.start()
        move.second()
        sums[0].last()
        move.third()
        move.last()
        near.arrived()
        relay.arrived()
        for copy in (near, across_middle, relay):
            copy.left()

    pair_parts = [(shape, HBM) for shape in partial_shapes(rows, width)]
    landing = [(shape, HBM) for shape in landing_shapes(rows, width)]
    outs = call(
        kernel,
        2,
        [(rows_all[0], HBM), (rows_all[1], HBM), (out_grads, VMEM), (feed_own, VMEM)]
        + [(weight, VMEM), (cosine, HBM), (sine, HBM)]
        + [(lengths, SMEM), (places[0], VMEM), (places[1], VMEM), (out_weight, VMEM)]
        + [(inputs, VMEM), (gain, VMEM)],
        [(bf16(2, CHIPS, tokens, 3 * HEAD), HBM)] * 2
        + [(bf16(2, CHIPS, tokens, HEAD), HBM)] * 2
        + [(f32(CHUNKS, rows, width), VMEM), (bf16(2, rows, width), VMEM)]
        + [(whole_pair, HBM)] * 2
        + [(bf16(planes, *feed_own.shape), HBM)]
        + pair_parts * 2
        + landing * 2,
        stage_shapes(rows, width)
        + [pltpu.VMEM((CHUNKS * tokens, HEAD), jnp.bfloat16)] * 2
        + [pltpu.VMEM((2, rows, width), jnp.bfloat16)]
        + wire_shapes(50),
        60,
    )
    return outs[:2], outs[2:4], outs[4], outs[5], outs[6], outs[7], outs[8]


def norm_back(values, gain, gradient):
    factor = lax.rsqrt(jnp.mean(values * values, axis=1, keepdims=True) + epsilon)
    scaled = values * factor
    pulled = gradient * gain
    back = factor * (pulled - scaled * jnp.mean(pulled * scaled, axis=1, keepdims=True))
    return back, gradient * scaled


def feed_forward(normed_own, normed_late, grads_late, weights, middle, out_grad_own, gain, units):
    _, rows, width = middle.shape
    tokens = 2 * rows
    shards, columns = weights.shape[0], weights.shape[2]
    whole_pair = bf16(2, CHIPS, tokens, width)

    def kernel(*refs):
        normed_ref, normed_late_ref, grads_late_ref = refs[:3]
        weight_ref, middle_ref, own_grad, gain_ref = refs[3:7]
        refs = (None, *refs)
        normed_early, branch, grads_early = refs[8], refs[9], refs[27]
        hidden, unit_grads = refs[10:12], refs[12:14]
        back_parts, out_parts = (refs[14:16], refs[16:18]), (refs[18:20], refs[20:22])
        middle_grad, gain_sum, landing = refs[22], refs[23], refs[24:27]
        down_parts = refs[28]
        stage, own_branch, wires = refs[29:33], refs[33], Wires(*refs[34:])
        meet(SIDES)
        gain_sum[...] = jnp.zeros(gain_sum.shape, jnp.float32)

        def done(chunk, span, total):
            back, gain_terms = norm_back(middle_ref[2 + chunk, span], gain_ref[...], total)
            gain_sum[...] += gain_terms
            back = back + own_grad[2 + chunk, span].astype(jnp.float32)
            middle_grad[chunk, span] = back
            own_branch[chunk, span] = back.astype(jnp.bfloat16)

        move = Gather(wires, [normed_ref.at[0], normed_ref.at[1]], normed_early)
        sums = Scatter(wires, *back_parts[1], landing, stage, done)
        late_move = Gather(wires, [own_branch.at[0], own_branch.at[1]], branch)
        grad_move = Gather(wires, [own_grad.at[0], own_grad.at[1]], grads_early)
        move.first()
        grad_move.first()
        feed_phase(
            normed_late_ref, grads_late_ref, hidden[1], unit_grads[1], back_parts[1], out_parts[1],
            weight_ref,
            {2: move.second, 3: grad_move.second, 5: move.third, 7: grad_move.third},
        )
        sums.first()
        move.last()
        grad_move.last()
        feed_phase(
            normed_early, grads_early, hidden[0], unit_grads[0], back_parts[0], out_parts[0], weight_ref,
            {1: sums.second, 4: sums.third, 6: lambda: (sums.last(), late_move.first()) and None},
        )
        late_move.second()
        pl.run_scoped(
            lambda total: down_grad_phase(
                hidden, (grads_early, grads_late_ref), down_parts, total, {30: late_move.third}
            ),
            pltpu.VMEM((units, columns), jnp.float32),
        )
        late_move.last()

    outs = call(
        kernel,
        3,
        [(normed_own, VMEM), (normed_late, HBM), (grads_late, HBM)]
        + [(weights, VMEM), (middle, VMEM), (out_grad_own, VMEM), (gain, VMEM)],
        [(whole_pair, HBM)] * 2
        + [(bf16(2, CHIPS, tokens, units), HBM)] * 2
        + [(bf16(shards, 2, CHIPS, tokens, columns), HBM)] * 2
        + [(shape, HBM) for shape in partial_shapes(rows, width)] * 4
        + [(f32(2, rows, width), VMEM), (f32(STRIPE, width), VMEM)]
        + [(shape, HBM) for shape in landing_shapes(rows, width)]
        + [(whole_pair, HBM), (bf16(shards, units, columns), HBM)],
        stage_shapes(rows, width) + [pltpu.VMEM((2, rows, width), jnp.bfloat16)] + wire_shapes(50),
        62,
    )
    return (
        outs[19], outs[0], outs[1], outs[20], outs[4:6], outs[6:8], (outs[10:12], outs[12:14]), outs[14],
        outs[15],
    )


def attend_back(
    states, lengths, places, out_weight, weight, cosine, sine, branch_late, back_early, out_parts,
    middle, out_grad_own, inputs, middle_grad_late, gains
):
    _, rows, width = middle.shape
    tokens = 2 * rows

    def kernel(*refs):
        states_in, (lengths_ref, place_q, place_k, out_ref, weight_ref, cosine_ref, sine_ref) = (
            refs[:2],
            refs[2:9],
        )
        late_branch, back_parts, outs_in = refs[9], refs[10:12], (refs[12:14], refs[14:16])
        middle_ref, own_grad, inputs_ref, late_grad, gain_one, gain_two = refs[16:22]
        head_grads, early_branch, output_groups, input_grad = refs[22:24], refs[24], refs[25], refs[26]
        gain_sums = refs[27]
        parts = (refs[28:30], refs[30:32])
        landings = [refs[32 + 3 * place : 35 + 3 * place] for place in range(5)]
        stage, early_grad, own_branch, keys, values = refs[47:51], refs[51], refs[52], refs[53], refs[54]
        sums, late_sums, outputs, wires = refs[55:57], refs[57:59], refs[59], Wires(*refs[60:])
        plane = lax.axis_index("fsdp")
        meet(SIDES + PLANES)
        gain_sums[...] = jnp.zeros(gain_sums.shape, jnp.float32)

        def middle_done(chunk, span, total):
            back, gain_terms = norm_back(
                middle_ref[chunk, span].astype(jnp.float32), gain_two[...], total
            )
            gain_sums[1] += gain_terms
            back = back + own_grad[chunk, span].astype(jnp.float32)
            early_grad[chunk, span] = back
            own_branch[chunk, span] = back.astype(jnp.bfloat16)

        def output_done(pair):
            def done(chunk, span, total):
                at = 2 * pair + chunk
                outputs[at, span] = (middle_ref[at, span] + total).astype(jnp.bfloat16)

            return done

        def input_done(pair):
            def done(chunk, span, total):
                at = 2 * pair + chunk
                back, gain_terms = norm_back(
                    inputs_ref[at, span].astype(jnp.float32), gain_one[...], total
                )
                gain_sums[0] += gain_terms
                direct = late_grad if pair == 1 else early_grad
                input_grad[at, span] = (direct[chunk, span] + back).astype(jnp.bfloat16)

            return done

        middle_sum = Scatter(wires, *back_parts, landings[0], stage, middle_done)
        move = Gather(wires, [own_branch.at[0], own_branch.at[1]], early_branch)
        output_sums = [
            Scatter(wires, *outs_in[pair], landings[1 + pair], stage, output_done(pair))
            for pair in range(2)
        ]
        input_sums = [
            Scatter(wires, *parts[pair], landings[3 + pair], stage, input_done(pair)) for pair in range(2)
        ]

        def back_through(pair, branch, actions):
            attend_back_phase(
                pair, branch, states_in, head_grads[pair], *parts[pair], lengths_ref,
                (place_q, place_k), out_ref, weight_ref, (cosine_ref.at[pair], sine_ref.at[pair]),
                keys, values, sums, late_sums, actions,
            )

        def both(*steps):
            def run():
                for step in steps:
                    step()

            return run

        back_to_planes = [
            Remote(wires, outputs.at[flip(plane, mask)], output_groups.at[plane], 0, mask)
            for mask in range(1, CHUNKS)
        ]

        def send_back():
            for copy in back_to_planes:
                copy.start()
            wires.load([(outputs.at[plane], output_groups.at[plane])])

        middle_sum.first()
        output_sums[1].first()
        output_sums[0].first()
        back_through(
            1,
            late_branch,
            {
                1: middle_sum.second,
                4: middle_sum.third,
                6: both(middle_sum.last, move.first),
                7: move.second,
            },
        )
        input_sums[1].first()
        output_sums[1].second()
        move.third()
        move.last()
        back_through(
            0,
            early_branch,
            {
                0: output_sums[1].third,
                2: both(output_sums[1].last, output_sums[0].second),
                4: output_sums[0].third,
                6: both(output_sums[0].last, send_back),
                7: input_sums[1].second,
            },
        )
        input_sums[0].first()
        input_sums[1].third()
        input_sums[0].second()
        input_sums[1].last()
        input_sums[0].third()
        input_sums[0].last()
        for copy in back_to_planes:
            copy.arrived()
        for copy in back_to_planes:
            copy.left()

    outs = call(
        kernel,
        4,
        [(state, HBM) for state in states]
        + [(lengths, SMEM), (places[0], VMEM), (places[1], VMEM), (out_weight, VMEM), (weight, VMEM)]
        + [(cosine, HBM), (sine, HBM), (branch_late, HBM)]
        + [(part, HBM) for part in back_early]
        + [(part, HBM) for parts in out_parts for part in parts]
        + [(middle, VMEM), (out_grad_own, VMEM), (inputs, VMEM), (middle_grad_late, VMEM)]
        + [(gains[0], VMEM), (gains[1], VMEM)],
        [(bf16(2, CHIPS, tokens, 3 * HEAD), HBM)] * 2
        + [(bf16(2, CHIPS, tokens, width), HBM)]
        + [(bf16(CHUNKS, rows, width), HBM), (bf16(CHUNKS, rows, width), VMEM)]
        + [(f32(2, STRIPE, width), VMEM)]
        + [(shape, HBM) for shape in partial_shapes(rows, width)] * 2
        + [(shape, HBM) for shape in landing_shapes(rows, width)] * 5,
        stage_shapes(rows, width)
        + [pltpu.VMEM((2, rows, width), jnp.float32), pltpu.VMEM((2, rows, width), jnp.bfloat16)]
        + [pltpu.VMEM((CHUNKS * tokens, HEAD), jnp.bfloat16)] * 2
        + [pltpu.VMEM((CHIPS, 2 * tokens, HEAD), jnp.float32)] * 2
        + [pltpu.VMEM((2 * tokens, HEAD), jnp.float32)] * 2
        + [pltpu.VMEM((CHUNKS, rows, width), jnp.bfloat16)]
        + wire_shapes(60),
        63,
    )
    return outs[:2], outs[2], outs[3], outs[4], outs[5]


def weight_grad_phase(rows_in, grads, total, fresh, actions):
    _, chips, tokens, width = rows_in.shape
    columns = grads.shape[3]

    def body(rows_ref, grads_ref):
        chunk, step = pl.program_id(0), pl.program_id(1)
        at_step(2 * chunk + step, actions)
        term = dot_tn(rows_ref[0].reshape(2 * tokens, width), grads_ref[0].reshape(2 * tokens, columns))
        if fresh:

            @pl.when(chunk + step == 0)
            def _():
                total[...] = jnp.zeros(total.shape, jnp.float32)

        total[...] += term

    here = lambda chunk, step: (chunk, step, 0, 0)
    pltpu.emit_pipeline(
        body,
        grid=(2, chips // 2),
        in_specs=[
            pl.BlockSpec((1, 2, tokens, width), here),
            pl.BlockSpec((1, 2, tokens, columns), here),
        ],
    )(rows_in, grads)


def finish(head_terms, output_terms, unit_sum, down_sum, output_groups, input_grad, gain_sums):
    devices, planes = lax.axis_size("dp"), lax.axis_size("fsdp")
    strips = unit_sum.shape[0]
    _, down_rows, columns = down_sum.shape
    _, rows, width = input_grad.shape
    in_rows = width // devices
    sub_rows = in_rows // planes

    def kernel(*refs):
        head_refs, output_refs, refs = refs[:4], refs[4:8], refs[8:]
        units_in, downs_in, output_groups_ref, grads_ref, gains = refs[:5]
        outputs, input_out, head_out, output_out, gate_up, downs, gain_out, square_out = refs[5:13]
        grad_groups, combined, other_half, mine, gathered = refs[13:18]
        head_landing, output_landing, head_two, output_two = refs[18:22]
        gain_parts, square_parts, units = refs[22:25]
        head_total, output_total, given, outs_in, wires = *refs[25:29], Wires(*refs[29:])
        place, plane = lax.axis_index("dp"), lax.axis_index("fsdp")
        core = lax.rem(place, 2)

        def part(mask):
            return combined.at[:, flip(plane, mask)], outs_in.at[:, columns_of(flip(plane, mask), columns)]

        def both(sources, targets, mask):
            return [Remote(wires, source, target, 0, mask) for source, target in zip(sources, targets)]

        landing = [(head_landing.at[index], output_landing.at[index]) for index in range(3)]
        third = both(part(3), landing[0], 1)
        first = both(part(1), landing[1], 1)
        second = both((head_two, output_two), landing[2], 2)
        core_half = Remote(wires, given, other_half, CORE)
        rows_back = [
            Remote(wires, grads_ref.at[flip(plane, mask)], grad_groups.at[plane], 0, mask)
            for mask in range(1, CHUNKS)
        ]
        spread, heads_back = [], []
        for mask in range(1, devices):
            other = flip(place, mask)
            spread.append(Remote(wires, units_in.at[:, columns_of(other, in_rows)], units.at[place], mask))
            spread.append(Remote(wires, downs_in.at[other], downs.at[place], mask))
            heads_back.append(Remote(wires, mine.at[other], gathered.at[place], mask))
        heads_over = [
            Remote(wires, gathered.at[pl.ds(2 * flip(plane, mask), 2)], head_out.at[plane], 0, mask)
            for mask in range(1, CHUNKS)
        ]

        def to_owners(groups, target):
            copies = []
            for group in range(2):
                copies.append(
                    Remote(
                        wires,
                        groups.at[2 * (1 - core) + group],
                        target.at[group, half_rows(core, rows)],
                        CORE,
                    )
                )
            return copies

        outputs_in = to_owners(output_groups_ref, outputs)
        grads_in = to_owners(grad_groups, input_out)

        def sum_over(parts_ref):
            steps = [(mask, 0) for mask in (CORE, SIDE_A, SIDE_B)] + [(0, 1), (0, 2)]
            copies = [
                Remote(wires, parts_ref.at[2 * index], parts_ref.at[2 * index + 1], mask, over)
                for index, (mask, over) in enumerate(steps)
            ]

            def step(index):
                copies[index].arrived()
                copies[index].left()
                parts_ref[2 * index + 2] = parts_ref[2 * index] + parts_ref[2 * index + 1]
                if index + 1 < len(copies):
                    copies[index + 1].start()

            return copies[0].start, step, len(steps)

        gains_start, gains_step, count = sum_over(gain_parts)
        squares_start, squares_step, _ = sum_over(square_parts)

        gain_parts[0] = jnp.concatenate(
            [jnp.sum(gains[index], axis=0, keepdims=True) for index in range(2)]
            + [jnp.zeros((6, width), jnp.float32)]
        )
        meet(PLANE + PLANES)
        for copy in rows_back + spread + outputs_in:
            copy.start()
        gains_start()
        units[place] = units_in[:, columns_of(place, in_rows)]
        downs[place] = downs_in[place]
        for group in range(2):
            move_rows(
                output_groups_ref.at[2 * core + group], outputs.at[group, half_rows(core, rows)]
            )
        move_rows(grads_ref.at[plane], grad_groups.at[plane])
        weight_grad_phase(head_refs[0], head_refs[1], head_total, True, {3: lambda: gains_step(0)})
        weight_grad_phase(
            head_refs[2], head_refs[3], head_total, False, {1: lambda: gains_step(1), 3: lambda: gains_step(2)}
        )

        def split(index):
            kept, sent = (1 + index) * HEAD, (2 - index) * HEAD

            @pl.loop(0, devices)
            def _(block):
                span = pl.ds(pl.multiple_of(block * in_rows, in_rows), in_rows)
                shape = (planes, sub_rows, HEAD)
                given[block] = head_total[span, sent : sent + HEAD].astype(jnp.bfloat16).reshape(shape)
                combined[block, :, :, :HEAD] = head_total[span, :HEAD].astype(jnp.bfloat16).reshape(shape)

        for index in range(2):
            pl.when(core == index)(functools.partial(split, index))
        core_half.start()
        weight_grad_phase(output_refs[0], output_refs[1], output_total, True, {})
        core_half.arrived()

        def join(index):
            kept = (1 + index) * HEAD

            @pl.loop(0, devices)
            def _(block):
                span = pl.ds(pl.multiple_of(block * in_rows, in_rows), in_rows)
                total = head_total[span, kept : kept + HEAD].reshape(planes, sub_rows, HEAD)
                total = total + other_half[block].astype(jnp.float32)
                combined[block, :, :, HEAD:] = total.astype(jnp.bfloat16)

        for index in range(2):
            pl.when(core == index)(functools.partial(join, index))
        third[0].start()
        weight_grad_phase(output_refs[2], output_refs[3], output_total, False, {})
        outs_in[...] = output_total[...].astype(jnp.bfloat16)
        third[1].start()
        third[0].arrived()
        head_two[...] = (
            combined[:, flip(plane, 2)].astype(jnp.float32) + head_landing[0].astype(jnp.float32)
        ).astype(jnp.bfloat16)
        second[0].start()
        third[1].arrived()
        output_two[...] = (
            outs_in[:, columns_of(flip(plane, 2), columns)].astype(jnp.float32)
            + output_landing[0].astype(jnp.float32)
        ).astype(jnp.bfloat16)
        second[1].start()
        for copy in first:
            copy.start()
        for index in range(3, count):
            gains_step(index)
        for copy in rows_back:
            copy.arrived()
        for copy in grads_in:
            copy.start()
        for group in range(2):
            move_rows(grad_groups.at[2 * core + group], input_out.at[group, half_rows(core, rows)])
        for copy in spread:
            copy.arrived()
        square = jnp.zeros((), jnp.float32)
        for index in range(devices):
            values = downs[index].astype(jnp.float32)
            square += jnp.sum(values * values)
            for block in range(strips // down_rows):
                values = units[index, block * down_rows : (block + 1) * down_rows].astype(jnp.float32)
                square += jnp.sum(values * values)
                matrix, run = block // 2, block % 2
                at = (run * devices + index) * down_rows
                gate_up[matrix, :, at : at + down_rows] = values.T.astype(jnp.bfloat16)
        for copy in first + second:
            copy.arrived()
        total = combined[:, plane].astype(jnp.float32)
        for index in (1, 2):
            total += head_landing[index].astype(jnp.float32)
        mine[...] = total.astype(jnp.bfloat16)
        for copy in heads_back:
            copy.start()
        gathered[place] = mine[place]
        total = outs_in[:, columns_of(plane, columns)].astype(jnp.float32)
        for index in (1, 2):
            total += output_landing[index].astype(jnp.float32)
        output_out[...] = total
        square += jnp.sum(total * total)
        for copy in heads_back:
            copy.arrived()
        for copy in heads_over:
            copy.start()
        head_out[plane] = gathered[pl.ds(2 * plane, 2)]
        for copy in heads_over:
            copy.arrived()
        for index in range(planes):
            values = head_out[index].astype(jnp.float32)
            square += jnp.sum(values * values)
        square_parts[0] = jnp.full(square_parts.shape[1:], square, jnp.float32)
        squares_start()
        for index in range(count):
            squares_step(index)
        gain_out[...] = gain_parts[2 * count]
        square_out[...] = square_parts[2 * count]
        for copy in outputs_in + grads_in:
            copy.arrived()
        for copy in (
            third + first + second + [core_half] + rows_back + spread + heads_back + heads_over
            + outputs_in + grads_in
        ):
            copy.left()

    own = bf16(2, 2 * rows, width)
    return call(
        kernel,
        5,
        [(array, HBM) for array in head_terms + output_terms]
        + [(array, VMEM) for array in (unit_sum, down_sum, output_groups, input_grad, gain_sums)],
        [(own, VMEM)] * 2
        + [(bf16(planes, 2, sub_rows, columns), VMEM), (f32(HEAD, columns), VMEM)]
        + [(bf16(2, in_rows, devices * strips // 2), VMEM), (bf16(devices, down_rows, columns), VMEM)]
        + [(f32(8, width), VMEM), (f32(8, 128), VMEM)],
        [
            pltpu.VMEM((CHUNKS, rows, width), jnp.bfloat16),
            pltpu.VMEM((devices, planes, sub_rows, columns), jnp.bfloat16),
            pltpu.VMEM((devices, planes, sub_rows, HEAD), jnp.bfloat16),
            pltpu.VMEM((devices, sub_rows, columns), jnp.bfloat16),
            pltpu.VMEM((devices, sub_rows, columns), jnp.bfloat16),
            pltpu.VMEM((3, devices, sub_rows, columns), jnp.bfloat16),
            pltpu.VMEM((3, HEAD, columns), jnp.bfloat16),
            pltpu.VMEM((devices, sub_rows, columns), jnp.bfloat16),
            pltpu.VMEM((HEAD, columns), jnp.bfloat16),
            pltpu.VMEM((11, 8, width), jnp.float32),
            pltpu.VMEM((11, 8, 128), jnp.float32),
            pltpu.VMEM((devices, strips, in_rows), jnp.bfloat16),
            pltpu.VMEM((width, 3 * HEAD), jnp.float32),
            pltpu.VMEM((HEAD, width), jnp.float32),
            pltpu.VMEM((devices, planes, sub_rows, HEAD), jnp.bfloat16),
            pltpu.VMEM((HEAD, width), jnp.bfloat16),
        ]
        + wire_shapes(70),
        62,
    )


def unit_weight_grads(unit_grads, rows_in):
    shards, chunks, chips, tokens, columns = unit_grads[0].shape
    width = rows_in[0].shape[3]
    count = chunks * chips * tokens

    def kernel(late_units, late_rows, early_units, early_rows, out):
        total = dot_tn(late_units[0].reshape(count, columns), late_rows[...].reshape(count, width))
        total += dot_tn(early_units[0].reshape(count, columns), early_rows[...].reshape(count, width))
        out[0] = total.astype(jnp.bfloat16)

    block = pl.BlockSpec((1, chunks, chips, tokens, columns), lambda shard: (shard, 0, 0, 0, 0))
    rows_block = whole(rows_in[0].shape)
    return pl.pallas_call(
        kernel,
        grid=(shards,),
        in_specs=[block, rows_block] * 2,
        out_specs=pl.BlockSpec((1, columns, width), lambda shard: (shard, 0, 0)),
        out_shape=bf16(shards, columns, width),
        compiler_params=params(62),
    )(unit_grads[1], rows_in[1], unit_grads[0], rows_in[0])


def dot(left, right):
    return jnp.dot(left, right, preferred_element_type=jnp.float32)


def dot_t(left, right):
    return lax.dot_general(
        left, right, (((1,), (1,)), ((), ())), preferred_element_type=jnp.float32
    )


def dot_tn(left, right):
    return lax.dot_general(
        left, right, (((0,), (0,)), ((), ())), preferred_element_type=jnp.float32
    )


def spin(values, cosine, sine):
    halfway = values.shape[1] // 2
    first, second = values[:, :halfway], values[:, halfway:]
    return jnp.concatenate(
        [first * cosine - second * sine, second * cosine + first * sine], axis=1
    )


def spin_back(values, cosine, sine):
    return spin(values, cosine, -sine)


def whole(shape):
    return pl.BlockSpec(shape, lambda *_: (0,) * len(shape), pipeline_mode=pl.Buffered(1))


def params(megabytes):
    return pltpu.CompilerParams(vmem_limit_bytes=megabytes * MB)


def seen(place_q, place_k, chunk, count, tokens, lengths_ref, chip):
    query_index = tokens * chunk + place_q
    key_index = place_k[:, :count]
    ahead_or_here = key_index <= query_index
    if tokens * (chunk + 1) <= PROMPT:
        return ahead_or_here

    def segment(index):
        found = jnp.full(index.shape, -1, jnp.int32)
        for slot in range(NCONT):
            found = jnp.where(index >= PROMPT + slot * CONT, slot, found)
        return found

    key_segment, query_segment = segment(key_index), segment(query_index)
    end = jnp.full(key_index.shape, PROMPT, jnp.int32)
    for slot in range(NCONT):
        end = jnp.where(
            key_segment == slot, PROMPT + slot * CONT + lengths_ref[chip, slot], end
        )
    alive = key_index < end
    return ahead_or_here & ((key_segment < 0) | ((key_segment == query_segment) & alive))


def token_dot(left, right):
    return lax.dot_general(
        left.reshape(-1, left.shape[-1]),
        right.reshape(-1, right.shape[-1]),
        (((0,), (0,)), ((), ())),
        preferred_element_type=jnp.float32,
    )


def exchange(value, axis):
    return lax.all_to_all(value, axis, split_axis=0, concat_axis=0, tiled=True)


def plane_device(
    activations,
    cotangent,
    continuation_lengths,
    query_weight,
    key_weight,
    value_weight,
    output_weight,
    gate_weight,
    up_weight,
    down_weight,
    attention_gain,
    feedforward_gain,
    moment_query,
    moment_key,
    moment_value,
    moment_output,
    moment_gate,
    moment_up,
    moment_down,
    moment_attention,
    moment_feedforward,
):
    devices, planes = lax.axis_size("dp"), lax.axis_size("fsdp")
    place, plane = lax.axis_index("dp"), lax.axis_index("fsdp")
    core = place % 2
    low = jnp.bfloat16
    kv_width = KV_HEADS * HEAD
    tokens = activations.shape[1]
    half = tokens // 2

    in_rows = query_weight.shape[0]
    sub_rows = in_rows // planes
    spread = devices * sub_rows

    mixed_kv = jnp.stack([key_weight.astype(low), value_weight.astype(low)], axis=1)
    block = jnp.concatenate([query_weight.astype(low).reshape(in_rows, 2, HEAD), mixed_kv], axis=2)
    head_block = block.reshape(planes, sub_rows, 2, 2 * HEAD).swapaxes(1, 2)

    strip = 128
    runs = gate_weight.shape[1] // (devices * strip)
    units = runs * strip * planes
    gate_up = jnp.stack(
        [
            gate_weight.astype(low).reshape(in_rows, runs, devices, strip),
            up_weight.astype(low).reshape(in_rows, runs, devices, strip),
        ]
    )
    gate_up = gate_up.transpose(3, 1, 0, 2, 4).reshape(devices, in_rows, 2 * runs * strip)
    down_columns = down_weight.shape[1]
    down = down_weight.astype(low).reshape(devices, strip, down_columns)

    gain_one, gain_two = attention_gain[None, :], feedforward_gain[None, :]
    length_block = jnp.zeros((8, 128), jnp.int32).at[:2, :NCONT].set(continuation_lengths)
    own_inputs, own_grads, rows_all, head_weight, head_output, feed_own, all_lengths = start_up(
        activations,
        cotangent,
        head_block,
        output_weight.astype(low),
        gate_up,
        down,
        length_block,
        gain_one,
    )

    first_core = place - core
    lengths = jnp.stack(
        [
            pick(pick(all_lengths, (first_core ^ mask) + plane // 2), plane % 2)[:NCONT]
            for mask in (0, SIDE_A, SIDE_B, SIDE_A + SIDE_B)
        ]
    )

    inside = jnp.concatenate(
        [core * half + jnp.arange(half), (1 - core) * half + jnp.arange(half)]
    ).astype(jnp.int32)
    order = (tokens * jnp.arange(CHUNKS, dtype=jnp.int32)[:, None] + inside[None, :]).reshape(-1)
    cosine, sine = rope_angles(token_places(order))
    cosine = cosine.reshape(2, 2, tokens, HEAD // 2)
    sine = sine.reshape(2, 2, tokens, HEAD // 2)
    place_q, place_k = inside[:, None], order[None, :]
    blocks = plane ^ jnp.arange(CHUNKS, dtype=jnp.int32)

    states, mixed, middle, normed_two, normed_late, grads_late, feed_weights = attend_and_norm(
        rows_all,
        own_grads,
        feed_own,
        head_weight,
        cosine,
        sine,
        lengths,
        (place_q, place_k),
        head_output,
        own_inputs,
        gain_two,
    )
    (
        grads_early,
        normed_early,
        branch_late,
        down_sum,
        unit_grads,
        back_early,
        out_parts,
        middle_grad,
        gain_sum,
    ) = feed_forward(normed_two, normed_late, grads_late, feed_weights, middle, own_grads, gain_two, units)
    down_sum = lax.psum_scatter(down_sum, "fsdp", scatter_dimension=0, tiled=False)
    unit_sum = unit_weight_grads(unit_grads, (normed_early, normed_late))
    unit_sum = lax.psum_scatter(unit_sum, "fsdp", scatter_dimension=0, tiled=False)
    head_grads, branch_early, output_groups, own_input_grad, gain_sums = attend_back(
        states,
        lengths,
        (place_q, place_k),
        head_output,
        head_weight,
        cosine,
        sine,
        branch_late,
        back_early,
        out_parts,
        middle,
        own_grads,
        own_inputs,
        middle_grad,
        (gain_one, gain_two),
    )

    outputs, input_grad, block, output_owned, gate_up_owned, downs_owned, gain_totals, squares = finish(
        [rows_all[1], head_grads[1], rows_all[0], head_grads[0]],
        [mixed[1], branch_late, mixed[0], branch_early],
        unit_sum,
        down_sum.reshape(devices, strip, down_columns),
        output_groups,
        own_input_grad,
        jnp.stack([gain_sums[0], gain_sums[1] + gain_sum]),
    )
    block = block.swapaxes(1, 2).reshape(in_rows, 2, 2 * HEAD)
    query_owned = block[:, :, :HEAD].reshape(in_rows, 2 * HEAD)
    key_owned, value_owned = block[:, 0, HEAD:], block[:, 1, HEAD:]
    down_owned = downs_owned.reshape(devices * strip, down_columns)

    owner_grads = [
        owned.astype(jnp.float32)
        for owned in (
            query_owned,
            key_owned,
            value_owned,
            output_owned,
            gate_up_owned[0],
            gate_up_owned[1],
            down_owned,
        )
    ]
    attention_total, feedforward_total = gain_totals[0], gain_totals[1]
    square_total = squares[0, 0]
    square_sum = (
        square_total
        + jnp.sum(attention_total * attention_total)
        + jnp.sum(feedforward_total * feedforward_total)
    )
    grad_norm = jnp.sqrt(square_sum)
    entry_count = 2 * D * D + 2 * D * kv_width + 3 * D * FF + 2 * D
    limit = clip_level * math.sqrt(entry_count)
    factor = limit / jnp.maximum(grad_norm, limit)
    gradients = owner_grads + [attention_total, feedforward_total]
    old_moments = [
        moment_query,
        moment_key,
        moment_value,
        moment_output,
        moment_gate,
        moment_up,
        moment_down,
        moment_attention,
        moment_feedforward,
    ]
    old_params = [
        query_weight,
        key_weight,
        value_weight,
        output_weight,
        gate_weight,
        up_weight,
        down_weight,
        attention_gain,
        feedforward_gain,
    ]
    new_moments = [
        0.5 * moment + 0.5 * factor * gradient for moment, gradient in zip(old_moments, gradients)
    ]
    new_params = []
    for at, param in enumerate(old_params):
        if at < 7:
            new_params.append(param - step_size * (new_moments[at] + decay_rate * param))
        else:
            new_params.append(param - gain_step * new_moments[at])
    return (outputs, input_grad, grad_norm, *new_moments, *new_params)


def solution(mesh):
    whole_groups_on_planes = mesh.shape["dp"] == HEADS and mesh.shape["fsdp"] == KV_HEADS
    body = plane_device if whole_groups_on_planes else on_device
    placed = (
        P("dp", "fsdp", None),
        P("dp", "fsdp", None),
        P("dp", None),
        P("dp", "fsdp"),
        P("dp", "fsdp"),
        P("dp", "fsdp"),
        P("dp", "fsdp"),
        P("dp", "fsdp"),
        P("dp", "fsdp"),
        P("dp", "fsdp"),
        P(),
        P(),
        P("dp", "fsdp"),
        P("dp", "fsdp"),
        P("dp", "fsdp"),
        P("dp", "fsdp"),
        P("dp", "fsdp"),
        P("dp", "fsdp"),
        P("dp", "fsdp"),
        P(),
        P(),
    )
    return jax.shard_map(
        body,
        mesh=mesh,
        in_specs=placed,
        out_specs=(
            P("dp", "fsdp", None),
            P("dp", "fsdp", None),
            P(),
            P("dp", "fsdp"),
            P("dp", "fsdp"),
            P("dp", "fsdp"),
            P("dp", "fsdp"),
            P("dp", "fsdp"),
            P("dp", "fsdp"),
            P("dp", "fsdp"),
            P(),
            P(),
            P("dp", "fsdp"),
            P("dp", "fsdp"),
            P("dp", "fsdp"),
            P("dp", "fsdp"),
            P("dp", "fsdp"),
            P("dp", "fsdp"),
            P("dp", "fsdp"),
            P(),
            P(),
        ),
        check_vma=False,
    )
```

```python
import functools
from functools import reduce
import math

import jax
import jax.numpy as jnp
from jax import lax
from jax.experimental import pallas as pl
from jax.experimental.pallas import tpu as pltpu
from jax.sharding import PartitionSpec as P

D = 2048
HEADS = 8
KV_HEADS = 4
HEAD = 256
FF = 8192
PROMPT = 1024
CONT = 64
NCONT = 2


epsilon = 1e-06
rope_base = 1000042.0
step_size = 0.2
gain_step = 4.0
decay_rate = 0.1
clip_level = 0.25
floor_score = -1e30


def rms_rows(values, gain):
    factor = lax.rsqrt(jnp.mean(values * values, axis=-1, keepdims=True) + epsilon)
    return (values * factor * gain, factor)


def rms_back(values, factor, gain, gradient):
    scaled = values * factor
    gain_grad = jnp.sum(gradient * scaled, axis=0)
    pulled = gradient * gain
    return (
        factor * (pulled - scaled * jnp.mean(pulled * scaled, axis=-1, keepdims=True)),
        gain_grad,
    )


def rope_angles(places):
    halfway = HEAD // 2
    freqs = rope_base ** (-(jnp.arange(halfway).astype(jnp.float32) * 2.0 / HEAD))
    angles = places.astype(jnp.float32)[:, None] * freqs[None, :]
    return (jnp.cos(angles), jnp.sin(angles))


def token_places(index):
    inside = index - PROMPT
    return jnp.where(index < PROMPT, index, PROMPT + inside % CONT)


def segment_of(index):
    return jnp.where(index < PROMPT, -1, (index - PROMPT) // CONT)


def visible(query_index, key_index, lengths):
    key_segment = segment_of(key_index)
    key_offset = key_index - PROMPT - key_segment * CONT
    slots = jnp.arange(NCONT, dtype=jnp.int32)
    limits = jnp.sum(jnp.where(key_segment[:, None] == slots[None, :], lengths[None, :], 0), axis=1)
    alive = key_offset < limits
    same = segment_of(query_index)[:, None] == key_segment[None, :]
    causal = key_index[None, :] <= query_index[:, None]
    return causal & ((key_index < PROMPT)[None, :] | same & alive[None, :])


def rotate(values, cosine, sine):
    halfway = values.shape[-1] // 2
    first, second = (values[..., :halfway], values[..., halfway:])
    cosine, sine = (cosine[:, None, :], sine[:, None, :])
    return jnp.concatenate(
        [first * cosine - second * sine, second * cosine + first * sine], axis=-1
    )


def rotate_back(grads, cosine, sine):
    halfway = grads.shape[-1] // 2
    first, second = (grads[..., :halfway], grads[..., halfway:])
    cosine, sine = (cosine[:, None, :], sine[:, None, :])
    return jnp.concatenate(
        [first * cosine + second * sine, second * cosine - first * sine], axis=-1
    )


def join_blocks(pieces, shard_count):
    height = pieces[0].shape[0]
    return jnp.concatenate(
        [member.reshape(height, shard_count, -1) for member in pieces], axis=2
    ).reshape(height, -1)


def split_blocks(merged, breadths, shard_count):
    height = merged.shape[0]
    blocks = merged.reshape(height, shard_count, -1)
    result = []
    offset = 0
    for breadth in breadths:
        result.append(
            blocks[:, :, offset : offset + breadth].reshape(height, shard_count * breadth)
        )
        offset = offset + breadth
    return result


def ahead(operand, shard):
    return jnp.dot(
        operand,
        lax.all_gather(shard, "fsdp", axis=1, tiled=True),
        preferred_element_type=jnp.float32,
    )


def behind(gradient, shard):
    return lax.dot_general(
        gradient,
        lax.all_gather(shard, "fsdp", axis=1, tiled=True),
        (((1,), (1,)), ((), ())),
        preferred_element_type=jnp.float32,
    )


def weight_term(gradient, operand):
    operand_all = lax.all_gather(operand, "fsdp", axis=0, tiled=True)
    owned_columns = lax.all_to_all(gradient, "fsdp", split_axis=1, concat_axis=0, tiled=True)
    return lax.dot_general(
        owned_columns, operand_all, (((0,), (0,)), ((), ())), preferred_element_type=jnp.float32
    )


def on_device(
    activations,
    cotangent,
    continuation_lengths,
    query_weight,
    key_weight,
    value_weight,
    output_weight,
    gate_weight,
    up_weight,
    down_weight,
    attention_gain,
    feedforward_gain,
    moment_query,
    moment_key,
    moment_value,
    moment_output,
    moment_gate,
    moment_up,
    moment_down,
    moment_attention,
    moment_feedforward,
):
    shard_count = lax.axis_size("fsdp")
    kv_width = KV_HEADS * HEAD
    repeat = HEADS // KV_HEADS
    scale = 1.0 / math.sqrt(HEAD)
    gathered = (
        lax.all_gather(query_weight.astype(jnp.bfloat16), "dp", axis=0, tiled=True),
        lax.all_gather(key_weight.astype(jnp.bfloat16), "dp", axis=0, tiled=True),
        lax.all_gather(value_weight.astype(jnp.bfloat16), "dp", axis=0, tiled=True),
        lax.all_gather(output_weight.astype(jnp.bfloat16), "dp", axis=0, tiled=True),
        lax.all_gather(gate_weight.astype(jnp.bfloat16), "dp", axis=0, tiled=True),
        lax.all_gather(up_weight.astype(jnp.bfloat16), "dp", axis=0, tiled=True),
        lax.all_gather(down_weight.astype(jnp.bfloat16), "dp", axis=0, tiled=True),
    )
    merged_attn = join_blocks(gathered[0:3], 1)
    merged_output = gathered[3]
    merged_ffn = join_blocks(gathered[4:6], 1)
    merged_down = gathered[6]
    query_cols = D // shard_count
    key_cols = kv_width // shard_count
    ffn_cols = FF // shard_count
    attn_breadths = (query_cols, key_cols, key_cols)
    ffn_breadths = (ffn_cols, ffn_cols)
    local_rows = activations.shape[1]
    group_rows = local_rows * shard_count
    query_index = lax.axis_index("fsdp") * local_rows + jnp.arange(local_rows, dtype=jnp.int32)
    key_index = jnp.arange(group_rows, dtype=jnp.int32)
    cosine, sine = rope_angles(token_places(query_index))
    sums = [jnp.zeros((matrix.shape[1], matrix.shape[0]), jnp.float32) for matrix in gathered]
    attention_sum = jnp.zeros((D,), jnp.float32)
    feedforward_sum = jnp.zeros((D,), jnp.float32)
    output_list = []
    input_list = []
    for micro_batch in range(activations.shape[0]):
        allowed = visible(query_index, key_index, continuation_lengths[micro_batch])
        inputs = activations[micro_batch].astype(jnp.float32)
        normed_float, factor_one = rms_rows(inputs, attention_gain)
        normed = normed_float.astype(jnp.bfloat16)
        pre_query, pre_key, pre_value = split_blocks(
            ahead(normed, merged_attn), attn_breadths, shard_count
        )
        queries = (
            rotate(pre_query.reshape(local_rows, HEADS, HEAD), cosine, sine)
            .astype(jnp.bfloat16)
            .reshape(local_rows, KV_HEADS, repeat, HEAD)
        )
        keys = rotate(pre_key.reshape(local_rows, KV_HEADS, HEAD), cosine, sine).astype(
            jnp.bfloat16
        )
        values = pre_value.astype(jnp.bfloat16).reshape(local_rows, KV_HEADS, HEAD)
        keys_all, values_all = (
            lax.all_gather(keys, "fsdp", axis=0, tiled=True),
            lax.all_gather(values, "fsdp", axis=0, tiled=True),
        )
        raw = (
            jnp.einsum("qgrd,kgd->grqk", queries, keys_all, preferred_element_type=jnp.float32)
            * scale
        )
        raw = jnp.where(allowed[None, None], raw, floor_score)
        highest = jnp.max(raw, axis=-1, keepdims=True)
        exponent = jnp.exp(raw - highest)
        denominator = jnp.sum(exponent, axis=-1, keepdims=True)
        logsum = highest + jnp.log(denominator)
        probs_low = (exponent / denominator).astype(jnp.bfloat16)
        mixed = (
            jnp.einsum("grqk,kgd->qgrd", probs_low, values_all, preferred_element_type=jnp.float32)
            .reshape(local_rows, D)
            .astype(jnp.bfloat16)
        )
        middle = inputs + ahead(mixed, merged_output)
        normed_two_float, factor_two = rms_rows(middle, feedforward_gain)
        normed_two = normed_two_float.astype(jnp.bfloat16)
        gate, upward = split_blocks(ahead(normed_two, merged_ffn), ffn_breadths, shard_count)
        sigmoid = jax.nn.sigmoid(gate)
        swish = gate * sigmoid
        hidden = (swish * upward).astype(jnp.bfloat16)
        result = middle + ahead(hidden, merged_down)
        output_list.append(result.astype(jnp.bfloat16))
        out_grad = cotangent[micro_batch]
        hidden_grad = behind(out_grad, merged_down)
        sums[6] = sums[6] + weight_term(out_grad, hidden)
        gate_grad = (hidden_grad * upward * sigmoid * (1.0 + gate * (1.0 - sigmoid))).astype(
            jnp.bfloat16
        )
        up_grad = (hidden_grad * swish).astype(jnp.bfloat16)
        ffn_grad = join_blocks((gate_grad, up_grad), shard_count)
        ffn_term = weight_term(ffn_grad, normed_two)
        sums[4] = sums[4] + ffn_term[:ffn_cols]
        sums[5] = sums[5] + ffn_term[ffn_cols:]
        normed_two_grad = behind(ffn_grad, merged_ffn)
        middle_back, feed_gain_grad = rms_back(
            middle, factor_two, feedforward_gain, normed_two_grad
        )
        middle_grad = out_grad.astype(jnp.float32) + middle_back
        branch_grad = middle_grad.astype(jnp.bfloat16)
        sums[3] = sums[3] + weight_term(branch_grad, mixed)
        mixed_grad = (
            behind(branch_grad, merged_output)
            .astype(jnp.bfloat16)
            .reshape(local_rows, KV_HEADS, repeat, HEAD)
        )
        raw_again = (
            jnp.einsum("qgrd,kgd->grqk", queries, keys_all, preferred_element_type=jnp.float32)
            * scale
        )
        raw_again = jnp.where(allowed[None, None], raw_again, floor_score)
        probs_again = jnp.exp(raw_again - logsum)
        value_part = jnp.einsum(
            "grqk,qgrd->kgd",
            probs_again.astype(jnp.bfloat16),
            mixed_grad,
            preferred_element_type=jnp.float32,
        )
        prob_grad = jnp.einsum(
            "qgrd,kgd->grqk", mixed_grad, values_all, preferred_element_type=jnp.float32
        )
        inner = jnp.sum(probs_again * prob_grad, axis=-1, keepdims=True)
        score_grad = (probs_again * (prob_grad - inner)).astype(jnp.bfloat16)
        query_grad = (
            jnp.einsum("grqk,kgd->qgrd", score_grad, keys_all, preferred_element_type=jnp.float32)
            * scale
        )
        key_part = (
            jnp.einsum("grqk,qgrd->kgd", score_grad, queries, preferred_element_type=jnp.float32)
            * scale
        )
        key_grad, value_grad = (
            lax.psum_scatter(
                key_part.astype(jnp.bfloat16), "fsdp", scatter_dimension=0, tiled=True
            ).astype(jnp.float32),
            lax.psum_scatter(
                value_part.astype(jnp.bfloat16), "fsdp", scatter_dimension=0, tiled=True
            ).astype(jnp.float32),
        )
        pre_query_grad = (
            rotate_back(query_grad.reshape(local_rows, HEADS, HEAD), cosine, sine)
            .reshape(local_rows, D)
            .astype(jnp.bfloat16)
        )
        pre_key_grad = (
            rotate_back(key_grad, cosine, sine).reshape(local_rows, kv_width).astype(jnp.bfloat16)
        )
        pre_value_grad = value_grad.reshape(local_rows, kv_width).astype(jnp.bfloat16)
        attn_grad = join_blocks((pre_query_grad, pre_key_grad, pre_value_grad), shard_count)
        attn_term = weight_term(attn_grad, normed)
        sums[0] = sums[0] + attn_term[:query_cols]
        sums[1] = sums[1] + attn_term[query_cols : query_cols + key_cols]
        sums[2] = sums[2] + attn_term[query_cols + key_cols :]
        normed_grad = behind(attn_grad, merged_attn)
        input_back, attn_gain_grad = rms_back(inputs, factor_one, attention_gain, normed_grad)
        input_list.append((middle_grad + input_back).astype(jnp.bfloat16))
        attention_sum = attention_sum + attn_gain_grad
        feedforward_sum = feedforward_sum + feed_gain_grad
    reduced = (
        lax.psum_scatter(
            sums[0].astype(jnp.bfloat16), "dp", scatter_dimension=1, tiled=True
        ).astype(jnp.float32),
        lax.psum_scatter(
            sums[1].astype(jnp.bfloat16), "dp", scatter_dimension=1, tiled=True
        ).astype(jnp.float32),
        lax.psum_scatter(
            sums[2].astype(jnp.bfloat16), "dp", scatter_dimension=1, tiled=True
        ).astype(jnp.float32),
        lax.psum_scatter(
            sums[3].astype(jnp.bfloat16), "dp", scatter_dimension=1, tiled=True
        ).astype(jnp.float32),
        lax.psum_scatter(
            sums[4].astype(jnp.bfloat16), "dp", scatter_dimension=1, tiled=True
        ).astype(jnp.float32),
        lax.psum_scatter(
            sums[5].astype(jnp.bfloat16), "dp", scatter_dimension=1, tiled=True
        ).astype(jnp.float32),
        lax.psum_scatter(
            sums[6].astype(jnp.bfloat16), "dp", scatter_dimension=1, tiled=True
        ).astype(jnp.float32),
    )
    owner_grads = [owned.T for owned in reduced]
    local_square = reduce(jnp.add, [jnp.sum(owned * owned) for owned in owner_grads])
    attention_total, feedforward_total, square_total = lax.psum(
        (attention_sum, feedforward_sum, local_square), ("dp", "fsdp")
    )
    square_sum = (
        square_total
        + jnp.sum(attention_total * attention_total)
        + jnp.sum(feedforward_total * feedforward_total)
    )
    grad_norm = jnp.sqrt(square_sum)
    entry_count = 2 * D * D + 2 * D * kv_width + 3 * D * FF + 2 * D
    limit = clip_level * math.sqrt(entry_count)
    factor = limit / jnp.maximum(grad_norm, limit)
    gradients = owner_grads + [attention_total, feedforward_total]
    old_moments = [
        moment_query,
        moment_key,
        moment_value,
        moment_output,
        moment_gate,
        moment_up,
        moment_down,
        moment_attention,
        moment_feedforward,
    ]
    old_params = [
        query_weight,
        key_weight,
        value_weight,
        output_weight,
        gate_weight,
        up_weight,
        down_weight,
        attention_gain,
        feedforward_gain,
    ]
    new_moments = [
        0.5 * moment + 0.5 * factor * gradient for moment, gradient in zip(old_moments, gradients)
    ]
    new_params = []
    for place, param in enumerate(old_params):
        if place < 7:
            new_params.append(param - step_size * (new_moments[place] + decay_rate * param))
        else:
            new_params.append(param - gain_step * new_moments[place])
    outputs = jnp.stack(output_list)
    input_grad = jnp.stack(input_list)
    return (
        outputs,
        input_grad,
        grad_norm,
        new_moments[0],
        new_moments[1],
        new_moments[2],
        new_moments[3],
        new_moments[4],
        new_moments[5],
        new_moments[6],
        new_moments[7],
        new_moments[8],
        new_params[0],
        new_params[1],
        new_params[2],
        new_params[3],
        new_params[4],
        new_params[5],
        new_params[6],
        new_params[7],
        new_params[8],
    )


CORE, SIDE_A, SIDE_B = 1, 2, 4
CHIPS = 4
CHUNKS = 4
MB = 1024 * 1024


def across(value, mask):
    count = lax.axis_size("dp")
    return lax.ppermute(value, "dp", [(place, place ^ mask) for place in range(count)])


def along(value, mask):
    count = lax.axis_size("fsdp")
    return lax.ppermute(value, "fsdp", [(place, place ^ mask) for place in range(count)])


def pick(values, index):
    return lax.dynamic_index_in_dim(values, index, 0, keepdims=False)


def after(value, *earlier):
    return lax.optimization_barrier((value, earlier))[0]


def trade_planes(parts, plane):
    found = [pick(parts, plane)]
    for mask in range(1, CHUNKS):
        found.append(along(pick(parts, plane ^ mask), mask))
    found = jnp.stack(found)
    return [pick(found, label ^ plane) for label in range(CHUNKS)]


def gather_planes(block):
    one, two = along(block, 1), along(block, 2)
    return [block, one, two, along(two, 1)]


def sum_planes(parts):
    two = (parts[2].astype(jnp.float32) + along(parts[3], 1).astype(jnp.float32)).astype(jnp.bfloat16)
    return (
        parts[0].astype(jnp.float32)
        + along(parts[1], 1).astype(jnp.float32)
        + along(two, 2).astype(jnp.float32)
    )


def sum_all(value):
    for mask in (CORE, SIDE_A, SIDE_B):
        value = value + across(value, mask)
    for mask in (1, 2):
        value = value + along(value, mask)
    return value


def to_planes(array, core, plane):
    halves = array.reshape(2, 2, array.shape[1] // 2, array.shape[2]).swapaxes(0, 1)
    keep = pick(halves, core)
    came = across(pick(halves, 1 - core), CORE)
    swap = core == 1
    parts = jnp.concatenate([jnp.where(swap, came, keep), jnp.where(swap, keep, came)])
    return trade_planes(parts, plane)


def from_planes(chunks, core, plane):
    groups = trade_planes(jnp.stack(chunks), plane)
    pairs = jnp.stack([jnp.stack(groups[:2]), jnp.stack(groups[2:])])
    keep = pick(pairs, core)
    came = across(pick(pairs, 1 - core), CORE)
    swap = core == 1
    return jnp.concatenate([jnp.where(swap, came, keep), jnp.where(swap, keep, came)], axis=1)


MESH = pl.DeviceIdType.MESH
SLOT = {0: 0, SIDE_A: 1, SIDE_B: 2}
ROUTES = ((SIDE_A, SIDE_B), (SIDE_B, SIDE_A))
STRIPE = 16


def flip(place, mask):
    for bit in (1, 2, 4):
        if mask & bit:
            place = place + bit - 2 * bit * lax.rem(lax.div(place, bit), 2)
    return place


def peer(mask, planes=0):
    return (flip(lax.axis_index("dp"), mask), flip(lax.axis_index("fsdp"), planes))


SIDES = ((CORE, 0), (SIDE_A, 0), (SIDE_B, 0))
PLANE = tuple((mask, 0) for mask in range(1, 8))
PLANES = tuple((0, mask) for mask in range(1, CHUNKS))


def meet(others):
    barrier = pltpu.get_barrier_semaphore()
    for mask, planes in others:
        pl.semaphore_signal(barrier, inc=1, device_id=peer(mask, planes), device_id_type=MESH)
    pl.semaphore_wait(barrier, len(others))


class Remote:
    def __init__(self, wires, source, target, mask, planes=0):
        self.wires, self.source, self.target, self.mask = wires, source, target, (mask, planes)
        self.place = wires.count
        wires.count += 1

    def make(self):
        return pltpu.make_async_remote_copy(
            src_ref=self.source,
            dst_ref=self.target,
            send_sem=self.wires.send.at[self.place],
            recv_sem=self.wires.recv.at[self.place],
            device_id=peer(*self.mask),
            device_id_type=MESH,
        )

    def start(self):
        self.make().start()

    def arrived(self):
        self.make().wait_recv()

    def left(self):
        self.make().wait_send()


class Wires:
    def __init__(self, send, recv, local):
        self.send, self.recv, self.local = send, recv, local
        self.count = 0
        self.local_count = 0

    def load(self, pairs):
        copies = [
            pltpu.make_async_copy(source, target, self.local.at[place])
            for place, (source, target) in enumerate(pairs)
        ]
        for copy in copies:
            copy.start()
        for copy in copies:
            copy.wait()


class Gather:
    def __init__(self, wires, own, target):
        rows = target.shape[2] // 2
        self.wires, self.own = wires, own
        self.near, self.far, self.core_first, self.core_near, self.core_far = [], [], [], [], []
        self.home = []

        def place(chunk, slot, half):
            return target.at[chunk, slot, pl.ds(half * rows, rows)]

        for chunk, (first, second) in enumerate(ROUTES):
            near, far = SLOT[first], SLOT[second]
            self.home.append((own[chunk], place(chunk, 0, 0)))
            self.near.append(Remote(wires, own[chunk], place(chunk, near, 0), first))
            self.core_first.append(Remote(wires, own[chunk], place(chunk, 0, 1), CORE))
            self.far.append(Remote(wires, own[chunk], place(chunk, far, 0), second))
            self.far.append(Remote(wires, place(chunk, near, 0), place(chunk, 3, 0), second))
            self.core_near.append(Remote(wires, place(chunk, near, 0), place(chunk, near, 1), CORE))
            self.core_far.append(Remote(wires, place(chunk, far, 0), place(chunk, far, 1), CORE))
            self.core_far.append(Remote(wires, place(chunk, 3, 0), place(chunk, 3, 1), CORE))

    def first(self):
        for copy in self.near + self.core_first:
            copy.start()
        self.wires.load(self.home)

    def second(self):
        for chunk, copy in enumerate(self.near):
            copy.arrived()
            self.far[2 * chunk].start()
            self.far[2 * chunk + 1].start()
            self.core_near[chunk].start()

    def third(self):
        for place, copy in enumerate(self.far):
            copy.arrived()
            self.core_far[place].start()

    def last(self):
        for copy in self.core_first + self.core_near + self.core_far:
            copy.arrived()
        for copy in self.near + self.far + self.core_first + self.core_near + self.core_far:
            copy.left()

    def steps(self):
        return [self.first, self.second, self.third, self.last]


class Scatter:
    def __init__(self, wires, own, other, landing, stage, done):
        from_core, from_far, from_near = landing
        self.wires, self.own, self.landing, self.stage, self.done = wires, own, landing, stage, done
        self.core = [Remote(wires, other.at[chunk], from_core.at[chunk], CORE) for chunk in range(2)]
        self.far = [
            Remote(wires, stage[0].at[chunk], from_far.at[chunk], first)
            for chunk, (_, first) in enumerate(ROUTES)
        ]
        self.near = [
            Remote(wires, stage[2].at[chunk, 0], from_near.at[chunk], last)
            for chunk, (last, _) in enumerate(ROUTES)
        ]

    def first(self):
        for copy in self.core:
            copy.start()

    def second(self):
        left, right = self.stage[:2]
        pairs = []
        for chunk, (_, first) in enumerate(ROUTES):
            self.core[chunk].arrived()
            for place, slot in enumerate((SLOT[first], 3)):
                pairs.append((self.own.at[chunk, slot], left.at[chunk, place]))
                pairs.append((self.landing[0].at[chunk, slot], right.at[chunk, place]))
        self.wires.load(pairs)
        for chunk in range(2):

            @pl.loop(0, left.shape[2] // STRIPE)
            def _(step):
                span = pl.ds(step * STRIPE, STRIPE)
                total = left[chunk, :, span].astype(jnp.float32) + right[chunk, :, span].astype(jnp.float32)
                left[chunk, :, span] = total.astype(jnp.bfloat16)

            self.far[chunk].start()

    def third(self):
        stage = self.stage[2]
        pairs = []
        for chunk, (last, _) in enumerate(ROUTES):
            self.far[chunk].arrived()
            pairs.append((self.own.at[chunk, SLOT[last]], stage.at[chunk, 0]))
            pairs.append((self.landing[0].at[chunk, SLOT[last]], stage.at[chunk, 1]))
            pairs.append((self.landing[1].at[chunk, 1], stage.at[chunk, 2]))
        self.wires.load(pairs)
        for chunk in range(2):

            @pl.loop(0, stage.shape[2] // STRIPE)
            def _(step):
                span = pl.ds(step * STRIPE, STRIPE)
                total = stage[chunk, 0, span].astype(jnp.float32)
                for place in range(1, 3):
                    total += stage[chunk, place, span].astype(jnp.float32)
                stage[chunk, 0, span] = total.astype(jnp.bfloat16)

            self.near[chunk].start()
        for copy in self.far:
            copy.left()

    def last(self):
        stage = self.stage[3]
        for chunk in range(2):
            self.near[chunk].arrived()
            self.wires.load(
                [
                    (self.own.at[chunk, 0], stage.at[0]),
                    (self.landing[0].at[chunk, 0], stage.at[1]),
                    (self.landing[1].at[chunk, 0], stage.at[2]),
                    (self.landing[2].at[chunk], stage.at[3]),
                ]
            )

            @pl.loop(0, stage.shape[1] // STRIPE)
            def _(step):
                span = pl.ds(step * STRIPE, STRIPE)
                total = stage[0, span].astype(jnp.float32)
                for place in range(1, 4):
                    total += stage[place, span].astype(jnp.float32)
                self.done(chunk, span, total)

        for copy in self.near + self.core:
            copy.left()

    def steps(self):
        return [self.first, self.second, self.third, self.last]


def stage_shapes(rows, width):
    return [
        pltpu.VMEM((2, 2, rows, width), jnp.bfloat16),
        pltpu.VMEM((2, 2, rows, width), jnp.bfloat16),
        pltpu.VMEM((2, 3, rows, width), jnp.bfloat16),
        pltpu.VMEM((4, rows, width), jnp.bfloat16),
    ]


def landing_shapes(rows, width):
    return [
        jax.ShapeDtypeStruct((2, CHIPS, rows, width), jnp.bfloat16),
        jax.ShapeDtypeStruct((2, 2, rows, width), jnp.bfloat16),
        jax.ShapeDtypeStruct((2, rows, width), jnp.bfloat16),
    ]


def partial_shapes(rows, width):
    return [jax.ShapeDtypeStruct((2, CHIPS, rows, width), jnp.bfloat16)] * 2


def wire_shapes(count):
    return [
        pltpu.SemaphoreType.DMA((count,)),
        pltpu.SemaphoreType.DMA((count,)),
        pltpu.SemaphoreType.DMA((8,)),
    ]


def call(kernel, identity, inputs, outputs, scratch, megabytes):
    return pl.pallas_call(
        kernel,
        in_specs=[pl.BlockSpec(memory_space=place) for _, place in inputs],
        out_specs=[pl.BlockSpec(memory_space=place) for _, place in outputs],
        out_shape=[shape for shape, _ in outputs],
        scratch_shapes=scratch,
        compiler_params=pltpu.CompilerParams(
            collective_id=identity, has_side_effects=True, vmem_limit_bytes=megabytes * MB
        ),
    )(*[array for array, _ in inputs])


HBM, VMEM, SMEM = pl.ANY, pltpu.VMEM, pltpu.SMEM


def move_rows(source, target):
    @pl.loop(0, source.shape[0] // STRIPE)
    def _(step):
        span = pl.ds(step * STRIPE, STRIPE)
        target[span] = source[span]


def half_rows(index, rows):
    return pl.ds(pl.multiple_of(index * rows, STRIPE), rows)


def columns_of(index, columns):
    return pl.ds(pl.multiple_of(index * columns, columns), columns)


def at_step(step, actions):
    for when, action in actions.items():
        pl.when(step == when)(action)


def project_phase(gathered, states, weight_ref, cosine, sine, actions):
    tokens = gathered.shape[2]

    def body(rows_ref, cosine_ref, sine_ref, out):
        at_step(pl.program_id(0) * CHIPS + pl.program_id(1), actions)
        product = dot(rows_ref[0, 0], weight_ref[...].reshape(D, 3 * HEAD))
        angles = (cosine_ref[0], sine_ref[0])
        query = spin(product[:, :HEAD], *angles) * (1.0 / math.sqrt(HEAD))
        key = spin(product[:, HEAD : 2 * HEAD], *angles)
        out[0, 0] = jnp.concatenate([query, key, product[:, 2 * HEAD :]], axis=1).astype(jnp.bfloat16)

    here = lambda chunk, chip: (chunk, chip, 0, 0)
    table = pl.BlockSpec((1, tokens, HEAD // 2), lambda chunk, chip: (chunk, 0, 0))
    pltpu.emit_pipeline(
        body,
        grid=(2, CHIPS),
        in_specs=[pl.BlockSpec((1, 1, tokens, gathered.shape[3]), here), table, table],
        out_specs=[pl.BlockSpec((1, 1, tokens, 3 * HEAD), here)],
    )(gathered, cosine, sine, states)


def attend_phase(pair, states, mixed, own, other, lengths_ref, places, weight_ref, keys, values, actions):
    tokens, rows, width = mixed.shape[2], own.shape[2], own.shape[3]
    blocks = 2 * (pair + 1)

    def body(*refs):
        state_refs, (mixed_ref, own_ref, other_ref) = refs[: pair + 1], refs[pair + 1 :]
        chip, side_at = pl.program_id(0), pl.program_id(1)
        at_step(2 * chip + side_at, actions)

        @pl.when(side_at == 0)
        def _():
            for block in range(blocks):
                ref = state_refs[block // 2]
                keys[pl.ds(block * tokens, tokens)] = ref[block % 2, 0, :, HEAD : 2 * HEAD]
                values[pl.ds(block * tokens, tokens)] = ref[block % 2, 0, :, 2 * HEAD :]

        for side in range(2):

            @pl.when(side_at == side)
            def _():
                chunk = 2 * pair + side
                count = tokens * (chunk + 1)
                scores = dot_t(state_refs[pair][side, 0, :, :HEAD], keys[:count])
                mask = seen(places[0][...], places[1][...], chunk, count, tokens, lengths_ref, chip)
                scores = jnp.where(mask, scores, floor_score)
                highest = jnp.max(scores, axis=1, keepdims=True)
                exponent = jnp.exp(scores - highest)
                total = jnp.sum(exponent, axis=1, keepdims=True)
                probs = (exponent * (1.0 / total)).astype(jnp.bfloat16)
                mixed_ref[0, 0] = dot(probs, values[:count]).astype(jnp.bfloat16)

        partial = dot(mixed_ref[0, 0], weight_ref[...]).astype(jnp.bfloat16)
        own_ref[0, 0] = partial[:rows]
        other_ref[0, 0] = partial[rows:]

    here = lambda chip, side: (side, chip, 0, 0)
    state = pl.BlockSpec((2, 1, tokens, 3 * HEAD), lambda chip, side: (0, chip, 0, 0))
    pltpu.emit_pipeline(
        body,
        grid=(CHIPS, 2),
        in_specs=[state] * (pair + 1),
        out_specs=[pl.BlockSpec((1, 1, tokens, HEAD), here)] + [pl.BlockSpec((1, 1, rows, width), here)] * 2,
    )(*states[: pair + 1], mixed, own, other)


def attend_back_phase(
    pair, branch, states, head_grads, own, other, lengths_ref, places, out_weight, weight_ref,
    tables, keys, values, sums, late_sums, actions
):
    tokens, rows, width = branch.shape[2], own.shape[2], own.shape[3]
    blocks = 2 * (pair + 1)
    edge = 2 * tokens

    def body(*refs):
        branch_ref, state_refs = refs[0], refs[1 : pair + 2]
        cosine_ref, sine_ref, grads_ref, own_ref, other_ref = refs[pair + 2 :]
        chip, step = pl.program_id(0), pl.program_id(1)
        at_step(2 * chip + step, actions)

        @pl.when(step == 0)
        def _():
            for block in range(blocks):
                ref = state_refs[block // 2]
                keys[pl.ds(block * tokens, tokens)] = ref[block % 2, 0, :, HEAD : 2 * HEAD]
                values[pl.ds(block * tokens, tokens)] = ref[block % 2, 0, :, 2 * HEAD :]
            if pair == 1:
                for place in range(2):
                    sums[place][chip] = jnp.zeros(sums[place].shape[1:], jnp.float32)
                    late_sums[place][...] = jnp.zeros(late_sums[place].shape, jnp.float32)

        def add(place, term):
            early = min(term.shape[0], edge)
            sums[place][chip, :early] += term[:early]
            if term.shape[0] > edge:
                late_sums[place][: term.shape[0] - edge] += term[edge:]

        for side in range(2):

            @pl.when(step == 1 - side)
            def _():
                chunk = 2 * pair + side
                count = tokens * (chunk + 1)
                mixed_grad = dot_t(branch_ref[0, 0], out_weight[...]).astype(jnp.bfloat16)
                query = state_refs[pair][side, 0, :, :HEAD]
                scores = dot_t(query, keys[:count])
                mask = seen(places[0][...], places[1][...], chunk, count, tokens, lengths_ref, chip)
                scores = jnp.where(mask, scores, floor_score)
                highest = jnp.max(scores, axis=1, keepdims=True)
                exponent = jnp.exp(scores - highest)
                probs = exponent * (1.0 / jnp.sum(exponent, axis=1, keepdims=True))
                add(1, dot_tn(probs.astype(jnp.bfloat16), mixed_grad))
                prob_grad = dot_t(mixed_grad, values[:count])
                inner = jnp.sum(probs * prob_grad, axis=1, keepdims=True)
                score_grad = (probs * (prob_grad - inner)).astype(jnp.bfloat16)
                add(0, dot_tn(score_grad, query))
                query_grad = dot(score_grad, keys[:count]) * (1.0 / math.sqrt(HEAD))
                angles = (cosine_ref[0], sine_ref[0])
                span = slice(side * tokens, (side + 1) * tokens)
                if pair == 1:
                    key_grad, value_grad = late_sums[0][span], late_sums[1][span]
                else:
                    key_grad, value_grad = sums[0][chip, span], sums[1][chip, span]
                grads_ref[0, 0] = jnp.concatenate(
                    [spin_back(query_grad, *angles), spin_back(key_grad, *angles), value_grad], axis=1
                ).astype(jnp.bfloat16)

        partial = dot_t(grads_ref[0, 0], weight_ref[...].reshape(D, 3 * HEAD)).astype(jnp.bfloat16)
        own_ref[0, 0] = partial[:rows]
        other_ref[0, 0] = partial[rows:]

    here = lambda chip, step: (1 - step, chip, 0, 0)
    state = pl.BlockSpec((2, 1, tokens, 3 * HEAD), lambda chip, step: (0, chip, 0, 0))
    table = pl.BlockSpec((1, tokens, HEAD // 2), lambda chip, step: (1 - step, 0, 0))
    pltpu.emit_pipeline(
        body,
        grid=(CHIPS, 2),
        in_specs=[pl.BlockSpec((1, 1, tokens, width), here)] + [state] * (pair + 1) + [table] * 2,
        out_specs=[pl.BlockSpec((1, 1, tokens, 3 * HEAD), here)]
        + [pl.BlockSpec((1, 1, rows, width), here)] * 2,
    )(branch, *states[: pair + 1], *tables, head_grads, own, other)


def feed_phase(rows_in, grads_in, hidden, unit_grads, back_parts, out_parts, weights, actions):
    tokens, width = rows_in.shape[2:]
    rows = tokens // 2
    shards, columns = weights.shape[0], weights.shape[2]
    share = columns // 2

    def body(rows_ref, out_grad_ref, hidden_ref, units_ref, back_own, back_other, out_own, out_other):
        at_step(pl.program_id(0) * CHIPS + pl.program_id(1), actions)
        hidden_grad = None
        for shard in range(shards):
            grad = out_grad_ref[0, 0, :, shard * columns : (shard + 1) * columns]
            term = dot_t(grad, weights[shard, width:, :])
            hidden_grad = term if hidden_grad is None else hidden_grad + term
        back = None
        for shard in range(shards):
            both = dot(rows_ref[0, 0], weights[shard, :width, :])
            gate, upward = both[:, :share], both[:, share:]
            grad = hidden_grad[:, shard * share : (shard + 1) * share]
            sigmoid = jax.nn.sigmoid(gate)
            swish = gate * sigmoid
            hidden_ref[0, 0, :, shard * share : (shard + 1) * share] = (swish * upward).astype(jnp.bfloat16)
            gate_grad = grad * upward * sigmoid * (1.0 + gate * (1.0 - sigmoid))
            units_ref[shard, 0, 0] = jnp.concatenate([gate_grad, grad * swish], axis=1).astype(jnp.bfloat16)
            term = dot_t(units_ref[shard, 0, 0], weights[shard, :width, :])
            back = term if back is None else back + term
        back = back.astype(jnp.bfloat16)
        back_own[0, 0] = back[:rows]
        back_other[0, 0] = back[rows:]
        for shard in range(shards):
            span = slice(shard * columns, (shard + 1) * columns)
            value = dot(hidden_ref[0, 0], weights[shard, width:, :]).astype(jnp.bfloat16)
            out_own[0, 0, :, span] = value[:rows]
            out_other[0, 0, :, span] = value[rows:]

    here = lambda chunk, chip: (chunk, chip, 0, 0)
    wide = pl.BlockSpec((1, 1, tokens, width), here)
    narrow = pl.BlockSpec((1, 1, rows, width), here)
    pltpu.emit_pipeline(
        body,
        grid=(2, CHIPS),
        in_specs=[wide, wide],
        out_specs=[
            pl.BlockSpec((1, 1, tokens, hidden.shape[3]), here),
            pl.BlockSpec((shards, 1, 1, tokens, columns), lambda chunk, chip: (0, chunk, chip, 0, 0)),
        ]
        + [narrow] * 4,
    )(rows_in, grads_in, hidden, unit_grads, *back_parts, *out_parts)


def down_grad_phase(hidden, grads, out, total, actions):
    _, chips, tokens, units = hidden[0].shape
    planes, _, columns = out.shape

    def body(*refs):
        out_ref = refs[4]
        block, step = pl.program_id(0), pl.program_id(1)
        at_step(8 * block + step, actions)

        @pl.when(step == 0)
        def _():
            total[...] = jnp.zeros(total.shape, jnp.float32)

        for place in range(2):

            @pl.when(lax.div(step, 4) == place)
            def _():
                left, right = refs[2 * place], refs[2 * place + 1]
                total[...] += dot_tn(
                    left[0].reshape(2 * tokens, units), right[0].reshape(2 * tokens, columns)
                )

        @pl.when(step == 7)
        def _():
            out_ref[0] = total[...].astype(jnp.bfloat16)

    specs, operands = [], []
    for pair in (1, 0):
        first = 0 if pair == 1 else 4

        def at(step, first=first):
            return jnp.clip(step - first, 0, 3)

        specs.append(
            pl.BlockSpec(
                (1, 2, tokens, units),
                lambda block, step, at=at: (lax.div(at(step), 2), lax.rem(at(step), 2), 0, 0),
            )
        )
        specs.append(
            pl.BlockSpec(
                (1, 2, tokens, columns),
                lambda block, step, at=at: (lax.div(at(step), 2), lax.rem(at(step), 2), 0, block),
            )
        )
        operands += [hidden[pair], grads[pair]]
    pltpu.emit_pipeline(
        body,
        grid=(planes, 8),
        in_specs=specs,
        out_specs=[pl.BlockSpec((1, units, columns), lambda block, step: (block, 0, 0))],
    )(*operands, out)


def bf16(*shape):
    return jax.ShapeDtypeStruct(shape, jnp.bfloat16)


def f32(*shape):
    return jax.ShapeDtypeStruct(shape, jnp.float32)


def start_up(
    activations, cotangent, head_block, out_block, unit_block, down_block, lengths_block, gain
):
    _, tokens, width = activations.shape
    rows = tokens // 2
    devices, unit_rows, columns = unit_block.shape
    down_rows = down_block.shape[1]
    planes, _, sub_rows, _ = head_block.shape
    edge = devices * unit_rows

    def kernel(*refs):
        act, cot, head_in, out_in, unit_in, down_in, length_in, gain_ref = refs[:8]
        own_rows, own_grads, gathered = refs[8], refs[9], refs[10:12]
        head_weight, head_output, feed_own, lengths_all = refs[12:16]
        act_groups, cot_groups, traded, spread, other_half, normed = refs[16:22]
        wires = Wires(*refs[22:])
        place, plane = lax.axis_index("dp"), lax.axis_index("fsdp")
        core = lax.rem(place, 2)

        def half(index):
            return pl.ds(pl.multiple_of(index * rows, STRIPE), rows)

        def move(source, target):
            @pl.loop(0, rows // STRIPE)
            def _(step):
                span = pl.ds(step * STRIPE, STRIPE)
                target[span] = source[span]

        def trade(array, groups, own):
            label = [2 * core + group for group in range(2)]
            inside = [
                Remote(wires, array.at[group, half(1 - core)], groups.at[label[group]], CORE)
                for group in range(2)
            ]
            outside = [
                Remote(wires, groups.at[flip(plane, mask)], own.at[plane], 0, mask)
                for mask in range(1, CHUNKS)
            ]

            def keep():
                for group in range(2):
                    move(array.at[group, half(core)], groups.at[label[group]])

            return inside, keep, outside, lambda: move(groups.at[plane], own.at[plane])

        act_inside, act_keep, act_outside, act_own = trade(act, act_groups, own_rows)
        cot_inside, cot_keep, cot_outside, cot_own = trade(cot, cot_groups, own_grads)
        head_trade = [
            Remote(wires, head_in.at[flip(plane, mask)], traded.at[plane], 0, mask)
            for mask in range(1, CHUNKS)
        ]
        head_spread, feed_spread = [], []
        for mask in range(1, devices):
            other = flip(place, mask)
            head_spread.append(
                Remote(
                    wires,
                    traded.at[lax.div(other, 2), lax.rem(other, 2)],
                    spread.at[place, plane],
                    mask,
                )
            )
            feed_spread.append(
                Remote(
                    wires,
                    unit_in.at[other],
                    feed_own.at[pl.ds(pl.multiple_of(place * unit_rows, unit_rows), unit_rows)],
                    mask,
                )
            )
            feed_spread.append(
                Remote(
                    wires,
                    down_in.at[other],
                    feed_own.at[pl.ds(pl.multiple_of(edge + place * down_rows, down_rows), down_rows)],
                    mask,
                )
            )
            feed_spread.append(Remote(wires, length_in, lengths_all.at[place], mask))

        def over_planes(block):
            mine, theirs = block(plane), block(flip(plane, 2))
            return (
                [Remote(wires, mine, mine, 0, 1), Remote(wires, mine, mine, 0, 2)],
                Remote(wires, theirs, theirs, 0, 1),
            )

        head_near, head_relay = over_planes(lambda index: spread.at[:, index])
        out_near, out_relay = over_planes(
            lambda index: head_output.at[:, pl.ds(pl.multiple_of(index * columns, columns), columns)]
        )
        core_half = Remote(wires, spread.at[:, :, :, pl.ds(HEAD, HEAD)], other_half, CORE)
        moves = [
            Gather(wires, [normed.at[2 * pair], normed.at[2 * pair + 1]], gathered[pair])
            for pair in range(2)
        ]

        meet(PLANE + PLANES)
        for copy in act_inside + cot_inside + head_trade + feed_spread:
            copy.start()
        act_keep()
        for copy in act_inside:
            copy.arrived()
        for copy in act_outside:
            copy.start()
        cot_keep()
        act_own()
        traded[plane] = head_in[plane]
        columns_at = pl.ds(pl.multiple_of(plane * columns, columns), columns)
        head_output[:, columns_at] = out_in[...]
        feed_own[pl.ds(pl.multiple_of(place * unit_rows, unit_rows), unit_rows)] = unit_in[place]
        feed_own[pl.ds(pl.multiple_of(edge + place * down_rows, down_rows), down_rows)] = down_in[place]
        lengths_all[place] = length_in[...]
        for copy in head_trade:
            copy.arrived()
        for copy in head_spread:
            copy.start()
        spread[place, plane] = traded[lax.div(place, 2), core]
        for copy in head_spread + cot_inside:
            copy.arrived()
        cot_own()
        for copy in act_outside:
            copy.arrived()
        for copy in head_near + out_near + cot_outside:
            copy.start()

        for chunk in range(CHUNKS):

            @pl.loop(0, rows // STRIPE)
            def _(step):
                span = pl.ds(step * STRIPE, STRIPE)
                values = own_rows[chunk, span].astype(jnp.float32)
                factor = lax.rsqrt(jnp.mean(values * values, axis=1, keepdims=True) + epsilon)
                normed[chunk, span] = (values * factor * gain_ref[...]).astype(jnp.bfloat16)

        moves[0].first()
        moves[0].second()
        moves[1].first()
        moves[0].third()
        moves[1].second()
        for copy in head_near + out_near:
            copy.arrived()
        head_relay.start()
        out_relay.start()
        moves[0].last()
        moves[1].third()
        head_relay.arrived()
        core_half.start()
        moves[1].last()
        out_relay.arrived()
        core_half.arrived()
        head_weight[:, :, :, :HEAD] = spread[:, :, :, :HEAD]
        for index in range(2):

            @pl.when(core == index)
            def _():
                mine, theirs = (1 + index) * HEAD, (2 - index) * HEAD
                head_weight[:, :, :, mine : mine + HEAD] = spread[:, :, :, HEAD:]
                head_weight[:, :, :, theirs : theirs + HEAD] = other_half[...]

        for copy in feed_spread + cot_outside:
            copy.arrived()
        for copy in (
            act_inside + cot_inside + head_trade + feed_spread + act_outside + head_spread
            + head_near + out_near + [head_relay, out_relay, core_half] + cot_outside
        ):
            copy.left()

    own = bf16(CHUNKS, rows, width)
    outs = call(
        kernel,
        1,
        [(activations, VMEM), (cotangent, VMEM), (head_block, VMEM), (out_block, VMEM)]
        + [(unit_block, VMEM), (down_block, VMEM), (lengths_block, VMEM), (gain, VMEM)],
        [(own, VMEM), (own, VMEM)]
        + [(bf16(2, CHIPS, tokens, width), HBM)] * 2
        + [(bf16(devices, planes, sub_rows, 3 * HEAD), VMEM), (bf16(HEAD, width), VMEM)]
        + [(bf16(devices * (unit_rows + down_rows), columns), VMEM)]
        + [(jax.ShapeDtypeStruct((devices,) + lengths_block.shape, jnp.int32), VMEM)],
        [
            pltpu.VMEM((CHUNKS, rows, width), jnp.bfloat16),
            pltpu.VMEM((CHUNKS, rows, width), jnp.bfloat16),
            pltpu.VMEM((planes, 2, sub_rows, columns), jnp.bfloat16),
            pltpu.VMEM((devices, planes, sub_rows, columns), jnp.bfloat16),
            pltpu.VMEM((devices, planes, sub_rows, HEAD), jnp.bfloat16),
            pltpu.VMEM((CHUNKS, rows, width), jnp.bfloat16),
        ]
        + wire_shapes(90),
        56,
    )
    return outs[0], outs[1], outs[2:4], outs[4], outs[5], outs[6], outs[7]


def attend_and_norm(
    rows_all, out_grads, feed_own, weight, cosine, sine, lengths, places, out_weight, inputs, gain
):
    _, rows, width = inputs.shape
    tokens = 2 * rows
    planes = CHUNKS
    whole_pair = bf16(2, CHIPS, tokens, width)

    def kernel(*refs):
        gathered, grads_ref, feed_ref, head_ref, cosine_ref, sine_ref = refs[:2], *refs[2:7]
        lengths_ref, place_q, place_k, weight_ref, inputs_ref, gain_ref = refs[7:13]
        refs = refs[13:]
        states, mixed, middle, normed, target, grads_all, feed_all = refs[:2], refs[2:4], *refs[4:9]
        parts, landings = (refs[9:11], refs[11:13]), (refs[13:16], refs[16:19])
        stage, keys, values, normed_late = refs[19:23], refs[23], refs[24], refs[25]
        wires = Wires(*refs[26:])
        plane = lax.axis_index("fsdp")

        def finish(pair):
            def done(chunk, span, total):
                at = 2 * pair + chunk
                total = total + inputs_ref[at, span].astype(jnp.float32)
                middle[at, span] = total
                factor = lax.rsqrt(jnp.mean(total * total, axis=1, keepdims=True) + epsilon)
                kept = normed if pair == 0 else normed_late
                kept[chunk, span] = (total * factor * gain_ref[...]).astype(jnp.bfloat16)

            return done

        sums = [
            Scatter(wires, *parts[pair], landings[pair], stage, finish(pair)) for pair in range(2)
        ]
        move = Gather(wires, [normed_late.at[0], normed_late.at[1]], target)
        grad_move = Gather(wires, [grads_ref.at[2], grads_ref.at[3]], grads_all)
        near = Remote(wires, feed_ref, feed_all.at[plane], 0, 1)
        across_middle = Remote(wires, feed_ref, feed_all.at[plane], 0, 2)
        relay = Remote(
            wires, feed_all.at[flip(plane, 2)], feed_all.at[flip(plane, 2)], 0, 1
        )
        places_in = (place_q, place_k)

        meet(SIDES + PLANES[:2])
        near.start()
        across_middle.start()
        grad_move.first()
        wires.load([(feed_ref, feed_all.at[plane])])
        project_phase(
            gathered[0], states[0], head_ref, cosine_ref.at[0], sine_ref.at[0], {7: grad_move.second}
        )
        project_phase(gathered[1], states[1], head_ref, cosine_ref.at[1], sine_ref.at[1], {})
        attend_phase(
            1, states, mixed[1], *parts[1], lengths_ref, places_in, weight_ref, keys, values,
            {3: grad_move.third},
        )
        sums[1].first()
        attend_phase(
            0, states, mixed[0], *parts[0], lengths_ref, places_in, weight_ref, keys, values,
            {5: sums[1].second},
        )
        sums[0].first()
        grad_move.last()
        sums[1].third()
        sums[0].second()
        sums[1].last()
        move.first()
        sums[0].third()
        across_middle.arrived()
        relay.start()
        move.second()
        sums[0].last()
        move.third()
        move.last()
        near.arrived()
        relay.arrived()
        for copy in (near, across_middle, relay):
            copy.left()

    pair_parts = [(shape, HBM) for shape in partial_shapes(rows, width)]
    landing = [(shape, HBM) for shape in landing_shapes(rows, width)]
    outs = call(
        kernel,
        2,
        [(rows_all[0], HBM), (rows_all[1], HBM), (out_grads, VMEM), (feed_own, VMEM)]
        + [(weight, VMEM), (cosine, HBM), (sine, HBM)]
        + [(lengths, SMEM), (places[0], VMEM), (places[1], VMEM), (out_weight, VMEM)]
        + [(inputs, VMEM), (gain, VMEM)],
        [(bf16(2, CHIPS, tokens, 3 * HEAD), HBM)] * 2
        + [(bf16(2, CHIPS, tokens, HEAD), HBM)] * 2
        + [(f32(CHUNKS, rows, width), VMEM), (bf16(2, rows, width), VMEM)]
        + [(whole_pair, HBM)] * 2
        + [(bf16(planes, *feed_own.shape), HBM)]
        + pair_parts * 2
        + landing * 2,
        stage_shapes(rows, width)
        + [pltpu.VMEM((CHUNKS * tokens, HEAD), jnp.bfloat16)] * 2
        + [pltpu.VMEM((2, rows, width), jnp.bfloat16)]
        + wire_shapes(50),
        60,
    )
    return outs[:2], outs[2:4], outs[4], outs[5], outs[6], outs[7], outs[8]


def norm_back(values, gain, gradient):
    factor = lax.rsqrt(jnp.mean(values * values, axis=1, keepdims=True) + epsilon)
    scaled = values * factor
    pulled = gradient * gain
    back = factor * (pulled - scaled * jnp.mean(pulled * scaled, axis=1, keepdims=True))
    return back, gradient * scaled


def feed_forward(normed_own, normed_late, grads_late, weights, middle, out_grad_own, gain, units):
    _, rows, width = middle.shape
    tokens = 2 * rows
    shards, columns = weights.shape[0], weights.shape[2]
    whole_pair = bf16(2, CHIPS, tokens, width)

    def kernel(*refs):
        normed_ref, normed_late_ref, grads_late_ref = refs[:3]
        weight_ref, middle_ref, own_grad, gain_ref = refs[3:7]
        refs = (None, *refs)
        normed_early, branch, grads_early = refs[8], refs[9], refs[27]
        hidden, unit_grads = refs[10:12], refs[12:14]
        back_parts, out_parts = (refs[14:16], refs[16:18]), (refs[18:20], refs[20:22])
        middle_grad, gain_sum, landing = refs[22], refs[23], refs[24:27]
        down_parts = refs[28]
        stage, own_branch, wires = refs[29:33], refs[33], Wires(*refs[34:])
        meet(SIDES)
        gain_sum[...] = jnp.zeros(gain_sum.shape, jnp.float32)

        def done(chunk, span, total):
            back, gain_terms = norm_back(middle_ref[2 + chunk, span], gain_ref[...], total)
            gain_sum[...] += gain_terms
            back = back + own_grad[2 + chunk, span].astype(jnp.float32)
            middle_grad[chunk, span] = back
            own_branch[chunk, span] = back.astype(jnp.bfloat16)

        move = Gather(wires, [normed_ref.at[0], normed_ref.at[1]], normed_early)
        sums = Scatter(wires, *back_parts[1], landing, stage, done)
        late_move = Gather(wires, [own_branch.at[0], own_branch.at[1]], branch)
        grad_move = Gather(wires, [own_grad.at[0], own_grad.at[1]], grads_early)
        move.first()
        grad_move.first()
        feed_phase(
            normed_late_ref, grads_late_ref, hidden[1], unit_grads[1], back_parts[1], out_parts[1],
            weight_ref,
            {2: move.second, 3: grad_move.second, 5: move.third, 7: grad_move.third},
        )
        sums.first()
        move.last()
        grad_move.last()
        feed_phase(
            normed_early, grads_early, hidden[0], unit_grads[0], back_parts[0], out_parts[0], weight_ref,
            {1: sums.second, 4: sums.third, 6: lambda: (sums.last(), late_move.first()) and None},
        )
        late_move.second()
        pl.run_scoped(
            lambda total: down_grad_phase(
                hidden, (grads_early, grads_late_ref), down_parts, total, {30: late_move.third}
            ),
            pltpu.VMEM((units, columns), jnp.float32),
        )
        late_move.last()

    outs = call(
        kernel,
        3,
        [(normed_own, VMEM), (normed_late, HBM), (grads_late, HBM)]
        + [(weights, VMEM), (middle, VMEM), (out_grad_own, VMEM), (gain, VMEM)],
        [(whole_pair, HBM)] * 2
        + [(bf16(2, CHIPS, tokens, units), HBM)] * 2
        + [(bf16(shards, 2, CHIPS, tokens, columns), HBM)] * 2
        + [(shape, HBM) for shape in partial_shapes(rows, width)] * 4
        + [(f32(2, rows, width), VMEM), (f32(STRIPE, width), VMEM)]
        + [(shape, HBM) for shape in landing_shapes(rows, width)]
        + [(whole_pair, HBM), (bf16(shards, units, columns), HBM)],
        stage_shapes(rows, width) + [pltpu.VMEM((2, rows, width), jnp.bfloat16)] + wire_shapes(50),
        62,
    )
    return (
        outs[19], outs[0], outs[1], outs[20], outs[4:6], outs[6:8], (outs[10:12], outs[12:14]), outs[14],
        outs[15],
    )


def attend_back(
    states, lengths, places, out_weight, weight, cosine, sine, branch_late, back_early, out_parts,
    middle, out_grad_own, inputs, middle_grad_late, gains
):
    _, rows, width = middle.shape
    tokens = 2 * rows

    def kernel(*refs):
        states_in, (lengths_ref, place_q, place_k, out_ref, weight_ref, cosine_ref, sine_ref) = (
            refs[:2],
            refs[2:9],
        )
        late_branch, back_parts, outs_in = refs[9], refs[10:12], (refs[12:14], refs[14:16])
        middle_ref, own_grad, inputs_ref, late_grad, gain_one, gain_two = refs[16:22]
        head_grads, early_branch, output_groups, input_grad = refs[22:24], refs[24], refs[25], refs[26]
        gain_sums = refs[27]
        parts = (refs[28:30], refs[30:32])
        landings = [refs[32 + 3 * place : 35 + 3 * place] for place in range(5)]
        stage, early_grad, own_branch, keys, values = refs[47:51], refs[51], refs[52], refs[53], refs[54]
        sums, late_sums, outputs, wires = refs[55:57], refs[57:59], refs[59], Wires(*refs[60:])
        plane = lax.axis_index("fsdp")
        meet(SIDES + PLANES)
        gain_sums[...] = jnp.zeros(gain_sums.shape, jnp.float32)

        def middle_done(chunk, span, total):
            back, gain_terms = norm_back(
                middle_ref[chunk, span].astype(jnp.float32), gain_two[...], total
            )
            gain_sums[1] += gain_terms
            back = back + own_grad[chunk, span].astype(jnp.float32)
            early_grad[chunk, span] = back
            own_branch[chunk, span] = back.astype(jnp.bfloat16)

        def output_done(pair):
            def done(chunk, span, total):
                at = 2 * pair + chunk
                outputs[at, span] = (middle_ref[at, span] + total).astype(jnp.bfloat16)

            return done

        def input_done(pair):
            def done(chunk, span, total):
                at = 2 * pair + chunk
                back, gain_terms = norm_back(
                    inputs_ref[at, span].astype(jnp.float32), gain_one[...], total
                )
                gain_sums[0] += gain_terms
                direct = late_grad if pair == 1 else early_grad
                input_grad[at, span] = (direct[chunk, span] + back).astype(jnp.bfloat16)

            return done

        middle_sum = Scatter(wires, *back_parts, landings[0], stage, middle_done)
        move = Gather(wires, [own_branch.at[0], own_branch.at[1]], early_branch)
        output_sums = [
            Scatter(wires, *outs_in[pair], landings[1 + pair], stage, output_done(pair))
            for pair in range(2)
        ]
        input_sums = [
            Scatter(wires, *parts[pair], landings[3 + pair], stage, input_done(pair)) for pair in range(2)
        ]

        def back_through(pair, branch, actions):
            attend_back_phase(
                pair, branch, states_in, head_grads[pair], *parts[pair], lengths_ref,
                (place_q, place_k), out_ref, weight_ref, (cosine_ref.at[pair], sine_ref.at[pair]),
                keys, values, sums, late_sums, actions,
            )

        def both(*steps):
            def run():
                for step in steps:
                    step()

            return run

        back_to_planes = [
            Remote(wires, outputs.at[flip(plane, mask)], output_groups.at[plane], 0, mask)
            for mask in range(1, CHUNKS)
        ]

        def send_back():
            for copy in back_to_planes:
                copy.start()
            wires.load([(outputs.at[plane], output_groups.at[plane])])

        middle_sum.first()
        back_through(
            1,
            late_branch,
            {
                1: middle_sum.second,
                3: output_sums[1].first,
                5: output_sums[0].first,
                7: middle_sum.third,
            },
        )
        input_sums[1].first()
        output_sums[1].second()
        middle_sum.last()
        move.first()
        move.second()
        output_sums[1].third()
        input_sums[1].second()
        move.third()
        output_sums[1].last()
        move.last()
        back_through(
            0,
            early_branch,
            {1: input_sums[1].third, 4: both(input_sums[1].last, output_sums[0].second), 7: output_sums[0].third},
        )
        input_sums[0].first()
        output_sums[0].last()
        send_back()
        input_sums[0].second()
        input_sums[0].third()
        input_sums[0].last()
        for copy in back_to_planes:
            copy.arrived()
        for copy in back_to_planes:
            copy.left()

    outs = call(
        kernel,
        4,
        [(state, HBM) for state in states]
        + [(lengths, SMEM), (places[0], VMEM), (places[1], VMEM), (out_weight, VMEM), (weight, VMEM)]
        + [(cosine, HBM), (sine, HBM), (branch_late, HBM)]
        + [(part, HBM) for part in back_early]
        + [(part, HBM) for parts in out_parts for part in parts]
        + [(middle, VMEM), (out_grad_own, VMEM), (inputs, VMEM), (middle_grad_late, VMEM)]
        + [(gains[0], VMEM), (gains[1], VMEM)],
        [(bf16(2, CHIPS, tokens, 3 * HEAD), HBM)] * 2
        + [(bf16(2, CHIPS, tokens, width), HBM)]
        + [(bf16(CHUNKS, rows, width), HBM), (bf16(CHUNKS, rows, width), VMEM)]
        + [(f32(2, STRIPE, width), VMEM)]
        + [(shape, HBM) for shape in partial_shapes(rows, width)] * 2
        + [(shape, HBM) for shape in landing_shapes(rows, width)] * 5,
        stage_shapes(rows, width)
        + [pltpu.VMEM((2, rows, width), jnp.float32), pltpu.VMEM((2, rows, width), jnp.bfloat16)]
        + [pltpu.VMEM((CHUNKS * tokens, HEAD), jnp.bfloat16)] * 2
        + [pltpu.VMEM((CHIPS, 2 * tokens, HEAD), jnp.float32)] * 2
        + [pltpu.VMEM((2 * tokens, HEAD), jnp.float32)] * 2
        + [pltpu.VMEM((CHUNKS, rows, width), jnp.bfloat16)]
        + wire_shapes(60),
        63,
    )
    return outs[:2], outs[2], outs[3], outs[4], outs[5]


def weight_grad_phase(rows_in, grads, total, fresh, actions):
    _, chips, tokens, width = rows_in.shape
    columns = grads.shape[3]

    def body(rows_ref, grads_ref):
        chunk, step = pl.program_id(0), pl.program_id(1)
        at_step(2 * chunk + step, actions)
        term = dot_tn(rows_ref[0].reshape(2 * tokens, width), grads_ref[0].reshape(2 * tokens, columns))
        if fresh:

            @pl.when(chunk + step == 0)
            def _():
                total[...] = jnp.zeros(total.shape, jnp.float32)

        total[...] += term

    here = lambda chunk, step: (chunk, step, 0, 0)
    pltpu.emit_pipeline(
        body,
        grid=(2, chips // 2),
        in_specs=[
            pl.BlockSpec((1, 2, tokens, width), here),
            pl.BlockSpec((1, 2, tokens, columns), here),
        ],
    )(rows_in, grads)


def finish(head_terms, output_terms, unit_sum, down_sum, output_groups, input_grad, gain_sums):
    devices, planes = lax.axis_size("dp"), lax.axis_size("fsdp")
    strips = unit_sum.shape[0]
    _, down_rows, columns = down_sum.shape
    _, rows, width = input_grad.shape
    in_rows = width // devices
    sub_rows = in_rows // planes

    def kernel(*refs):
        head_refs, output_refs, refs = refs[:4], refs[4:8], refs[8:]
        units_in, downs_in, output_groups_ref, grads_ref, gains = refs[:5]
        outputs, input_out, head_out, output_out, gate_up, downs, gain_out, square_out = refs[5:13]
        grad_groups, combined, other_half, mine, gathered = refs[13:18]
        head_landing, output_landing, head_two, output_two = refs[18:22]
        gain_parts, square_parts, units = refs[22:25]
        head_total, output_total, given, outs_in, wires = *refs[25:29], Wires(*refs[29:])
        place, plane = lax.axis_index("dp"), lax.axis_index("fsdp")
        core = lax.rem(place, 2)

        def part(mask):
            return combined.at[:, flip(plane, mask)], outs_in.at[:, columns_of(flip(plane, mask), columns)]

        def both(sources, targets, mask):
            return [Remote(wires, source, target, 0, mask) for source, target in zip(sources, targets)]

        landing = [(head_landing.at[index], output_landing.at[index]) for index in range(3)]
        third = both(part(3), landing[0], 1)
        first = both(part(1), landing[1], 1)
        second = both((head_two, output_two), landing[2], 2)
        core_half = Remote(wires, given, other_half, CORE)
        rows_back = [
            Remote(wires, grads_ref.at[flip(plane, mask)], grad_groups.at[plane], 0, mask)
            for mask in range(1, CHUNKS)
        ]
        spread, heads_back = [], []
        for mask in range(1, devices):
            other = flip(place, mask)
            spread.append(Remote(wires, units_in.at[:, columns_of(other, in_rows)], units.at[place], mask))
            spread.append(Remote(wires, downs_in.at[other], downs.at[place], mask))
            heads_back.append(Remote(wires, mine.at[other], gathered.at[place], mask))
        heads_over = [
            Remote(wires, gathered.at[pl.ds(2 * flip(plane, mask), 2)], head_out.at[plane], 0, mask)
            for mask in range(1, CHUNKS)
        ]

        def to_owners(groups, target):
            copies = []
            for group in range(2):
                copies.append(
                    Remote(
                        wires,
                        groups.at[2 * (1 - core) + group],
                        target.at[group, half_rows(core, rows)],
                        CORE,
                    )
                )
            return copies

        outputs_in = to_owners(output_groups_ref, outputs)
        grads_in = to_owners(grad_groups, input_out)

        def sum_over(parts_ref):
            steps = [(mask, 0) for mask in (CORE, SIDE_A, SIDE_B)] + [(0, 1), (0, 2)]
            copies = [
                Remote(wires, parts_ref.at[2 * index], parts_ref.at[2 * index + 1], mask, over)
                for index, (mask, over) in enumerate(steps)
            ]

            def step(index):
                copies[index].arrived()
                copies[index].left()
                parts_ref[2 * index + 2] = parts_ref[2 * index] + parts_ref[2 * index + 1]
                if index + 1 < len(copies):
                    copies[index + 1].start()

            return copies[0].start, step, len(steps)

        gains_start, gains_step, count = sum_over(gain_parts)
        squares_start, squares_step, _ = sum_over(square_parts)

        gain_parts[0] = jnp.concatenate(
            [jnp.sum(gains[index], axis=0, keepdims=True) for index in range(2)]
            + [jnp.zeros((6, width), jnp.float32)]
        )
        meet(PLANE + PLANES)
        for copy in rows_back + spread + outputs_in:
            copy.start()
        gains_start()
        units[place] = units_in[:, columns_of(place, in_rows)]
        downs[place] = downs_in[place]
        for group in range(2):
            move_rows(
                output_groups_ref.at[2 * core + group], outputs.at[group, half_rows(core, rows)]
            )
        move_rows(grads_ref.at[plane], grad_groups.at[plane])
        weight_grad_phase(head_refs[0], head_refs[1], head_total, True, {3: lambda: gains_step(0)})
        weight_grad_phase(
            head_refs[2], head_refs[3], head_total, False, {1: lambda: gains_step(1), 3: lambda: gains_step(2)}
        )

        def split(index):
            kept, sent = (1 + index) * HEAD, (2 - index) * HEAD

            @pl.loop(0, devices)
            def _(block):
                span = pl.ds(pl.multiple_of(block * in_rows, in_rows), in_rows)
                shape = (planes, sub_rows, HEAD)
                given[block] = head_total[span, sent : sent + HEAD].astype(jnp.bfloat16).reshape(shape)
                combined[block, :, :, :HEAD] = head_total[span, :HEAD].astype(jnp.bfloat16).reshape(shape)

        for index in range(2):
            pl.when(core == index)(functools.partial(split, index))
        core_half.start()
        weight_grad_phase(output_refs[0], output_refs[1], output_total, True, {})
        core_half.arrived()

        def join(index):
            kept = (1 + index) * HEAD

            @pl.loop(0, devices)
            def _(block):
                span = pl.ds(pl.multiple_of(block * in_rows, in_rows), in_rows)
                total = head_total[span, kept : kept + HEAD].reshape(planes, sub_rows, HEAD)
                total = total + other_half[block].astype(jnp.float32)
                combined[block, :, :, HEAD:] = total.astype(jnp.bfloat16)

        for index in range(2):
            pl.when(core == index)(functools.partial(join, index))
        third[0].start()
        weight_grad_phase(output_refs[2], output_refs[3], output_total, False, {})
        outs_in[...] = output_total[...].astype(jnp.bfloat16)
        third[1].start()
        for copy in first:
            copy.start()
        third[0].arrived()
        head_two[...] = (
            combined[:, flip(plane, 2)].astype(jnp.float32) + head_landing[0].astype(jnp.float32)
        ).astype(jnp.bfloat16)
        second[0].start()
        third[1].arrived()
        output_two[...] = (
            outs_in[:, columns_of(flip(plane, 2), columns)].astype(jnp.float32)
            + output_landing[0].astype(jnp.float32)
        ).astype(jnp.bfloat16)
        second[1].start()
        for index in range(3, count):
            gains_step(index)
        for copy in rows_back:
            copy.arrived()
        for copy in grads_in:
            copy.start()
        for group in range(2):
            move_rows(grad_groups.at[2 * core + group], input_out.at[group, half_rows(core, rows)])
        for copy in spread:
            copy.arrived()
        square = jnp.zeros((), jnp.float32)
        for index in range(devices):
            values = downs[index].astype(jnp.float32)
            square += jnp.sum(values * values)
            for block in range(strips // down_rows):
                values = units[index, block * down_rows : (block + 1) * down_rows].astype(jnp.float32)
                square += jnp.sum(values * values)
                matrix, run = block // 2, block % 2
                at = (run * devices + index) * down_rows
                gate_up[matrix, :, at : at + down_rows] = values.T.astype(jnp.bfloat16)
        for copy in first + second:
            copy.arrived()
        total = combined[:, plane].astype(jnp.float32)
        for index in (1, 2):
            total += head_landing[index].astype(jnp.float32)
        mine[...] = total.astype(jnp.bfloat16)
        for copy in heads_back:
            copy.start()
        gathered[place] = mine[place]
        total = outs_in[:, columns_of(plane, columns)].astype(jnp.float32)
        for index in (1, 2):
            total += output_landing[index].astype(jnp.float32)
        output_out[...] = total
        square += jnp.sum(total * total)
        for copy in heads_back:
            copy.arrived()
        for copy in heads_over:
            copy.start()
        head_out[plane] = gathered[pl.ds(2 * plane, 2)]
        for copy in heads_over:
            copy.arrived()
        for index in range(planes):
            values = head_out[index].astype(jnp.float32)
            square += jnp.sum(values * values)
        square_parts[0] = jnp.full(square_parts.shape[1:], square, jnp.float32)
        squares_start()
        for index in range(count):
            squares_step(index)
        gain_out[...] = gain_parts[2 * count]
        square_out[...] = square_parts[2 * count]
        for copy in outputs_in + grads_in:
            copy.arrived()
        for copy in (
            third + first + second + [core_half] + rows_back + spread + heads_back + heads_over
            + outputs_in + grads_in
        ):
            copy.left()

    own = bf16(2, 2 * rows, width)
    return call(
        kernel,
        5,
        [(array, HBM) for array in head_terms + output_terms]
        + [(array, VMEM) for array in (unit_sum, down_sum, output_groups, input_grad, gain_sums)],
        [(own, VMEM)] * 2
        + [(bf16(planes, 2, sub_rows, columns), VMEM), (f32(HEAD, columns), VMEM)]
        + [(bf16(2, in_rows, devices * strips // 2), VMEM), (bf16(devices, down_rows, columns), VMEM)]
        + [(f32(8, width), VMEM), (f32(8, 128), VMEM)],
        [
            pltpu.VMEM((CHUNKS, rows, width), jnp.bfloat16),
            pltpu.VMEM((devices, planes, sub_rows, columns), jnp.bfloat16),
            pltpu.VMEM((devices, planes, sub_rows, HEAD), jnp.bfloat16),
            pltpu.VMEM((devices, sub_rows, columns), jnp.bfloat16),
            pltpu.VMEM((devices, sub_rows, columns), jnp.bfloat16),
            pltpu.VMEM((3, devices, sub_rows, columns), jnp.bfloat16),
            pltpu.VMEM((3, HEAD, columns), jnp.bfloat16),
            pltpu.VMEM((devices, sub_rows, columns), jnp.bfloat16),
            pltpu.VMEM((HEAD, columns), jnp.bfloat16),
            pltpu.VMEM((11, 8, width), jnp.float32),
            pltpu.VMEM((11, 8, 128), jnp.float32),
            pltpu.VMEM((devices, strips, in_rows), jnp.bfloat16),
            pltpu.VMEM((width, 3 * HEAD), jnp.float32),
            pltpu.VMEM((HEAD, width), jnp.float32),
            pltpu.VMEM((devices, planes, sub_rows, HEAD), jnp.bfloat16),
            pltpu.VMEM((HEAD, width), jnp.bfloat16),
        ]
        + wire_shapes(70),
        62,
    )


def unit_weight_grads(unit_grads, rows_in):
    shards, chunks, chips, tokens, columns = unit_grads[0].shape
    width = rows_in[0].shape[3]
    count = chunks * chips * tokens

    def kernel(late_units, late_rows, early_units, early_rows, out):
        total = dot_tn(late_units[0].reshape(count, columns), late_rows[...].reshape(count, width))
        total += dot_tn(early_units[0].reshape(count, columns), early_rows[...].reshape(count, width))
        out[0] = total.astype(jnp.bfloat16)

    block = pl.BlockSpec((1, chunks, chips, tokens, columns), lambda shard: (shard, 0, 0, 0, 0))
    rows_block = whole(rows_in[0].shape)
    return pl.pallas_call(
        kernel,
        grid=(shards,),
        in_specs=[block, rows_block] * 2,
        out_specs=pl.BlockSpec((1, columns, width), lambda shard: (shard, 0, 0)),
        out_shape=bf16(shards, columns, width),
        compiler_params=params(62),
    )(unit_grads[1], rows_in[1], unit_grads[0], rows_in[0])


def dot(left, right):
    return jnp.dot(left, right, preferred_element_type=jnp.float32)


def dot_t(left, right):
    return lax.dot_general(
        left, right, (((1,), (1,)), ((), ())), preferred_element_type=jnp.float32
    )


def dot_tn(left, right):
    return lax.dot_general(
        left, right, (((0,), (0,)), ((), ())), preferred_element_type=jnp.float32
    )


def spin(values, cosine, sine):
    halfway = values.shape[1] // 2
    first, second = values[:, :halfway], values[:, halfway:]
    return jnp.concatenate(
        [first * cosine - second * sine, second * cosine + first * sine], axis=1
    )


def spin_back(values, cosine, sine):
    return spin(values, cosine, -sine)


def whole(shape):
    return pl.BlockSpec(shape, lambda *_: (0,) * len(shape), pipeline_mode=pl.Buffered(1))


def params(megabytes):
    return pltpu.CompilerParams(vmem_limit_bytes=megabytes * MB)


def seen(place_q, place_k, chunk, count, tokens, lengths_ref, chip):
    query_index = tokens * chunk + place_q
    key_index = place_k[:, :count]
    ahead_or_here = key_index <= query_index
    if tokens * (chunk + 1) <= PROMPT:
        return ahead_or_here

    def segment(index):
        found = jnp.full(index.shape, -1, jnp.int32)
        for slot in range(NCONT):
            found = jnp.where(index >= PROMPT + slot * CONT, slot, found)
        return found

    key_segment, query_segment = segment(key_index), segment(query_index)
    end = jnp.full(key_index.shape, PROMPT, jnp.int32)
    for slot in range(NCONT):
        end = jnp.where(
            key_segment == slot, PROMPT + slot * CONT + lengths_ref[chip, slot], end
        )
    alive = key_index < end
    return ahead_or_here & ((key_segment < 0) | ((key_segment == query_segment) & alive))


def token_dot(left, right):
    return lax.dot_general(
        left.reshape(-1, left.shape[-1]),
        right.reshape(-1, right.shape[-1]),
        (((0,), (0,)), ((), ())),
        preferred_element_type=jnp.float32,
    )


def exchange(value, axis):
    return lax.all_to_all(value, axis, split_axis=0, concat_axis=0, tiled=True)


def plane_device(
    activations,
    cotangent,
    continuation_lengths,
    query_weight,
    key_weight,
    value_weight,
    output_weight,
    gate_weight,
    up_weight,
    down_weight,
    attention_gain,
    feedforward_gain,
    moment_query,
    moment_key,
    moment_value,
    moment_output,
    moment_gate,
    moment_up,
    moment_down,
    moment_attention,
    moment_feedforward,
):
    devices, planes = lax.axis_size("dp"), lax.axis_size("fsdp")
    place, plane = lax.axis_index("dp"), lax.axis_index("fsdp")
    core = place % 2
    low = jnp.bfloat16
    kv_width = KV_HEADS * HEAD
    tokens = activations.shape[1]
    half = tokens // 2

    in_rows = query_weight.shape[0]
    sub_rows = in_rows // planes
    spread = devices * sub_rows

    mixed_kv = jnp.stack([key_weight.astype(low), value_weight.astype(low)], axis=1)
    block = jnp.concatenate([query_weight.astype(low).reshape(in_rows, 2, HEAD), mixed_kv], axis=2)
    head_block = block.reshape(planes, sub_rows, 2, 2 * HEAD).swapaxes(1, 2)

    strip = 128
    runs = gate_weight.shape[1] // (devices * strip)
    units = runs * strip * planes
    gate_up = jnp.stack(
        [
            gate_weight.astype(low).reshape(in_rows, runs, devices, strip),
            up_weight.astype(low).reshape(in_rows, runs, devices, strip),
        ]
    )
    gate_up = gate_up.transpose(3, 1, 0, 2, 4).reshape(devices, in_rows, 2 * runs * strip)
    down_columns = down_weight.shape[1]
    down = down_weight.astype(low).reshape(devices, strip, down_columns)

    gain_one, gain_two = attention_gain[None, :], feedforward_gain[None, :]
    length_block = jnp.zeros((8, 128), jnp.int32).at[:2, :NCONT].set(continuation_lengths)
    own_inputs, own_grads, rows_all, head_weight, head_output, feed_own, all_lengths = start_up(
        activations,
        cotangent,
        head_block,
        output_weight.astype(low),
        gate_up,
        down,
        length_block,
        gain_one,
    )

    first_core = place - core
    lengths = jnp.stack(
        [
            pick(pick(all_lengths, (first_core ^ mask) + plane // 2), plane % 2)[:NCONT]
            for mask in (0, SIDE_A, SIDE_B, SIDE_A + SIDE_B)
        ]
    )

    inside = jnp.concatenate(
        [core * half + jnp.arange(half), (1 - core) * half + jnp.arange(half)]
    ).astype(jnp.int32)
    order = (tokens * jnp.arange(CHUNKS, dtype=jnp.int32)[:, None] + inside[None, :]).reshape(-1)
    cosine, sine = rope_angles(token_places(order))
    cosine = cosine.reshape(2, 2, tokens, HEAD // 2)
    sine = sine.reshape(2, 2, tokens, HEAD // 2)
    place_q, place_k = inside[:, None], order[None, :]
    blocks = plane ^ jnp.arange(CHUNKS, dtype=jnp.int32)

    states, mixed, middle, normed_two, normed_late, grads_late, feed_weights = attend_and_norm(
        rows_all,
        own_grads,
        feed_own,
        head_weight,
        cosine,
        sine,
        lengths,
        (place_q, place_k),
        head_output,
        own_inputs,
        gain_two,
    )
    (
        grads_early,
        normed_early,
        branch_late,
        down_sum,
        unit_grads,
        back_early,
        out_parts,
        middle_grad,
        gain_sum,
    ) = feed_forward(normed_two, normed_late, grads_late, feed_weights, middle, own_grads, gain_two, units)
    down_sum = lax.psum_scatter(down_sum, "fsdp", scatter_dimension=0, tiled=False)
    unit_sum = unit_weight_grads(unit_grads, (normed_early, normed_late))
    unit_sum = lax.psum_scatter(unit_sum, "fsdp", scatter_dimension=0, tiled=False)
    head_grads, branch_early, output_groups, own_input_grad, gain_sums = attend_back(
        states,
        lengths,
        (place_q, place_k),
        head_output,
        head_weight,
        cosine,
        sine,
        branch_late,
        back_early,
        out_parts,
        middle,
        own_grads,
        own_inputs,
        middle_grad,
        (gain_one, gain_two),
    )

    outputs, input_grad, block, output_owned, gate_up_owned, downs_owned, gain_totals, squares = finish(
        [rows_all[1], head_grads[1], rows_all[0], head_grads[0]],
        [mixed[1], branch_late, mixed[0], branch_early],
        unit_sum,
        down_sum.reshape(devices, strip, down_columns),
        output_groups,
        own_input_grad,
        jnp.stack([gain_sums[0], gain_sums[1] + gain_sum]),
    )
    block = block.swapaxes(1, 2).reshape(in_rows, 2, 2 * HEAD)
    query_owned = block[:, :, :HEAD].reshape(in_rows, 2 * HEAD)
    key_owned, value_owned = block[:, 0, HEAD:], block[:, 1, HEAD:]
    down_owned = downs_owned.reshape(devices * strip, down_columns)

    owner_grads = [
        owned.astype(jnp.float32)
        for owned in (
            query_owned,
            key_owned,
            value_owned,
            output_owned,
            gate_up_owned[0],
            gate_up_owned[1],
            down_owned,
        )
    ]
    attention_total, feedforward_total = gain_totals[0], gain_totals[1]
    square_total = squares[0, 0]
    square_sum = (
        square_total
        + jnp.sum(attention_total * attention_total)
        + jnp.sum(feedforward_total * feedforward_total)
    )
    grad_norm = jnp.sqrt(square_sum)
    entry_count = 2 * D * D + 2 * D * kv_width + 3 * D * FF + 2 * D
    limit = clip_level * math.sqrt(entry_count)
    factor = limit / jnp.maximum(grad_norm, limit)
    gradients = owner_grads + [attention_total, feedforward_total]
    old_moments = [
        moment_query,
        moment_key,
        moment_value,
        moment_output,
        moment_gate,
        moment_up,
        moment_down,
        moment_attention,
        moment_feedforward,
    ]
    old_params = [
        query_weight,
        key_weight,
        value_weight,
        output_weight,
        gate_weight,
        up_weight,
        down_weight,
        attention_gain,
        feedforward_gain,
    ]
    new_moments = [
        0.5 * moment + 0.5 * factor * gradient for moment, gradient in zip(old_moments, gradients)
    ]
    new_params = []
    for at, param in enumerate(old_params):
        if at < 7:
            new_params.append(param - step_size * (new_moments[at] + decay_rate * param))
        else:
            new_params.append(param - gain_step * new_moments[at])
    return (outputs, input_grad, grad_norm, *new_moments, *new_params)


def solution(mesh):
    whole_groups_on_planes = mesh.shape["dp"] == HEADS and mesh.shape["fsdp"] == KV_HEADS
    body = plane_device if whole_groups_on_planes else on_device
    placed = (
        P("dp", "fsdp", None),
        P("dp", "fsdp", None),
        P("dp", None),
        P("dp", "fsdp"),
        P("dp", "fsdp"),
        P("dp", "fsdp"),
        P("dp", "fsdp"),
        P("dp", "fsdp"),
        P("dp", "fsdp"),
        P("dp", "fsdp"),
        P(),
        P(),
        P("dp", "fsdp"),
        P("dp", "fsdp"),
        P("dp", "fsdp"),
        P("dp", "fsdp"),
        P("dp", "fsdp"),
        P("dp", "fsdp"),
        P("dp", "fsdp"),
        P(),
        P(),
    )
    return jax.shard_map(
        body,
        mesh=mesh,
        in_specs=placed,
        out_specs=(
            P("dp", "fsdp", None),
            P("dp", "fsdp", None),
            P(),
            P("dp", "fsdp"),
            P("dp", "fsdp"),
            P("dp", "fsdp"),
            P("dp", "fsdp"),
            P("dp", "fsdp"),
            P("dp", "fsdp"),
            P("dp", "fsdp"),
            P(),
            P(),
            P("dp", "fsdp"),
            P("dp", "fsdp"),
            P("dp", "fsdp"),
            P("dp", "fsdp"),
            P("dp", "fsdp"),
            P("dp", "fsdp"),
            P("dp", "fsdp"),
            P(),
            P(),
        ),
        check_vma=False,
    )
```
